32 devices in a mesh: dp: 16 (over z, y, x), mp: 2 (over core).
Axes of the slice: x: 2, y: 2, z: 4, core: 2. Of those that a mesh axis runs over, the one named last changes fastest.
Arguments:
- sentence_layer_entry: bfloat16 [8192, 768], P('dp'), may hold values from -6 to 6
- sentence_word_ids: int32 [8192], P('dp'), may hold values from 0 to 31999, as said below
- picture_tile_activations: bfloat16 [512, 145, 768], P(('dp', 'mp')), may hold values from -6 to 6
- picture_detail_flag: int32 [512], P(('dp', 'mp')), may hold values 0 or 1
- matched_picture_ids: int32 [512], P('dp'), may hold values from 0 to 511, each once
- mixer_layernorm_gamma: float32 [768], replicated, may hold values from 0.5 to 1.5
- mixer_layernorm_offset: float32 [768], replicated, may hold values from -1.5 to 1.5
- mixer_triple_matrix: bfloat16 [3, 768, 768], P(None, None, 'mp'), may hold values from -0.21875 to 0.21875
- mixer_pair_offsets: float32 [2, 768], P(None, 'mp'), may hold values from -1.5 to 1.5
- mixer_result_matrix: bfloat16 [768, 768], P('mp'), may hold values from -0.4375 to 0.4375
- mixer_result_offset: float32 [768], replicated, may hold values from -1.5 to 1.5
- perceptron_layernorm_gamma: float32 [768], replicated, may hold values from 0.5 to 1.5
- perceptron_layernorm_offset: float32 [768], replicated, may hold values from -1.5 to 1.5
- widening_matrix: bfloat16 [768, 3072], P(None, 'mp'), may hold values from -0.21875 to 0.21875
- widening_offset: float32 [3072], P('mp'), may hold values from -1.5 to 1.5
- narrowing_matrix: bfloat16 [3072, 768], P('mp'), may hold values from -0.109375 to 0.109375
- narrowing_offset: float32 [768], replicated, may hold values from -1.5 to 1.5
- sharpening_log: float32 [1], replicated, may hold values from 3.7 to 4.2
- locked_layernorm_gammas: float32 [2, 768], replicated, may hold values from 0.5 to 1.5
- locked_mixer_triple_matrix: bfloat16 [3, 768, 768], replicated, may hold values from -0.21875 to 0.21875
- locked_mixer_result_matrix: bfloat16 [768, 768], replicated, may hold values from -0.875 to 0.875
- locked_widening_matrix: bfloat16 [768, 3072], replicated, may hold values from -0.21875 to 0.21875
- locked_narrowing_matrix: bfloat16 [3072, 768], replicated, may hold values from -0.109375 to 0.109375
Outputs:
- training_error: float32 [1], replicated
- grad_input: float32 [8192, 768], P('dp')
- grad_qkv: float32 [3, 768, 768], P(None, None, 'mp')
- grad_b_qv: float32 [2, 768], P(None, 'mp')
- grad_w_out: float32 [768, 768], P('mp')
- grad_b_out: float32 [768], replicated
- grad_w_up: float32 [768, 3072], P(None, 'mp')
- grad_b_up: float32 [3072], P('mp')
- grad_w_down: float32 [3072, 768], P('mp')
- grad_b_down: float32 [768], replicated
- grad_ln1_gain: float32 [768], replicated
- grad_ln1_bias: float32 [768], replicated
- grad_ln2_gain: float32 [768], replicated
- grad_ln2_bias: float32 [768], replicated
- grad_temperature: float32 [1], replicated
The draws below stay inside these ranges and needn't reach their ends.
Inputs may be any that keep to these rules, and one draw needn't show every extreme that they name: `sentence_word_ids`: in each caption of 16 positions the nonzero ids form a prefix of 2 or more positions and 0 fills the rest; in every draw some caption has no 0 and some caption has exactly 2 nonzero ids.
All inputs are finite; a program needn't handle non-finite values. No bound on the sum of `picture_detail_flag` on one device may be relied on, other than what follows from the above.
Results may differ from the reference program's by a relative error of at most 0.0095.
The reference program's roundings to bfloat16 on the way count: a program that leaves them out, or rounds other values in their place, can miss the bound.
Values may be sent and summed in bfloat16 or wider, within the bound.
No kernel may reach another device: no remote copies, remote signals or barrier semaphores. Data moves between devices by JAX's collectives and lax.ppermute only.
A program may use at most 128 MiB of HBM per device.

```python
import jax
import jax.numpy as jnp
from jax import lax

D = 768
HEADS = 12
HEAD = 64
FF = 3072
CAP_LEN = 16
IMG_TOK = 145
LOW_TOK = 50
VOCAB = 32000
PAIRS_DEV = 32
PAIRS = 512
TEXT_TOK = 8192
N_DP = 16


def draw_sentence_word_ids(key, part):
    key = jax.random.fold_in(key, 11)
    len_key, token_key, full_key = jax.random.split(key, 3)
    lengths = jax.random.randint(len_key, (PAIRS,), 2, CAP_LEN + 1)
    full_at = jax.random.randint(full_key, (), 0, PAIRS)
    short_at = (full_at + 1) % PAIRS
    places = jnp.arange(PAIRS)
    lengths = jnp.where(places == full_at, CAP_LEN, lengths)
    lengths = jnp.where(places == short_at, 2, lengths)
    token_ids = jax.random.randint(token_key, (PAIRS, CAP_LEN), 1, VOCAB)
    top_place = (places[:, None] == full_at) & (jnp.arange(CAP_LEN)[None, :] == 0)
    token_ids = jnp.where(top_place, VOCAB - 1, token_ids)
    token_ids = jnp.where(jnp.arange(CAP_LEN)[None, :] < lengths[:, None], token_ids, 0)
    return token_ids.reshape(PAIRS * CAP_LEN).astype(jnp.int32)


def with_ends(entries, key, smallest, top_value):
    place = [jax.random.randint(jax.random.fold_in(key, axis), (), 0, length) for axis, length in enumerate(entries.shape)]
    longest = entries.shape.index(max(entries.shape))
    beside = place[:longest] + [(place[longest] + 1) % entries.shape[longest]] + place[longest + 1:]
    return entries.at[tuple(place)].set(smallest).at[tuple(beside)].set(top_value)


def shard_levels(stream_key, shape, cuts, low, largest):
    def one(position, shards_of):
        steps = jax.random.uniform(jax.random.fold_in(jax.random.fold_in(stream_key, 6), position), (shards_of,), jnp.float32, low / len(cuts), largest / len(cuts))
        return jnp.repeat(jnp.exp(steps), shape[position] // shards_of).reshape((-1,) + (1,) * (len(shape) - position - 1))

    level = one(*cuts[0])
    for cut in cuts[1:]:
        level = level * one(*cut)
    return level


def centred(own_key, dims, scale, reach, cuts=(), kind=jnp.bfloat16):
    level = shard_levels(own_key, dims, cuts, -0.22, 0.18) if cuts else 1.0
    result = jax.random.normal(own_key, dims, jnp.float32) * scale * level
    return jnp.minimum(jnp.maximum(result, -reach), reach).astype(kind)


def setup_inputs(seed: int = 0) -> dict:
    keys = jax.random.split(jax.random.key(seed), 24)
    sentence_layer_entry = centred(keys[0], (TEXT_TOK, D), 1.0, 6.0, ((0, 16),))
    sentence_word_ids = draw_sentence_word_ids(jax.random.fold_in(keys[23], 71), 0)
    picture_tile_activations = centred(keys[2], (PAIRS, IMG_TOK, D), 1.0, 6.0, ((0, 32),))
    picture_detail_flag = with_ends((jax.random.randint(keys[3], (PAIRS,), 0, 10) < 3).astype(jnp.int32), jax.random.fold_in(keys[3], 1), 0, 1)
    matched_picture_ids = jax.random.permutation(keys[4], PAIRS).astype(jnp.int32)
    mixer_layernorm_gamma = jnp.clip(1.0 + 0.1 * jax.random.normal(keys[5], (D,), jnp.float32), 0.5, 1.5)
    mixer_layernorm_offset = centred(keys[6], (D,), 0.3, 1.5, (), jnp.float32)
    mixer_triple_matrix = centred(keys[7], (3, D, D), D ** -0.5, 0.21875, ((2, 2),))
    mixer_pair_offsets = centred(keys[8], (2, D), 0.3, 1.5, ((1, 2),), jnp.float32)
    mixer_result_matrix = centred(keys[9], (D, D), (D // 4) ** -0.5, 0.4375, ((0, 2),))
    mixer_result_offset = centred(keys[10], (D,), 0.3, 1.5, (), jnp.float32)
    perceptron_layernorm_gamma = jnp.clip(1.0 + 0.1 * jax.random.normal(keys[11], (D,), jnp.float32), 0.5, 1.5)
    perceptron_layernorm_offset = centred(keys[12], (D,), 0.3, 1.5, (), jnp.float32)
    widening_matrix = centred(keys[13], (D, FF), D ** -0.5, 0.21875, ((1, 2),))
    widening_offset = centred(keys[14], (FF,), 0.3, 1.5, ((0, 2),), jnp.float32)
    narrowing_matrix = centred(keys[15], (FF, D), FF ** -0.5, 0.109375, ((0, 2),))
    narrowing_offset = centred(keys[16], (D,), 0.3, 1.5, (), jnp.float32)
    sharpening_log = jnp.clip(jax.random.uniform(keys[17], (1,), jnp.float32, 3.7, 4.2), 3.7, 4.2)
    locked_layernorm_gammas = jnp.clip(1.0 + 0.1 * jax.random.normal(keys[18], (2, D), jnp.float32), 0.5, 1.5)
    locked_mixer_triple_matrix = centred(keys[19], (3, D, D), D ** -0.5, 0.21875)
    locked_mixer_result_matrix = centred(keys[20], (D, D), (D // 16) ** -0.5, 0.875)
    locked_widening_matrix = centred(keys[21], (D, FF), D ** -0.5, 0.21875)
    locked_narrowing_matrix = centred(keys[22], (FF, D), FF ** -0.5, 0.109375)
    return dict(sentence_layer_entry=sentence_layer_entry, sentence_word_ids=sentence_word_ids, picture_tile_activations=picture_tile_activations, picture_detail_flag=picture_detail_flag, matched_picture_ids=matched_picture_ids, mixer_layernorm_gamma=mixer_layernorm_gamma, mixer_layernorm_offset=mixer_layernorm_offset, mixer_triple_matrix=mixer_triple_matrix, mixer_pair_offsets=mixer_pair_offsets, mixer_result_matrix=mixer_result_matrix, mixer_result_offset=mixer_result_offset, perceptron_layernorm_gamma=perceptron_layernorm_gamma, perceptron_layernorm_offset=perceptron_layernorm_offset, widening_matrix=widening_matrix, widening_offset=widening_offset, narrowing_matrix=narrowing_matrix, narrowing_offset=narrowing_offset, sharpening_log=sharpening_log, locked_layernorm_gammas=locked_layernorm_gammas, locked_mixer_triple_matrix=locked_mixer_triple_matrix, locked_mixer_result_matrix=locked_mixer_result_matrix, locked_widening_matrix=locked_widening_matrix, locked_narrowing_matrix=locked_narrowing_matrix)


EPS_TEXT = 1e-05
EPS_UNIT = 1e-06
MASKED_SCORE = -1e+30
PRECISE = lax.Precision.HIGHEST

@jax.custom_vjp
def low(v):
    return lax.optimization_barrier(v.astype(jnp.bfloat16)).astype(jnp.float32)

@jax.custom_vjp
def low_back(v):
    return v

def low_keep(v):
    return (low(v), None)

def low_pass(kept, grad):
    return (grad,)

def back_keep(v):
    return (v, None)

def back_low(kept, grad):
    return (low(grad),)
low.defvjp(low_keep, low_pass)
low_back.defvjp(back_keep, back_low)

def matmul_high(left, right):
    return jnp.dot(left, right, precision=PRECISE, preferred_element_type=jnp.float32)

def einsum_high(form, left, right):
    return jnp.einsum(form, left, right, precision=PRECISE, preferred_element_type=jnp.float32)

def layer_norm(values, gain, shift, epsilon):
    centered = values - lax.optimization_barrier(jnp.mean(values, axis=-1, keepdims=True))
    variance = lax.optimization_barrier(jnp.mean(centered * centered, axis=-1, keepdims=True))
    return centered * lax.rsqrt(variance + epsilon) * gain + shift

def gelu_exact(values):
    return jax.nn.gelu(values, approximate=False)

def image_block(tokens, live_len, locked_layernorm_gammas, locked_mixer_triple_matrix, locked_mixer_result_matrix, locked_widening_matrix, locked_narrowing_matrix):
    batch_size, seq_len, model_width = tokens.shape
    normed = low(layer_norm(tokens, locked_layernorm_gammas[0], 0.0, EPS_UNIT))

    def project(weight):
        return low(einsum_high('bsd,de->bse', normed, weight)).reshape(batch_size, seq_len, HEADS, HEAD)
    queries, keys_in, values = (project(locked_mixer_triple_matrix[0]), project(locked_mixer_triple_matrix[1]), project(locked_mixer_triple_matrix[2]))
    scores = einsum_high('bqhe,bkhe->bhqk', queries, keys_in) * HEAD ** (-0.5)
    key_live = jnp.arange(seq_len, dtype=jnp.int32)[None, :] < live_len[:, None]
    scores = jnp.where(key_live[:, None, None, :], scores, MASKED_SCORE)
    soft_weights = low(jax.nn.softmax(scores, axis=-1))
    mixed_heads = low(einsum_high('bhqk,bkhe->bqhe', soft_weights, values)).reshape(batch_size, seq_len, model_width)
    residual = tokens + einsum_high('bsc,cd->bsd', mixed_heads, locked_mixer_result_matrix)
    normed2 = low(layer_norm(residual, locked_layernorm_gammas[1], 0.0, EPS_UNIT))
    hidden = low(gelu_exact(einsum_high('bsd,df->bsf', normed2, locked_widening_matrix)))
    output = residual + einsum_high('bsf,fd->bsd', hidden, locked_narrowing_matrix)
    pool_weight = key_live.astype(jnp.float32) / live_len.astype(jnp.float32)[:, None]
    pooled = lax.optimization_barrier(jnp.sum(output * pool_weight[:, :, None], axis=1))
    return low(pooled * lax.rsqrt(lax.optimization_barrier(jnp.sum(pooled * pooled, axis=-1, keepdims=True)) + EPS_UNIT))

def text_block(rows, valid, learned_tensors):
    mixer_layernorm_gamma, mixer_layernorm_offset, mixer_triple_matrix, mixer_pair_offsets, mixer_result_matrix, mixer_result_offset, perceptron_layernorm_gamma, perceptron_layernorm_offset, widening_matrix, widening_offset, narrowing_matrix, narrowing_offset = learned_tensors
    groups = valid.shape[0]

    def to_heads(values):
        return values.reshape(groups, CAP_LEN, HEADS, HEAD)
    normed = low(layer_norm(rows, mixer_layernorm_gamma, mixer_layernorm_offset, EPS_TEXT))
    queries = to_heads(low_back(low(matmul_high(normed, mixer_triple_matrix[0]) + mixer_pair_offsets[0])))
    keys_in = to_heads(low_back(low(matmul_high(normed, mixer_triple_matrix[1]))))
    values = to_heads(low_back(low(matmul_high(normed, mixer_triple_matrix[2]) + mixer_pair_offsets[1])))
    scores = low_back(einsum_high('gqhe,gkhe->ghqk', queries, keys_in) * HEAD ** (-0.5))
    scores = jnp.where(valid[:, None, None, :], scores, MASKED_SCORE)
    soft_weights = low(jax.nn.softmax(scores, axis=-1))
    mixed_heads = low_back(low(einsum_high('ghqk,gkhe->gqhe', soft_weights, values)))
    mixed_rows = mixed_heads.reshape(groups * CAP_LEN, D)
    residual = rows + low_back(matmul_high(mixed_rows, mixer_result_matrix) + mixer_result_offset)
    normed2 = low(layer_norm(residual, perceptron_layernorm_gamma, perceptron_layernorm_offset, EPS_TEXT))
    hidden = low(gelu_exact(low_back(matmul_high(normed2, widening_matrix) + widening_offset)))
    output = residual + low_back(matmul_high(hidden, narrowing_matrix) + narrowing_offset)
    valid_f = valid.astype(jnp.float32)
    pool_weight = valid_f / lax.optimization_barrier(jnp.sum(valid_f, axis=1, keepdims=True))
    pooled = lax.optimization_barrier(jnp.sum(output.reshape(groups, CAP_LEN, D) * pool_weight[:, :, None], axis=1))
    return pooled * lax.rsqrt(lax.optimization_barrier(jnp.sum(pooled * pooled, axis=-1, keepdims=True)) + EPS_UNIT)

def paired_matching_loss(sentence_normalized_matrix, picture_feature_matrix, sharpening_log, matched_picture_ids):
    text_low = low(sentence_normalized_matrix)
    angular_agreement_matrix = low_back(matmul_high(text_low, picture_feature_matrix.T))
    pairwise_score_matrix = jnp.exp(sharpening_log[0]) * angular_agreement_matrix
    row_lse = jax.nn.logsumexp(pairwise_score_matrix, axis=1)
    col_lse = jax.nn.logsumexp(pairwise_score_matrix, axis=0)
    positive = jnp.sum(jnp.take_along_axis(pairwise_score_matrix, matched_picture_ids[:, None], axis=1))
    return (jnp.sum(row_lse) + jnp.sum(col_lse) - 2.0 * positive) / (2.0 * PAIRS)

def reference(sentence_layer_entry, sentence_word_ids, picture_tile_activations, picture_detail_flag, matched_picture_ids, mixer_layernorm_gamma, mixer_layernorm_offset, mixer_triple_matrix, mixer_pair_offsets, mixer_result_matrix, mixer_result_offset, perceptron_layernorm_gamma, perceptron_layernorm_offset, widening_matrix, widening_offset, narrowing_matrix, narrowing_offset, sharpening_log, locked_layernorm_gammas, locked_mixer_triple_matrix, locked_mixer_result_matrix, locked_widening_matrix, locked_narrowing_matrix):
    image_live = jnp.where(picture_detail_flag == 1, IMG_TOK, LOW_TOK).astype(jnp.int32)
    vit_f = (locked_mixer_triple_matrix.astype(jnp.float32), locked_mixer_result_matrix.astype(jnp.float32), locked_widening_matrix.astype(jnp.float32), locked_narrowing_matrix.astype(jnp.float32))

    def image_group(pieces):
        return image_block(pieces[0].astype(jnp.float32), pieces[1], locked_layernorm_gammas, vit_f[0], vit_f[1], vit_f[2], vit_f[3])
    picture_feature_matrix = lax.map(image_group, (picture_tile_activations.reshape(N_DP, PAIRS_DEV, IMG_TOK, D), image_live.reshape(N_DP, PAIRS_DEV))).reshape(PAIRS, D)
    valid = (sentence_word_ids != 0).reshape(N_DP, PAIRS_DEV, CAP_LEN)
    learned_tensors = (mixer_layernorm_gamma, mixer_layernorm_offset, mixer_triple_matrix.astype(jnp.float32), mixer_pair_offsets, mixer_result_matrix.astype(jnp.float32), mixer_result_offset, perceptron_layernorm_gamma, perceptron_layernorm_offset, widening_matrix.astype(jnp.float32), widening_offset, narrowing_matrix.astype(jnp.float32), narrowing_offset)
    sentence_feature_matrix = sentence_layer_entry.astype(jnp.float32)

    def primal_evaluation(rows, weights, temp_value):

        def group_fn(pieces):
            return text_block(pieces[0], pieces[1], weights)
        pooled = lax.map(jax.checkpoint(group_fn), (rows.reshape(N_DP, PAIRS_DEV * CAP_LEN, D), valid)).reshape(PAIRS, D)
        return paired_matching_loss(pooled, picture_feature_matrix, temp_value, matched_picture_ids)
    training_error, reverse_derivative_rule = jax.vjp(primal_evaluation, sentence_feature_matrix, learned_tensors, sharpening_log)
    grad_rows, grad_params, grad_temp = reverse_derivative_rule(jnp.ones_like(training_error))
    return (training_error.reshape(1), grad_rows, grad_params[2], grad_params[3], grad_params[4], grad_params[5], grad_params[8], grad_params[9], grad_params[10], grad_params[11], grad_params[0], grad_params[1], grad_params[6], grad_params[7], grad_temp)
```

```python
import jax
import jax.numpy as jnp
from jax import lax
from jax.sharding import PartitionSpec as P

HEAD = 64
IMG_TOK = 145
LOW_TOK = 50


EPS_TEXT = 1e-05
EPS_UNIT = 1e-06
MASKED_SCORE = -1e30
BF16 = jnp.bfloat16
F32 = jnp.float32


def layer_norm(values, gain, shift, epsilon):
    centered = values - jnp.mean(values, axis=-1, keepdims=True)
    variance = jnp.mean(centered * centered, axis=-1, keepdims=True)
    return centered * lax.rsqrt(variance + epsilon) * gain + shift


def text_norm(values, gain, shift):
    return layer_norm(values, gain, shift, EPS_TEXT)


def gelu_exact(values):
    return jax.nn.gelu(values, approximate=False)


def mp_other(values):
    return lax.ppermute(values, "mp", [(0, 1), (1, 0)])


def mp_sum(values):
    return values + mp_other(values)


def dp_gather(values):
    size = lax.axis_size("dp")
    copies = jnp.broadcast_to(values[None], (size,) + values.shape)
    return lax.all_to_all(copies, "dp", 0, 0, tiled=True)


def mp_join(values):
    other = mp_other(values)
    first = lax.axis_index("mp") == 0
    return jnp.concatenate(
        [jnp.where(first, values, other), jnp.where(first, other, values)], axis=1
    )


def image_block(
    tokens,
    live_len,
    locked_layernorm_gammas,
    locked_mixer_triple_matrix,
    locked_mixer_result_matrix,
    locked_widening_matrix,
    locked_narrowing_matrix,
):
    batch_size, seq_len, model_width = tokens.shape
    heads_all = model_width // HEAD
    tokens_f = tokens.astype(jnp.float32)
    normed = layer_norm(tokens_f, locked_layernorm_gammas[0], 0.0, EPS_UNIT).astype(jnp.bfloat16)

    def project(weight):
        return (
            jnp.einsum("bsd,de->bse", normed, weight, preferred_element_type=jnp.float32)
            .astype(jnp.bfloat16)
            .reshape(batch_size, seq_len, heads_all, HEAD)
        )

    queries, keys_in, values = (
        project(locked_mixer_triple_matrix[0]),
        project(locked_mixer_triple_matrix[1]),
        project(locked_mixer_triple_matrix[2]),
    )
    scores = jnp.einsum(
        "bqhe,bkhe->bhqk", queries, keys_in, preferred_element_type=jnp.float32
    ) * HEAD ** (-0.5)
    key_live = jnp.arange(seq_len, dtype=jnp.int32)[None, :] < live_len[:, None]
    scores = jnp.where(key_live[:, None, None, :], scores, MASKED_SCORE)
    soft_weights = jax.nn.softmax(scores, axis=-1).astype(jnp.bfloat16)
    mixed_heads = (
        jnp.einsum("bhqk,bkhe->bqhe", soft_weights, values, preferred_element_type=jnp.float32)
        .astype(jnp.bfloat16)
        .reshape(batch_size, seq_len, model_width)
    )
    residual = tokens_f + jnp.einsum(
        "bsc,cd->bsd", mixed_heads, locked_mixer_result_matrix, preferred_element_type=jnp.float32
    )
    normed2 = layer_norm(residual, locked_layernorm_gammas[1], 0.0, EPS_UNIT).astype(jnp.bfloat16)
    hidden = gelu_exact(
        jnp.einsum(
            "bsd,df->bsf", normed2, locked_widening_matrix, preferred_element_type=jnp.float32
        )
    ).astype(jnp.bfloat16)
    live = key_live.astype(jnp.float32)[:, :, None]
    return jnp.sum(residual * live, axis=1), jnp.sum(hidden.astype(F32) * live, axis=1)


def wide_dot(left, right):
    high = left.astype(BF16)
    rest = (left - high.astype(F32)).astype(BF16)
    return jnp.dot(high, right, preferred_element_type=F32) + jnp.dot(
        rest, right, preferred_element_type=F32
    )


def local(
    sentence_layer_entry,
    sentence_word_ids,
    picture_tile_activations,
    picture_detail_flag,
    matched_picture_ids,
    mixer_layernorm_gamma,
    mixer_layernorm_offset,
    mixer_triple_matrix,
    mixer_pair_offsets,
    mixer_result_matrix,
    mixer_result_offset,
    perceptron_layernorm_gamma,
    perceptron_layernorm_offset,
    widening_matrix,
    widening_offset,
    narrowing_matrix,
    narrowing_offset,
    sharpening_log,
    locked_layernorm_gammas,
    locked_mixer_triple_matrix,
    locked_mixer_result_matrix,
    locked_widening_matrix,
    locked_narrowing_matrix,
):
    captions = matched_picture_ids.shape[0]
    tokens = sentence_layer_entry.shape[0]
    cap_len = tokens // captions
    model_width = sentence_layer_entry.shape[1]
    local_heads = mixer_triple_matrix.shape[2] // HEAD
    local_width = local_heads * HEAD
    head_scale = HEAD ** (-0.5)
    devices = lax.axis_size("dp")
    all_pairs = captions * devices
    core = lax.axis_index("mp")
    valid = (sentence_word_ids != 0).reshape(captions, cap_len)
    valid_f = valid.astype(jnp.float32)
    count = jnp.sum(valid_f, axis=1, keepdims=True)
    local_images = picture_tile_activations.shape[0]
    img_block = 4
    image_live = jnp.where(picture_detail_flag == 1, IMG_TOK, LOW_TOK).astype(jnp.int32)

    def to_heads(values):
        return values.reshape(captions, cap_len, local_heads, HEAD)

    x_float = sentence_layer_entry.astype(jnp.float32)
    normed_f, norm1_pull = jax.vjp(
        text_norm, x_float, mixer_layernorm_gamma, mixer_layernorm_offset
    )
    normed = normed_f.astype(jnp.bfloat16)
    queries = to_heads(
        (
            jnp.dot(normed, mixer_triple_matrix[0], preferred_element_type=jnp.float32)
            + mixer_pair_offsets[0]
        ).astype(jnp.bfloat16)
    )
    keys_low = to_heads(
        jnp.dot(normed, mixer_triple_matrix[1], preferred_element_type=jnp.float32).astype(
            jnp.bfloat16
        )
    )
    values_low = to_heads(
        (
            jnp.dot(normed, mixer_triple_matrix[2], preferred_element_type=jnp.float32)
            + mixer_pair_offsets[1]
        ).astype(jnp.bfloat16)
    )
    scores = (
        jnp.einsum("gqhe,gkhe->ghqk", queries, keys_low, preferred_element_type=jnp.float32)
        * head_scale
    )
    scores = jnp.where(valid[:, None, None, :], scores, MASKED_SCORE)
    soft_f = jax.nn.softmax(scores, axis=-1)
    soft_low = soft_f.astype(jnp.bfloat16)
    mixed_heads = jnp.einsum(
        "ghqk,gkhe->gqhe", soft_low, values_low, preferred_element_type=jnp.float32
    ).astype(jnp.bfloat16)
    mixed_rows = mixed_heads.reshape(tokens, local_width)
    attended = mp_sum(
        jnp.dot(mixed_rows, mixer_result_matrix, preferred_element_type=jnp.float32)
    )

    def image_group(pieces):
        return image_block(
            pieces[0],
            pieces[1],
            locked_layernorm_gammas,
            locked_mixer_triple_matrix,
            locked_mixer_result_matrix,
            locked_widening_matrix,
            locked_narrowing_matrix,
        )

    resid_sum, hidden_sum = lax.map(
        image_group,
        (
            picture_tile_activations.reshape(
                local_images // img_block, img_block, picture_tile_activations.shape[1], model_width
            ),
            image_live.reshape(local_images // img_block, img_block),
        ),
    )
    resid_sum = resid_sum.reshape(local_images, model_width)
    hidden_sum = hidden_sum.reshape(local_images, -1)
    image_pooled = (
        resid_sum + wide_dot(hidden_sum, locked_narrowing_matrix)
    ) / image_live.astype(F32)[:, None]
    image_emb = (
        image_pooled
        * lax.rsqrt(jnp.sum(image_pooled * image_pooled, axis=-1, keepdims=True) + EPS_UNIT)
    ).astype(BF16)
    all_images = mp_join(dp_gather(image_emb)).reshape(all_pairs, model_width)

    residual = x_float + attended + mixer_result_offset
    normed2_f, norm2_pull = jax.vjp(
        text_norm, residual, perceptron_layernorm_gamma, perceptron_layernorm_offset
    )
    normed2 = normed2_f.astype(jnp.bfloat16)
    pre_act = (
        jnp.dot(normed2, widening_matrix, preferred_element_type=jnp.float32) + widening_offset
    )
    hidden_f, gelu_pull = jax.vjp(gelu_exact, pre_act)
    hidden = hidden_f.astype(jnp.bfloat16)

    def caption_sum(rows):
        return jnp.sum(
            rows.astype(F32).reshape(captions, cap_len, rows.shape[1]) * valid_f[:, :, None], axis=1
        )

    hidden_sums = caption_sum(hidden)
    branch_two = mp_sum(wide_dot(hidden_sums, narrowing_matrix))
    pooled = (caption_sum(residual) + branch_two) / count + narrowing_offset
    inverse = lax.rsqrt(jnp.sum(pooled * pooled, axis=-1, keepdims=True) + EPS_UNIT)
    text_unit = pooled * inverse
    text_emb = text_unit.astype(jnp.bfloat16)
    all_hidden_sums = dp_gather(hidden_sums.astype(BF16)).reshape(all_pairs, -1)

    scale = jnp.exp(sharpening_log[0])
    logits = scale * jnp.einsum(
        "cd,nd->cn", text_emb, all_images, preferred_element_type=jnp.float32
    )
    powers = jnp.exp(logits)
    row_sum = jnp.sum(powers, axis=1, keepdims=True)
    col_sum = jnp.sum(dp_gather(jnp.sum(powers, axis=0)), axis=0)
    is_positive = (
        matched_picture_ids[:, None] == jnp.arange(all_pairs, dtype=jnp.int32)[None, :]
    ).astype(F32)
    positive = jnp.sum(is_positive * logits)
    row_part = jnp.sum(jnp.log(row_sum)) - 2.0 * positive
    col_part = jnp.sum(jnp.log(col_sum))
    score_derivative = (
        powers / row_sum + powers / col_sum[None, :] - 2.0 * is_positive
    ) / (2.0 * all_pairs)
    temp_grad = jnp.sum(score_derivative * logits)
    text_grad = jnp.dot(
        (score_derivative * scale).astype(BF16), all_images, preferred_element_type=jnp.float32
    )
    grad_caption = (
        text_grad - text_unit * jnp.sum(text_unit * text_grad, axis=-1, keepdims=True)
    ) * (inverse / count)
    grad_caption_low = grad_caption.astype(BF16)

    half = captions // 2
    mine = lax.dynamic_slice_in_dim(grad_caption_low, core * half, half, 0)
    all_caption_grads = mp_join(dp_gather(mine)).reshape(all_pairs, model_width)
    grad_w_down = jnp.einsum(
        "cf,cd->fd", all_hidden_sums, all_caption_grads, preferred_element_type=jnp.float32
    )
    grad_b_down = jnp.sum(grad_caption_low.astype(F32) * count, axis=0)

    def spread(rows):
        return (rows[:, None, :] * valid_f[:, :, None]).reshape(tokens, rows.shape[1])

    (grad_pre,) = gelu_pull(
        spread(
            jnp.einsum(
                "td,fd->tf", grad_caption_low, narrowing_matrix, preferred_element_type=jnp.float32
            )
        )
    )
    grad_pre_low = grad_pre.astype(jnp.bfloat16)
    grad_b_up = jnp.sum(grad_pre_low.astype(jnp.float32), axis=0)
    grad_w_up = jnp.einsum("td,tf->df", normed2, grad_pre_low, preferred_element_type=jnp.float32)
    grad_normed2 = mp_sum(
        jnp.einsum("tf,df->td", grad_pre_low, widening_matrix, preferred_element_type=jnp.float32)
    )
    grad_res_norm, grad_ln2_gain, grad_ln2_bias = norm2_pull(grad_normed2)
    grad_residual = spread(grad_caption) + grad_res_norm
    grad_branch1 = grad_residual.astype(jnp.bfloat16)
    grad_b_out = jnp.sum(grad_branch1.astype(jnp.float32), axis=0)
    grad_w_out = jnp.einsum(
        "tc,td->cd", mixed_rows, grad_branch1, preferred_element_type=jnp.float32
    )
    grad_mixed = to_heads(
        jnp.einsum(
            "td,cd->tc", grad_branch1, mixer_result_matrix, preferred_element_type=jnp.float32
        ).astype(jnp.bfloat16)
    )
    grad_soft = jnp.einsum(
        "gqhe,gkhe->ghqk", grad_mixed, values_low, preferred_element_type=jnp.float32
    )
    grad_values = jnp.einsum(
        "ghqk,gqhe->gkhe", soft_low, grad_mixed, preferred_element_type=jnp.float32
    ).astype(jnp.bfloat16)
    grad_scores = (
        soft_f * (grad_soft - jnp.sum(grad_soft * soft_f, axis=-1, keepdims=True))
    ).astype(jnp.bfloat16)
    grad_queries = (
        jnp.einsum("ghqk,gkhe->gqhe", grad_scores, keys_low, preferred_element_type=jnp.float32)
        * head_scale
    ).astype(jnp.bfloat16)
    grad_keys = (
        jnp.einsum("ghqk,gqhe->gkhe", grad_scores, queries, preferred_element_type=jnp.float32)
        * head_scale
    ).astype(jnp.bfloat16)
    flat_grads = (
        grad_queries.reshape(tokens, local_width),
        grad_keys.reshape(tokens, local_width),
        grad_values.reshape(tokens, local_width),
    )
    grad_qkv = jnp.stack(
        [
            jnp.einsum("td,tc->dc", normed, part_grad, preferred_element_type=jnp.float32)
            for part_grad in flat_grads
        ]
    )
    grad_b_qv = jnp.stack(
        [
            jnp.sum(flat_grads[0].astype(jnp.float32), axis=0),
            jnp.sum(flat_grads[2].astype(jnp.float32), axis=0),
        ]
    )
    normed_terms = sum(
        jnp.einsum(
            "tc,dc->td", flat_grads[part], mixer_triple_matrix[part], preferred_element_type=F32
        )
        for part in range(3)
    )
    grad_normed = mp_sum(normed_terms)
    grad_in_norm, grad_ln1_gain, grad_ln1_bias = norm1_pull(grad_normed)
    grad_input = grad_residual + grad_in_norm

    big = lax.psum((grad_qkv.astype(BF16), grad_w_out.astype(BF16), grad_w_up.astype(BF16)), "dp")
    small = (
        grad_b_qv,
        grad_b_out,
        grad_b_up,
        grad_b_down,
        grad_ln1_gain,
        grad_ln1_bias,
        grad_ln2_gain,
        grad_ln2_bias,
        temp_grad.reshape(1),
        row_part.reshape(1),
    )
    packed = jnp.concatenate([part.reshape(-1) for part in small])
    padding = -packed.shape[0] % 1024
    packed = jnp.pad(packed, (0, padding)).reshape(-1, 128)
    packed = jnp.sum(dp_gather(packed), axis=0).reshape(-1)
    sums, start = [], 0
    for part in small:
        sums.append(packed[start : start + part.size].reshape(part.shape))
        start += part.size
    training_error = (sums[9] + col_part) / (2.0 * all_pairs)
    return (
        training_error,
        grad_input,
        big[0].astype(F32),
        sums[0],
        big[1].astype(F32),
        sums[1],
        big[2].astype(F32),
        sums[2],
        grad_w_down,
        sums[3],
        sums[4],
        sums[5],
        sums[6],
        sums[7],
        sums[8],
    )


def solution(mesh):
    placed = (
        P("dp", None),
        P("dp"),
        P(("dp", "mp"), None, None),
        P(("dp", "mp")),
        P("dp"),
        P(),
        P(),
        P(None, None, "mp"),
        P(None, "mp"),
        P("mp", None),
        P(),
        P(),
        P(),
        P(None, "mp"),
        P("mp"),
        P("mp", None),
        P(),
        P(),
        P(),
        P(),
        P(),
        P(),
        P(),
    )
    return jax.shard_map(
        local,
        mesh=mesh,
        in_specs=placed,
        out_specs=(
            P(),
            P("dp", None),
            P(None, None, "mp"),
            P(None, "mp"),
            P("mp", None),
            P(),
            P(None, "mp"),
            P("mp"),
            P("mp", None),
            P(),
            P(),
            P(),
            P(),
            P(),
            P(),
        ),
        check_vma=False,
    )
```

```python
import jax
import jax.numpy as jnp
from jax import lax
from jax.experimental import pallas as pl
from jax.experimental.pallas import tpu as pltpu
from jax.sharding import PartitionSpec as P

HEAD = 64
IMG_TOK = 145
LOW_TOK = 50


EPS_TEXT = 1e-05
EPS_UNIT = 1e-06
MASKED_SCORE = -1e30
BF16 = jnp.bfloat16
F32 = jnp.float32


def layer_norm(values, gain, shift, epsilon):
    centered = values - jnp.mean(values, axis=-1, keepdims=True)
    variance = jnp.mean(centered * centered, axis=-1, keepdims=True)
    return centered * lax.rsqrt(variance + epsilon) * gain + shift


def text_norm(values, gain, shift):
    return layer_norm(values, gain, shift, EPS_TEXT)


def gelu_exact(values):
    return jax.nn.gelu(values, approximate=False)


def mp_other(values):
    return lax.ppermute(values, "mp", [(0, 1), (1, 0)])


def mp_sum(values):
    return values + mp_other(values)


def dp_gather(values):
    size = lax.axis_size("dp")
    copies = jnp.broadcast_to(values[None], (size,) + values.shape)
    return lax.all_to_all(copies, "dp", 0, 0, tiled=True)


def mp_join(values):
    other = mp_other(values)
    first = lax.axis_index("mp") == 0
    return jnp.concatenate(
        [jnp.where(first, values, other), jnp.where(first, other, values)], axis=1
    )


HIGH_ROWS = 160
LOW_ROWS = 64
TILE = 256
PAIR = 2 * HEAD
NT = (((1,), (1,)), ((), ()))
VMEM_LIMIT = 56 * 1024 * 1024


def dot(left, right):
    return jnp.dot(left, right, preferred_element_type=F32)


def wide_dot(left, right):
    high = left.astype(BF16)
    rest = (left - high.astype(F32)).astype(BF16)
    return dot(high, right) + dot(rest, right)


def standard(values, epsilon):
    centered = values - jnp.mean(values, axis=-1, keepdims=True)
    variance = jnp.mean(centered * centered, axis=-1, keepdims=True)
    return centered * lax.rsqrt(variance + epsilon)


def gelu(values):
    return (0.5 * values) * (1.0 + lax.erf(values * (0.5**0.5)))


def image_kernel(
    flag_ref,
    token_ref,
    gain_ref,
    triple_hbm,
    result_hbm,
    widen_hbm,
    narrow_hbm,
    out_ref,
    packed,
    queries,
    keys,
    values,
    triple,
    result,
    widen,
    narrow,
    resid_sum,
    hidden_sum,
    starts,
    sems,
):
    images, _, width = token_ref.shape
    hidden = widen.shape[1]
    pairs = (
        (triple_hbm, triple),
        (result_hbm, result),
        (widen_hbm, widen),
        (narrow_hbm, narrow),
    )
    copies = [
        pltpu.make_async_copy(source, target, sems.at[place])
        for place, (source, target) in enumerate(pairs)
    ]
    for copy in copies:
        copy.start()
    resid_sum[...] = jnp.zeros_like(resid_sum)
    hidden_sum[...] = jnp.zeros_like(hidden_sum)

    tail = IMG_TOK // 16 * 16

    def pack(image, start):
        start = pl.multiple_of(start, 16)
        starts[image] = start
        high = flag_ref[image] == 1

        @pl.when(high)
        def _():
            packed[pl.ds(start, tail), :] = token_ref[image, 0:tail, :]
            last = token_ref[image, tail:IMG_TOK, :].astype(F32)
            row = lax.broadcasted_iota(jnp.int32, (HIGH_ROWS - tail, width), 0)
            packed[pl.ds(start + tail, HIGH_ROWS - tail), :] = jnp.where(
                row == 0, last, 0.0
            ).astype(BF16)

        @pl.when(jnp.logical_not(high))
        def _():
            packed[pl.ds(start, LOW_ROWS), :] = token_ref[image, 0:LOW_ROWS, :]

        return start + jnp.where(high, HIGH_ROWS, LOW_ROWS)

    total = lax.fori_loop(0, images, pack, jnp.int32(0))
    packed[pl.ds(pl.multiple_of(total, 16), TILE), :] = jnp.zeros((TILE, width), BF16)
    tiles = lax.div(total + (TILE - 1), jnp.int32(TILE))

    copies[0].wait()

    def project(tile, carry):
        rows = pl.ds(pl.multiple_of(tile * TILE, TILE), TILE)
        normed = (standard(packed[rows, :].astype(F32), EPS_UNIT) * gain_ref[0:1, :]).astype(BF16)
        queries[rows, :] = (dot(normed, triple[0]) * HEAD ** (-0.5)).astype(BF16)
        keys[rows, :] = dot(normed, triple[1]).astype(BF16)
        values[rows, :] = dot(normed, triple[2]).astype(BF16)
        return carry

    lax.fori_loop(0, tiles, project, 0)

    def attend(start, count, live):
        rows = pl.ds(start, count)
        left = lax.broadcasted_iota(jnp.int32, (count, PAIR), 1) < HEAD
        key_live = lax.broadcasted_iota(jnp.int32, (2 * count, count), 1) < live
        for pair in range(width // PAIR):
            lanes = slice(pair * PAIR, (pair + 1) * PAIR)
            q, k, v = queries[rows, lanes], keys[rows, lanes], values[rows, lanes]
            zero, one = jnp.zeros_like(q), jnp.ones_like(v)
            both = jnp.concatenate([jnp.where(left, q, zero), jnp.where(left, zero, q)], axis=0)
            scores = lax.dot_general(both, k, NT, preferred_element_type=F32)
            scores = jnp.where(key_live, scores, MASKED_SCORE)
            powers = jnp.exp(scores - jnp.max(scores, axis=-1, keepdims=True)).astype(BF16)
            first = dot(powers[:count], jnp.where(left, v, one))
            second = dot(powers[count:], jnp.where(left, one, v))
            sums = pltpu.roll(jnp.where(left, second, first), HEAD, 1)
            queries[rows, lanes] = (jnp.where(left, first, second) / sums).astype(BF16)

    def mix(image, carry):
        start = pl.multiple_of(starts[image], 16)
        high = flag_ref[image] == 1

        @pl.when(high)
        def _():
            attend(start, HIGH_ROWS, IMG_TOK)

        @pl.when(jnp.logical_not(high))
        def _():
            attend(start, LOW_ROWS, LOW_TOK)

        return carry

    lax.fori_loop(0, images, mix, 0)

    slot = lax.broadcasted_iota(jnp.int32, (images, 1), 0)
    begin = jnp.zeros((images, 1), jnp.int32)
    live = jnp.zeros((images, 1), jnp.int32)
    for image in range(images):
        begin = jnp.where(slot == image, starts[image], begin)
        live = jnp.where(
            slot == image, jnp.where(flag_ref[image] == 1, IMG_TOK, LOW_TOK), live
        )
    copies[1].wait()
    copies[2].wait()

    def perceptron(tile, carry):
        base = pl.multiple_of(tile * TILE, TILE)
        rows = pl.ds(base, TILE)
        place = base + lax.broadcasted_iota(jnp.int32, (images, TILE), 1)
        pool = jnp.where((place >= begin) & (place < begin + live), 1.0, 0.0).astype(BF16)
        residual = packed[rows, :].astype(F32) + dot(queries[rows, :], result[...])
        upper = residual.astype(BF16)
        lower = (residual - upper.astype(F32)).astype(BF16)
        resid_sum[...] += dot(pool, upper) + dot(pool, lower)
        normed = (standard(residual, EPS_UNIT) * gain_ref[1:2, :]).astype(BF16)
        for chunk in range(hidden // width):
            lanes = slice(chunk * width, (chunk + 1) * width)
            units = gelu(dot(normed, widen[:, lanes])).astype(BF16)
            hidden_sum[:, lanes] += dot(pool, units)
        return carry

    lax.fori_loop(0, tiles, perceptron, 0)
    copies[3].wait()
    pooled = (resid_sum[...] + wide_dot(hidden_sum[...], narrow[...])) / live.astype(F32)
    out_ref[...] = (
        pooled * lax.rsqrt(jnp.sum(pooled * pooled, axis=-1, keepdims=True) + EPS_UNIT)
    ).astype(BF16)


def image_tower(flags, tokens, gains, triple, result, widen, narrow):
    images, _, width = tokens.shape
    rows = images * HIGH_ROWS + TILE
    outside = pl.BlockSpec(memory_space=pl.ANY)
    inside = pl.BlockSpec(memory_space=pltpu.VMEM)
    return pl.pallas_call(
        image_kernel,
        out_shape=jax.ShapeDtypeStruct((images, width), BF16),
        in_specs=[pl.BlockSpec(memory_space=pltpu.SMEM), inside, inside]
        + [outside] * 4,
        out_specs=inside,
        scratch_shapes=[pltpu.VMEM((rows, width), BF16)] * 4
        + [pltpu.VMEM(weight.shape, BF16) for weight in (triple, result, widen, narrow)]
        + [
            pltpu.VMEM((images, width), F32),
            pltpu.VMEM((images, widen.shape[1]), F32),
            pltpu.SMEM((images,), jnp.int32),
            pltpu.SemaphoreType.DMA((4,)),
        ],
        compiler_params=pltpu.CompilerParams(vmem_limit_bytes=VMEM_LIMIT),
        cost_estimate=pl.CostEstimate(
            flops=30_000_000_000, bytes_accessed=20_000_000, transcendentals=10_000_000
        ),
    )(flags, tokens, gains, triple, result, widen, narrow)


def local(
    sentence_layer_entry,
    sentence_word_ids,
    picture_tile_activations,
    picture_detail_flag,
    matched_picture_ids,
    mixer_layernorm_gamma,
    mixer_layernorm_offset,
    mixer_triple_matrix,
    mixer_pair_offsets,
    mixer_result_matrix,
    mixer_result_offset,
    perceptron_layernorm_gamma,
    perceptron_layernorm_offset,
    widening_matrix,
    widening_offset,
    narrowing_matrix,
    narrowing_offset,
    sharpening_log,
    locked_layernorm_gammas,
    locked_mixer_triple_matrix,
    locked_mixer_result_matrix,
    locked_widening_matrix,
    locked_narrowing_matrix,
):
    captions = matched_picture_ids.shape[0]
    tokens = sentence_layer_entry.shape[0]
    cap_len = tokens // captions
    model_width = sentence_layer_entry.shape[1]
    local_heads = mixer_triple_matrix.shape[2] // HEAD
    local_width = local_heads * HEAD
    head_scale = HEAD ** (-0.5)
    devices = lax.axis_size("dp")
    all_pairs = captions * devices
    core = lax.axis_index("mp")
    valid = (sentence_word_ids != 0).reshape(captions, cap_len)
    valid_f = valid.astype(jnp.float32)
    count = jnp.sum(valid_f, axis=1, keepdims=True)

    def to_heads(values):
        return values.reshape(captions, cap_len, local_heads, HEAD)

    x_float = sentence_layer_entry.astype(jnp.float32)
    normed_f, norm1_pull = jax.vjp(
        text_norm, x_float, mixer_layernorm_gamma, mixer_layernorm_offset
    )
    normed = normed_f.astype(jnp.bfloat16)
    queries = to_heads(
        (
            jnp.dot(normed, mixer_triple_matrix[0], preferred_element_type=jnp.float32)
            + mixer_pair_offsets[0]
        ).astype(jnp.bfloat16)
    )
    keys_low = to_heads(
        jnp.dot(normed, mixer_triple_matrix[1], preferred_element_type=jnp.float32).astype(
            jnp.bfloat16
        )
    )
    values_low = to_heads(
        (
            jnp.dot(normed, mixer_triple_matrix[2], preferred_element_type=jnp.float32)
            + mixer_pair_offsets[1]
        ).astype(jnp.bfloat16)
    )
    scores = (
        jnp.einsum("gqhe,gkhe->ghqk", queries, keys_low, preferred_element_type=jnp.float32)
        * head_scale
    )
    scores = jnp.where(valid[:, None, None, :], scores, MASKED_SCORE)
    soft_f = jax.nn.softmax(scores, axis=-1)
    soft_low = soft_f.astype(jnp.bfloat16)
    mixed_heads = jnp.einsum(
        "ghqk,gkhe->gqhe", soft_low, values_low, preferred_element_type=jnp.float32
    ).astype(jnp.bfloat16)
    mixed_rows = mixed_heads.reshape(tokens, local_width)
    attended = mp_sum(
        jnp.dot(mixed_rows, mixer_result_matrix, preferred_element_type=jnp.float32)
    )

    image_emb = image_tower(
        picture_detail_flag,
        picture_tile_activations,
        locked_layernorm_gammas,
        locked_mixer_triple_matrix,
        locked_mixer_result_matrix,
        locked_widening_matrix,
        locked_narrowing_matrix,
    )
    all_images = mp_join(dp_gather(image_emb)).reshape(all_pairs, model_width)

    residual = x_float + attended + mixer_result_offset
    normed2_f, norm2_pull = jax.vjp(
        text_norm, residual, perceptron_layernorm_gamma, perceptron_layernorm_offset
    )
    normed2 = normed2_f.astype(jnp.bfloat16)
    pre_act = (
        jnp.dot(normed2, widening_matrix, preferred_element_type=jnp.float32) + widening_offset
    )
    hidden_f, gelu_pull = jax.vjp(gelu_exact, pre_act)
    hidden = hidden_f.astype(jnp.bfloat16)

    def caption_sum(rows):
        return jnp.sum(
            rows.astype(F32).reshape(captions, cap_len, rows.shape[1]) * valid_f[:, :, None], axis=1
        )

    hidden_sums = caption_sum(hidden)
    branch_two = mp_sum(wide_dot(hidden_sums, narrowing_matrix))
    pooled = (caption_sum(residual) + branch_two) / count + narrowing_offset
    inverse = lax.rsqrt(jnp.sum(pooled * pooled, axis=-1, keepdims=True) + EPS_UNIT)
    text_unit = pooled * inverse
    text_emb = text_unit.astype(jnp.bfloat16)
    all_hidden_sums = dp_gather(hidden_sums.astype(BF16)).reshape(all_pairs, -1)

    scale = jnp.exp(sharpening_log[0])
    logits = scale * jnp.einsum(
        "cd,nd->cn", text_emb, all_images, preferred_element_type=jnp.float32
    )
    powers = jnp.exp(logits)
    row_sum = jnp.sum(powers, axis=1, keepdims=True)
    col_sum = jnp.sum(dp_gather(jnp.sum(powers, axis=0)), axis=0)
    is_positive = (
        matched_picture_ids[:, None] == jnp.arange(all_pairs, dtype=jnp.int32)[None, :]
    ).astype(F32)
    positive = jnp.sum(is_positive * logits)
    row_part = jnp.sum(jnp.log(row_sum)) - 2.0 * positive
    col_part = jnp.sum(jnp.log(col_sum))
    score_derivative = (
        powers / row_sum + powers / col_sum[None, :] - 2.0 * is_positive
    ) / (2.0 * all_pairs)
    temp_grad = jnp.sum(score_derivative * logits)
    text_grad = jnp.dot(
        (score_derivative * scale).astype(BF16), all_images, preferred_element_type=jnp.float32
    )
    grad_caption = (
        text_grad - text_unit * jnp.sum(text_unit * text_grad, axis=-1, keepdims=True)
    ) * (inverse / count)
    grad_caption_low = grad_caption.astype(BF16)

    half = captions // 2
    mine = lax.dynamic_slice_in_dim(grad_caption_low, core * half, half, 0)
    all_caption_grads = mp_join(dp_gather(mine)).reshape(all_pairs, model_width)
    grad_w_down = jnp.einsum(
        "cf,cd->fd", all_hidden_sums, all_caption_grads, preferred_element_type=jnp.float32
    )
    grad_b_down = jnp.sum(grad_caption_low.astype(F32) * count, axis=0)

    def spread(rows):
        return (rows[:, None, :] * valid_f[:, :, None]).reshape(tokens, rows.shape[1])

    (grad_pre,) = gelu_pull(
        spread(
            jnp.einsum(
                "td,fd->tf", grad_caption_low, narrowing_matrix, preferred_element_type=jnp.float32
            )
        )
    )
    grad_pre_low = grad_pre.astype(jnp.bfloat16)
    grad_b_up = jnp.sum(grad_pre_low.astype(jnp.float32), axis=0)
    grad_w_up = jnp.einsum("td,tf->df", normed2, grad_pre_low, preferred_element_type=jnp.float32)
    grad_normed2 = mp_sum(
        jnp.einsum("tf,df->td", grad_pre_low, widening_matrix, preferred_element_type=jnp.float32)
    )
    grad_res_norm, grad_ln2_gain, grad_ln2_bias = norm2_pull(grad_normed2)
    grad_residual = spread(grad_caption) + grad_res_norm
    grad_branch1 = grad_residual.astype(jnp.bfloat16)
    grad_b_out = jnp.sum(grad_branch1.astype(jnp.float32), axis=0)
    grad_w_out = jnp.einsum(
        "tc,td->cd", mixed_rows, grad_branch1, preferred_element_type=jnp.float32
    )
    grad_mixed = to_heads(
        jnp.einsum(
            "td,cd->tc", grad_branch1, mixer_result_matrix, preferred_element_type=jnp.float32
        ).astype(jnp.bfloat16)
    )
    grad_soft = jnp.einsum(
        "gqhe,gkhe->ghqk", grad_mixed, values_low, preferred_element_type=jnp.float32
    )
    grad_values = jnp.einsum(
        "ghqk,gqhe->gkhe", soft_low, grad_mixed, preferred_element_type=jnp.float32
    ).astype(jnp.bfloat16)
    grad_scores = (
        soft_f * (grad_soft - jnp.sum(grad_soft * soft_f, axis=-1, keepdims=True))
    ).astype(jnp.bfloat16)
    grad_queries = (
        jnp.einsum("ghqk,gkhe->gqhe", grad_scores, keys_low, preferred_element_type=jnp.float32)
        * head_scale
    ).astype(jnp.bfloat16)
    grad_keys = (
        jnp.einsum("ghqk,gqhe->gkhe", grad_scores, queries, preferred_element_type=jnp.float32)
        * head_scale
    ).astype(jnp.bfloat16)
    flat_grads = (
        grad_queries.reshape(tokens, local_width),
        grad_keys.reshape(tokens, local_width),
        grad_values.reshape(tokens, local_width),
    )
    grad_qkv = jnp.stack(
        [
            jnp.einsum("td,tc->dc", normed, part_grad, preferred_element_type=jnp.float32)
            for part_grad in flat_grads
        ]
    )
    grad_b_qv = jnp.stack(
        [
            jnp.sum(flat_grads[0].astype(jnp.float32), axis=0),
            jnp.sum(flat_grads[2].astype(jnp.float32), axis=0),
        ]
    )
    normed_terms = sum(
        jnp.einsum(
            "tc,dc->td", flat_grads[part], mixer_triple_matrix[part], preferred_element_type=F32
        )
        for part in range(3)
    )
    grad_normed = mp_sum(normed_terms)
    grad_in_norm, grad_ln1_gain, grad_ln1_bias = norm1_pull(grad_normed)
    grad_input = grad_residual + grad_in_norm

    big = lax.psum((grad_qkv.astype(BF16), grad_w_out.astype(BF16), grad_w_up.astype(BF16)), "dp")
    small = (
        grad_b_qv,
        grad_b_out,
        grad_b_up,
        grad_b_down,
        grad_ln1_gain,
        grad_ln1_bias,
        grad_ln2_gain,
        grad_ln2_bias,
        temp_grad.reshape(1),
        row_part.reshape(1),
    )
    packed = jnp.concatenate([part.reshape(-1) for part in small])
    padding = -packed.shape[0] % 1024
    packed = jnp.pad(packed, (0, padding)).reshape(-1, 128)
    packed = jnp.sum(dp_gather(packed), axis=0).reshape(-1)
    sums, start = [], 0
    for part in small:
        sums.append(packed[start : start + part.size].reshape(part.shape))
        start += part.size
    training_error = (sums[9] + col_part) / (2.0 * all_pairs)
    return (
        training_error,
        grad_input,
        big[0].astype(F32),
        sums[0],
        big[1].astype(F32),
        sums[1],
        big[2].astype(F32),
        sums[2],
        grad_w_down,
        sums[3],
        sums[4],
        sums[5],
        sums[6],
        sums[7],
        sums[8],
    )


def solution(mesh):
    placed = (
        P("dp", None),
        P("dp"),
        P(("dp", "mp"), None, None),
        P(("dp", "mp")),
        P("dp"),
        P(),
        P(),
        P(None, None, "mp"),
        P(None, "mp"),
        P("mp", None),
        P(),
        P(),
        P(),
        P(None, "mp"),
        P("mp"),
        P("mp", None),
        P(),
        P(),
        P(),
        P(),
        P(),
        P(),
        P(),
    )
    return jax.shard_map(
        local,
        mesh=mesh,
        in_specs=placed,
        out_specs=(
            P(),
            P("dp", None),
            P(None, None, "mp"),
            P(None, "mp"),
            P("mp", None),
            P(),
            P(None, "mp"),
            P("mp"),
            P("mp", None),
            P(),
            P(),
            P(),
            P(),
            P(),
            P(),
        ),
        check_vma=False,
    )
```

```python
import functools

import jax
import jax.numpy as jnp
from jax import lax
from jax.experimental import pallas as pl
from jax.experimental.pallas import tpu as pltpu
from jax.sharding import PartitionSpec as P

HEAD = 64
IMG_TOK = 145
LOW_TOK = 50
CAP_LEN = 16


EPS_TEXT = 1e-05
EPS_UNIT = 1e-06
MASKED_SCORE = -1e30
BF16 = jnp.bfloat16
F32 = jnp.float32


def mp_other(values):
    return lax.ppermute(values, "mp", [(0, 1), (1, 0)])


def dp_swap(values, mask):
    size = lax.axis_size("dp")
    return lax.ppermute(values, "dp", [(index, index ^ mask) for index in range(size)])


def group_steps(size):
    steps, stride = [], 1
    while stride < size:
        steps.append([stride, 2 * stride, 3 * stride])
        stride *= 4
    return steps


def gather_masks(steps):
    masks = [0]
    for step in steps:
        masks = [mask ^ base for mask in [0] + step for base in masks]
    return masks


def dp_parts(values, step):
    return [values] + [dp_swap(values, mask) for mask in step]


def dp_gather(values, steps, waits):
    for step, wait in zip(steps, waits):
        parts = dp_parts(values, step)
        shape = (len(parts) * values.shape[0], values.shape[1])
        (values,) = call(stack_kernel, parts, ((shape, values.dtype),), after=(wait,))
    return values


def dp_sum(values):
    mask = 1
    while mask < lax.axis_size("dp"):
        values = values + dp_swap(values, mask)
        mask *= 2
    return values


HIGH_ROWS = 160
LOW_ROWS = 64
TILE = 256
PAIR = 2 * HEAD
NT = (((1,), (1,)), ((), ()))
VMEM_LIMIT = 56 * 1024 * 1024
BUSY = 10**12


def dot(left, right):
    return jnp.dot(left, right, preferred_element_type=F32)


def wide_dot(left, right):
    high = left.astype(BF16)
    rest = (left - high.astype(F32)).astype(BF16)
    return dot(high, right) + dot(rest, right)


def standard(values, epsilon):
    centered = values - jnp.mean(values, axis=-1, keepdims=True)
    variance = jnp.mean(centered * centered, axis=-1, keepdims=True)
    return centered * lax.rsqrt(variance + epsilon)


def gelu(values):
    return (0.5 * values) * (1.0 + lax.erf(values * (0.5**0.5)))


def image_kernel(
    flag_ref,
    token_ref,
    gain_ref,
    triple_hbm,
    result_hbm,
    widen_hbm,
    narrow_hbm,
    out_ref,
    packed,
    queries,
    keys,
    values,
    triple,
    result,
    widen,
    narrow,
    resid_sum,
    hidden_sum,
    starts,
    sems,
):
    images, _, width = token_ref.shape
    hidden = widen.shape[1]
    pairs = (
        (triple_hbm, triple),
        (result_hbm, result),
        (widen_hbm, widen),
        (narrow_hbm, narrow),
    )
    copies = [
        pltpu.make_async_copy(source, target, sems.at[place])
        for place, (source, target) in enumerate(pairs)
    ]
    for copy in copies:
        copy.start()
    resid_sum[...] = jnp.zeros_like(resid_sum)
    hidden_sum[...] = jnp.zeros_like(hidden_sum)

    tail = IMG_TOK // 16 * 16

    def pack(image, start):
        start = pl.multiple_of(start, 16)
        starts[image] = start
        high = flag_ref[image] == 1

        @pl.when(high)
        def _():
            packed[pl.ds(start, tail), :] = token_ref[image, 0:tail, :]
            last = token_ref[image, tail:IMG_TOK, :].astype(F32)
            row = lax.broadcasted_iota(jnp.int32, (HIGH_ROWS - tail, width), 0)
            packed[pl.ds(start + tail, HIGH_ROWS - tail), :] = jnp.where(
                row == 0, last, 0.0
            ).astype(BF16)

        @pl.when(jnp.logical_not(high))
        def _():
            packed[pl.ds(start, LOW_ROWS), :] = token_ref[image, 0:LOW_ROWS, :]

        return start + jnp.where(high, HIGH_ROWS, LOW_ROWS)

    total = lax.fori_loop(0, images, pack, jnp.int32(0))
    packed[pl.ds(pl.multiple_of(total, 16), TILE), :] = jnp.zeros((TILE, width), BF16)
    tiles = lax.div(total + (TILE - 1), jnp.int32(TILE))

    copies[0].wait()

    def project(tile, carry):
        rows = pl.ds(pl.multiple_of(tile * TILE, TILE), TILE)
        normed = (standard(packed[rows, :].astype(F32), EPS_UNIT) * gain_ref[0:1, :]).astype(BF16)
        queries[rows, :] = (dot(normed, triple[0]) * HEAD ** (-0.5)).astype(BF16)
        keys[rows, :] = dot(normed, triple[1]).astype(BF16)
        values[rows, :] = dot(normed, triple[2]).astype(BF16)
        return carry

    lax.fori_loop(0, tiles, project, 0)

    def attend(start, count, live):
        rows = pl.ds(start, count)
        left = lax.broadcasted_iota(jnp.int32, (count, PAIR), 1) < HEAD
        key_live = lax.broadcasted_iota(jnp.int32, (2 * count, count), 1) < live
        for pair in range(width // PAIR):
            lanes = slice(pair * PAIR, (pair + 1) * PAIR)
            q, k, v = queries[rows, lanes], keys[rows, lanes], values[rows, lanes]
            zero, one = jnp.zeros_like(q), jnp.ones_like(v)
            both = jnp.concatenate([jnp.where(left, q, zero), jnp.where(left, zero, q)], axis=0)
            scores = lax.dot_general(both, k, NT, preferred_element_type=F32)
            scores = jnp.where(key_live, scores, MASKED_SCORE)
            powers = jnp.exp(scores - jnp.max(scores, axis=-1, keepdims=True)).astype(BF16)
            first = dot(powers[:count], jnp.where(left, v, one))
            second = dot(powers[count:], jnp.where(left, one, v))
            sums = pltpu.roll(jnp.where(left, second, first), HEAD, 1)
            queries[rows, lanes] = (jnp.where(left, first, second) / sums).astype(BF16)

    def mix(image, carry):
        start = pl.multiple_of(starts[image], 16)
        high = flag_ref[image] == 1

        @pl.when(high)
        def _():
            attend(start, HIGH_ROWS, IMG_TOK)

        @pl.when(jnp.logical_not(high))
        def _():
            attend(start, LOW_ROWS, LOW_TOK)

        return carry

    lax.fori_loop(0, images, mix, 0)

    slot = lax.broadcasted_iota(jnp.int32, (images, 1), 0)
    begin = jnp.zeros((images, 1), jnp.int32)
    live = jnp.zeros((images, 1), jnp.int32)
    for image in range(images):
        begin = jnp.where(slot == image, starts[image], begin)
        live = jnp.where(
            slot == image, jnp.where(flag_ref[image] == 1, IMG_TOK, LOW_TOK), live
        )
    copies[1].wait()
    copies[2].wait()

    def perceptron(tile, carry):
        base = pl.multiple_of(tile * TILE, TILE)
        rows = pl.ds(base, TILE)
        place = base + lax.broadcasted_iota(jnp.int32, (images, TILE), 1)
        pool = jnp.where((place >= begin) & (place < begin + live), 1.0, 0.0).astype(BF16)
        residual = packed[rows, :].astype(F32) + dot(queries[rows, :], result[...])
        upper = residual.astype(BF16)
        lower = (residual - upper.astype(F32)).astype(BF16)
        resid_sum[...] += dot(pool, upper) + dot(pool, lower)
        normed = (standard(residual, EPS_UNIT) * gain_ref[1:2, :]).astype(BF16)
        for chunk in range(hidden // width):
            lanes = slice(chunk * width, (chunk + 1) * width)
            units = gelu(dot(normed, widen[:, lanes])).astype(BF16)
            hidden_sum[:, lanes] += dot(pool, units)
        return carry

    lax.fori_loop(0, tiles, perceptron, 0)
    copies[3].wait()
    pooled = (resid_sum[...] + wide_dot(hidden_sum[...], narrow[...])) / live.astype(F32)
    out_ref[...] = (
        pooled * lax.rsqrt(jnp.sum(pooled * pooled, axis=-1, keepdims=True) + EPS_UNIT)
    ).astype(BF16)


def image_tower(flags, tokens, gains, triple, result, widen, narrow):
    images, _, width = tokens.shape
    rows = images * HIGH_ROWS + TILE
    outside = pl.BlockSpec(memory_space=pl.ANY)
    inside = pl.BlockSpec(memory_space=pltpu.VMEM)
    return pl.pallas_call(
        image_kernel,
        out_shape=jax.ShapeDtypeStruct((images, width), BF16),
        in_specs=[pl.BlockSpec(memory_space=pltpu.SMEM), inside, inside]
        + [outside] * 4,
        out_specs=inside,
        scratch_shapes=[pltpu.VMEM((rows, width), BF16)] * 4
        + [pltpu.VMEM(weight.shape, BF16) for weight in (triple, result, widen, narrow)]
        + [
            pltpu.VMEM((images, width), F32),
            pltpu.VMEM((images, widen.shape[1]), F32),
            pltpu.SMEM((images,), jnp.int32),
            pltpu.SemaphoreType.DMA((4,)),
        ],
        compiler_params=pltpu.CompilerParams(vmem_limit_bytes=VMEM_LIMIT),
        cost_estimate=pl.CostEstimate(
            flops=30_000_000_000, bytes_accessed=20_000_000, transcendentals=10_000_000
        ),
    )(flags, tokens, gains, triple, result, widen, narrow)


TN = (((0,), (0,)), ((), ()))
BLOCK = 128
ROOT_HALF = 0.5**0.5
DENSITY = 0.3989422804014327


def dot_t(left, right):
    return lax.dot_general(left, right, NT, preferred_element_type=F32)


def t_dot(left, right):
    return lax.dot_general(left, right, TN, preferred_element_type=F32)


def fetch(sources, targets, sems):
    copies = [
        pltpu.make_async_copy(source, target, sems.at[place])
        for place, (source, target) in enumerate(zip(sources, targets))
    ]
    for copy in copies:
        copy.start()
    return copies


def stack_kernel(*refs):
    rows = refs[0].shape[0]
    for place, ref in enumerate(refs[:-1]):
        refs[-1][place * rows : (place + 1) * rows, :] = ref[...]


def caption_pool(ids_ref, captions):
    ids_row = ids_ref[...].reshape(1, -1)
    tokens = ids_row.shape[1]
    shape = (captions, tokens)
    caption = lax.broadcasted_iota(jnp.int32, shape, 0)
    token = lax.broadcasted_iota(jnp.int32, shape, 1)
    inside = (token // (tokens // captions)) == caption
    return jnp.where(inside & (ids_row != 0), 1.0, 0.0)


def valid_column(pool):
    pool = pool.astype(BF16)
    return t_dot(pool, jnp.ones((pool.shape[0], 128), BF16))[:, 0:1]


def number_column(ref):
    shape = (ref.shape[0], 1)
    place = lax.broadcasted_iota(jnp.int32, shape, 0)
    column = jnp.zeros(shape, jnp.int32)
    for index in range(shape[0]):
        column = jnp.where(place == index, ref[index], column)
    return column


def as_row(ref):
    return ref[...].reshape(1, -1)


def pair_masks(rows, pair_width):
    return lax.broadcasted_iota(jnp.int32, (rows, pair_width), 1) < HEAD


def two_heads(values, left):
    zero = jnp.zeros_like(values)
    return jnp.concatenate(
        [jnp.where(left, values, zero), jnp.where(left, zero, values)], axis=0
    )


def text_mix_kernel(
    entry_ref,
    ids_ref,
    gain_ref,
    shift_ref,
    triple_ref,
    pair_ref,
    result_ref,
    normed_ref,
    qkv_ref,
    soft_ref,
    mixed_ref,
    part_ref,
):
    tokens = entry_ref.shape[0]
    width = result_ref.shape[0]
    normed = (
        standard(entry_ref[...].astype(F32), EPS_TEXT) * as_row(gain_ref) + as_row(shift_ref)
    ).astype(BF16)
    normed_ref[...] = normed
    qkv_ref[0] = (dot(normed, triple_ref[0]) + pair_ref[0:1, :]).astype(BF16)
    qkv_ref[1] = dot(normed, triple_ref[1]).astype(BF16)
    qkv_ref[2] = (dot(normed, triple_ref[2]) + pair_ref[1:2, :]).astype(BF16)
    ids = as_row(ids_ref)
    left = pair_masks(BLOCK, PAIR)
    shape = (2 * BLOCK, BLOCK)
    query_caption = lax.broadcasted_iota(jnp.int32, shape, 0) % BLOCK // CAP_LEN
    same = query_caption == lax.broadcasted_iota(jnp.int32, shape, 1) // CAP_LEN
    for block in range(tokens // BLOCK):
        rows = slice(block * BLOCK, (block + 1) * BLOCK)
        seen = same & (ids[:, rows] != 0)
        for pair in range(width // PAIR):
            lanes = slice(pair * PAIR, (pair + 1) * PAIR)
            scores = dot_t(two_heads(qkv_ref[0, rows, lanes], left), qkv_ref[1, rows, lanes])
            scores = jnp.where(seen, scores * HEAD ** (-0.5), MASKED_SCORE)
            powers = jnp.exp(scores - jnp.max(scores, axis=-1, keepdims=True))
            soft = powers / jnp.sum(powers, axis=-1, keepdims=True)
            soft_ref[block, pair] = soft
            low = soft.astype(BF16)
            value = qkv_ref[2, rows, lanes]
            mixed_ref[rows, lanes] = jnp.where(
                left, dot(low[:BLOCK], value), dot(low[BLOCK:], value)
            ).astype(BF16)
    part_ref[...] = dot(mixed_ref[...], result_ref[...])


def text_widen_kernel(
    entry_ref,
    own_ref,
    other_ref,
    result_offset_ref,
    gain_ref,
    shift_ref,
    widen_offset_ref,
    ids_ref,
    widen_hbm,
    narrow_hbm,
    residual_ref,
    normed_ref,
    slope_ref,
    sums_ref,
    resid_sum_ref,
    branch_ref,
    widen,
    narrow,
    hidden_sum,
    sems,
):
    captions = sums_ref.shape[0]
    width = entry_ref.shape[1]
    copies = fetch((widen_hbm, narrow_hbm), (widen, narrow), sems)
    residual = entry_ref[...].astype(F32) + (
        (own_ref[...] + other_ref[...]) + as_row(result_offset_ref)
    )
    residual_ref[...] = residual
    normed = (standard(residual, EPS_TEXT) * as_row(gain_ref) + as_row(shift_ref)).astype(BF16)
    normed_ref[...] = normed
    pool = caption_pool(ids_ref, captions).astype(BF16)
    widen_offset = as_row(widen_offset_ref)
    upper = residual.astype(BF16)
    resid_sum_ref[...] = dot(pool, upper) + dot(
        pool, (residual - upper.astype(F32)).astype(BF16)
    )
    valid = valid_column(pool)
    copies[0].wait()
    for chunk in range(widen.shape[1] // width):
        lanes = slice(chunk * width, (chunk + 1) * width)
        before = dot(normed, widen[:, lanes]) + widen_offset[:, lanes]
        share = 0.5 * (1.0 + lax.erf(before * ROOT_HALF))
        hidden_sum[:, lanes] = dot(pool, (before * share).astype(BF16))
        slope = share + before * (jnp.exp(-0.5 * before * before) * DENSITY)
        slope_ref[:, lanes] = slope * valid
    sums_ref[...] = hidden_sum[...].astype(BF16)
    copies[1].wait()
    branch_ref[...] = wide_dot(hidden_sum[...], narrow[...])


def logits_kernel(
    masks,
    index_ref,
    matched_ref,
    sharpen_ref,
    near_ref,
    far_ref,
    resid_sum_ref,
    own_ref,
    other_ref,
    narrow_offset_ref,
    ids_ref,
    images_ref,
    unit_ref,
    factor_ref,
    logits_ref,
    powers_ref,
    row_sum_ref,
    col_sum_ref,
    loss_ref,
):
    captions, pairs = logits_ref.shape
    rows = images_ref.shape[0] // (2 * len(masks))
    core = index_ref[1]
    for place, mask in enumerate(masks):
        start = (index_ref[0] ^ mask) * (2 * rows)
        images_ref[pl.ds(pl.multiple_of(start + core * rows, rows), rows), :] = near_ref[
            place * rows : (place + 1) * rows, :
        ]
        images_ref[pl.ds(pl.multiple_of(start + (1 - core) * rows, rows), rows), :] = far_ref[
            place * rows : (place + 1) * rows, :
        ]
    count = jnp.sum(caption_pool(ids_ref, captions), axis=1, keepdims=True)
    pooled = (resid_sum_ref[...] + (own_ref[...] + other_ref[...])) / count + as_row(
        narrow_offset_ref
    )
    inverse = lax.rsqrt(jnp.sum(pooled * pooled, axis=-1, keepdims=True) + EPS_UNIT)
    unit = pooled * inverse
    unit_ref[...] = unit
    factor_ref[...] = jnp.broadcast_to(inverse / count, factor_ref.shape)
    logits = jnp.exp(jnp.full((1, 1), sharpen_ref[0], F32)) * dot_t(unit.astype(BF16), images_ref[...])
    logits_ref[...] = logits
    powers = jnp.exp(logits)
    powers_ref[...] = powers
    row_sum = jnp.sum(powers, axis=1, keepdims=True)
    row_sum_ref[...] = jnp.broadcast_to(row_sum, row_sum_ref.shape)
    col_sum_ref[...] = jnp.broadcast_to(
        jnp.sum(powers, axis=0, keepdims=True)[None], col_sum_ref.shape
    )
    positive = number_column(matched_ref) == lax.broadcasted_iota(jnp.int32, (captions, pairs), 1)
    wanted = jnp.sum(jnp.where(positive, logits, 0.0), axis=1, keepdims=True)
    loss_ref[...] = jnp.broadcast_to(
        jnp.sum(jnp.log(row_sum) - 2.0 * wanted, axis=0, keepdims=True), loss_ref.shape
    )


def loss_grad_kernel(
    matched_ref,
    sharpen_ref,
    col_parts_ref,
    logits_ref,
    powers_ref,
    row_sum_ref,
    unit_ref,
    factor_ref,
    images_ref,
    ids_ref,
    loss_ref,
    narrow_hbm,
    slope_hbm,
    widen_hbm,
    grad_ref,
    low_ref,
    before_ref,
    part_ref,
    stat_ref,
    narrow,
    slope,
    widen,
    sems,
):
    captions, pairs = logits_ref.shape
    tokens, hidden = slope.shape
    width = grad_ref.shape[1]
    copies = fetch((narrow_hbm, slope_hbm, widen_hbm), (narrow, slope, widen), sems)
    logits, powers = logits_ref[...], powers_ref[...]
    col_sum = jnp.sum(col_parts_ref[...], axis=0)
    positive = number_column(matched_ref) == lax.broadcasted_iota(jnp.int32, (captions, pairs), 1)
    derivative = (
        powers / row_sum_ref[:, 0:1] + powers / col_sum - jnp.where(positive, 2.0, 0.0)
    ) / (2.0 * pairs)
    temperature = jnp.sum(
        jnp.sum(derivative * logits, axis=1, keepdims=True), axis=0, keepdims=True
    )
    col_loss = jnp.sum(jnp.log(col_sum), axis=1, keepdims=True)
    text = dot((derivative * jnp.exp(jnp.full((1, 1), sharpen_ref[0], F32))).astype(BF16), images_ref[...])
    unit = unit_ref[...]
    grad = (text - unit * jnp.sum(unit * text, axis=-1, keepdims=True)) * factor_ref[:, 0:1]
    grad_ref[...] = grad
    low = grad.astype(BF16)
    low_ref[...] = low
    copies[0].wait()
    copies[1].wait()
    copies[2].wait()
    ones = jnp.ones((8, tokens), BF16)
    part = jnp.zeros(part_ref.shape, F32)
    for chunk in range(hidden // width):
        lanes = slice(chunk * width, (chunk + 1) * width)
        back = dot_t(low, narrow[lanes, :])
        before = (
            (back[:, None, :] * slope[:, lanes].reshape(captions, CAP_LEN, width))
            .reshape(tokens, width)
            .astype(BF16)
        )
        before_ref[:, lanes] = before
        stat_ref[chunk : chunk + 1, :] = dot(ones, before)[0:1]
        part = part + dot_t(before, widen[:, lanes])
    part_ref[...] = part
    count = jnp.sum(caption_pool(ids_ref, captions), axis=1, keepdims=True)
    stat_ref[2:3, :] = jnp.sum(low.astype(F32) * count, axis=0, keepdims=True)
    lane = lax.broadcasted_iota(jnp.int32, (1, width), 1)
    stat_ref[3:4, :] = jnp.where(
        lane == 0,
        temperature,
        jnp.where(lane == 1, loss_ref[0:1, 0:1], jnp.where(lane == 2, col_loss, 0.0)),
    )
    stat_ref[4:8, :] = jnp.zeros((4, width), F32)


def deal(index_ref, first, second, outs):
    half = first.shape[0] // 2
    for place, (values, bit) in enumerate(((first, 1), (second, 2))):
        mine = index_ref[0] // bit % 2
        for ref, which in ((outs[2 * place], 1 - mine), (outs[2 * place + 1], mine)):
            ref[...] = values[pl.ds(pl.multiple_of(which * half, half), half), :]


def widen_grad_kernel(index_ref, normed_ref, before_ref, *refs):
    outs, (first, second) = refs[:4], refs[4:]
    width = first.shape[1]
    normed = normed_ref[...]
    first[...] = t_dot(normed, before_ref[:, :width]).astype(BF16)
    second[...] = t_dot(normed, before_ref[:, width:]).astype(BF16)
    deal(index_ref, first, second, outs)


def mixer_back_kernel(
    own_ref,
    other_ref,
    residual_ref,
    grad_ref,
    ids_ref,
    gain_ref,
    result_ref,
    qkv_hbm,
    soft_hbm,
    triple_hbm,
    grad_residual_ref,
    low_ref,
    flat_ref,
    part_ref,
    stat_ref,
    qkv,
    soft_all,
    triple,
    sems,
):
    tokens, width = residual_ref.shape
    captions = grad_ref.shape[0]
    local_width = result_ref.shape[0]
    copies = fetch((qkv_hbm, soft_hbm, triple_hbm), (qkv, soft_all, triple), sems)
    residual = residual_ref[...]
    centered = residual - jnp.mean(residual, axis=-1, keepdims=True)
    rate = lax.rsqrt(jnp.mean(centered * centered, axis=-1, keepdims=True) + EPS_TEXT)
    unit = centered * rate
    grad = own_ref[...] + other_ref[...]
    stat_ref[1:2, :] = jnp.sum(grad * unit, axis=0, keepdims=True)
    stat_ref[2:3, :] = jnp.sum(grad, axis=0, keepdims=True)
    scaled = grad * as_row(gain_ref)
    inner = rate * (
        scaled
        - jnp.mean(scaled, axis=-1, keepdims=True)
        - unit * jnp.mean(scaled * unit, axis=-1, keepdims=True)
    )
    spread = jnp.broadcast_to(
        grad_ref[...][:, None, :], (captions, tokens // captions, width)
    ).reshape(tokens, width)
    grad_residual = spread * valid_column(caption_pool(ids_ref, captions)) + inner
    grad_residual_ref[...] = grad_residual
    low = grad_residual.astype(BF16)
    low_ref[...] = low
    ones = jnp.ones((8, tokens), BF16)
    stat_ref[0:1, :] = dot(ones, low)[0:1]
    grad_mixed = dot_t(low, result_ref[...]).astype(BF16)
    for copy in copies:
        copy.wait()
    left = pair_masks(BLOCK, PAIR)
    for block in range(tokens // BLOCK):
        rows = slice(block * BLOCK, (block + 1) * BLOCK)
        for pair in range(local_width // PAIR):
            lanes = slice(pair * PAIR, (pair + 1) * PAIR)
            soft = soft_all[block, pair]
            mixed = two_heads(grad_mixed[rows, lanes], left)
            query, key = qkv[0, rows, lanes], qkv[1, rows, lanes]
            grad_soft = dot_t(mixed, qkv[2, rows, lanes])
            flat_ref[2, rows, lanes] = t_dot(soft.astype(BF16), mixed).astype(BF16)
            scores = (
                soft * (grad_soft - jnp.sum(grad_soft * soft, axis=-1, keepdims=True))
            ).astype(BF16)
            back = jnp.where(left, dot(scores[:BLOCK], key), dot(scores[BLOCK:], key))
            flat_ref[0, rows, lanes] = (back * HEAD ** (-0.5)).astype(BF16)
            flat_ref[1, rows, lanes] = (
                t_dot(scores, two_heads(query, left)) * HEAD ** (-0.5)
            ).astype(BF16)
    part_ref[...] = (
        dot_t(flat_ref[0], triple[0])
        + dot_t(flat_ref[1], triple[1])
        + dot_t(flat_ref[2], triple[2])
    )
    stat_ref[3:4, :local_width] = dot(ones, flat_ref[0])[0:1]
    stat_ref[3:4, local_width:] = dot(ones, flat_ref[2])[0:1]
    stat_ref[4:8, :] = jnp.zeros((4, width), F32)


def mixer_grad_kernel(index_ref, normed_ref, flat_ref, mixed_ref, low_ref, *refs):
    outs, (first, second) = refs[:4], refs[4:]
    half = flat_ref.shape[2]
    rows = first.shape[0] // 2
    normed = normed_ref[...]
    for part, (target, place) in enumerate(((first, 0), (first, rows), (second, 0))):
        grad = t_dot(normed, flat_ref[part]).astype(BF16)
        target[place : place + rows, :half] = grad[:rows]
        target[place : place + rows, half:] = grad[rows:]
    second[rows:, :] = t_dot(mixed_ref[...], low_ref[...]).astype(BF16)
    deal(index_ref, first, second, outs)


def narrow_grad_kernel(half, index_ref, sums_ref, near_ref, far_ref, out_ref, grads):
    width = grads.shape[1]
    core = index_ref[0]
    for place in range(near_ref.shape[0] // half):
        for ref, which in ((near_ref, core), (far_ref, 1 - core)):
            start = pl.multiple_of((2 * place + which) * half, half)
            grads[pl.ds(start, half), :] = ref[place * half : (place + 1) * half, :]
    for chunk in range(sums_ref.shape[1] // width):
        lanes = slice(chunk * width, (chunk + 1) * width)
        out_ref[lanes, :] = t_dot(sums_ref[:, lanes], grads[...])


def entry_grad_kernel(
    own_ref,
    other_ref,
    entry_ref,
    gain_ref,
    grad_residual_ref,
    loss_stat_ref,
    mixer_stat_ref,
    out_ref,
    pack_ref,
):
    entry = entry_ref[...].astype(F32)
    centered = entry - jnp.mean(entry, axis=-1, keepdims=True)
    rate = lax.rsqrt(jnp.mean(centered * centered, axis=-1, keepdims=True) + EPS_TEXT)
    unit = centered * rate
    grad = own_ref[...] + other_ref[...]
    pack_ref[0:8, :] = loss_stat_ref[...]
    pack_ref[8:16, :] = mixer_stat_ref[...]
    pack_ref[4:5, :] = jnp.sum(grad * unit, axis=0, keepdims=True)
    pack_ref[5:6, :] = jnp.sum(grad, axis=0, keepdims=True)
    scaled = grad * as_row(gain_ref)
    out_ref[...] = grad_residual_ref[...] + rate * (
        scaled
        - jnp.mean(scaled, axis=-1, keepdims=True)
        - unit * jnp.mean(scaled * unit, axis=-1, keepdims=True)
    )


def call(kernel, inside, shapes, outside=(), scratch=(), index=(), small=(), after=()):
    vmem = pl.BlockSpec(memory_space=pltpu.VMEM)
    extra = [pltpu.VMEM(array.shape, array.dtype) for array in outside]
    extra += list(scratch)
    if outside:
        extra += [pltpu.SemaphoreType.DMA((len(outside),))]
    index = [jnp.stack(index).astype(jnp.int32)] if index else []
    small = index + list(small)
    before = len(small) + len(inside) + len(outside)

    def body(*refs):
        kernel(*refs[:before], *refs[before + len(after) :])

    return pl.pallas_call(
        body,
        out_shape=[jax.ShapeDtypeStruct(shape, kind) for shape, kind in shapes],
        in_specs=[pl.BlockSpec(memory_space=pltpu.SMEM)] * len(small)
        + [vmem] * len(inside)
        + [pl.BlockSpec(memory_space=pl.ANY)] * (len(outside) + len(after)),
        out_specs=[vmem] * len(shapes),
        scratch_shapes=extra,
        compiler_params=pltpu.CompilerParams(vmem_limit_bytes=VMEM_LIMIT),
        cost_estimate=pl.CostEstimate(flops=BUSY, bytes_accessed=BUSY, transcendentals=0),
    )(*small, *inside, *outside, *after)


GROUP = 16
Z_STRIDE, Z_SIZE = 4, 4


def fold_kernel(index_ref, *refs):
    ins, outs = refs[:4], refs[4:]
    half = ins[0].shape[0] // 2
    for place, bit in ((0, 2), (1, 1)):
        total = ins[2 * place][...].astype(F32) + ins[2 * place + 1][...].astype(F32)
        upper = index_ref[0] // bit % 2 == 1
        low, high = total[:half], total[half:]
        outs[2 * place][...] = jnp.where(upper, low, high).astype(BF16)
        outs[2 * place + 1][...] = jnp.where(upper, high, low)


def cut_kernel(index_ref, *refs):
    ins, outs, total = refs[:4], refs[4:-1], refs[-1]
    rows = total.shape[0] // (2 * Z_SIZE)
    for place in range(2):
        total[pl.ds(place * rows * Z_SIZE, rows * Z_SIZE), :] = ins[2 * place][...] + ins[
            2 * place + 1
        ][...].astype(F32)
        for step in range(Z_SIZE):
            block = (index_ref[0] // Z_STRIDE % Z_SIZE) ^ step
            start = pl.multiple_of((place * Z_SIZE + block) * rows, rows)
            outs[step][place * rows : (place + 1) * rows, :] = total[
                pl.ds(start, rows), :
            ].astype(outs[step].dtype)


def add_kernel(own_ref, *refs):
    out_ref = refs[-1]
    rows = own_ref.shape[0]
    total = own_ref[...]
    for ref in refs[: Z_SIZE - 1]:
        total = total + ref[...].astype(F32)
    out_ref[:rows, :] = total.astype(out_ref.dtype)
    if out_ref.shape[0] > rows:
        out_ref[rows:, :] = refs[Z_SIZE - 1][...]


def join_kernel(extra, *refs):
    ins, out = refs[:Z_SIZE], refs[Z_SIZE]
    rows = (ins[0].shape[0] - extra) // 2
    start = 0
    for first, count in ((0, rows), (2 * rows, extra), (rows, rows)):
        for ref in ins:
            if count:
                out[start : start + count, :] = ref[first : first + count, :]
            start += count


def scatter_steps(dealt, place, extra=None):
    first_sent, first_kept, second_sent, second_kept = dealt
    rows, width = first_sent.shape
    after = yield
    arrived = (dp_swap(first_sent, 1), dp_swap(second_sent, 2))
    half = (rows // 2, width)
    first_sent, first_kept, second_sent, second_kept = call(
        fold_kernel,
        (first_kept, arrived[0], second_kept, arrived[1]),
        ((half, BF16), (half, F32), (half, BF16), (half, F32)),
        index=(place,),
        after=after,
    )
    after = yield first_kept
    arrived = (dp_swap(first_sent, 2), dp_swap(second_sent, 1))
    block = (rows // Z_SIZE, width)
    own, *sent = call(
        cut_kernel,
        (first_kept, arrived[0], second_kept, arrived[1]),
        ((block, F32),) + ((block, BF16),) * (Z_SIZE - 1),
        scratch=(pltpu.VMEM((rows, width), F32),),
        index=(place,),
        after=after,
    )
    after = yield own
    arrived = [dp_swap(values, step * Z_STRIDE) for step, values in enumerate(sent, 1)]
    size = lax.axis_size("dp")
    more = 0 if extra is None else extra.shape[0]
    if size > GROUP:
        (mine,) = call(add_kernel, (own, *arrived), ((own.shape, F32),), after=after)
        groups = [list(range(index, size, GROUP)) for index in range(GROUP)]
        mine = lax.psum(mine, "dp", axis_index_groups=groups).astype(BF16)
        if more:
            mine = jnp.concatenate([mine, extra], axis=0)
    else:
        (mine,) = call(
            add_kernel,
            (own, *arrived) + ((extra,) if more else ()),
            (((block[0] + more, width), BF16),),
            after=after,
        )
    after = yield mine
    pieces = [mine] + [dp_swap(mine, step * Z_STRIDE) for step in range(1, Z_SIZE)]
    (joined,) = call(
        functools.partial(join_kernel, more),
        pieces,
        (((Z_SIZE * (block[0] + more), width), BF16),),
        after=after,
    )
    cut = Z_SIZE * (block[0] // 2 + more)
    along_x, along_y = dp_swap(joined, 1), dp_swap(joined, 2)
    after = yield joined
    yield joined, along_x, along_y, dp_swap(along_y[:cut], 1), dp_swap(along_x[cut:], 2)


def block_home(index, block, outer, inner):
    high = (block // 8) ^ (index // outer % 2)
    middle = (block // 4 % 2) ^ (index // inner % 2)
    return high * 8 + middle * 4 + ((block % 4) ^ (index // Z_STRIDE % Z_SIZE))


def relative_blocks(refs, tensor):
    joined, along_x, along_y, first_far, second_far = refs
    size = second_far.shape[0]
    start = joined.shape[0] - size if tensor else 0
    if tensor:
        pieces = ((joined, start), (along_x, start), (along_y, start), (second_far, 0))
    else:
        pieces = ((joined, 0), (along_y, 0), (along_x, 0), (first_far, 0))
    rows = size // Z_SIZE
    for piece, (ref, start) in enumerate(pieces):
        for step in range(Z_SIZE):
            first = start + step * rows
            yield piece * Z_SIZE + step, rows, ref[first : first + rows, :]


def unpack_widen_kernel(index_ref, *refs):
    refs, (out_ref, extra_ref) = refs[:-2], refs[-2:]
    width = out_ref.shape[1] // 2
    for tensor, bits in ((0, (1, 2)), (1, (2, 1))):
        for block, rows, values in relative_blocks(refs, tensor):
            start = pl.multiple_of(block_home(index_ref[0], block, *bits) * rows, rows)
            out_ref[pl.ds(start, rows), tensor * width : (tensor + 1) * width] = values.astype(F32)
    first, count = refs[4].shape[0], extra_ref.shape[0] // 4
    for place, ref in enumerate(refs[:4]):
        extra_ref[place * count : (place + 1) * count, :] = ref[first : first + count, :]


def unpack_mixer_kernel(index_ref, *refs):
    refs, (triple_ref, result_ref) = refs[:-2], refs[-2:]
    half, split = triple_ref.shape[2], triple_ref.shape[1] // 2
    for block, rows, values in relative_blocks(refs, 0):
        home = block_home(index_ref[0], block, 1, 2)
        part, row = home // 8, pl.multiple_of(home % 8 * rows, rows)
        triple_ref[part, pl.ds(row, rows), :] = values[:, :half].astype(F32)
        triple_ref[part, pl.ds(split + row, rows), :] = values[:, half:].astype(F32)
    for block, rows, values in relative_blocks(refs, 1):
        home = block_home(index_ref[0], block, 2, 1)
        row = pl.multiple_of(home % 8 * rows, rows)

        @pl.when(home < 8)
        def _():
            triple_ref[2, pl.ds(row, rows), :] = values[:, :half].astype(F32)
            triple_ref[2, pl.ds(split + row, rows), :] = values[:, half:].astype(F32)

        @pl.when(home >= 8)
        def _():
            result_ref[pl.ds(row, rows), :] = values.astype(F32)


def local(
    sentence_layer_entry,
    sentence_word_ids,
    picture_tile_activations,
    picture_detail_flag,
    matched_picture_ids,
    mixer_layernorm_gamma,
    mixer_layernorm_offset,
    mixer_triple_matrix,
    mixer_pair_offsets,
    mixer_result_matrix,
    mixer_result_offset,
    perceptron_layernorm_gamma,
    perceptron_layernorm_offset,
    widening_matrix,
    widening_offset,
    narrowing_matrix,
    narrowing_offset,
    sharpening_log,
    locked_layernorm_gammas,
    locked_mixer_triple_matrix,
    locked_mixer_result_matrix,
    locked_widening_matrix,
    locked_narrowing_matrix,
):
    captions = matched_picture_ids.shape[0]
    tokens, model_width = sentence_layer_entry.shape
    local_width = mixer_result_matrix.shape[0]
    hidden = narrowing_matrix.shape[0]
    devices = lax.axis_size("dp")
    all_pairs = captions * devices
    place, core = lax.axis_index("dp"), lax.axis_index("mp")
    blocks = tokens // BLOCK
    full = (tokens, model_width)
    short = (captions, model_width)
    square = (model_width, model_width)
    half_square = (model_width // 2, model_width)
    dealt = ((half_square, BF16),) * 4

    steps = group_steps(devices)

    image_emb = image_tower(
        picture_detail_flag,
        picture_tile_activations,
        locked_layernorm_gammas,
        locked_mixer_triple_matrix,
        locked_mixer_result_matrix,
        locked_widening_matrix,
        locked_narrowing_matrix,
    )
    normed, qkv, soft, mixed, part = call(
        text_mix_kernel,
        (
            sentence_layer_entry,
            sentence_word_ids,
            mixer_layernorm_gamma,
            mixer_layernorm_offset,
            mixer_triple_matrix,
            mixer_pair_offsets,
            mixer_result_matrix,
        ),
        (
            (full, BF16),
            ((3, tokens, local_width), BF16),
            ((blocks, local_width // PAIR, 2 * BLOCK, BLOCK), F32),
            ((tokens, local_width), BF16),
            (full, F32),
        ),
        after=(image_emb,),
    )
    other = mp_other(part)
    near_images = dp_gather(image_emb, steps[:0:-1], [part] * (len(steps) - 1))
    residual, normed2, slope, hidden_sums, resid_sum, branch = call(
        text_widen_kernel,
        (
            sentence_layer_entry,
            part,
            other,
            mixer_result_offset,
            perceptron_layernorm_gamma,
            perceptron_layernorm_offset,
            widening_offset,
            sentence_word_ids,
        ),
        (
            (full, F32),
            (full, BF16),
            ((tokens, hidden), F32),
            ((captions, hidden), BF16),
            (short, F32),
            (short, F32),
        ),
        outside=(widening_matrix, narrowing_matrix),
        scratch=(pltpu.VMEM((captions, hidden), F32),),
        after=(near_images,),
    )

    near_images = dp_gather(near_images, steps[:1], (branch,))
    sums_parts = dp_parts(hidden_sums, steps[-1])
    images, unit, factor, logits, powers, row_sum, col_sum, row_loss = call(
        functools.partial(logits_kernel, gather_masks(steps[::-1])),
        (
            near_images,
            mp_other(near_images),
            resid_sum,
            branch,
            mp_other(branch),
            narrowing_offset,
            sentence_word_ids,
        ),
        (
            ((all_pairs, model_width), BF16),
            (short, F32),
            ((captions, 128), F32),
            ((captions, all_pairs), F32),
            ((captions, all_pairs), F32),
            ((captions, 128), F32),
            ((devices, 1, all_pairs), F32),
            ((8, 128), F32),
        ),
        index=(place, core),
        small=(matched_picture_ids, sharpening_log),
    )
    col_parts = lax.all_to_all(col_sum, "dp", 0, 0, tiled=True)
    for step in steps[-2::-1]:
        shape = (len(sums_parts) * sums_parts[0].shape[0], hidden)
        (joined_sums,) = call(stack_kernel, sums_parts, ((shape, BF16),), after=(unit,))
        sums_parts = dp_parts(joined_sums, step)
    grad_caption, grad_caption_low, grad_pre, part, loss_stat = call(
        loss_grad_kernel,
        (
            col_parts,
            logits,
            powers,
            row_sum,
            unit,
            factor,
            images,
            sentence_word_ids,
            row_loss,
        ),
        (
            (short, F32),
            (short, BF16),
            ((tokens, hidden), BF16),
            (full, F32),
            ((8, model_width), F32),
        ),
        outside=(narrowing_matrix, slope, widening_matrix),
        after=(joined_sums,),
        small=(matched_picture_ids, sharpening_log),
    )

    other = mp_other(part)
    widen_dealt = call(
        widen_grad_kernel,
        (normed2, grad_pre),
        dealt,
        scratch=(pltpu.VMEM(square, BF16),) * 2,
        index=(place,),
    )
    half = captions // 2
    mine = lax.dynamic_slice_in_dim(grad_caption_low, core * half, half, 0)
    mine = dp_gather(mine, steps[:1:-1], [part] * len(steps))
    widen_sum = scatter_steps(widen_dealt, place, mine)
    next(widen_sum)
    (all_sums,) = call(
        stack_kernel,
        sums_parts,
        (((all_pairs, hidden), BF16),),
        after=(widen_dealt[0],),
    )
    grad_residual, grad_branch1, flat, part, mixer_stat = call(
        mixer_back_kernel,
        (
            part,
            other,
            residual,
            grad_caption,
            sentence_word_ids,
            perceptron_layernorm_gamma,
            mixer_result_matrix,
        ),
        (
            (full, F32),
            (full, BF16),
            ((3, tokens, local_width), BF16),
            (full, F32),
            ((8, model_width), F32),
        ),
        outside=(qkv, soft, mixer_triple_matrix),
        after=(all_sums,),
    )
    other = mp_other(part)
    mixer_dealt = call(
        mixer_grad_kernel,
        (normed, flat, mixed, grad_branch1),
        dealt,
        scratch=(pltpu.VMEM(square, BF16),) * 2,
        index=(place,),
    )
    mixer_sum = scatter_steps(mixer_dealt, place)
    next(mixer_sum)
    folded = widen_sum.send((mixer_dealt[0],))
    grad_input, pack = call(
        entry_grad_kernel,
        (
            part,
            other,
            sentence_layer_entry,
            mixer_layernorm_gamma,
            grad_residual,
            loss_stat,
            mixer_stat,
        ),
        ((full, F32), ((16, model_width), F32)),
        after=(folded,),
    )
    cut = widen_sum.send((pack,))
    fold = mixer_sum.send((cut,))
    added = widen_sum.send((fold,))
    cut = mixer_sum.send((added,))
    joined = widen_sum.send((cut,))
    added = mixer_sum.send((joined,))
    widen_pieces = widen_sum.send(())
    joined = mixer_sum.send((added,))
    grad_w_up, near_grads = call(
        unpack_widen_kernel,
        widen_pieces,
        ((widening_matrix.shape, F32), ((all_pairs // 2, model_width), BF16)),
        index=(place,),
        after=(joined,),
    )
    grad_qkv, grad_w_out = call(
        unpack_mixer_kernel,
        mixer_sum.send(()),
        ((mixer_triple_matrix.shape, F32), (mixer_result_matrix.shape, F32)),
        index=(place,),
    )
    (grad_w_down,) = call(
        functools.partial(narrow_grad_kernel, half),
        (all_sums, near_grads, mp_other(near_grads)),
        ((narrowing_matrix.shape, F32),),
        scratch=(pltpu.VMEM((all_pairs, model_width), BF16),),
        index=(core,),
    )
    stats = dp_sum(pack)
    training_error = (stats[3, 1:2] + loss_stat[3, 2:3]) / (2.0 * all_pairs)
    return (
        training_error,
        grad_input,
        grad_qkv,
        stats[11].reshape(2, local_width),
        grad_w_out,
        stats[8],
        grad_w_up,
        stats[0:2].reshape(hidden),
        grad_w_down,
        stats[2],
        stats[4],
        stats[5],
        stats[9],
        stats[10],
        stats[3, 0:1],
    )


def solution(mesh):
    placed = (
        P("dp", None),
        P("dp"),
        P(("dp", "mp"), None, None),
        P(("dp", "mp")),
        P("dp"),
        P(),
        P(),
        P(None, None, "mp"),
        P(None, "mp"),
        P("mp", None),
        P(),
        P(),
        P(),
        P(None, "mp"),
        P("mp"),
        P("mp", None),
        P(),
        P(),
        P(),
        P(),
        P(),
        P(),
        P(),
    )
    return jax.shard_map(
        local,
        mesh=mesh,
        in_specs=placed,
        out_specs=(
            P(),
            P("dp", None),
            P(None, None, "mp"),
            P(None, "mp"),
            P("mp", None),
            P(),
            P(None, "mp"),
            P("mp"),
            P("mp", None),
            P(),
            P(),
            P(),
            P(),
            P(),
            P(),
        ),
        check_vma=False,
    )
```

```python
import functools

import jax
import jax.numpy as jnp
from jax import lax
from jax.experimental import pallas as pl
from jax.experimental.pallas import tpu as pltpu
from jax.sharding import PartitionSpec as P

HEAD = 64
IMG_TOK = 145
LOW_TOK = 50
CAP_LEN = 16


EPS_TEXT = 1e-05
EPS_UNIT = 1e-06
MASKED_SCORE = -1e30
BF16 = jnp.bfloat16
F32 = jnp.float32


def mp_other(values):
    return lax.ppermute(values, "mp", [(0, 1), (1, 0)])


def dp_swap(values, mask):
    size = lax.axis_size("dp")
    return lax.ppermute(values, "dp", [(index, index ^ mask) for index in range(size)])


def group_steps(size):
    steps, stride = [], 1
    while stride < size:
        steps.append([stride, 2 * stride, 3 * stride])
        stride *= 4
    return steps


def gather_masks(steps):
    masks = [0]
    for step in steps:
        masks = [mask ^ base for mask in [0] + step for base in masks]
    return masks


def dp_parts(values, step):
    return [values] + [dp_swap(values, mask) for mask in step]


def dp_gather(values, steps, waits):
    for step, wait in zip(steps, waits):
        parts = dp_parts(values, step)
        rows = values.shape[0]
        (values,) = move(
            parts,
            (len(parts) * rows,),
            [(place, 0, rows, 0, place * rows) for place in range(len(parts))],
            (wait,),
        )
    return values


HIGH_ROWS = 160
LOW_ROWS = 64
TILE = 256
PAIR = 2 * HEAD
LANES = 128
POOL_ROWS = 32
NT = (((1,), (1,)), ((), ()))
VMEM_LIMIT = 60 * 1024 * 1024
BUSY = 10**12


def dot(left, right):
    return jnp.dot(left, right, preferred_element_type=F32)


def wide_dot(left, right):
    high = left.astype(BF16)
    rest = (left - high.astype(F32)).astype(BF16)
    return dot(high, right) + dot(rest, right)


def standard(values, epsilon):
    centered = values - jnp.mean(values, axis=-1, keepdims=True)
    variance = jnp.mean(centered * centered, axis=-1, keepdims=True)
    return centered * lax.rsqrt(variance + epsilon)


def gelu(values):
    return (0.5 * values) * (1.0 + lax.erf(values * (0.5**0.5)))


def image_kernel(
    flag_ref,
    token_ref,
    gain_ref,
    triple_hbm,
    result_hbm,
    widen_hbm,
    narrow_hbm,
    out_ref,
    wide,
    packed,
    queries,
    keys,
    values,
    triple,
    result,
    widen,
    narrow,
    resid_groups,
    hidden_groups,
    pooled,
    starts,
    sems,
):
    _, images, width = token_ref.shape
    hidden = widen.shape[1]
    copies = fetch(
        (triple_hbm, result_hbm, widen_hbm, narrow_hbm), (triple, result, widen, narrow), sems
    )
    lane_tiles = [slice(lane, lane + LANES) for lane in range(0, width, LANES)]

    def spread(position, carry):
        rows = pl.ds(pl.multiple_of(position * images, images), images)
        for place, lanes in enumerate(lane_tiles):
            wide[place, rows, :] = token_ref[position, :, lanes].astype(F32)
        return carry

    def begin(image, start):
        starts[image] = start
        return start + jnp.where(flag_ref[image] == 1, HIGH_ROWS, LOW_ROWS)

    total = lax.fori_loop(0, images, begin, jnp.int32(0))
    lax.fori_loop(0, LOW_ROWS, spread, 0, unroll=4)

    @pl.when(total > images * LOW_ROWS)
    def _():
        lax.fori_loop(LOW_ROWS, IMG_TOK, spread, 0, unroll=3)

    tail = IMG_TOK // 16 * 16

    def pack(image, carry):
        start = pl.multiple_of(starts[image], POOL_ROWS)
        high = flag_ref[image] == 1

        @pl.when(high)
        def _():
            row = lax.broadcasted_iota(jnp.int32, (HIGH_ROWS - tail, LANES), 0)
            for place, lanes in enumerate(lane_tiles):
                packed[pl.ds(start, tail), lanes] = wide[
                    place, pl.ds(image, tail, stride=images), :
                ].astype(BF16)
                last = wide[place, pl.ds(image + tail * images, 1), :]
                packed[pl.ds(start + tail, HIGH_ROWS - tail), lanes] = jnp.where(
                    row == 0, last, 0.0
                ).astype(BF16)

        @pl.when(jnp.logical_not(high))
        def _():
            for place, lanes in enumerate(lane_tiles):
                packed[pl.ds(start, LOW_ROWS), lanes] = wide[
                    place, pl.ds(image, LOW_ROWS, stride=images), :
                ].astype(BF16)

        return carry

    lax.fori_loop(0, images, pack, 0)
    packed[pl.ds(pl.multiple_of(total, POOL_ROWS), TILE), :] = jnp.zeros((TILE, width), BF16)
    tiles = lax.div(total + (TILE - 1), jnp.int32(TILE))

    copies[0].wait()

    def project(tile, carry):
        rows = pl.ds(pl.multiple_of(tile * TILE, TILE), TILE)
        normed = (standard(packed[rows, :].astype(F32), EPS_UNIT) * gain_ref[0:1, :]).astype(BF16)
        queries[rows, :] = (dot(normed, triple[0]) * HEAD ** (-0.5)).astype(BF16)
        keys[rows, :] = dot(normed, triple[1]).astype(BF16)
        values[rows, :] = dot(normed, triple[2]).astype(BF16)
        return carry

    lax.fori_loop(0, tiles, project, 0)

    def attend(start, count, live):
        rows = pl.ds(start, count)
        left = lax.broadcasted_iota(jnp.int32, (count, PAIR), 1) < HEAD
        key_live = lax.broadcasted_iota(jnp.int32, (2 * count, count), 1) < live
        for pair in range(width // PAIR):
            lanes = slice(pair * PAIR, (pair + 1) * PAIR)
            q, k, v = queries[rows, lanes], keys[rows, lanes], values[rows, lanes]
            one = jnp.ones_like(v)
            scores = dot_t(two_heads(q, left), k)
            scores = jnp.where(key_live, scores, MASKED_SCORE)
            powers = jnp.exp(scores - jnp.max(scores, axis=-1, keepdims=True)).astype(BF16)
            first = dot(powers[:count], jnp.where(left, v, one))
            second = dot(powers[count:], jnp.where(left, one, v))
            sums = pltpu.roll(jnp.where(left, second, first), HEAD, 1)
            queries[rows, lanes] = (jnp.where(left, first, second) / sums).astype(BF16)

    def mix(image, carry):
        start = pl.multiple_of(starts[image], POOL_ROWS)
        high = flag_ref[image] == 1

        @pl.when(high)
        def _():
            attend(start, HIGH_ROWS, IMG_TOK)

        @pl.when(jnp.logical_not(high))
        def _():
            attend(start, LOW_ROWS, LOW_TOK)

        return carry

    lax.fori_loop(0, images, mix, 0)

    slot = lax.broadcasted_iota(jnp.int32, (1, images), 1)
    first_row = jnp.zeros((1, images), jnp.int32)
    live_rows = jnp.zeros((1, images), jnp.int32)
    for image in range(images):
        first_row = jnp.where(slot == image, starts[image], first_row)
        live_rows = jnp.where(
            slot == image, jnp.where(flag_ref[image] == 1, IMG_TOK, LOW_TOK), live_rows
        )
    copies[1].wait()
    copies[2].wait()
    groups = TILE // POOL_ROWS

    def group_sum(rows):
        return jnp.sum(rows.reshape(groups, POOL_ROWS // 8, 8, rows.shape[1]), axis=1)

    def perceptron(tile, carry):
        base = pl.multiple_of(tile * TILE, TILE)
        rows = pl.ds(base, TILE)
        place = base + lax.broadcasted_iota(jnp.int32, (TILE, images), 0)
        alive = jnp.sum(
            jnp.where((place >= first_row) & (place < first_row + live_rows), 1.0, 0.0),
            axis=1,
            keepdims=True,
        )
        residual = (packed[rows, :].astype(F32) + dot(queries[rows, :], result[...])) * alive
        group = pl.ds(pl.multiple_of(tile * groups, groups), groups)
        resid_groups[group] = group_sum(residual)
        normed = (standard(residual, EPS_UNIT) * gain_ref[1:2, :]).astype(BF16)
        for chunk in range(hidden // width):
            lanes = slice(chunk * width, (chunk + 1) * width)
            units = gelu(dot(normed, widen[:, lanes])).astype(BF16)
            hidden_groups[group, :, lanes] = group_sum(units.astype(F32))
        return carry

    lax.fori_loop(0, tiles, perceptron, 0)

    def pool(image, carry):
        group = lax.div(starts[image], jnp.int32(POOL_ROWS))
        high = flag_ref[image] == 1

        def add(count):
            residual, units = resid_groups[group], hidden_groups[group]
            for step in range(1, count):
                residual = residual + resid_groups[group + step]
                units = units + hidden_groups[group + step]
            pooled[pl.ds(image, 1), :width] = jnp.sum(residual, axis=0, keepdims=True)
            pooled[pl.ds(image, 1), width:] = jnp.sum(units, axis=0, keepdims=True)

        @pl.when(high)
        def _():
            add(HIGH_ROWS // POOL_ROWS)

        @pl.when(jnp.logical_not(high))
        def _():
            add(LOW_ROWS // POOL_ROWS)

        return carry

    lax.fori_loop(0, images, pool, 0)
    copies[3].wait()
    units = pooled[:, width:]
    upper = units.astype(BF16)
    lower = (units - upper.astype(F32)).astype(BF16)
    branch = dot(jnp.concatenate([upper, lower], axis=0), narrow[...])
    live = jnp.where(number_column(flag_ref) == 1, IMG_TOK, LOW_TOK).astype(F32)
    mean = (pooled[:, :width] + branch[:images] + branch[images:]) / live
    out_ref[...] = (
        mean * lax.rsqrt(jnp.sum(mean * mean, axis=-1, keepdims=True) + EPS_UNIT)
    ).astype(BF16)


def image_tower(flags, tokens, gains, triple, result, widen, narrow):
    images, _, width = tokens.shape
    hidden = widen.shape[1]
    rows = images * HIGH_ROWS + TILE
    groups = rows // POOL_ROWS
    outside = pl.BlockSpec(memory_space=pl.ANY)
    inside = pl.BlockSpec(memory_space=pltpu.VMEM)
    return pl.pallas_call(
        image_kernel,
        out_shape=jax.ShapeDtypeStruct((images, width), BF16),
        in_specs=[pl.BlockSpec(memory_space=pltpu.SMEM), inside, inside]
        + [outside] * 4,
        out_specs=inside,
        scratch_shapes=[pltpu.VMEM((width // LANES, IMG_TOK * images, LANES), F32)]
        + [pltpu.VMEM((rows, width), BF16)] * 4
        + [pltpu.VMEM(weight.shape, BF16) for weight in (triple, result, widen, narrow)]
        + [
            pltpu.VMEM((groups, 8, width), F32),
            pltpu.VMEM((groups, 8, hidden), F32),
            pltpu.VMEM((images, width + hidden), F32),
            pltpu.SMEM((images,), jnp.int32),
            pltpu.SemaphoreType.DMA((4,)),
        ],
        compiler_params=pltpu.CompilerParams(vmem_limit_bytes=VMEM_LIMIT),
        cost_estimate=pl.CostEstimate(flops=BUSY, bytes_accessed=BUSY, transcendentals=0),
    )(flags, jnp.transpose(tokens, (1, 0, 2)), gains, triple, result, widen, narrow)


TN = (((0,), (0,)), ((), ()))
BLOCK = 128
ROOT_HALF = 0.5**0.5
DENSITY = 0.3989422804014327


def dot_t(left, right):
    return lax.dot_general(left, right, NT, preferred_element_type=F32)


def t_dot(left, right):
    return lax.dot_general(left, right, TN, preferred_element_type=F32)


def fetch(sources, targets, sems):
    copies = [
        pltpu.make_async_copy(source, target, sems.at[place])
        for place, (source, target) in enumerate(zip(sources, targets))
    ]
    for copy in copies:
        copy.start()
    return copies


def caption_pool(ids_ref, captions):
    ids_row = ids_ref[...].reshape(1, -1)
    tokens = ids_row.shape[1]
    shape = (captions, tokens)
    caption = lax.broadcasted_iota(jnp.int32, shape, 0)
    token = lax.broadcasted_iota(jnp.int32, shape, 1)
    inside = (token // (tokens // captions)) == caption
    return jnp.where(inside & (ids_row != 0), 1.0, 0.0)


def valid_column(pool):
    pool = pool.astype(BF16)
    return t_dot(pool, jnp.ones((pool.shape[0], 128), BF16))[:, 0:1]


def number_column(ref):
    shape = (ref.shape[0], 1)
    place = lax.broadcasted_iota(jnp.int32, shape, 0)
    column = jnp.zeros(shape, jnp.int32)
    for index in range(shape[0]):
        column = jnp.where(place == index, ref[index], column)
    return column


def as_row(ref):
    return ref[...].reshape(1, -1)


def pair_masks(rows, pair_width):
    return lax.broadcasted_iota(jnp.int32, (rows, pair_width), 1) < HEAD


def two_heads(values, left):
    zero = jnp.zeros_like(values)
    return jnp.concatenate(
        [jnp.where(left, values, zero), jnp.where(left, zero, values)], axis=0
    )


def text_mix_kernel(
    entry_ref,
    ids_ref,
    gain_ref,
    shift_ref,
    triple_ref,
    pair_ref,
    result_ref,
    normed_ref,
    qkv_ref,
    soft_ref,
    mixed_ref,
    part_ref,
):
    tokens = entry_ref.shape[0]
    width = result_ref.shape[0]
    normed = (
        standard(entry_ref[...].astype(F32), EPS_TEXT) * as_row(gain_ref) + as_row(shift_ref)
    ).astype(BF16)
    normed_ref[...] = normed
    qkv_ref[0] = (dot(normed, triple_ref[0]) + pair_ref[0:1, :]).astype(BF16)
    qkv_ref[1] = dot(normed, triple_ref[1]).astype(BF16)
    qkv_ref[2] = (dot(normed, triple_ref[2]) + pair_ref[1:2, :]).astype(BF16)
    ids = as_row(ids_ref)
    left = pair_masks(BLOCK, PAIR)
    shape = (2 * BLOCK, BLOCK)
    query_caption = lax.broadcasted_iota(jnp.int32, shape, 0) % BLOCK // CAP_LEN
    same = query_caption == lax.broadcasted_iota(jnp.int32, shape, 1) // CAP_LEN
    for block in range(tokens // BLOCK):
        rows = slice(block * BLOCK, (block + 1) * BLOCK)
        seen = same & (ids[:, rows] != 0)
        for pair in range(width // PAIR):
            lanes = slice(pair * PAIR, (pair + 1) * PAIR)
            scores = dot_t(two_heads(qkv_ref[0, rows, lanes], left), qkv_ref[1, rows, lanes])
            scores = jnp.where(seen, scores * HEAD ** (-0.5), MASKED_SCORE)
            powers = jnp.exp(scores - jnp.max(scores, axis=-1, keepdims=True))
            soft = powers / jnp.sum(powers, axis=-1, keepdims=True)
            soft_ref[block, pair] = soft
            low = soft.astype(BF16)
            value = qkv_ref[2, rows, lanes]
            mixed_ref[rows, lanes] = jnp.where(
                left, dot(low[:BLOCK], value), dot(low[BLOCK:], value)
            ).astype(BF16)
    part_ref[...] = dot(mixed_ref[...], result_ref[...])


def text_widen_kernel(
    entry_ref,
    own_ref,
    other_ref,
    result_offset_ref,
    gain_ref,
    shift_ref,
    widen_offset_ref,
    ids_ref,
    widen_hbm,
    narrow_hbm,
    residual_ref,
    normed_ref,
    slope_ref,
    sums_ref,
    resid_sum_ref,
    branch_ref,
    widen,
    narrow,
    hidden_sum,
    sems,
):
    captions = sums_ref.shape[0]
    width = entry_ref.shape[1]
    copies = fetch((widen_hbm, narrow_hbm), (widen, narrow), sems)
    residual = entry_ref[...].astype(F32) + (
        (own_ref[...] + other_ref[...]) + as_row(result_offset_ref)
    )
    residual_ref[...] = residual
    normed = (standard(residual, EPS_TEXT) * as_row(gain_ref) + as_row(shift_ref)).astype(BF16)
    normed_ref[...] = normed
    pool = caption_pool(ids_ref, captions).astype(BF16)
    widen_offset = as_row(widen_offset_ref)
    upper = residual.astype(BF16)
    resid_sum_ref[...] = dot(pool, upper) + dot(
        pool, (residual - upper.astype(F32)).astype(BF16)
    )
    valid = valid_column(pool)
    copies[0].wait()
    for chunk in range(widen.shape[1] // width):
        lanes = slice(chunk * width, (chunk + 1) * width)
        before = dot(normed, widen[:, lanes]) + widen_offset[:, lanes]
        share = 0.5 * (1.0 + lax.erf(before * ROOT_HALF))
        hidden_sum[:, lanes] = dot(pool, (before * share).astype(BF16))
        slope = share + before * (jnp.exp(-0.5 * before * before) * DENSITY)
        slope_ref[:, lanes] = slope * valid
    sums_ref[...] = hidden_sum[...].astype(BF16)
    copies[1].wait()
    branch_ref[...] = wide_dot(hidden_sum[...], narrow[...])


def logits_kernel(
    masks,
    index_ref,
    matched_ref,
    sharpen_ref,
    near_ref,
    far_ref,
    resid_sum_ref,
    own_ref,
    other_ref,
    narrow_offset_ref,
    ids_ref,
    images_ref,
    unit_ref,
    factor_ref,
    logits_ref,
    powers_ref,
    row_sum_ref,
    col_sum_ref,
    loss_ref,
):
    captions, pairs = logits_ref.shape
    rows = images_ref.shape[0] // (2 * len(masks))
    core = index_ref[1]
    for place, mask in enumerate(masks):
        start = (index_ref[0] ^ mask) * (2 * rows)
        images_ref[pl.ds(pl.multiple_of(start + core * rows, rows), rows), :] = near_ref[
            place * rows : (place + 1) * rows, :
        ]
        images_ref[pl.ds(pl.multiple_of(start + (1 - core) * rows, rows), rows), :] = far_ref[
            place * rows : (place + 1) * rows, :
        ]
    count = jnp.sum(caption_pool(ids_ref, captions), axis=1, keepdims=True)
    pooled = (resid_sum_ref[...] + (own_ref[...] + other_ref[...])) / count + as_row(
        narrow_offset_ref
    )
    inverse = lax.rsqrt(jnp.sum(pooled * pooled, axis=-1, keepdims=True) + EPS_UNIT)
    unit = pooled * inverse
    unit_ref[...] = unit
    factor_ref[...] = jnp.broadcast_to(inverse / count, factor_ref.shape)
    logits = jnp.exp(jnp.full((1, 1), sharpen_ref[0], F32)) * dot_t(unit.astype(BF16), images_ref[...])
    logits_ref[...] = logits
    powers = jnp.exp(logits)
    powers_ref[...] = powers
    row_sum = jnp.sum(powers, axis=1, keepdims=True)
    row_sum_ref[...] = jnp.broadcast_to(row_sum, row_sum_ref.shape)
    col_sum_ref[...] = jnp.sum(powers, axis=0, keepdims=True)
    positive = number_column(matched_ref) == lax.broadcasted_iota(jnp.int32, (captions, pairs), 1)
    wanted = jnp.sum(jnp.where(positive, logits, 0.0), axis=1, keepdims=True)
    loss_ref[...] = jnp.broadcast_to(
        jnp.sum(jnp.log(row_sum) - 2.0 * wanted, axis=0, keepdims=True), loss_ref.shape
    )


def sum_kernel(first_ref, second_ref, third_ref, fourth_ref, out_ref):
    out_ref[...] = (first_ref[...] + second_ref[...]) + (third_ref[...] + fourth_ref[...])


def loss_grad_kernel(
    matched_ref,
    sharpen_ref,
    col_ref,
    col1_ref,
    col2_ref,
    col3_ref,
    logits_ref,
    powers_ref,
    row_sum_ref,
    unit_ref,
    factor_ref,
    images_ref,
    ids_ref,
    loss_ref,
    narrow_hbm,
    slope_hbm,
    widen_hbm,
    grad_ref,
    low_ref,
    before_ref,
    part_ref,
    stat_ref,
    narrow,
    slope,
    widen,
    sems,
):
    captions, pairs = logits_ref.shape
    tokens, hidden = slope.shape
    width = grad_ref.shape[1]
    copies = fetch((narrow_hbm, slope_hbm, widen_hbm), (narrow, slope, widen), sems)
    logits, powers = logits_ref[...], powers_ref[...]
    col_sum = (col_ref[...] + col1_ref[...]) + (col2_ref[...] + col3_ref[...])
    positive = number_column(matched_ref) == lax.broadcasted_iota(jnp.int32, (captions, pairs), 1)
    derivative = (
        powers / row_sum_ref[:, 0:1] + powers / col_sum - jnp.where(positive, 2.0, 0.0)
    ) / (2.0 * pairs)
    temperature = jnp.sum(
        jnp.sum(derivative * logits, axis=1, keepdims=True), axis=0, keepdims=True
    )
    col_loss = jnp.sum(jnp.log(col_sum), axis=1, keepdims=True)
    text = dot((derivative * jnp.exp(jnp.full((1, 1), sharpen_ref[0], F32))).astype(BF16), images_ref[...])
    unit = unit_ref[...]
    grad = (text - unit * jnp.sum(unit * text, axis=-1, keepdims=True)) * factor_ref[:, 0:1]
    grad_ref[...] = grad
    low = grad.astype(BF16)
    low_ref[...] = low
    copies[0].wait()
    copies[1].wait()
    copies[2].wait()
    ones = jnp.ones((8, tokens), BF16)
    part = jnp.zeros(part_ref.shape, F32)
    for chunk in range(hidden // width):
        lanes = slice(chunk * width, (chunk + 1) * width)
        back = dot_t(low, narrow[lanes, :])
        before = (
            (back[:, None, :] * slope[:, lanes].reshape(captions, CAP_LEN, width))
            .reshape(tokens, width)
            .astype(BF16)
        )
        before_ref[:, lanes] = before
        stat_ref[chunk : chunk + 1, :] = dot(ones, before)[0:1]
        part = part + dot_t(before, widen[:, lanes])
    part_ref[...] = part
    count = jnp.sum(caption_pool(ids_ref, captions), axis=1, keepdims=True)
    stat_ref[2:3, :] = jnp.sum(low.astype(F32) * count, axis=0, keepdims=True)
    lane = lax.broadcasted_iota(jnp.int32, (1, width), 1)
    stat_ref[3:4, :] = jnp.where(
        lane == 0,
        temperature,
        jnp.where(lane == 1, loss_ref[0:1, 0:1], jnp.where(lane == 2, col_loss, 0.0)),
    )
    stat_ref[4:8, :] = jnp.zeros((4, width), F32)


def deal(index_ref, first, second, outs):
    half = first.shape[0] // 2
    for place, (values, bit) in enumerate(((first, 1), (second, 2))):
        mine = index_ref[0] // bit % 2
        for ref, which in ((outs[2 * place], 1 - mine), (outs[2 * place + 1], mine)):
            ref[...] = values[pl.ds(pl.multiple_of(which * half, half), half), :]


def widen_grad_kernel(index_ref, normed_ref, before_ref, *refs):
    outs, (first, second) = refs[:4], refs[4:]
    width = first.shape[1]
    normed = normed_ref[...]
    first[...] = t_dot(normed, before_ref[:, :width]).astype(BF16)
    second[...] = t_dot(normed, before_ref[:, width:]).astype(BF16)
    deal(index_ref, first, second, outs)


def mixer_back_kernel(
    own_ref,
    other_ref,
    residual_ref,
    grad_ref,
    ids_ref,
    gain_ref,
    result_ref,
    qkv_hbm,
    soft_hbm,
    triple_hbm,
    grad_residual_ref,
    low_ref,
    flat_ref,
    part_ref,
    stat_ref,
    qkv,
    soft_all,
    triple,
    sems,
):
    tokens, width = residual_ref.shape
    captions = grad_ref.shape[0]
    local_width = result_ref.shape[0]
    copies = fetch((qkv_hbm, soft_hbm, triple_hbm), (qkv, soft_all, triple), sems)
    residual = residual_ref[...]
    centered = residual - jnp.mean(residual, axis=-1, keepdims=True)
    rate = lax.rsqrt(jnp.mean(centered * centered, axis=-1, keepdims=True) + EPS_TEXT)
    unit = centered * rate
    grad = own_ref[...] + other_ref[...]
    stat_ref[1:2, :] = jnp.sum(grad * unit, axis=0, keepdims=True)
    stat_ref[2:3, :] = jnp.sum(grad, axis=0, keepdims=True)
    scaled = grad * as_row(gain_ref)
    inner = rate * (
        scaled
        - jnp.mean(scaled, axis=-1, keepdims=True)
        - unit * jnp.mean(scaled * unit, axis=-1, keepdims=True)
    )
    spread = jnp.broadcast_to(
        grad_ref[...][:, None, :], (captions, tokens // captions, width)
    ).reshape(tokens, width)
    grad_residual = spread * valid_column(caption_pool(ids_ref, captions)) + inner
    grad_residual_ref[...] = grad_residual
    low = grad_residual.astype(BF16)
    low_ref[...] = low
    ones = jnp.ones((8, tokens), BF16)
    stat_ref[0:1, :] = dot(ones, low)[0:1]
    grad_mixed = dot_t(low, result_ref[...]).astype(BF16)
    for copy in copies:
        copy.wait()
    left = pair_masks(BLOCK, PAIR)
    for block in range(tokens // BLOCK):
        rows = slice(block * BLOCK, (block + 1) * BLOCK)
        for pair in range(local_width // PAIR):
            lanes = slice(pair * PAIR, (pair + 1) * PAIR)
            soft = soft_all[block, pair]
            mixed = two_heads(grad_mixed[rows, lanes], left)
            query, key = qkv[0, rows, lanes], qkv[1, rows, lanes]
            grad_soft = dot_t(mixed, qkv[2, rows, lanes])
            flat_ref[2, rows, lanes] = t_dot(soft.astype(BF16), mixed).astype(BF16)
            scores = (
                soft * (grad_soft - jnp.sum(grad_soft * soft, axis=-1, keepdims=True))
            ).astype(BF16)
            back = jnp.where(left, dot(scores[:BLOCK], key), dot(scores[BLOCK:], key))
            flat_ref[0, rows, lanes] = (back * HEAD ** (-0.5)).astype(BF16)
            flat_ref[1, rows, lanes] = (
                t_dot(scores, two_heads(query, left)) * HEAD ** (-0.5)
            ).astype(BF16)
    part_ref[...] = (
        dot_t(flat_ref[0], triple[0])
        + dot_t(flat_ref[1], triple[1])
        + dot_t(flat_ref[2], triple[2])
    )
    stat_ref[3:4, :local_width] = dot(ones, flat_ref[0])[0:1]
    stat_ref[3:4, local_width:] = dot(ones, flat_ref[2])[0:1]
    stat_ref[4:8, :] = jnp.zeros((4, width), F32)


def mixer_grad_kernel(index_ref, normed_ref, flat_ref, mixed_ref, low_ref, *refs):
    outs, (first, second) = refs[:4], refs[4:]
    half = flat_ref.shape[2]
    rows = first.shape[0] // 2
    normed = normed_ref[...]
    for part, (target, place) in enumerate(((first, 0), (first, rows), (second, 0))):
        grad = t_dot(normed, flat_ref[part]).astype(BF16)
        target[place : place + rows, :half] = grad[:rows]
        target[place : place + rows, half:] = grad[rows:]
    second[rows:, :] = t_dot(mixed_ref[...], low_ref[...]).astype(BF16)
    deal(index_ref, first, second, outs)


def narrow_grad_kernel(half, index_ref, *refs):
    parts, (near_ref, far_ref, out_ref, grads) = refs[:-4], refs[-4:]
    rows, width = parts[0].shape[0], grads.shape[1]
    for place in range(near_ref.shape[0] // half):
        for ref, which in ((near_ref, index_ref[0]), (far_ref, 1 - index_ref[0])):
            start = pl.multiple_of((2 * place + which) * half, half)
            grads[pl.ds(start, half), :] = ref[place * half : (place + 1) * half, :]
    for chunk in range(out_ref.shape[0] // width):
        lanes = slice(chunk * width, (chunk + 1) * width)
        total = t_dot(parts[0][:, lanes], grads[:rows, :])
        for place in range(1, len(parts)):
            total = total + t_dot(
                parts[place][:, lanes], grads[place * rows : (place + 1) * rows, :]
            )
        out_ref[lanes, :] = total


def entry_grad_kernel(
    index_ref,
    own_ref,
    other_ref,
    entry_ref,
    gain_ref,
    grad_residual_ref,
    loss_stat_ref,
    mixer_stat_ref,
    caption_ref,
    out_ref,
    extra_ref,
    pack,
):
    entry = entry_ref[...].astype(F32)
    centered = entry - jnp.mean(entry, axis=-1, keepdims=True)
    rate = lax.rsqrt(jnp.mean(centered * centered, axis=-1, keepdims=True) + EPS_TEXT)
    unit = centered * rate
    grad = own_ref[...] + other_ref[...]
    pack[0:8, :] = loss_stat_ref[...]
    pack[8:16, :] = mixer_stat_ref[...]
    pack[4:5, :] = jnp.sum(grad * unit, axis=0, keepdims=True)
    pack[5:6, :] = jnp.sum(grad, axis=0, keepdims=True)
    half = caption_ref.shape[0] // 2
    extra_ref[:half, :] = caption_ref[
        pl.ds(pl.multiple_of(index_ref[0] * half, half), half), :
    ]
    upper = pack[...].astype(BF16).astype(F32)
    pack[15:16, :] = (pack[...] - upper)[3:4, :]
    extra_ref[half:, :] = pack[...].astype(BF16)
    scaled = grad * as_row(gain_ref)
    out_ref[...] = grad_residual_ref[...] + rate * (
        scaled
        - jnp.mean(scaled, axis=-1, keepdims=True)
        - unit * jnp.mean(scaled * unit, axis=-1, keepdims=True)
    )


def tree_sum(values):
    while len(values) > 1:
        values = [values[place] + values[place + 1] for place in range(0, len(values), 2)]
    return values[0]


def collect_kernel(
    scale,
    rows,
    joined_ref,
    along_x_ref,
    along_y_ref,
    first_far_ref,
    second_far_ref,
    loss_ref,
    near_ref,
    error_ref,
    pair_ref,
    result_ref,
    widen_ref,
    narrow_ref,
    gain1_ref,
    shift1_ref,
    gain2_ref,
    shift2_ref,
    temperature_ref,
):
    half = rows - 16
    first = second_far_ref.shape[0]
    count = (first_far_ref.shape[0] - first) // rows
    totals = []
    for piece, ref in enumerate((joined_ref, along_x_ref, along_y_ref, first_far_ref)):
        for place in range(count):
            row = first + place * rows
            near_ref[pl.ds((piece * count + place) * half, half), :] = ref[row : row + half, :]
            totals.append(ref[row + half : row + rows, :].astype(F32))
    total = tree_sum(totals)
    scalars = total[3:4] + total[15:16]
    error_ref[...] = ((scalars[:, 1:2] + loss_ref[3:4, 2:3]) * scale).reshape(1)
    temperature_ref[...] = scalars[:, 0:1].reshape(1)
    lanes = pair_ref.shape[1]
    pair_ref[0:1, :] = total[11:12, :lanes]
    pair_ref[1:2, :] = total[11:12, lanes:]
    width = total.shape[1]
    for chunk in range(widen_ref.shape[0] // width):
        widen_ref[chunk * width : (chunk + 1) * width] = total[chunk]
    for ref, place in (
        (narrow_ref, 2),
        (gain1_ref, 4),
        (shift1_ref, 5),
        (result_ref, 8),
        (gain2_ref, 9),
        (shift2_ref, 10),
    ):
        ref[...] = total[place]


def call(kernel, inside, shapes, outside=(), scratch=(), index=(), small=(), after=(), limit=24):
    vmem = pl.BlockSpec(memory_space=pltpu.VMEM)
    extra = [pltpu.VMEM(array.shape, array.dtype) for array in outside]
    extra += list(scratch)
    if outside:
        extra += [pltpu.SemaphoreType.DMA((len(outside),))]
    index = [jnp.stack(index).astype(jnp.int32)] if index else []
    small = index + list(small)
    before = len(small) + len(inside) + len(outside)

    def body(*refs):
        kernel(*refs[:before], *refs[before + len(after) :])

    return pl.pallas_call(
        body,
        out_shape=[jax.ShapeDtypeStruct(shape, kind) for shape, kind in shapes],
        in_specs=[pl.BlockSpec(memory_space=pltpu.SMEM)] * len(small)
        + [vmem] * len(inside)
        + [pl.BlockSpec(memory_space=pl.ANY)] * (len(outside) + len(after)),
        out_specs=[vmem] * len(shapes),
        scratch_shapes=extra,
        compiler_params=pltpu.CompilerParams(vmem_limit_bytes=limit * 1024 * 1024),
        cost_estimate=pl.CostEstimate(flops=BUSY, bytes_accessed=BUSY, transcendentals=0),
    )(*small, *inside, *outside, *after)


def move(arrays, sizes, plan, after=()):
    width, kind = arrays[0].shape[1], arrays[0].dtype

    def body(*refs):
        ins, outs = refs[: len(arrays)], refs[len(arrays) :]
        for source, first, rows, target, start in plan:
            outs[target][start : start + rows, :] = ins[source][first : first + rows, :]

    return call(body, arrays, tuple(((size, width), kind) for size in sizes), after=after)


GROUP = 16
Z_STRIDE, Z_SIZE = 4, 4


def block_rows(block, rows):
    return pl.ds(pl.multiple_of(block * rows, rows), rows)


def fold_kernel(index_ref, *refs):
    ins, outs = refs[:4], refs[4:]
    half = outs[0].shape[0]
    for place, bit in ((0, 2), (1, 1)):
        mine = index_ref[0] // bit % 2
        for out, which in ((outs[2 * place], 1 - mine), (outs[2 * place + 1], mine)):
            rows = block_rows(which, half)
            out[...] = (
                ins[2 * place][rows, :].astype(F32) + ins[2 * place + 1][rows, :].astype(F32)
            ).astype(out.dtype)


def cut_kernel(index_ref, *refs):
    ins, outs = refs[:4], refs[4:]
    rows = ins[0].shape[0] // Z_SIZE
    for place in range(2):
        for step, out in enumerate(outs):
            block = block_rows((index_ref[0] // Z_STRIDE % Z_SIZE) ^ step, rows)
            out[place * rows : (place + 1) * rows, :] = (
                ins[2 * place][block, :] + ins[2 * place + 1][block, :].astype(F32)
            ).astype(out.dtype)


def add_kernel(own_ref, *refs):
    out_ref = refs[-1]
    rows = own_ref.shape[0]
    total = own_ref[...]
    for ref in refs[: Z_SIZE - 1]:
        total = total + ref[...].astype(F32)
    out_ref[:rows, :] = total.astype(out_ref.dtype)
    if out_ref.shape[0] > rows:
        out_ref[rows:, :] = refs[Z_SIZE - 1][...]


def scatter_steps(dealt, place, extra=None):
    first_sent, first_kept, second_sent, second_kept = dealt
    rows, width = first_sent.shape
    after = yield
    arrived = (dp_swap(first_sent, 1), dp_swap(second_sent, 2))
    half = (rows // 2, width)
    first_sent, first_kept, second_sent, second_kept = call(
        fold_kernel,
        (first_kept, arrived[0], second_kept, arrived[1]),
        ((half, BF16), (half, F32), (half, BF16), (half, F32)),
        index=(place,),
        after=after,
    )
    after = yield first_kept
    arrived = (dp_swap(first_sent, 2), dp_swap(second_sent, 1))
    block = (rows // Z_SIZE, width)
    own, *sent = call(
        cut_kernel,
        (first_kept, arrived[0], second_kept, arrived[1]),
        ((block, F32),) + ((block, BF16),) * (Z_SIZE - 1),
        index=(place,),
        after=after,
    )
    after = yield own
    arrived = [dp_swap(values, step * Z_STRIDE) for step, values in enumerate(sent, 1)]
    size = lax.axis_size("dp")
    more = 0 if extra is None else extra[0].shape[0]
    if size > GROUP:
        (mine,) = call(add_kernel, (own, *arrived), ((own.shape, F32),), after=after)
        groups = [list(range(index, size, GROUP)) for index in range(GROUP)]
        mine = lax.psum(mine, "dp", axis_index_groups=groups).astype(BF16)
        if more:
            mine = jnp.concatenate([mine, *extra], axis=0)
    else:
        (mine,) = call(
            add_kernel,
            (own, *arrived) + (tuple(extra) if more else ()),
            (((block[0] + more, width), BF16),),
            after=after,
        )
    after = yield mine
    pieces = [mine] + [dp_swap(mine, step * Z_STRIDE) for step in range(1, Z_SIZE)]
    half = block[0] // 2
    plan, start = [], 0
    for first, count in ((0, half), (2 * half, more), (half, half)):
        for piece in range(Z_SIZE):
            if count:
                plan.append((piece, first, count, 0, start))
            start += count
    (joined,) = move(pieces, (start,), plan, after)
    along_x, along_y = dp_swap(joined, 1), dp_swap(joined, 2)
    after = yield joined
    share = Z_SIZE * half
    first, second = move(
        (along_y, along_x),
        (start - share, share),
        ((0, 0, start - share, 0, 0), (1, start - share, share, 1, 0)),
        after,
    )
    after = yield first
    yield joined, along_x, along_y, dp_swap(first, 1), dp_swap(second, 2)


def block_home(index, block, outer, inner):
    high = (block // 8) ^ (index // outer % 2)
    middle = (block // 4 % 2) ^ (index // inner % 2)
    return high * 8 + middle * 4 + ((block % 4) ^ (index // Z_STRIDE % Z_SIZE))


def relative_blocks(refs, tensor):
    joined, along_x, along_y, first_far, second_far = refs
    size = second_far.shape[0]
    start = joined.shape[0] - size if tensor else 0
    if tensor:
        pieces = ((joined, start), (along_x, start), (along_y, start), (second_far, 0))
    else:
        pieces = ((joined, 0), (along_y, 0), (along_x, 0), (first_far, 0))
    rows = size // Z_SIZE
    for piece, (ref, start) in enumerate(pieces):
        for step in range(Z_SIZE):
            first = start + step * rows
            yield piece * Z_SIZE + step, rows, ref[first : first + rows, :]


def unpack_widen_kernel(index_ref, *refs):
    refs, out_ref = refs[:-1], refs[-1]
    width = out_ref.shape[1] // 2
    for tensor, bits in ((0, (1, 2)), (1, (2, 1))):
        for block, rows, values in relative_blocks(refs, tensor):
            start = pl.multiple_of(block_home(index_ref[0], block, *bits) * rows, rows)
            out_ref[pl.ds(start, rows), tensor * width : (tensor + 1) * width] = values.astype(F32)


def unpack_mixer_kernel(index_ref, *refs):
    refs, (triple_ref, result_ref) = refs[:-2], refs[-2:]
    half, split = triple_ref.shape[2], triple_ref.shape[1] // 2
    for block, rows, values in relative_blocks(refs, 0):
        home = block_home(index_ref[0], block, 1, 2)
        part, row = home // 8, pl.multiple_of(home % 8 * rows, rows)
        triple_ref[part, pl.ds(row, rows), :] = values[:, :half].astype(F32)
        triple_ref[part, pl.ds(split + row, rows), :] = values[:, half:].astype(F32)
    for block, rows, values in relative_blocks(refs, 1):
        home = block_home(index_ref[0], block, 2, 1)
        row = pl.multiple_of(home % 8 * rows, rows)

        @pl.when(home < 8)
        def _():
            triple_ref[2, pl.ds(row, rows), :] = values[:, :half].astype(F32)
            triple_ref[2, pl.ds(split + row, rows), :] = values[:, half:].astype(F32)

        @pl.when(home >= 8)
        def _():
            result_ref[pl.ds(row, rows), :] = values.astype(F32)


def local(
    sentence_layer_entry,
    sentence_word_ids,
    picture_tile_activations,
    picture_detail_flag,
    matched_picture_ids,
    mixer_layernorm_gamma,
    mixer_layernorm_offset,
    mixer_triple_matrix,
    mixer_pair_offsets,
    mixer_result_matrix,
    mixer_result_offset,
    perceptron_layernorm_gamma,
    perceptron_layernorm_offset,
    widening_matrix,
    widening_offset,
    narrowing_matrix,
    narrowing_offset,
    sharpening_log,
    locked_layernorm_gammas,
    locked_mixer_triple_matrix,
    locked_mixer_result_matrix,
    locked_widening_matrix,
    locked_narrowing_matrix,
):
    captions = matched_picture_ids.shape[0]
    tokens, model_width = sentence_layer_entry.shape
    local_width = mixer_result_matrix.shape[0]
    hidden = narrowing_matrix.shape[0]
    devices = lax.axis_size("dp")
    all_pairs = captions * devices
    place, core = lax.axis_index("dp"), lax.axis_index("mp")
    blocks = tokens // BLOCK
    full = (tokens, model_width)
    short = (captions, model_width)
    square = (model_width, model_width)
    half_square = (model_width // 2, model_width)
    dealt = ((half_square, BF16),) * 4

    steps = group_steps(devices)

    image_emb = image_tower(
        picture_detail_flag,
        picture_tile_activations,
        locked_layernorm_gammas,
        locked_mixer_triple_matrix,
        locked_mixer_result_matrix,
        locked_widening_matrix,
        locked_narrowing_matrix,
    )
    normed, qkv, soft, mixed, part = call(
        text_mix_kernel,
        (
            sentence_layer_entry,
            sentence_word_ids,
            mixer_layernorm_gamma,
            mixer_layernorm_offset,
            mixer_triple_matrix,
            mixer_pair_offsets,
            mixer_result_matrix,
        ),
        (
            (full, BF16),
            ((3, tokens, local_width), BF16),
            ((blocks, local_width // PAIR, 2 * BLOCK, BLOCK), F32),
            ((tokens, local_width), BF16),
            (full, F32),
        ),
        after=(image_emb,),
    )
    other = mp_other(part)
    near_images = dp_gather(image_emb, steps[:0:-1], [part] * (len(steps) - 1))
    residual, normed2, slope, hidden_sums, resid_sum, branch = call(
        text_widen_kernel,
        (
            sentence_layer_entry,
            part,
            other,
            mixer_result_offset,
            perceptron_layernorm_gamma,
            perceptron_layernorm_offset,
            widening_offset,
            sentence_word_ids,
        ),
        (
            (full, F32),
            (full, BF16),
            ((tokens, hidden), F32),
            ((captions, hidden), BF16),
            (short, F32),
            (short, F32),
        ),
        outside=(widening_matrix, narrowing_matrix),
        scratch=(pltpu.VMEM((captions, hidden), F32),),
        after=(near_images,),
    )

    near_images = dp_gather(near_images, steps[:1], (branch,))
    sums_parts = dp_parts(hidden_sums, steps[-1])
    images, unit, factor, logits, powers, row_sum, col_sum, row_loss = call(
        functools.partial(logits_kernel, gather_masks(steps[::-1])),
        (
            near_images,
            mp_other(near_images),
            resid_sum,
            branch,
            mp_other(branch),
            narrowing_offset,
            sentence_word_ids,
        ),
        (
            ((all_pairs, model_width), BF16),
            (short, F32),
            ((captions, 128), F32),
            ((captions, all_pairs), F32),
            ((captions, all_pairs), F32),
            ((captions, 128), F32),
            ((1, all_pairs), F32),
            ((8, 128), F32),
        ),
        index=(place, core),
        small=(matched_picture_ids, sharpening_log),
    )
    after = (unit,)
    for step in steps[-2::-1]:
        rows = sums_parts[0].shape[0]
        (joined_sums,) = move(
            sums_parts,
            (4 * rows,),
            [(place, 0, rows, 0, place * rows) for place in range(4)],
            after,
        )
        sums_parts, after = dp_parts(joined_sums, step), (joined_sums,)
    col_parts = dp_parts(col_sum, steps[0])
    for step in steps[1:]:
        (col_sum,) = call(sum_kernel, col_parts, ((col_sum.shape, F32),), after=after)
        col_parts = dp_parts(col_sum, step)
    grad_caption, grad_caption_low, grad_pre, part, loss_stat = call(
        loss_grad_kernel,
        (
            *col_parts,
            logits,
            powers,
            row_sum,
            unit,
            factor,
            images,
            sentence_word_ids,
            row_loss,
        ),
        (
            (short, F32),
            (short, BF16),
            ((tokens, hidden), BF16),
            (full, F32),
            ((8, model_width), F32),
        ),
        outside=(narrowing_matrix, slope, widening_matrix),
        small=(matched_picture_ids, sharpening_log),
    )

    other = mp_other(part)
    widen_dealt = call(
        widen_grad_kernel,
        (normed2, grad_pre),
        dealt,
        scratch=(pltpu.VMEM(square, BF16),) * 2,
        index=(place,),
    )
    grad_residual, grad_branch1, flat, part, mixer_stat = call(
        mixer_back_kernel,
        (
            part,
            other,
            residual,
            grad_caption,
            sentence_word_ids,
            perceptron_layernorm_gamma,
            mixer_result_matrix,
        ),
        (
            (full, F32),
            (full, BF16),
            ((3, tokens, local_width), BF16),
            (full, F32),
            ((8, model_width), F32),
        ),
        outside=(qkv, soft, mixer_triple_matrix),
        after=(widen_dealt[0],),
    )
    other = mp_other(part)
    extra = []
    widen_sum = scatter_steps(widen_dealt, place, extra)
    next(widen_sum)
    last = widen_sum.send((part, *sums_parts))
    mixer_dealt = call(
        mixer_grad_kernel,
        (normed, flat, mixed, grad_branch1),
        dealt,
        scratch=(pltpu.VMEM(square, BF16),) * 2,
        index=(place,),
        after=(last,),
    )
    mixer_sum = scatter_steps(mixer_dealt, place)
    next(mixer_sum)
    last = widen_sum.send((mixer_dealt[0],))
    extra_rows = captions // 2 + 16
    grad_input, mine = call(
        entry_grad_kernel,
        (
            part,
            other,
            sentence_layer_entry,
            mixer_layernorm_gamma,
            grad_residual,
            loss_stat,
            mixer_stat,
            grad_caption_low,
        ),
        ((full, F32), ((extra_rows, model_width), BF16)),
        scratch=(pltpu.VMEM((16, model_width), F32),),
        index=(core,),
        after=(last,),
    )
    extra.append(dp_gather(mine, steps[:1:-1], [mine] * len(steps)))
    last = mixer_sum.send((mine,))
    last = widen_sum.send((last,))
    last = mixer_sum.send((last,))
    last = widen_sum.send((last,))
    last = mixer_sum.send((last,))
    last = widen_sum.send((last,))
    last = mixer_sum.send((last,))
    widen_pieces = widen_sum.send(())
    near_grads, *results = call(
        functools.partial(collect_kernel, 1.0 / (2.0 * all_pairs), extra_rows),
        (*widen_pieces, loss_stat),
        (
            ((all_pairs // 2, model_width), BF16),
            ((1,), F32),
            ((2, local_width), F32),
            ((model_width,), F32),
            ((hidden,), F32),
        )
        + (((model_width,), F32),) * 5
        + (((1,), F32),),
        after=(last,),
    )
    error, grad_pair, grad_b_out, grad_b_up, grad_b_down = results[:5]
    (grad_w_up,) = call(
        unpack_widen_kernel,
        widen_pieces,
        ((widening_matrix.shape, F32),),
        index=(place,),
        after=(near_grads,),
    )
    last = mixer_sum.send((grad_w_up,))
    (grad_w_down,) = call(
        functools.partial(narrow_grad_kernel, captions // 2),
        (*sums_parts, near_grads, mp_other(near_grads)),
        ((narrowing_matrix.shape, F32),),
        scratch=(pltpu.VMEM((all_pairs, model_width), BF16),),
        index=(core,),
        after=(last,),
    )
    grad_qkv, grad_w_out = call(
        unpack_mixer_kernel,
        mixer_sum.send(()),
        ((mixer_triple_matrix.shape, F32), (mixer_result_matrix.shape, F32)),
        index=(place,),
        after=(grad_w_down,),
        limit=56,
    )
    return (
        error,
        grad_input,
        grad_qkv,
        grad_pair,
        grad_w_out,
        grad_b_out,
        grad_w_up,
        grad_b_up,
        grad_w_down,
        grad_b_down,
        *results[5:],
    )


def solution(mesh):
    placed = (
        P("dp", None),
        P("dp"),
        P(("dp", "mp"), None, None),
        P(("dp", "mp")),
        P("dp"),
        P(),
        P(),
        P(None, None, "mp"),
        P(None, "mp"),
        P("mp", None),
        P(),
        P(),
        P(),
        P(None, "mp"),
        P("mp"),
        P("mp", None),
        P(),
        P(),
        P(),
        P(),
        P(),
        P(),
        P(),
    )
    return jax.shard_map(
        local,
        mesh=mesh,
        in_specs=placed,
        out_specs=(
            P(),
            P("dp", None),
            P(None, None, "mp"),
            P(None, "mp"),
            P("mp", None),
            P(),
            P(None, "mp"),
            P("mp"),
            P("mp", None),
            P(),
            P(),
            P(),
            P(),
            P(),
            P(),
        ),
        check_vma=False,
    )
```

```python
import functools

import jax
import jax.numpy as jnp
from jax import lax
from jax.experimental import pallas as pl
from jax.experimental.pallas import tpu as pltpu
from jax.sharding import PartitionSpec as P

HEAD = 64
IMG_TOK = 145
LOW_TOK = 50
CAP_LEN = 16


EPS_TEXT = 1e-05
EPS_UNIT = 1e-06
MASKED_SCORE = -1e30
BF16 = jnp.bfloat16
F32 = jnp.float32


def mp_other(values):
    return lax.ppermute(values, "mp", [(0, 1), (1, 0)])


def dp_swap(values, mask):
    size = lax.axis_size("dp")
    return lax.ppermute(values, "dp", [(index, index ^ mask) for index in range(size)])


def group_steps(size):
    steps, stride = [], 1
    while stride < size:
        steps.append([stride, 2 * stride, 3 * stride])
        stride *= 4
    return steps


def gather_masks(steps):
    masks = [0]
    for step in steps:
        masks = [mask ^ base for mask in [0] + step for base in masks]
    return masks


def dp_parts(values, step):
    return [values] + [dp_swap(values, mask) for mask in step]


def dp_gather(values, steps, waits):
    for step, wait in zip(steps, waits):
        parts = dp_parts(values, step)
        rows = values.shape[0]
        (values,) = move(
            parts,
            (len(parts) * rows,),
            [(place, 0, rows, 0, place * rows) for place in range(len(parts))],
            (wait,),
        )
    return values


HIGH_ROWS = 160
LOW_ROWS = 64
TILE = 256
PAIR = 2 * HEAD
LANES = 128
POOL_ROWS = 32
NT = (((1,), (1,)), ((), ()))
VMEM_LIMIT = 60 * 1024 * 1024
BUSY = 10**12


def dot(left, right):
    return jnp.dot(left, right, preferred_element_type=F32)


def wide_dot(left, right):
    high = left.astype(BF16)
    rest = (left - high.astype(F32)).astype(BF16)
    return dot(high, right) + dot(rest, right)


def standard(values, epsilon):
    centered = values - jnp.mean(values, axis=-1, keepdims=True)
    variance = jnp.mean(centered * centered, axis=-1, keepdims=True)
    return centered * lax.rsqrt(variance + epsilon)


def gelu(values):
    return (0.5 * values) * (1.0 + lax.erf(values * (0.5**0.5)))


def image_kernel(
    flag_ref,
    token_ref,
    gain_ref,
    triple_hbm,
    result_hbm,
    widen_hbm,
    narrow_hbm,
    out_ref,
    wide,
    packed,
    mixed,
    queries,
    keys,
    values,
    triple,
    result,
    widen,
    narrow,
    resid_groups,
    hidden_groups,
    pooled,
    ready,
    starts,
    high_starts,
    low_starts,
    sems,
):
    _, images, width = token_ref.shape
    hidden = widen.shape[1]
    copies = fetch(
        (triple_hbm, result_hbm, widen_hbm, narrow_hbm), (triple, result, widen, narrow), sems
    )
    lane_tiles = [slice(lane, lane + LANES) for lane in range(0, width, LANES)]

    def spread(position, carry):
        rows = pl.ds(pl.multiple_of(position * images, images), images)
        for place, lanes in enumerate(lane_tiles):
            wide[place, rows, :] = token_ref[position, :, lanes].astype(F32)
        return carry

    def begin(image, carry):
        start, highs = carry
        starts[image] = start
        high = flag_ref[image] == 1

        @pl.when(high)
        def _():
            high_starts[highs] = start

        @pl.when(jnp.logical_not(high))
        def _():
            low_starts[image - highs] = start

        return start + jnp.where(high, HIGH_ROWS, LOW_ROWS), highs + jnp.where(high, 1, 0)

    total, highs = lax.fori_loop(0, images, begin, (jnp.int32(0), jnp.int32(0)))
    lax.fori_loop(0, LOW_ROWS, spread, 0, unroll=4)

    @pl.when(total > images * LOW_ROWS)
    def _():
        lax.fori_loop(LOW_ROWS, IMG_TOK, spread, 0, unroll=3)

    tail = IMG_TOK // 16 * 16

    def pack(image, carry):
        start = pl.multiple_of(starts[image], POOL_ROWS)
        high = flag_ref[image] == 1

        @pl.when(high)
        def _():
            row = lax.broadcasted_iota(jnp.int32, (HIGH_ROWS - tail, LANES), 0)
            for place, lanes in enumerate(lane_tiles):
                packed[pl.ds(start, tail), lanes] = wide[
                    place, pl.ds(image, tail, stride=images), :
                ].astype(BF16)
                last = wide[place, pl.ds(image + tail * images, 1), :]
                packed[pl.ds(start + tail, HIGH_ROWS - tail), lanes] = jnp.where(
                    row == 0, last, 0.0
                ).astype(BF16)

        @pl.when(jnp.logical_not(high))
        def _():
            for place, lanes in enumerate(lane_tiles):
                packed[pl.ds(start, LOW_ROWS), lanes] = wide[
                    place, pl.ds(image, LOW_ROWS, stride=images), :
                ].astype(BF16)

        return carry

    lax.fori_loop(0, images, pack, 0)
    packed[pl.ds(pl.multiple_of(total, POOL_ROWS), TILE), :] = jnp.zeros((TILE, width), BF16)
    tiles = lax.div(total + (TILE - 1), jnp.int32(TILE))

    copies[0].wait()

    def prepare(tile):
        rows = pl.ds(pl.multiple_of(tile * TILE, TILE), TILE)
        ready[tile % 2] = (
            standard(packed[rows, :].astype(F32), EPS_UNIT) * gain_ref[0:1, :]
        ).astype(BF16)

    def project(tile, carry):
        rows = pl.ds(pl.multiple_of(tile * TILE, TILE), TILE)
        normed = ready[tile % 2]
        queries[rows, :] = (dot(normed, triple[0]) * HEAD ** (-0.5)).astype(BF16)
        prepare(tile + 1)
        keys[rows, :] = dot(normed, triple[1]).astype(BF16)
        values[rows, :] = dot(normed, triple[2]).astype(BF16)
        return carry

    prepare(jnp.int32(0))
    lax.fori_loop(0, tiles, project, 0)

    def attend(begins, count, live):
        left = lax.broadcasted_iota(jnp.int32, (count, PAIR), 1) < HEAD
        key_live = lax.broadcasted_iota(jnp.int32, (2 * count, count), 1) < live
        places = [
            (pl.ds(pl.multiple_of(start, POOL_ROWS), count), slice(lane, lane + PAIR))
            for start in begins
            for lane in range(0, width, PAIR)
        ]
        all_scores = [dot_t(two_heads(queries[place], left), keys[place]) for place in places]
        all_powers = []
        for scores in all_scores:
            scores = jnp.where(key_live, scores, MASKED_SCORE)
            top = jnp.max(scores, axis=-1, keepdims=True)
            all_powers.append(jnp.exp(scores - top).astype(BF16))
        for place, powers in zip(places, all_powers):
            value = values[place]
            one = jnp.ones_like(value)
            first = dot(powers[:count], jnp.where(left, value, one))
            second = dot(powers[count:], jnp.where(left, one, value))
            sums = pltpu.roll(jnp.where(left, second, first), HEAD, 1)
            mixed[place] = (jnp.where(left, first, second) / sums).astype(BF16)

    def attend_all(begins, number, together, count, live):
        groups = lax.div(number, jnp.int32(together))

        def group(index, carry):
            attend([begins[index * together + step] for step in range(together)], count, live)
            return carry

        def rest(index, carry):
            attend([begins[index]], count, live)
            return carry

        lax.fori_loop(0, groups, group, 0)
        if together > 1:
            lax.fori_loop(groups * together, number, rest, 0)

    attend_all(high_starts, highs, 1, HIGH_ROWS, IMG_TOK)
    attend_all(low_starts, images - highs, 4, LOW_ROWS, LOW_TOK)

    slot = lax.broadcasted_iota(jnp.int32, (1, images), 1)
    first_row = jnp.zeros((1, images), jnp.int32)
    live_rows = jnp.zeros((1, images), jnp.int32)
    for image in range(images):
        first_row = jnp.where(slot == image, starts[image], first_row)
        live_rows = jnp.where(
            slot == image, jnp.where(flag_ref[image] == 1, IMG_TOK, LOW_TOK), live_rows
        )
    copies[1].wait()
    copies[2].wait()
    groups = TILE // POOL_ROWS

    def group_sum(rows):
        return jnp.sum(rows.reshape(groups, POOL_ROWS // 8, 8, rows.shape[1]), axis=1)

    def resume(tile):
        base = pl.multiple_of(tile * TILE, TILE)
        rows = pl.ds(base, TILE)
        place = base + lax.broadcasted_iota(jnp.int32, (TILE, images), 0)
        alive = jnp.sum(
            jnp.where((place >= first_row) & (place < first_row + live_rows), 1.0, 0.0),
            axis=1,
            keepdims=True,
        )
        residual = (packed[rows, :].astype(F32) + dot(mixed[rows, :], result[...])) * alive
        group = pl.ds(pl.multiple_of(tile * groups, groups), groups)
        resid_groups[group] = group_sum(residual)
        ready[tile % 2] = (standard(residual, EPS_UNIT) * gain_ref[1:2, :]).astype(BF16)

    def perceptron(tile, carry):
        group = pl.ds(pl.multiple_of(tile * groups, groups), groups)
        normed = ready[tile % 2]
        for chunk in range(hidden // width):
            if chunk == 1:
                resume(tile + 1)
            lanes = slice(chunk * width, (chunk + 1) * width)
            units = gelu(dot(normed, widen[:, lanes])).astype(BF16)
            hidden_groups[group, :, lanes] = group_sum(units.astype(F32))
        return carry

    resume(jnp.int32(0))
    lax.fori_loop(0, tiles, perceptron, 0)

    def pool(image, carry):
        group = lax.div(starts[image], jnp.int32(POOL_ROWS))
        high = flag_ref[image] == 1

        def add(count):
            residual, units = resid_groups[group], hidden_groups[group]
            for step in range(1, count):
                residual = residual + resid_groups[group + step]
                units = units + hidden_groups[group + step]
            pooled[pl.ds(image, 1), :width] = jnp.sum(residual, axis=0, keepdims=True)
            pooled[pl.ds(image, 1), width:] = jnp.sum(units, axis=0, keepdims=True)

        @pl.when(high)
        def _():
            add(HIGH_ROWS // POOL_ROWS)

        @pl.when(jnp.logical_not(high))
        def _():
            add(LOW_ROWS // POOL_ROWS)

        return carry

    lax.fori_loop(0, images, pool, 0)
    copies[3].wait()
    units = pooled[:, width:]
    upper = units.astype(BF16)
    lower = (units - upper.astype(F32)).astype(BF16)
    branch = dot(jnp.concatenate([upper, lower], axis=0), narrow[...])
    live = jnp.where(number_column(flag_ref) == 1, IMG_TOK, LOW_TOK).astype(F32)
    mean = (pooled[:, :width] + branch[:images] + branch[images:]) / live
    out_ref[...] = (
        mean * lax.rsqrt(jnp.sum(mean * mean, axis=-1, keepdims=True) + EPS_UNIT)
    ).astype(BF16)


def image_tower(flags, tokens, gains, triple, result, widen, narrow):
    images, _, width = tokens.shape
    hidden = widen.shape[1]
    rows = images * HIGH_ROWS + TILE
    groups = rows // POOL_ROWS
    outside = pl.BlockSpec(memory_space=pl.ANY)
    inside = pl.BlockSpec(memory_space=pltpu.VMEM)
    return pl.pallas_call(
        image_kernel,
        out_shape=jax.ShapeDtypeStruct((images, width), BF16),
        in_specs=[pl.BlockSpec(memory_space=pltpu.SMEM), inside, inside]
        + [outside] * 4,
        out_specs=inside,
        scratch_shapes=[pltpu.VMEM((width // LANES, IMG_TOK * images, LANES), F32)]
        + [pltpu.VMEM((rows, width), BF16)] * 5
        + [pltpu.VMEM(weight.shape, BF16) for weight in (triple, result, widen, narrow)]
        + [
            pltpu.VMEM((groups, 8, width), F32),
            pltpu.VMEM((groups, 8, hidden), F32),
            pltpu.VMEM((images, width + hidden), F32),
            pltpu.VMEM((2, TILE, width), BF16),
            pltpu.SMEM((images,), jnp.int32),
            pltpu.SMEM((images,), jnp.int32),
            pltpu.SMEM((images,), jnp.int32),
            pltpu.SemaphoreType.DMA((4,)),
        ],
        compiler_params=pltpu.CompilerParams(vmem_limit_bytes=VMEM_LIMIT),
        cost_estimate=pl.CostEstimate(flops=BUSY, bytes_accessed=BUSY, transcendentals=0),
    )(flags, jnp.transpose(tokens, (1, 0, 2)), gains, triple, result, widen, narrow)


TN = (((0,), (0,)), ((), ()))
BLOCK = 128
ROOT_HALF = 0.5**0.5
DENSITY = 0.3989422804014327


def dot_t(left, right):
    return lax.dot_general(left, right, NT, preferred_element_type=F32)


def t_dot(left, right):
    return lax.dot_general(left, right, TN, preferred_element_type=F32)


def fetch(sources, targets, sems):
    copies = [
        pltpu.make_async_copy(source, target, sems.at[place])
        for place, (source, target) in enumerate(zip(sources, targets))
    ]
    for copy in copies:
        copy.start()
    return copies


def caption_pool(ids_ref, captions):
    ids_row = ids_ref[...].reshape(1, -1)
    tokens = ids_row.shape[1]
    shape = (captions, tokens)
    caption = lax.broadcasted_iota(jnp.int32, shape, 0)
    token = lax.broadcasted_iota(jnp.int32, shape, 1)
    inside = (token // (tokens // captions)) == caption
    return jnp.where(inside & (ids_row != 0), 1.0, 0.0)


def valid_column(pool):
    pool = pool.astype(BF16)
    return t_dot(pool, jnp.ones((pool.shape[0], 128), BF16))[:, 0:1]


def number_column(ref):
    shape = (ref.shape[0], 1)
    place = lax.broadcasted_iota(jnp.int32, shape, 0)
    column = jnp.zeros(shape, jnp.int32)
    for index in range(shape[0]):
        column = jnp.where(place == index, ref[index], column)
    return column


def as_row(ref):
    return ref[...].reshape(1, -1)


def pair_masks(rows, pair_width):
    return lax.broadcasted_iota(jnp.int32, (rows, pair_width), 1) < HEAD


def two_heads(values, left):
    zero = jnp.zeros_like(values)
    return jnp.concatenate(
        [jnp.where(left, values, zero), jnp.where(left, zero, values)], axis=0
    )


def text_mix_kernel(
    entry_ref,
    ids_ref,
    gain_ref,
    shift_ref,
    triple_ref,
    pair_ref,
    result_ref,
    normed_ref,
    qkv_ref,
    soft_ref,
    mixed_ref,
    part_ref,
):
    tokens = entry_ref.shape[0]
    width = result_ref.shape[0]
    normed = (
        standard(entry_ref[...].astype(F32), EPS_TEXT) * as_row(gain_ref) + as_row(shift_ref)
    ).astype(BF16)
    normed_ref[...] = normed
    qkv_ref[0] = (dot(normed, triple_ref[0]) + pair_ref[0:1, :]).astype(BF16)
    qkv_ref[1] = dot(normed, triple_ref[1]).astype(BF16)
    qkv_ref[2] = (dot(normed, triple_ref[2]) + pair_ref[1:2, :]).astype(BF16)
    ids = as_row(ids_ref)
    left = pair_masks(BLOCK, PAIR)
    shape = (2 * BLOCK, BLOCK)
    query_caption = lax.broadcasted_iota(jnp.int32, shape, 0) % BLOCK // CAP_LEN
    same = query_caption == lax.broadcasted_iota(jnp.int32, shape, 1) // CAP_LEN
    for block in range(tokens // BLOCK):
        rows = slice(block * BLOCK, (block + 1) * BLOCK)
        seen = same & (ids[:, rows] != 0)
        for pair in range(width // PAIR):
            lanes = slice(pair * PAIR, (pair + 1) * PAIR)
            scores = dot_t(two_heads(qkv_ref[0, rows, lanes], left), qkv_ref[1, rows, lanes])
            scores = jnp.where(seen, scores * HEAD ** (-0.5), MASKED_SCORE)
            powers = jnp.exp(scores - jnp.max(scores, axis=-1, keepdims=True))
            soft = powers / jnp.sum(powers, axis=-1, keepdims=True)
            soft_ref[block, pair] = soft
            low = soft.astype(BF16)
            value = qkv_ref[2, rows, lanes]
            mixed_ref[rows, lanes] = jnp.where(
                left, dot(low[:BLOCK], value), dot(low[BLOCK:], value)
            ).astype(BF16)
    part_ref[...] = dot(mixed_ref[...], result_ref[...])


def text_widen_kernel(
    entry_ref,
    own_ref,
    other_ref,
    result_offset_ref,
    gain_ref,
    shift_ref,
    widen_offset_ref,
    ids_ref,
    widen_hbm,
    narrow_hbm,
    residual_ref,
    normed_ref,
    slope_ref,
    sums_ref,
    resid_sum_ref,
    branch_ref,
    widen,
    narrow,
    hidden_sum,
    sems,
):
    captions = sums_ref.shape[0]
    width = entry_ref.shape[1]
    copies = fetch((widen_hbm, narrow_hbm), (widen, narrow), sems)
    residual = entry_ref[...].astype(F32) + (
        (own_ref[...] + other_ref[...]) + as_row(result_offset_ref)
    )
    residual_ref[...] = residual
    normed = (standard(residual, EPS_TEXT) * as_row(gain_ref) + as_row(shift_ref)).astype(BF16)
    normed_ref[...] = normed
    pool = caption_pool(ids_ref, captions).astype(BF16)
    widen_offset = as_row(widen_offset_ref)
    upper = residual.astype(BF16)
    resid_sum_ref[...] = dot(pool, upper) + dot(
        pool, (residual - upper.astype(F32)).astype(BF16)
    )
    valid = valid_column(pool)
    copies[0].wait()
    for chunk in range(widen.shape[1] // width):
        lanes = slice(chunk * width, (chunk + 1) * width)
        before = dot(normed, widen[:, lanes]) + widen_offset[:, lanes]
        share = 0.5 * (1.0 + lax.erf(before * ROOT_HALF))
        hidden_sum[:, lanes] = dot(pool, (before * share).astype(BF16))
        slope = share + before * (jnp.exp(-0.5 * before * before) * DENSITY)
        slope_ref[:, lanes] = slope * valid
    sums_ref[...] = hidden_sum[...].astype(BF16)
    copies[1].wait()
    branch_ref[...] = wide_dot(hidden_sum[...], narrow[...])


def logits_kernel(
    masks,
    index_ref,
    matched_ref,
    sharpen_ref,
    near_ref,
    far_ref,
    resid_sum_ref,
    own_ref,
    other_ref,
    narrow_offset_ref,
    ids_ref,
    images_ref,
    unit_ref,
    factor_ref,
    logits_ref,
    powers_ref,
    row_sum_ref,
    col_sum_ref,
    loss_ref,
):
    captions, pairs = logits_ref.shape
    rows = images_ref.shape[0] // (2 * len(masks))
    core = index_ref[1]
    for place, mask in enumerate(masks):
        start = (index_ref[0] ^ mask) * (2 * rows)
        images_ref[pl.ds(pl.multiple_of(start + core * rows, rows), rows), :] = near_ref[
            place * rows : (place + 1) * rows, :
        ]
        images_ref[pl.ds(pl.multiple_of(start + (1 - core) * rows, rows), rows), :] = far_ref[
            place * rows : (place + 1) * rows, :
        ]
    count = jnp.sum(caption_pool(ids_ref, captions), axis=1, keepdims=True)
    pooled = (resid_sum_ref[...] + (own_ref[...] + other_ref[...])) / count + as_row(
        narrow_offset_ref
    )
    inverse = lax.rsqrt(jnp.sum(pooled * pooled, axis=-1, keepdims=True) + EPS_UNIT)
    unit = pooled * inverse
    unit_ref[...] = unit
    factor_ref[...] = jnp.broadcast_to(inverse / count, factor_ref.shape)
    logits = jnp.exp(jnp.full((1, 1), sharpen_ref[0], F32)) * dot_t(unit.astype(BF16), images_ref[...])
    logits_ref[...] = logits
    powers = jnp.exp(logits)
    powers_ref[...] = powers
    row_sum = jnp.sum(powers, axis=1, keepdims=True)
    row_sum_ref[...] = jnp.broadcast_to(row_sum, row_sum_ref.shape)
    col_sum_ref[...] = jnp.sum(powers, axis=0, keepdims=True)
    positive = number_column(matched_ref) == lax.broadcasted_iota(jnp.int32, (captions, pairs), 1)
    wanted = jnp.sum(jnp.where(positive, logits, 0.0), axis=1, keepdims=True)
    loss_ref[...] = jnp.broadcast_to(
        jnp.sum(jnp.log(row_sum) - 2.0 * wanted, axis=0, keepdims=True), loss_ref.shape
    )


def sum_kernel(first_ref, second_ref, third_ref, fourth_ref, out_ref):
    out_ref[...] = (first_ref[...] + second_ref[...]) + (third_ref[...] + fourth_ref[...])


def loss_grad_kernel(
    matched_ref,
    sharpen_ref,
    col_ref,
    col1_ref,
    col2_ref,
    col3_ref,
    logits_ref,
    powers_ref,
    row_sum_ref,
    unit_ref,
    factor_ref,
    images_ref,
    ids_ref,
    loss_ref,
    narrow_hbm,
    slope_hbm,
    widen_hbm,
    grad_ref,
    low_ref,
    before_ref,
    part_ref,
    stat_ref,
    narrow,
    slope,
    widen,
    sems,
):
    captions, pairs = logits_ref.shape
    tokens, hidden = slope.shape
    width = grad_ref.shape[1]
    copies = fetch((narrow_hbm, slope_hbm, widen_hbm), (narrow, slope, widen), sems)
    logits, powers = logits_ref[...], powers_ref[...]
    col_sum = (col_ref[...] + col1_ref[...]) + (col2_ref[...] + col3_ref[...])
    positive = number_column(matched_ref) == lax.broadcasted_iota(jnp.int32, (captions, pairs), 1)
    derivative = (
        powers / row_sum_ref[:, 0:1] + powers / col_sum - jnp.where(positive, 2.0, 0.0)
    ) / (2.0 * pairs)
    temperature = jnp.sum(
        jnp.sum(derivative * logits, axis=1, keepdims=True), axis=0, keepdims=True
    )
    col_loss = jnp.sum(jnp.log(col_sum), axis=1, keepdims=True)
    text = dot((derivative * jnp.exp(jnp.full((1, 1), sharpen_ref[0], F32))).astype(BF16), images_ref[...])
    unit = unit_ref[...]
    grad = (text - unit * jnp.sum(unit * text, axis=-1, keepdims=True)) * factor_ref[:, 0:1]
    grad_ref[...] = grad
    low = grad.astype(BF16)
    low_ref[...] = low
    copies[0].wait()
    copies[1].wait()
    copies[2].wait()
    ones = jnp.ones((8, tokens), BF16)
    part = jnp.zeros(part_ref.shape, F32)
    for chunk in range(hidden // width):
        lanes = slice(chunk * width, (chunk + 1) * width)
        back = dot_t(low, narrow[lanes, :])
        before = (
            (back[:, None, :] * slope[:, lanes].reshape(captions, CAP_LEN, width))
            .reshape(tokens, width)
            .astype(BF16)
        )
        before_ref[:, lanes] = before
        stat_ref[chunk : chunk + 1, :] = dot(ones, before)[0:1]
        part = part + dot_t(before, widen[:, lanes])
    part_ref[...] = part
    count = jnp.sum(caption_pool(ids_ref, captions), axis=1, keepdims=True)
    stat_ref[2:3, :] = jnp.sum(low.astype(F32) * count, axis=0, keepdims=True)
    lane = lax.broadcasted_iota(jnp.int32, (1, width), 1)
    stat_ref[3:4, :] = jnp.where(
        lane == 0,
        temperature,
        jnp.where(lane == 1, loss_ref[0:1, 0:1], jnp.where(lane == 2, col_loss, 0.0)),
    )
    stat_ref[4:8, :] = jnp.zeros((4, width), F32)


def deal(index_ref, first, second, outs):
    half = first.shape[0] // 2
    for place, (values, bit) in enumerate(((first, 1), (second, 2))):
        mine = index_ref[0] // bit % 2
        for ref, which in ((outs[2 * place], 1 - mine), (outs[2 * place + 1], mine)):
            ref[...] = values[pl.ds(pl.multiple_of(which * half, half), half), :]


def widen_grad_kernel(index_ref, normed_ref, before_ref, *refs):
    outs, (first, second) = refs[:4], refs[4:]
    width = first.shape[1]
    normed = normed_ref[...]
    first[...] = t_dot(normed, before_ref[:, :width]).astype(BF16)
    second[...] = t_dot(normed, before_ref[:, width:]).astype(BF16)
    deal(index_ref, first, second, outs)


def mixer_back_kernel(
    own_ref,
    other_ref,
    residual_ref,
    grad_ref,
    ids_ref,
    gain_ref,
    result_ref,
    qkv_hbm,
    soft_hbm,
    triple_hbm,
    grad_residual_ref,
    low_ref,
    flat_ref,
    part_ref,
    stat_ref,
    qkv,
    soft_all,
    triple,
    sems,
):
    tokens, width = residual_ref.shape
    captions = grad_ref.shape[0]
    local_width = result_ref.shape[0]
    copies = fetch((qkv_hbm, soft_hbm, triple_hbm), (qkv, soft_all, triple), sems)
    residual = residual_ref[...]
    centered = residual - jnp.mean(residual, axis=-1, keepdims=True)
    rate = lax.rsqrt(jnp.mean(centered * centered, axis=-1, keepdims=True) + EPS_TEXT)
    unit = centered * rate
    grad = own_ref[...] + other_ref[...]
    stat_ref[1:2, :] = jnp.sum(grad * unit, axis=0, keepdims=True)
    stat_ref[2:3, :] = jnp.sum(grad, axis=0, keepdims=True)
    scaled = grad * as_row(gain_ref)
    inner = rate * (
        scaled
        - jnp.mean(scaled, axis=-1, keepdims=True)
        - unit * jnp.mean(scaled * unit, axis=-1, keepdims=True)
    )
    spread = jnp.broadcast_to(
        grad_ref[...][:, None, :], (captions, tokens // captions, width)
    ).reshape(tokens, width)
    grad_residual = spread * valid_column(caption_pool(ids_ref, captions)) + inner
    grad_residual_ref[...] = grad_residual
    low = grad_residual.astype(BF16)
    low_ref[...] = low
    ones = jnp.ones((8, tokens), BF16)
    stat_ref[0:1, :] = dot(ones, low)[0:1]
    grad_mixed = dot_t(low, result_ref[...]).astype(BF16)
    for copy in copies:
        copy.wait()
    left = pair_masks(BLOCK, PAIR)
    places = [
        (block, pair, slice(block * BLOCK, (block + 1) * BLOCK), slice(pair * PAIR, (pair + 1) * PAIR))
        for block in range(tokens // BLOCK)
        for pair in range(local_width // PAIR)
    ]
    mixed = [two_heads(grad_mixed[rows, lanes], left) for _, _, rows, lanes in places]
    softs = [soft_all[block, pair] for block, pair, _, _ in places]
    grads = [
        dot_t(value, qkv[2, rows, lanes]) for value, (_, _, rows, lanes) in zip(mixed, places)
    ]
    scores = [
        (soft * (grad - jnp.sum(grad * soft, axis=-1, keepdims=True))).astype(BF16)
        for soft, grad in zip(softs, grads)
    ]
    for value, soft, (_, _, rows, lanes) in zip(mixed, softs, places):
        flat_ref[2, rows, lanes] = t_dot(soft.astype(BF16), value).astype(BF16)
    for score, (_, _, rows, lanes) in zip(scores, places):
        key = qkv[1, rows, lanes]
        back = jnp.where(left, dot(score[:BLOCK], key), dot(score[BLOCK:], key))
        flat_ref[0, rows, lanes] = (back * HEAD ** (-0.5)).astype(BF16)
    for score, (_, _, rows, lanes) in zip(scores, places):
        flat_ref[1, rows, lanes] = (
            t_dot(score, two_heads(qkv[0, rows, lanes], left)) * HEAD ** (-0.5)
        ).astype(BF16)
    part_ref[...] = (
        dot_t(flat_ref[0], triple[0])
        + dot_t(flat_ref[1], triple[1])
        + dot_t(flat_ref[2], triple[2])
    )
    stat_ref[3:4, :local_width] = dot(ones, flat_ref[0])[0:1]
    stat_ref[3:4, local_width:] = dot(ones, flat_ref[2])[0:1]
    stat_ref[4:8, :] = jnp.zeros((4, width), F32)


def mixer_grad_kernel(index_ref, normed_ref, flat_ref, mixed_ref, low_ref, *refs):
    outs, (first, second) = refs[:4], refs[4:]
    half = flat_ref.shape[2]
    rows = first.shape[0] // 2
    normed = normed_ref[...]
    for part, (target, place) in enumerate(((first, 0), (first, rows), (second, 0))):
        grad = t_dot(normed, flat_ref[part]).astype(BF16)
        target[place : place + rows, :half] = grad[:rows]
        target[place : place + rows, half:] = grad[rows:]
    second[rows:, :] = t_dot(mixed_ref[...], low_ref[...]).astype(BF16)
    deal(index_ref, first, second, outs)


def narrow_grad_kernel(half, index_ref, *refs):
    parts, (near_ref, far_ref, out_ref, grads) = refs[:-4], refs[-4:]
    rows, width = parts[0].shape[0], grads.shape[1]
    for place in range(near_ref.shape[0] // half):
        for ref, which in ((near_ref, index_ref[0]), (far_ref, 1 - index_ref[0])):
            start = pl.multiple_of((2 * place + which) * half, half)
            grads[pl.ds(start, half), :] = ref[place * half : (place + 1) * half, :]
    for chunk in range(out_ref.shape[0] // width):
        lanes = slice(chunk * width, (chunk + 1) * width)
        total = t_dot(parts[0][:, lanes], grads[:rows, :])
        for place in range(1, len(parts)):
            total = total + t_dot(
                parts[place][:, lanes], grads[place * rows : (place + 1) * rows, :]
            )
        out_ref[lanes, :] = total


def entry_grad_kernel(
    index_ref,
    own_ref,
    other_ref,
    entry_ref,
    gain_ref,
    grad_residual_ref,
    loss_stat_ref,
    mixer_stat_ref,
    caption_ref,
    out_ref,
    extra_ref,
    pack,
):
    entry = entry_ref[...].astype(F32)
    centered = entry - jnp.mean(entry, axis=-1, keepdims=True)
    rate = lax.rsqrt(jnp.mean(centered * centered, axis=-1, keepdims=True) + EPS_TEXT)
    unit = centered * rate
    grad = own_ref[...] + other_ref[...]
    pack[0:8, :] = loss_stat_ref[...]
    pack[8:16, :] = mixer_stat_ref[...]
    pack[4:5, :] = jnp.sum(grad * unit, axis=0, keepdims=True)
    pack[5:6, :] = jnp.sum(grad, axis=0, keepdims=True)
    half = caption_ref.shape[0] // 2
    extra_ref[:half, :] = caption_ref[
        pl.ds(pl.multiple_of(index_ref[0] * half, half), half), :
    ]
    upper = pack[...].astype(BF16).astype(F32)
    pack[15:16, :] = (pack[...] - upper)[3:4, :]
    extra_ref[half:, :] = pack[...].astype(BF16)
    scaled = grad * as_row(gain_ref)
    out_ref[...] = grad_residual_ref[...] + rate * (
        scaled
        - jnp.mean(scaled, axis=-1, keepdims=True)
        - unit * jnp.mean(scaled * unit, axis=-1, keepdims=True)
    )


def tree_sum(values):
    while len(values) > 1:
        values = [values[place] + values[place + 1] for place in range(0, len(values), 2)]
    return values[0]


def collect_kernel(
    scale,
    rows,
    joined_ref,
    along_x_ref,
    along_y_ref,
    first_far_ref,
    second_far_ref,
    loss_ref,
    near_ref,
    error_ref,
    pair_ref,
    result_ref,
    widen_ref,
    narrow_ref,
    gain1_ref,
    shift1_ref,
    gain2_ref,
    shift2_ref,
    temperature_ref,
):
    half = rows - 16
    first = second_far_ref.shape[0]
    count = (first_far_ref.shape[0] - first) // rows
    totals = []
    for piece, ref in enumerate((joined_ref, along_x_ref, along_y_ref, first_far_ref)):
        for place in range(count):
            row = first + place * rows
            near_ref[pl.ds((piece * count + place) * half, half), :] = ref[row : row + half, :]
            totals.append(ref[row + half : row + rows, :].astype(F32))
    total = tree_sum(totals)
    scalars = total[3:4] + total[15:16]
    error_ref[...] = ((scalars[:, 1:2] + loss_ref[3:4, 2:3]) * scale).reshape(1)
    temperature_ref[...] = scalars[:, 0:1].reshape(1)
    lanes = pair_ref.shape[1]
    pair_ref[0:1, :] = total[11:12, :lanes]
    pair_ref[1:2, :] = total[11:12, lanes:]
    width = total.shape[1]
    for chunk in range(widen_ref.shape[0] // width):
        widen_ref[chunk * width : (chunk + 1) * width] = total[chunk]
    for ref, place in (
        (narrow_ref, 2),
        (gain1_ref, 4),
        (shift1_ref, 5),
        (result_ref, 8),
        (gain2_ref, 9),
        (shift2_ref, 10),
    ):
        ref[...] = total[place]


def call(kernel, inside, shapes, outside=(), scratch=(), index=(), small=(), after=(), limit=24):
    vmem = pl.BlockSpec(memory_space=pltpu.VMEM)
    extra = [pltpu.VMEM(array.shape, array.dtype) for array in outside]
    extra += list(scratch)
    if outside:
        extra += [pltpu.SemaphoreType.DMA((len(outside),))]
    index = [jnp.stack(index).astype(jnp.int32)] if index else []
    small = index + list(small)
    before = len(small) + len(inside) + len(outside)

    def body(*refs):
        kernel(*refs[:before], *refs[before + len(after) :])

    return pl.pallas_call(
        body,
        out_shape=[jax.ShapeDtypeStruct(shape, kind) for shape, kind in shapes],
        in_specs=[pl.BlockSpec(memory_space=pltpu.SMEM)] * len(small)
        + [vmem] * len(inside)
        + [pl.BlockSpec(memory_space=pl.ANY)] * (len(outside) + len(after)),
        out_specs=[vmem] * len(shapes),
        scratch_shapes=extra,
        compiler_params=pltpu.CompilerParams(vmem_limit_bytes=limit * 1024 * 1024),
        cost_estimate=pl.CostEstimate(flops=BUSY, bytes_accessed=BUSY, transcendentals=0),
    )(*small, *inside, *outside, *after)


def move(arrays, sizes, plan, after=()):
    width, kind = arrays[0].shape[1], arrays[0].dtype

    def body(*refs):
        ins, outs = refs[: len(arrays)], refs[len(arrays) :]
        for source, first, rows, target, start in plan:
            outs[target][start : start + rows, :] = ins[source][first : first + rows, :]

    return call(body, arrays, tuple(((size, width), kind) for size in sizes), after=after)


GROUP = 16
Z_STRIDE, Z_SIZE = 4, 4


def block_rows(block, rows):
    return pl.ds(pl.multiple_of(block * rows, rows), rows)


def fold_kernel(index_ref, *refs):
    ins, outs = refs[:4], refs[4:]
    half = outs[0].shape[0]
    for place, bit in ((0, 2), (1, 1)):
        mine = index_ref[0] // bit % 2
        for out, which in ((outs[2 * place], 1 - mine), (outs[2 * place + 1], mine)):
            rows = block_rows(which, half)
            out[...] = (
                ins[2 * place][rows, :].astype(F32) + ins[2 * place + 1][rows, :].astype(F32)
            ).astype(out.dtype)


def cut_kernel(index_ref, *refs):
    ins, outs = refs[:4], refs[4:]
    rows = ins[0].shape[0] // Z_SIZE
    for place in range(2):
        for step, out in enumerate(outs):
            block = block_rows((index_ref[0] // Z_STRIDE % Z_SIZE) ^ step, rows)
            out[place * rows : (place + 1) * rows, :] = (
                ins[2 * place][block, :] + ins[2 * place + 1][block, :].astype(F32)
            ).astype(out.dtype)


def add_kernel(own_ref, *refs):
    out_ref = refs[-1]
    rows = own_ref.shape[0]
    total = own_ref[...]
    for ref in refs[: Z_SIZE - 1]:
        total = total + ref[...].astype(F32)
    out_ref[:rows, :] = total.astype(out_ref.dtype)
    if out_ref.shape[0] > rows:
        out_ref[rows:, :] = refs[Z_SIZE - 1][...]


def scatter_steps(dealt, place, extra=None):
    first_sent, first_kept, second_sent, second_kept = dealt
    rows, width = first_sent.shape
    after = yield
    arrived = (dp_swap(first_sent, 1), dp_swap(second_sent, 2))
    half = (rows // 2, width)
    first_sent, first_kept, second_sent, second_kept = call(
        fold_kernel,
        (first_kept, arrived[0], second_kept, arrived[1]),
        ((half, BF16), (half, F32), (half, BF16), (half, F32)),
        index=(place,),
        after=after,
    )
    after = yield first_kept
    arrived = (dp_swap(first_sent, 2), dp_swap(second_sent, 1))
    block = (rows // Z_SIZE, width)
    own, *sent = call(
        cut_kernel,
        (first_kept, arrived[0], second_kept, arrived[1]),
        ((block, F32),) + ((block, BF16),) * (Z_SIZE - 1),
        index=(place,),
        after=after,
    )
    after = yield own
    arrived = [dp_swap(values, step * Z_STRIDE) for step, values in enumerate(sent, 1)]
    size = lax.axis_size("dp")
    more = 0 if extra is None else extra[0].shape[0]
    if size > GROUP:
        (mine,) = call(add_kernel, (own, *arrived), ((own.shape, F32),), after=after)
        groups = [list(range(index, size, GROUP)) for index in range(GROUP)]
        mine = lax.psum(mine, "dp", axis_index_groups=groups).astype(BF16)
        if more:
            mine = jnp.concatenate([mine, *extra], axis=0)
    else:
        (mine,) = call(
            add_kernel,
            (own, *arrived) + (tuple(extra) if more else ()),
            (((block[0] + more, width), BF16),),
            after=after,
        )
    after = yield mine
    pieces = [mine] + [dp_swap(mine, step * Z_STRIDE) for step in range(1, Z_SIZE)]
    half = block[0] // 2
    plan, start = [], 0
    for first, count in ((0, half), (2 * half, more), (half, half)):
        for piece in range(Z_SIZE):
            if count:
                plan.append((piece, first, count, 0, start))
            start += count
    (joined,) = move(pieces, (start,), plan, after)
    along_x, along_y = dp_swap(joined, 1), dp_swap(joined, 2)
    after = yield joined
    share = Z_SIZE * half
    first, second = move(
        (along_y, along_x),
        (start - share, share),
        ((0, 0, start - share, 0, 0), (1, start - share, share, 1, 0)),
        after,
    )
    after = yield first
    yield joined, along_x, along_y, dp_swap(first, 1), dp_swap(second, 2)


def block_home(index, block, outer, inner):
    high = (block // 8) ^ (index // outer % 2)
    middle = (block // 4 % 2) ^ (index // inner % 2)
    return high * 8 + middle * 4 + ((block % 4) ^ (index // Z_STRIDE % Z_SIZE))


def relative_blocks(refs, tensor):
    joined, along_x, along_y, first_far, second_far = refs
    size = second_far.shape[0]
    start = joined.shape[0] - size if tensor else 0
    if tensor:
        pieces = ((joined, start), (along_x, start), (along_y, start), (second_far, 0))
    else:
        pieces = ((joined, 0), (along_y, 0), (along_x, 0), (first_far, 0))
    rows = size // Z_SIZE
    for piece, (ref, start) in enumerate(pieces):
        for step in range(Z_SIZE):
            first = start + step * rows
            yield piece * Z_SIZE + step, rows, ref[first : first + rows, :]


def unpack_widen_kernel(index_ref, *refs):
    refs, out_ref = refs[:-1], refs[-1]
    width = out_ref.shape[1] // 2
    for tensor, bits in ((0, (1, 2)), (1, (2, 1))):
        for block, rows, values in relative_blocks(refs, tensor):
            start = pl.multiple_of(block_home(index_ref[0], block, *bits) * rows, rows)
            out_ref[pl.ds(start, rows), tensor * width : (tensor + 1) * width] = values.astype(F32)


def unpack_mixer_kernel(index_ref, *refs):
    refs, (triple_ref, result_ref) = refs[:-2], refs[-2:]
    half, split = triple_ref.shape[2], triple_ref.shape[1] // 2
    for block, rows, values in relative_blocks(refs, 0):
        home = block_home(index_ref[0], block, 1, 2)
        part, row = home // 8, pl.multiple_of(home % 8 * rows, rows)
        triple_ref[part, pl.ds(row, rows), :] = values[:, :half].astype(F32)
        triple_ref[part, pl.ds(split + row, rows), :] = values[:, half:].astype(F32)
    for block, rows, values in relative_blocks(refs, 1):
        home = block_home(index_ref[0], block, 2, 1)
        row = pl.multiple_of(home % 8 * rows, rows)

        @pl.when(home < 8)
        def _():
            triple_ref[2, pl.ds(row, rows), :] = values[:, :half].astype(F32)
            triple_ref[2, pl.ds(split + row, rows), :] = values[:, half:].astype(F32)

        @pl.when(home >= 8)
        def _():
            result_ref[pl.ds(row, rows), :] = values.astype(F32)


def local(
    sentence_layer_entry,
    sentence_word_ids,
    picture_tile_activations,
    picture_detail_flag,
    matched_picture_ids,
    mixer_layernorm_gamma,
    mixer_layernorm_offset,
    mixer_triple_matrix,
    mixer_pair_offsets,
    mixer_result_matrix,
    mixer_result_offset,
    perceptron_layernorm_gamma,
    perceptron_layernorm_offset,
    widening_matrix,
    widening_offset,
    narrowing_matrix,
    narrowing_offset,
    sharpening_log,
    locked_layernorm_gammas,
    locked_mixer_triple_matrix,
    locked_mixer_result_matrix,
    locked_widening_matrix,
    locked_narrowing_matrix,
):
    captions = matched_picture_ids.shape[0]
    tokens, model_width = sentence_layer_entry.shape
    local_width = mixer_result_matrix.shape[0]
    hidden = narrowing_matrix.shape[0]
    devices = lax.axis_size("dp")
    all_pairs = captions * devices
    place, core = lax.axis_index("dp"), lax.axis_index("mp")
    blocks = tokens // BLOCK
    full = (tokens, model_width)
    short = (captions, model_width)
    square = (model_width, model_width)
    half_square = (model_width // 2, model_width)
    dealt = ((half_square, BF16),) * 4

    steps = group_steps(devices)

    image_emb = image_tower(
        picture_detail_flag,
        picture_tile_activations,
        locked_layernorm_gammas,
        locked_mixer_triple_matrix,
        locked_mixer_result_matrix,
        locked_widening_matrix,
        locked_narrowing_matrix,
    )
    normed, qkv, soft, mixed, part = call(
        text_mix_kernel,
        (
            sentence_layer_entry,
            sentence_word_ids,
            mixer_layernorm_gamma,
            mixer_layernorm_offset,
            mixer_triple_matrix,
            mixer_pair_offsets,
            mixer_result_matrix,
        ),
        (
            (full, BF16),
            ((3, tokens, local_width), BF16),
            ((blocks, local_width // PAIR, 2 * BLOCK, BLOCK), F32),
            ((tokens, local_width), BF16),
            (full, F32),
        ),
        after=(image_emb,),
        limit=60,
    )
    other = mp_other(part)
    near_images = dp_gather(image_emb, steps[:0:-1], [part] * (len(steps) - 1))
    residual, normed2, slope, hidden_sums, resid_sum, branch = call(
        text_widen_kernel,
        (
            sentence_layer_entry,
            part,
            other,
            mixer_result_offset,
            perceptron_layernorm_gamma,
            perceptron_layernorm_offset,
            widening_offset,
            sentence_word_ids,
        ),
        (
            (full, F32),
            (full, BF16),
            ((tokens, hidden), F32),
            ((captions, hidden), BF16),
            (short, F32),
            (short, F32),
        ),
        outside=(widening_matrix, narrowing_matrix),
        scratch=(pltpu.VMEM((captions, hidden), F32),),
        after=(near_images,),
    )

    near_images = dp_gather(near_images, steps[:1], (branch,))
    sums_parts = dp_parts(hidden_sums, steps[-1])
    images, unit, factor, logits, powers, row_sum, col_sum, row_loss = call(
        functools.partial(logits_kernel, gather_masks(steps[::-1])),
        (
            near_images,
            mp_other(near_images),
            resid_sum,
            branch,
            mp_other(branch),
            narrowing_offset,
            sentence_word_ids,
        ),
        (
            ((all_pairs, model_width), BF16),
            (short, F32),
            ((captions, 128), F32),
            ((captions, all_pairs), F32),
            ((captions, all_pairs), F32),
            ((captions, 128), F32),
            ((1, all_pairs), F32),
            ((8, 128), F32),
        ),
        index=(place, core),
        small=(matched_picture_ids, sharpening_log),
    )
    after = (unit,)
    for step in steps[-2::-1]:
        rows = sums_parts[0].shape[0]
        (joined_sums,) = move(
            sums_parts,
            (4 * rows,),
            [(place, 0, rows, 0, place * rows) for place in range(4)],
            after,
        )
        sums_parts, after = dp_parts(joined_sums, step), (joined_sums,)
    col_parts = dp_parts(col_sum, steps[0])
    for step in steps[1:]:
        (col_sum,) = call(sum_kernel, col_parts, ((col_sum.shape, F32),), after=after)
        col_parts = dp_parts(col_sum, step)
    grad_caption, grad_caption_low, grad_pre, part, loss_stat = call(
        loss_grad_kernel,
        (
            *col_parts,
            logits,
            powers,
            row_sum,
            unit,
            factor,
            images,
            sentence_word_ids,
            row_loss,
        ),
        (
            (short, F32),
            (short, BF16),
            ((tokens, hidden), BF16),
            (full, F32),
            ((8, model_width), F32),
        ),
        outside=(narrowing_matrix, slope, widening_matrix),
        small=(matched_picture_ids, sharpening_log),
    )

    other = mp_other(part)
    widen_dealt = call(
        widen_grad_kernel,
        (normed2, grad_pre),
        dealt,
        scratch=(pltpu.VMEM(square, BF16),) * 2,
        index=(place,),
    )
    grad_residual, grad_branch1, flat, part, mixer_stat = call(
        mixer_back_kernel,
        (
            part,
            other,
            residual,
            grad_caption,
            sentence_word_ids,
            perceptron_layernorm_gamma,
            mixer_result_matrix,
        ),
        (
            (full, F32),
            (full, BF16),
            ((3, tokens, local_width), BF16),
            (full, F32),
            ((8, model_width), F32),
        ),
        outside=(qkv, soft, mixer_triple_matrix),
        after=(widen_dealt[0],),
    )
    other = mp_other(part)
    extra = []
    widen_sum = scatter_steps(widen_dealt, place, extra)
    next(widen_sum)
    mixer_dealt = call(
        mixer_grad_kernel,
        (normed, flat, mixed, grad_branch1),
        dealt,
        scratch=(pltpu.VMEM(square, BF16),) * 2,
        index=(place,),
        after=sums_parts,
    )
    mixer_sum = scatter_steps(mixer_dealt, place)
    next(mixer_sum)
    last = widen_sum.send((mixer_dealt[0],))
    last = widen_sum.send((last,))
    extra_rows = captions // 2 + 16
    grad_input, mine = call(
        entry_grad_kernel,
        (
            part,
            other,
            sentence_layer_entry,
            mixer_layernorm_gamma,
            grad_residual,
            loss_stat,
            mixer_stat,
            grad_caption_low,
        ),
        ((full, F32), ((extra_rows, model_width), BF16)),
        scratch=(pltpu.VMEM((16, model_width), F32),),
        index=(core,),
        after=(last,),
    )
    extra.append(dp_gather(mine, steps[:1:-1], [mine] * len(steps)))
    last = mixer_sum.send((mine,))
    last = widen_sum.send((last,))
    last = mixer_sum.send((last,))
    last = widen_sum.send((last,))
    last = mixer_sum.send((last,))
    last = widen_sum.send((last,))
    last = mixer_sum.send((last,))
    widen_pieces = widen_sum.send(())
    near_grads, *results = call(
        functools.partial(collect_kernel, 1.0 / (2.0 * all_pairs), extra_rows),
        (*widen_pieces, loss_stat),
        (
            ((all_pairs // 2, model_width), BF16),
            ((1,), F32),
            ((2, local_width), F32),
            ((model_width,), F32),
            ((hidden,), F32),
        )
        + (((model_width,), F32),) * 5
        + (((1,), F32),),
        after=(last,),
    )
    error, grad_pair, grad_b_out, grad_b_up, grad_b_down = results[:5]
    (grad_w_up,) = call(
        unpack_widen_kernel,
        widen_pieces,
        ((widening_matrix.shape, F32),),
        index=(place,),
        after=(near_grads,),
        limit=56,
    )
    last = mixer_sum.send((grad_w_up,))
    (grad_w_down,) = call(
        functools.partial(narrow_grad_kernel, captions // 2),
        (*sums_parts, near_grads, mp_other(near_grads)),
        ((narrowing_matrix.shape, F32),),
        scratch=(pltpu.VMEM((all_pairs, model_width), BF16),),
        index=(core,),
        after=(last,),
    )
    grad_qkv, grad_w_out = call(
        unpack_mixer_kernel,
        mixer_sum.send(()),
        ((mixer_triple_matrix.shape, F32), (mixer_result_matrix.shape, F32)),
        index=(place,),
        after=(grad_w_down,),
        limit=56,
    )
    return (
        error,
        grad_input,
        grad_qkv,
        grad_pair,
        grad_w_out,
        grad_b_out,
        grad_w_up,
        grad_b_up,
        grad_w_down,
        grad_b_down,
        *results[5:],
    )


def solution(mesh):
    placed = (
        P("dp", None),
        P("dp"),
        P(("dp", "mp"), None, None),
        P(("dp", "mp")),
        P("dp"),
        P(),
        P(),
        P(None, None, "mp"),
        P(None, "mp"),
        P("mp", None),
        P(),
        P(),
        P(),
        P(None, "mp"),
        P("mp"),
        P("mp", None),
        P(),
        P(),
        P(),
        P(),
        P(),
        P(),
        P(),
    )
    return jax.shard_map(
        local,
        mesh=mesh,
        in_specs=placed,
        out_specs=(
            P(),
            P("dp", None),
            P(None, None, "mp"),
            P(None, "mp"),
            P("mp", None),
            P(),
            P(None, "mp"),
            P("mp"),
            P("mp", None),
            P(),
            P(),
            P(),
            P(),
            P(),
            P(),
        ),
        check_vma=False,
    )
```

```python
import functools

import jax
import jax.numpy as jnp
from jax import lax
from jax.experimental import pallas as pl
from jax.experimental.pallas import tpu as pltpu
from jax.sharding import PartitionSpec as P

HEAD = 64
IMG_TOK = 145
LOW_TOK = 50
CAP_LEN = 16


EPS_TEXT = 1e-05
EPS_UNIT = 1e-06
MASKED_SCORE = -1e30
BF16 = jnp.bfloat16
F32 = jnp.float32


def mp_other(values):
    return lax.ppermute(values, "mp", [(0, 1), (1, 0)])


def dp_swap(values, mask):
    size = lax.axis_size("dp")
    return lax.ppermute(values, "dp", [(index, index ^ mask) for index in range(size)])


def group_steps(size):
    steps, stride = [], 1
    while stride < size:
        steps.append([stride, 2 * stride, 3 * stride])
        stride *= 4
    return steps


def gather_masks(steps):
    masks = [0]
    for step in steps:
        masks = [mask ^ base for mask in [0] + step for base in masks]
    return masks


def dp_parts(values, step):
    return [values] + [dp_swap(values, mask) for mask in step]


def dp_gather(values, steps, waits):
    for step, wait in zip(steps, waits):
        parts = dp_parts(values, step)
        rows = values.shape[0]
        (values,) = move(
            parts,
            (len(parts) * rows,),
            [(place, 0, rows, 0, place * rows) for place in range(len(parts))],
            (wait,),
        )
    return values


HIGH_ROWS = 160
LOW_ROWS = 64
TILE = 256
PAIR = 2 * HEAD
LANES = 128
POOL_ROWS = 32
NT = (((1,), (1,)), ((), ()))
VMEM_LIMIT = 60 * 1024 * 1024
BUSY = 10**12


def dot(left, right):
    return jnp.dot(left, right, preferred_element_type=F32)


def wide_dot(left, right):
    high = left.astype(BF16)
    rest = (left - high.astype(F32)).astype(BF16)
    return dot(high, right) + dot(rest, right)


def standard(values, epsilon):
    centered = values - jnp.mean(values, axis=-1, keepdims=True)
    variance = jnp.mean(centered * centered, axis=-1, keepdims=True)
    return centered * lax.rsqrt(variance + epsilon)


def gelu(values):
    return (0.5 * values) * (1.0 + lax.erf(values * (0.5**0.5)))


def image_kernel(
    flag_ref,
    token_ref,
    gain_ref,
    triple_hbm,
    result_hbm,
    widen_hbm,
    narrow_hbm,
    out_ref,
    wide,
    packed,
    mixed,
    queries,
    keys,
    values,
    triple,
    result,
    widen,
    narrow,
    resid_groups,
    hidden_groups,
    pooled,
    ready,
    starts,
    high_starts,
    low_starts,
    sems,
):
    _, images, width = token_ref.shape
    hidden = widen.shape[1]
    copies = fetch(
        (triple_hbm, result_hbm, widen_hbm, narrow_hbm), (triple, result, widen, narrow), sems
    )
    lane_tiles = [slice(lane, lane + LANES) for lane in range(0, width, LANES)]

    def spread(position, carry):
        rows = pl.ds(pl.multiple_of(position * images, images), images)
        for place, lanes in enumerate(lane_tiles):
            wide[place, rows, :] = token_ref[position, :, lanes].astype(F32)
        return carry

    def begin(image, carry):
        start, highs = carry
        starts[image] = start
        high = flag_ref[image] == 1

        @pl.when(high)
        def _():
            high_starts[highs] = start

        @pl.when(jnp.logical_not(high))
        def _():
            low_starts[image - highs] = start

        return start + jnp.where(high, HIGH_ROWS, LOW_ROWS), highs + jnp.where(high, 1, 0)

    total, highs = lax.fori_loop(0, images, begin, (jnp.int32(0), jnp.int32(0)))
    lax.fori_loop(0, LOW_ROWS, spread, 0, unroll=4)

    @pl.when(total > images * LOW_ROWS)
    def _():
        lax.fori_loop(LOW_ROWS, IMG_TOK, spread, 0, unroll=3)

    tail = IMG_TOK // 16 * 16

    def pack(image, carry):
        start = pl.multiple_of(starts[image], POOL_ROWS)
        high = flag_ref[image] == 1

        @pl.when(high)
        def _():
            row = lax.broadcasted_iota(jnp.int32, (HIGH_ROWS - tail, LANES), 0)
            for place, lanes in enumerate(lane_tiles):
                packed[pl.ds(start, tail), lanes] = wide[
                    place, pl.ds(image, tail, stride=images), :
                ].astype(BF16)
                last = wide[place, pl.ds(image + tail * images, 1), :]
                packed[pl.ds(start + tail, HIGH_ROWS - tail), lanes] = jnp.where(
                    row == 0, last, 0.0
                ).astype(BF16)

        @pl.when(jnp.logical_not(high))
        def _():
            for place, lanes in enumerate(lane_tiles):
                packed[pl.ds(start, LOW_ROWS), lanes] = wide[
                    place, pl.ds(image, LOW_ROWS, stride=images), :
                ].astype(BF16)

        return carry

    lax.fori_loop(0, images, pack, 0)
    packed[pl.ds(pl.multiple_of(total, POOL_ROWS), TILE), :] = jnp.zeros((TILE, width), BF16)
    tiles = lax.div(total + (TILE - 1), jnp.int32(TILE))

    copies[0].wait()

    def prepare(tile):
        rows = pl.ds(pl.multiple_of(tile * TILE, TILE), TILE)
        ready[tile % 2] = (
            standard(packed[rows, :].astype(F32), EPS_UNIT) * gain_ref[0:1, :]
        ).astype(BF16)

    def project(tile, carry):
        rows = pl.ds(pl.multiple_of(tile * TILE, TILE), TILE)
        normed = ready[tile % 2]
        queries[rows, :] = (dot(normed, triple[0]) * HEAD ** (-0.5)).astype(BF16)
        prepare(tile + 1)
        keys[rows, :] = dot(normed, triple[1]).astype(BF16)
        values[rows, :] = dot(normed, triple[2]).astype(BF16)
        return carry

    prepare(jnp.int32(0))
    lax.fori_loop(0, tiles, project, 0)

    def attend(begins, count, live):
        left = lax.broadcasted_iota(jnp.int32, (count, PAIR), 1) < HEAD
        key_live = lax.broadcasted_iota(jnp.int32, (2 * count, count), 1) < live
        places = [
            (pl.ds(pl.multiple_of(start, POOL_ROWS), count), slice(lane, lane + PAIR))
            for start in begins
            for lane in range(0, width, PAIR)
        ]
        all_scores = [dot_t(two_heads(queries[place], left), keys[place]) for place in places]
        all_powers = []
        for scores in all_scores:
            scores = jnp.where(key_live, scores, MASKED_SCORE)
            top = jnp.max(scores, axis=-1, keepdims=True)
            all_powers.append(jnp.exp(scores - top).astype(BF16))
        for place, powers in zip(places, all_powers):
            value = values[place]
            one = jnp.ones_like(value)
            first = dot(powers[:count], jnp.where(left, value, one))
            second = dot(powers[count:], jnp.where(left, one, value))
            sums = pltpu.roll(jnp.where(left, second, first), HEAD, 1)
            mixed[place] = (jnp.where(left, first, second) / sums).astype(BF16)

    def attend_all(begins, number, together, count, live):
        groups = lax.div(number, jnp.int32(together))

        def group(index, carry):
            attend([begins[index * together + step] for step in range(together)], count, live)
            return carry

        def rest(index, carry):
            attend([begins[index]], count, live)
            return carry

        lax.fori_loop(0, groups, group, 0)
        if together > 1:
            lax.fori_loop(groups * together, number, rest, 0)

    attend_all(high_starts, highs, 1, HIGH_ROWS, IMG_TOK)
    attend_all(low_starts, images - highs, 4, LOW_ROWS, LOW_TOK)

    slot = lax.broadcasted_iota(jnp.int32, (1, images), 1)
    first_row = jnp.zeros((1, images), jnp.int32)
    live_rows = jnp.zeros((1, images), jnp.int32)
    for image in range(images):
        first_row = jnp.where(slot == image, starts[image], first_row)
        live_rows = jnp.where(
            slot == image, jnp.where(flag_ref[image] == 1, IMG_TOK, LOW_TOK), live_rows
        )
    copies[1].wait()
    copies[2].wait()
    groups = TILE // POOL_ROWS

    def group_sum(rows):
        return jnp.sum(rows.reshape(groups, POOL_ROWS // 8, 8, rows.shape[1]), axis=1)

    def resume(tile):
        base = pl.multiple_of(tile * TILE, TILE)
        rows = pl.ds(base, TILE)
        place = base + lax.broadcasted_iota(jnp.int32, (TILE, images), 0)
        alive = jnp.sum(
            jnp.where((place >= first_row) & (place < first_row + live_rows), 1.0, 0.0),
            axis=1,
            keepdims=True,
        )
        residual = (packed[rows, :].astype(F32) + dot(mixed[rows, :], result[...])) * alive
        group = pl.ds(pl.multiple_of(tile * groups, groups), groups)
        resid_groups[group] = group_sum(residual)
        ready[tile % 2] = (standard(residual, EPS_UNIT) * gain_ref[1:2, :]).astype(BF16)

    def perceptron(tile, carry):
        group = pl.ds(pl.multiple_of(tile * groups, groups), groups)
        normed = ready[tile % 2]
        for chunk in range(hidden // width):
            if chunk == 1:
                resume(tile + 1)
            lanes = slice(chunk * width, (chunk + 1) * width)
            units = gelu(dot(normed, widen[:, lanes])).astype(BF16)
            hidden_groups[group, :, lanes] = group_sum(units.astype(F32))
        return carry

    resume(jnp.int32(0))
    lax.fori_loop(0, tiles, perceptron, 0)

    def pool(image, carry):
        group = lax.div(starts[image], jnp.int32(POOL_ROWS))
        high = flag_ref[image] == 1

        def add(count):
            residual, units = resid_groups[group], hidden_groups[group]
            for step in range(1, count):
                residual = residual + resid_groups[group + step]
                units = units + hidden_groups[group + step]
            pooled[pl.ds(image, 1), :width] = jnp.sum(residual, axis=0, keepdims=True)
            pooled[pl.ds(image, 1), width:] = jnp.sum(units, axis=0, keepdims=True)

        @pl.when(high)
        def _():
            add(HIGH_ROWS // POOL_ROWS)

        @pl.when(jnp.logical_not(high))
        def _():
            add(LOW_ROWS // POOL_ROWS)

        return carry

    lax.fori_loop(0, images, pool, 0)
    copies[3].wait()
    units = pooled[:, width:]
    upper = units.astype(BF16)
    lower = (units - upper.astype(F32)).astype(BF16)
    branch = dot(jnp.concatenate([upper, lower], axis=0), narrow[...])
    live = jnp.where(number_column(flag_ref) == 1, IMG_TOK, LOW_TOK).astype(F32)
    mean = (pooled[:, :width] + branch[:images] + branch[images:]) / live
    out_ref[...] = (
        mean * lax.rsqrt(jnp.sum(mean * mean, axis=-1, keepdims=True) + EPS_UNIT)
    ).astype(BF16)


def image_tower(flags, tokens, gains, triple, result, widen, narrow):
    images, _, width = tokens.shape
    hidden = widen.shape[1]
    rows = images * HIGH_ROWS + TILE
    groups = rows // POOL_ROWS
    outside = pl.BlockSpec(memory_space=pl.ANY)
    inside = pl.BlockSpec(memory_space=pltpu.VMEM)
    return pl.pallas_call(
        image_kernel,
        out_shape=jax.ShapeDtypeStruct((images, width), BF16),
        in_specs=[pl.BlockSpec(memory_space=pltpu.SMEM), inside, inside]
        + [outside] * 4,
        out_specs=inside,
        scratch_shapes=[pltpu.VMEM((width // LANES, IMG_TOK * images, LANES), F32)]
        + [pltpu.VMEM((rows, width), BF16)] * 5
        + [pltpu.VMEM(weight.shape, BF16) for weight in (triple, result, widen, narrow)]
        + [
            pltpu.VMEM((groups, 8, width), F32),
            pltpu.VMEM((groups, 8, hidden), F32),
            pltpu.VMEM((images, width + hidden), F32),
            pltpu.VMEM((2, TILE, width), BF16),
            pltpu.SMEM((images,), jnp.int32),
            pltpu.SMEM((images,), jnp.int32),
            pltpu.SMEM((images,), jnp.int32),
            pltpu.SemaphoreType.DMA((4,)),
        ],
        compiler_params=pltpu.CompilerParams(vmem_limit_bytes=VMEM_LIMIT),
        cost_estimate=pl.CostEstimate(flops=BUSY, bytes_accessed=BUSY, transcendentals=0),
    )(flags, jnp.transpose(tokens, (1, 0, 2)), gains, triple, result, widen, narrow)


TN = (((0,), (0,)), ((), ()))
BLOCK = 128
ROOT_HALF = 0.5**0.5
DENSITY = 0.3989422804014327


def dot_t(left, right):
    return lax.dot_general(left, right, NT, preferred_element_type=F32)


def t_dot(left, right):
    return lax.dot_general(left, right, TN, preferred_element_type=F32)


def fetch(sources, targets, sems):
    copies = [
        pltpu.make_async_copy(source, target, sems.at[place])
        for place, (source, target) in enumerate(zip(sources, targets))
    ]
    for copy in copies:
        copy.start()
    return copies


def caption_pool(ids_ref, captions):
    ids_row = ids_ref[...].reshape(1, -1)
    tokens = ids_row.shape[1]
    shape = (captions, tokens)
    caption = lax.broadcasted_iota(jnp.int32, shape, 0)
    token = lax.broadcasted_iota(jnp.int32, shape, 1)
    inside = (token // (tokens // captions)) == caption
    return jnp.where(inside & (ids_row != 0), 1.0, 0.0)


def valid_column(pool):
    pool = pool.astype(BF16)
    return t_dot(pool, jnp.ones((pool.shape[0], 128), BF16))[:, 0:1]


def number_column(ref):
    shape = (ref.shape[0], 1)
    place = lax.broadcasted_iota(jnp.int32, shape, 0)
    column = jnp.zeros(shape, jnp.int32)
    for index in range(shape[0]):
        column = jnp.where(place == index, ref[index], column)
    return column


def as_row(ref):
    return ref[...].reshape(1, -1)


def pair_masks(rows, pair_width):
    return lax.broadcasted_iota(jnp.int32, (rows, pair_width), 1) < HEAD


def two_heads(values, left):
    zero = jnp.zeros_like(values)
    return jnp.concatenate(
        [jnp.where(left, values, zero), jnp.where(left, zero, values)], axis=0
    )


def text_mix_kernel(
    entry_ref,
    ids_ref,
    gain_ref,
    shift_ref,
    triple_ref,
    pair_ref,
    result_ref,
    normed_ref,
    qkv_ref,
    soft_ref,
    mixed_ref,
    part_ref,
):
    tokens = entry_ref.shape[0]
    width = result_ref.shape[0]
    normed = (
        standard(entry_ref[...].astype(F32), EPS_TEXT) * as_row(gain_ref) + as_row(shift_ref)
    ).astype(BF16)
    normed_ref[...] = normed
    qkv_ref[0] = (dot(normed, triple_ref[0]) + pair_ref[0:1, :]).astype(BF16)
    qkv_ref[1] = dot(normed, triple_ref[1]).astype(BF16)
    qkv_ref[2] = (dot(normed, triple_ref[2]) + pair_ref[1:2, :]).astype(BF16)
    ids = as_row(ids_ref)
    left = pair_masks(BLOCK, PAIR)
    shape = (2 * BLOCK, BLOCK)
    query_caption = lax.broadcasted_iota(jnp.int32, shape, 0) % BLOCK // CAP_LEN
    same = query_caption == lax.broadcasted_iota(jnp.int32, shape, 1) // CAP_LEN
    for block in range(tokens // BLOCK):
        rows = slice(block * BLOCK, (block + 1) * BLOCK)
        seen = same & (ids[:, rows] != 0)
        for pair in range(width // PAIR):
            lanes = slice(pair * PAIR, (pair + 1) * PAIR)
            scores = dot_t(two_heads(qkv_ref[0, rows, lanes], left), qkv_ref[1, rows, lanes])
            scores = jnp.where(seen, scores * HEAD ** (-0.5), MASKED_SCORE)
            powers = jnp.exp(scores - jnp.max(scores, axis=-1, keepdims=True))
            soft = powers / jnp.sum(powers, axis=-1, keepdims=True)
            soft_ref[block, pair] = soft
            low = soft.astype(BF16)
            value = qkv_ref[2, rows, lanes]
            mixed_ref[rows, lanes] = jnp.where(
                left, dot(low[:BLOCK], value), dot(low[BLOCK:], value)
            ).astype(BF16)
    part_ref[...] = dot(mixed_ref[...], result_ref[...])


def text_widen_kernel(
    entry_ref,
    own_ref,
    other_ref,
    result_offset_ref,
    gain_ref,
    shift_ref,
    widen_offset_ref,
    ids_ref,
    widen_hbm,
    narrow_hbm,
    residual_ref,
    normed_ref,
    slope_ref,
    sums_ref,
    resid_sum_ref,
    branch_ref,
    widen,
    narrow,
    hidden_sum,
    sems,
):
    captions = sums_ref.shape[0]
    width = entry_ref.shape[1]
    copies = fetch((widen_hbm, narrow_hbm), (widen, narrow), sems)
    residual = entry_ref[...].astype(F32) + (
        (own_ref[...] + other_ref[...]) + as_row(result_offset_ref)
    )
    residual_ref[...] = residual
    normed = (standard(residual, EPS_TEXT) * as_row(gain_ref) + as_row(shift_ref)).astype(BF16)
    normed_ref[...] = normed
    pool = caption_pool(ids_ref, captions).astype(BF16)
    widen_offset = as_row(widen_offset_ref)
    upper = residual.astype(BF16)
    resid_sum_ref[...] = dot(pool, upper) + dot(
        pool, (residual - upper.astype(F32)).astype(BF16)
    )
    valid = valid_column(pool)
    copies[0].wait()
    for chunk in range(widen.shape[1] // width):
        lanes = slice(chunk * width, (chunk + 1) * width)
        before = dot(normed, widen[:, lanes]) + widen_offset[:, lanes]
        share = 0.5 * (1.0 + lax.erf(before * ROOT_HALF))
        hidden_sum[:, lanes] = dot(pool, (before * share).astype(BF16))
        slope = share + before * (jnp.exp(-0.5 * before * before) * DENSITY)
        slope_ref[:, lanes] = slope * valid
    sums_ref[...] = hidden_sum[...].astype(BF16)
    copies[1].wait()
    branch_ref[...] = wide_dot(hidden_sum[...], narrow[...])


def logits_kernel(
    masks,
    index_ref,
    matched_ref,
    sharpen_ref,
    near_ref,
    far_ref,
    resid_sum_ref,
    own_ref,
    other_ref,
    narrow_offset_ref,
    ids_ref,
    images_ref,
    unit_ref,
    factor_ref,
    logits_ref,
    powers_ref,
    row_sum_ref,
    col_sum_ref,
    loss_ref,
):
    captions, pairs = logits_ref.shape
    rows = images_ref.shape[0] // (2 * len(masks))
    core = index_ref[1]
    for place, mask in enumerate(masks):
        start = (index_ref[0] ^ mask) * (2 * rows)
        images_ref[pl.ds(pl.multiple_of(start + core * rows, rows), rows), :] = near_ref[
            place * rows : (place + 1) * rows, :
        ]
        images_ref[pl.ds(pl.multiple_of(start + (1 - core) * rows, rows), rows), :] = far_ref[
            place * rows : (place + 1) * rows, :
        ]
    count = jnp.sum(caption_pool(ids_ref, captions), axis=1, keepdims=True)
    pooled = (resid_sum_ref[...] + (own_ref[...] + other_ref[...])) / count + as_row(
        narrow_offset_ref
    )
    inverse = lax.rsqrt(jnp.sum(pooled * pooled, axis=-1, keepdims=True) + EPS_UNIT)
    unit = pooled * inverse
    unit_ref[...] = unit
    factor_ref[...] = jnp.broadcast_to(inverse / count, factor_ref.shape)
    logits = jnp.exp(jnp.full((1, 1), sharpen_ref[0], F32)) * dot_t(unit.astype(BF16), images_ref[...])
    logits_ref[...] = logits
    powers = jnp.exp(logits)
    powers_ref[...] = powers
    row_sum = jnp.sum(powers, axis=1, keepdims=True)
    row_sum_ref[...] = jnp.broadcast_to(row_sum, row_sum_ref.shape)
    col_sum_ref[...] = jnp.sum(powers, axis=0, keepdims=True)
    positive = number_column(matched_ref) == lax.broadcasted_iota(jnp.int32, (captions, pairs), 1)
    wanted = jnp.sum(jnp.where(positive, logits, 0.0), axis=1, keepdims=True)
    loss_ref[...] = jnp.broadcast_to(
        jnp.sum(jnp.log(row_sum) - 2.0 * wanted, axis=0, keepdims=True), loss_ref.shape
    )


def sum_kernel(first_ref, second_ref, third_ref, fourth_ref, out_ref):
    out_ref[...] = (first_ref[...] + second_ref[...]) + (third_ref[...] + fourth_ref[...])


def loss_grad_kernel(
    matched_ref,
    sharpen_ref,
    col_ref,
    col1_ref,
    col2_ref,
    col3_ref,
    logits_ref,
    powers_ref,
    row_sum_ref,
    unit_ref,
    factor_ref,
    images_ref,
    ids_ref,
    loss_ref,
    narrow_hbm,
    slope_hbm,
    widen_hbm,
    grad_ref,
    low_ref,
    before_ref,
    part_ref,
    stat_ref,
    narrow,
    slope,
    widen,
    sems,
):
    captions, pairs = logits_ref.shape
    tokens, hidden = slope.shape
    width = grad_ref.shape[1]
    copies = fetch((narrow_hbm, slope_hbm, widen_hbm), (narrow, slope, widen), sems)
    logits, powers = logits_ref[...], powers_ref[...]
    col_sum = (col_ref[...] + col1_ref[...]) + (col2_ref[...] + col3_ref[...])
    positive = number_column(matched_ref) == lax.broadcasted_iota(jnp.int32, (captions, pairs), 1)
    derivative = (
        powers / row_sum_ref[:, 0:1] + powers / col_sum - jnp.where(positive, 2.0, 0.0)
    ) / (2.0 * pairs)
    temperature = jnp.sum(
        jnp.sum(derivative * logits, axis=1, keepdims=True), axis=0, keepdims=True
    )
    col_loss = jnp.sum(jnp.log(col_sum), axis=1, keepdims=True)
    text = dot((derivative * jnp.exp(jnp.full((1, 1), sharpen_ref[0], F32))).astype(BF16), images_ref[...])
    unit = unit_ref[...]
    grad = (text - unit * jnp.sum(unit * text, axis=-1, keepdims=True)) * factor_ref[:, 0:1]
    grad_ref[...] = grad
    low = grad.astype(BF16)
    low_ref[...] = low
    copies[0].wait()
    copies[1].wait()
    copies[2].wait()
    ones = jnp.ones((8, tokens), BF16)
    part = jnp.zeros(part_ref.shape, F32)
    for chunk in range(hidden // width):
        lanes = slice(chunk * width, (chunk + 1) * width)
        back = dot_t(low, narrow[lanes, :])
        before = (
            (back[:, None, :] * slope[:, lanes].reshape(captions, CAP_LEN, width))
            .reshape(tokens, width)
            .astype(BF16)
        )
        before_ref[:, lanes] = before
        stat_ref[chunk : chunk + 1, :] = dot(ones, before)[0:1]
        part = part + dot_t(before, widen[:, lanes])
    part_ref[...] = part
    count = jnp.sum(caption_pool(ids_ref, captions), axis=1, keepdims=True)
    stat_ref[2:3, :] = jnp.sum(low.astype(F32) * count, axis=0, keepdims=True)
    lane = lax.broadcasted_iota(jnp.int32, (1, width), 1)
    stat_ref[3:4, :] = jnp.where(
        lane == 0,
        temperature,
        jnp.where(lane == 1, loss_ref[0:1, 0:1], jnp.where(lane == 2, col_loss, 0.0)),
    )
    stat_ref[4:8, :] = jnp.zeros((4, width), F32)


def deal(index_ref, first, second, outs):
    half = first.shape[0] // 2
    for place, (values, bit) in enumerate(((first, 1), (second, 2))):
        mine = index_ref[0] // bit % 2
        for ref, which in ((outs[2 * place], 1 - mine), (outs[2 * place + 1], mine)):
            ref[...] = values[pl.ds(pl.multiple_of(which * half, half), half), :]


def widen_grad_kernel(index_ref, normed_ref, before_ref, *refs):
    outs, (first, second) = refs[:4], refs[4:]
    width = first.shape[1]
    normed = normed_ref[...]
    first[...] = t_dot(normed, before_ref[:, :width]).astype(BF16)
    second[...] = t_dot(normed, before_ref[:, width:]).astype(BF16)
    deal(index_ref, first, second, outs)


def mixer_back_kernel(
    own_ref,
    other_ref,
    residual_ref,
    grad_ref,
    ids_ref,
    gain_ref,
    result_ref,
    qkv_hbm,
    soft_hbm,
    triple_hbm,
    grad_residual_ref,
    low_ref,
    flat_ref,
    part_ref,
    stat_ref,
    qkv,
    soft_all,
    triple,
    sems,
):
    tokens, width = residual_ref.shape
    captions = grad_ref.shape[0]
    local_width = result_ref.shape[0]
    copies = fetch((qkv_hbm, soft_hbm, triple_hbm), (qkv, soft_all, triple), sems)
    residual = residual_ref[...]
    centered = residual - jnp.mean(residual, axis=-1, keepdims=True)
    rate = lax.rsqrt(jnp.mean(centered * centered, axis=-1, keepdims=True) + EPS_TEXT)
    unit = centered * rate
    grad = own_ref[...] + other_ref[...]
    stat_ref[1:2, :] = jnp.sum(grad * unit, axis=0, keepdims=True)
    stat_ref[2:3, :] = jnp.sum(grad, axis=0, keepdims=True)
    scaled = grad * as_row(gain_ref)
    inner = rate * (
        scaled
        - jnp.mean(scaled, axis=-1, keepdims=True)
        - unit * jnp.mean(scaled * unit, axis=-1, keepdims=True)
    )
    spread = jnp.broadcast_to(
        grad_ref[...][:, None, :], (captions, tokens // captions, width)
    ).reshape(tokens, width)
    grad_residual = spread * valid_column(caption_pool(ids_ref, captions)) + inner
    grad_residual_ref[...] = grad_residual
    low = grad_residual.astype(BF16)
    low_ref[...] = low
    ones = jnp.ones((8, tokens), BF16)
    stat_ref[0:1, :] = dot(ones, low)[0:1]
    grad_mixed = dot_t(low, result_ref[...]).astype(BF16)
    for copy in copies:
        copy.wait()
    left = pair_masks(BLOCK, PAIR)
    places = [
        (block, pair, slice(block * BLOCK, (block + 1) * BLOCK), slice(pair * PAIR, (pair + 1) * PAIR))
        for block in range(tokens // BLOCK)
        for pair in range(local_width // PAIR)
    ]
    mixed = [two_heads(grad_mixed[rows, lanes], left) for _, _, rows, lanes in places]
    softs = [soft_all[block, pair] for block, pair, _, _ in places]
    grads = [
        dot_t(value, qkv[2, rows, lanes]) for value, (_, _, rows, lanes) in zip(mixed, places)
    ]
    scores = [
        (soft * (grad - jnp.sum(grad * soft, axis=-1, keepdims=True))).astype(BF16)
        for soft, grad in zip(softs, grads)
    ]
    for value, soft, (_, _, rows, lanes) in zip(mixed, softs, places):
        flat_ref[2, rows, lanes] = t_dot(soft.astype(BF16), value).astype(BF16)
    for score, (_, _, rows, lanes) in zip(scores, places):
        key = qkv[1, rows, lanes]
        back = jnp.where(left, dot(score[:BLOCK], key), dot(score[BLOCK:], key))
        flat_ref[0, rows, lanes] = (back * HEAD ** (-0.5)).astype(BF16)
    for score, (_, _, rows, lanes) in zip(scores, places):
        flat_ref[1, rows, lanes] = (
            t_dot(score, two_heads(qkv[0, rows, lanes], left)) * HEAD ** (-0.5)
        ).astype(BF16)
    part_ref[...] = (
        dot_t(flat_ref[0], triple[0])
        + dot_t(flat_ref[1], triple[1])
        + dot_t(flat_ref[2], triple[2])
    )
    stat_ref[3:4, :local_width] = dot(ones, flat_ref[0])[0:1]
    stat_ref[3:4, local_width:] = dot(ones, flat_ref[2])[0:1]
    stat_ref[4:8, :] = jnp.zeros((4, width), F32)


def mixer_grad_kernel(index_ref, normed_ref, flat_ref, mixed_ref, low_ref, *refs):
    outs, (first, second) = refs[:4], refs[4:]
    half = flat_ref.shape[2]
    rows = first.shape[0] // 2
    normed = normed_ref[...]
    for part, (target, place) in enumerate(((first, 0), (first, rows), (second, 0))):
        grad = t_dot(normed, flat_ref[part]).astype(BF16)
        target[place : place + rows, :half] = grad[:rows]
        target[place : place + rows, half:] = grad[rows:]
    second[rows:, :] = t_dot(mixed_ref[...], low_ref[...]).astype(BF16)
    deal(index_ref, first, second, outs)


def narrow_grad_kernel(half, index_ref, *refs):
    parts, (near_ref, far_ref, out_ref, grads) = refs[:-4], refs[-4:]
    rows, width = parts[0].shape[0], grads.shape[1]
    devices = near_ref.shape[0] // half
    for place in range(devices):
        plane, group, high = place % 4, place // 4 % (devices // GROUP), place * 4 // devices
        source = (plane * Z_SIZE + high) * (devices // GROUP) + group
        for ref, which in ((near_ref, index_ref[0]), (far_ref, 1 - index_ref[0])):
            start = pl.multiple_of((2 * place + which) * half, half)
            grads[pl.ds(start, half), :] = ref[source * half : (source + 1) * half, :]
    for chunk in range(out_ref.shape[0] // width):
        lanes = slice(chunk * width, (chunk + 1) * width)
        total = t_dot(parts[0][:, lanes], grads[:rows, :])
        for place in range(1, len(parts)):
            total = total + t_dot(
                parts[place][:, lanes], grads[place * rows : (place + 1) * rows, :]
            )
        out_ref[lanes, :] = total


def entry_grad_kernel(
    index_ref,
    own_ref,
    other_ref,
    entry_ref,
    gain_ref,
    grad_residual_ref,
    loss_stat_ref,
    mixer_stat_ref,
    caption_ref,
    out_ref,
    extra_ref,
    pack,
):
    entry = entry_ref[...].astype(F32)
    centered = entry - jnp.mean(entry, axis=-1, keepdims=True)
    rate = lax.rsqrt(jnp.mean(centered * centered, axis=-1, keepdims=True) + EPS_TEXT)
    unit = centered * rate
    grad = own_ref[...] + other_ref[...]
    pack[0:8, :] = loss_stat_ref[...]
    pack[8:16, :] = mixer_stat_ref[...]
    pack[4:5, :] = jnp.sum(grad * unit, axis=0, keepdims=True)
    pack[5:6, :] = jnp.sum(grad, axis=0, keepdims=True)
    half = caption_ref.shape[0] // 2
    extra_ref[:half, :] = caption_ref[
        pl.ds(pl.multiple_of(index_ref[0] * half, half), half), :
    ]
    upper = pack[...].astype(BF16).astype(F32)
    pack[15:16, :] = (pack[...] - upper)[3:4, :]
    extra_ref[half:, :] = pack[...].astype(BF16)
    scaled = grad * as_row(gain_ref)
    out_ref[...] = grad_residual_ref[...] + rate * (
        scaled
        - jnp.mean(scaled, axis=-1, keepdims=True)
        - unit * jnp.mean(scaled * unit, axis=-1, keepdims=True)
    )


def tree_sum(values):
    while len(values) > 1:
        values = [values[place] + values[place + 1] for place in range(0, len(values), 2)]
    return values[0]


def collect_kernel(
    scale,
    rows,
    joined_ref,
    along_x_ref,
    along_y_ref,
    first_far_ref,
    second_far_ref,
    loss_ref,
    near_ref,
    error_ref,
    pair_ref,
    result_ref,
    widen_ref,
    narrow_ref,
    gain1_ref,
    shift1_ref,
    gain2_ref,
    shift2_ref,
    temperature_ref,
):
    half = rows - 16
    first = second_far_ref.shape[0]
    count = (first_far_ref.shape[0] - first) // rows
    totals = []
    for piece, ref in enumerate((joined_ref, along_x_ref, along_y_ref, first_far_ref)):
        for place in range(count):
            row = first + place * rows
            near_ref[pl.ds((piece * count + place) * half, half), :] = ref[row : row + half, :]
            totals.append(ref[row + half : row + rows, :].astype(F32))
    total = tree_sum(totals)
    scalars = total[3:4] + total[15:16]
    error_ref[...] = ((scalars[:, 1:2] + loss_ref[3:4, 2:3]) * scale).reshape(1)
    temperature_ref[...] = scalars[:, 0:1].reshape(1)
    lanes = pair_ref.shape[1]
    pair_ref[0:1, :] = total[11:12, :lanes]
    pair_ref[1:2, :] = total[11:12, lanes:]
    width = total.shape[1]
    for chunk in range(widen_ref.shape[0] // width):
        widen_ref[chunk * width : (chunk + 1) * width] = total[chunk]
    for ref, place in (
        (narrow_ref, 2),
        (gain1_ref, 4),
        (shift1_ref, 5),
        (result_ref, 8),
        (gain2_ref, 9),
        (shift2_ref, 10),
    ):
        ref[...] = total[place]


def call(kernel, inside, shapes, outside=(), scratch=(), index=(), small=(), after=(), limit=24, mark=False, busy=BUSY):
    vmem = pl.BlockSpec(memory_space=pltpu.VMEM)
    extra = [pltpu.VMEM(array.shape, array.dtype) for array in outside]
    extra += list(scratch)
    if outside:
        extra += [pltpu.SemaphoreType.DMA((len(outside),))]
    index = [jnp.stack(index).astype(jnp.int32)] if index else []
    small = index + list(small)
    before = len(small) + len(inside) + len(outside)

    if mark:
        shapes = tuple(shapes) + (((8, 128), F32),)

    def body(*refs):
        refs = refs[:before] + refs[before + len(after) :]
        if mark:
            last = before + len(shapes) - 1
            refs[last][...] = jnp.zeros((8, 128), F32)
            refs = refs[:last] + refs[last + 1 :]
        kernel(*refs)

    return pl.pallas_call(
        body,
        out_shape=[jax.ShapeDtypeStruct(shape, kind) for shape, kind in shapes],
        in_specs=[pl.BlockSpec(memory_space=pltpu.SMEM)] * len(small)
        + [vmem] * len(inside)
        + [pl.BlockSpec(memory_space=pl.ANY)] * (len(outside) + len(after)),
        out_specs=[vmem] * len(shapes),
        scratch_shapes=extra,
        compiler_params=pltpu.CompilerParams(vmem_limit_bytes=limit * 1024 * 1024),
        cost_estimate=pl.CostEstimate(flops=busy, bytes_accessed=busy, transcendentals=0),
    )(*small, *inside, *outside, *after)


def move(arrays, sizes, plan, after=(), mark=False, busy=BUSY):
    width, kind = arrays[0].shape[1], arrays[0].dtype

    def body(*refs):
        ins, outs = refs[: len(arrays)], refs[len(arrays) :]
        for source, first, rows, target, start in plan:
            outs[target][start : start + rows, :] = ins[source][first : first + rows, :]

    return call(body, arrays, tuple(((size, width), kind) for size in sizes), after=after, mark=mark, busy=busy)


GROUP = 16
Z_STRIDE, Z_SIZE = 4, 4


def block_rows(block, rows):
    return pl.ds(pl.multiple_of(block * rows, rows), rows)


def fold_kernel(index_ref, *refs):
    ins, outs = refs[:4], refs[4:]
    half = outs[0].shape[0]
    for place, bit in ((0, 2), (1, 1)):
        mine = index_ref[0] // bit % 2
        for out, which in ((outs[2 * place], 1 - mine), (outs[2 * place + 1], mine)):
            rows = block_rows(which, half)
            out[...] = (
                ins[2 * place][rows, :].astype(F32) + ins[2 * place + 1][rows, :].astype(F32)
            ).astype(out.dtype)


def cut_kernel(index_ref, *refs):
    ins, outs = refs[:4], refs[4:]
    rows = ins[0].shape[0] // Z_SIZE
    for place in range(2):
        for step, out in enumerate(outs):
            block = block_rows((index_ref[0] // Z_STRIDE % Z_SIZE) ^ step, rows)
            out[place * rows : (place + 1) * rows, :] = (
                ins[2 * place][block, :] + ins[2 * place + 1][block, :].astype(F32)
            ).astype(out.dtype)


def add_kernel(own_ref, *refs):
    out_ref = refs[-1]
    rows = own_ref.shape[0]
    total = own_ref[...]
    for ref in refs[: Z_SIZE - 1]:
        total = total + ref[...].astype(F32)
    out_ref[:rows, :] = total.astype(out_ref.dtype)
    if out_ref.shape[0] > rows:
        out_ref[rows:, :] = refs[Z_SIZE - 1][...]


def scatter_steps(dealt, place, extra=None):
    first_sent, first_kept, second_sent, second_kept = dealt
    rows, width = first_sent.shape
    after = yield
    arrived = (dp_swap(first_sent, 1), dp_swap(second_sent, 2))
    half = (rows // 2, width)
    first_sent, first_kept, second_sent, second_kept, mark = call(
        fold_kernel,
        (first_kept, arrived[0], second_kept, arrived[1]),
        ((half, BF16), (half, F32), (half, BF16), (half, F32)),
        index=(place,),
        after=after,
        mark=True, busy=1,
    )
    after = yield mark
    arrived = (dp_swap(first_sent, 2), dp_swap(second_sent, 1))
    block = (rows // Z_SIZE, width)
    own, *sent, mark = call(
        cut_kernel,
        (first_kept, arrived[0], second_kept, arrived[1]),
        ((block, F32),) + ((block, BF16),) * (Z_SIZE - 1),
        index=(place,),
        after=after,
        mark=True, busy=1,
    )
    after = yield mark
    arrived = [dp_swap(values, step * Z_STRIDE) for step, values in enumerate(sent, 1)]
    size = lax.axis_size("dp")
    more = 0 if extra is None else extra[0].shape[0]
    if size > GROUP:
        mine, mark = call(
            add_kernel, (own, *arrived), ((own.shape, F32),), after=after, mark=True, busy=1
        )
        groups = [list(range(index, size, GROUP)) for index in range(GROUP)]
        mine = lax.psum(mine, "dp", axis_index_groups=groups).astype(BF16)
        if more:
            mine = jnp.concatenate([mine, *extra], axis=0)
    else:
        mine, mark = call(
            add_kernel,
            (own, *arrived) + (tuple(extra) if more else ()),
            (((block[0] + more, width), BF16),),
            after=after,
            mark=True, busy=1,
        )
    after = yield mark
    high = dp_swap(mine, 2 * Z_STRIDE)
    pieces = [mine, dp_swap(mine, Z_STRIDE), high, dp_swap(high, Z_STRIDE)]
    half = block[0] // 2
    plan, start = [], 0
    for first, count in ((0, half), (2 * half, more), (half, half)):
        for piece in range(Z_SIZE):
            if count:
                plan.append((piece, first, count, 0, start))
            start += count
    joined, mark = move(pieces, (start,), plan, after, mark=True, busy=1)
    along_x, along_y = dp_swap(joined, 1), dp_swap(joined, 2)
    after = yield mark
    share = Z_SIZE * half
    first, second, mark = move(
        (along_y, along_x),
        (start - share, share),
        ((0, 0, start - share, 0, 0), (1, start - share, share, 1, 0)),
        after,
        mark=True, busy=1,
    )
    after = yield mark
    yield joined, along_x, along_y, dp_swap(first, 1), dp_swap(second, 2)


def block_home(index, block, outer, inner):
    high = (block // 8) ^ (index // outer % 2)
    middle = (block // 4 % 2) ^ (index // inner % 2)
    return high * 8 + middle * 4 + ((block % 4) ^ (index // Z_STRIDE % Z_SIZE))


def relative_blocks(refs, tensor):
    joined, along_x, along_y, first_far, second_far = refs
    size = second_far.shape[0]
    start = joined.shape[0] - size if tensor else 0
    if tensor:
        pieces = ((joined, start), (along_x, start), (along_y, start), (second_far, 0))
    else:
        pieces = ((joined, 0), (along_y, 0), (along_x, 0), (first_far, 0))
    rows = size // Z_SIZE
    for piece, (ref, start) in enumerate(pieces):
        for step in range(Z_SIZE):
            first = start + step * rows
            yield piece * Z_SIZE + step, rows, ref[first : first + rows, :]


def unpack_widen_kernel(index_ref, *refs):
    refs, out_ref = refs[:-1], refs[-1]
    width = out_ref.shape[1] // 2
    for tensor, bits in ((0, (1, 2)), (1, (2, 1))):
        for block, rows, values in relative_blocks(refs, tensor):
            start = pl.multiple_of(block_home(index_ref[0], block, *bits) * rows, rows)
            out_ref[pl.ds(start, rows), tensor * width : (tensor + 1) * width] = values.astype(F32)


def unpack_mixer_kernel(index_ref, *refs):
    refs, (triple_ref, result_ref) = refs[:-2], refs[-2:]
    half, split = triple_ref.shape[2], triple_ref.shape[1] // 2
    for block, rows, values in relative_blocks(refs, 0):
        home = block_home(index_ref[0], block, 1, 2)
        part, row = home // 8, pl.multiple_of(home % 8 * rows, rows)
        triple_ref[part, pl.ds(row, rows), :] = values[:, :half].astype(F32)
        triple_ref[part, pl.ds(split + row, rows), :] = values[:, half:].astype(F32)
    for block, rows, values in relative_blocks(refs, 1):
        home = block_home(index_ref[0], block, 2, 1)
        row = pl.multiple_of(home % 8 * rows, rows)

        @pl.when(home < 8)
        def _():
            triple_ref[2, pl.ds(row, rows), :] = values[:, :half].astype(F32)
            triple_ref[2, pl.ds(split + row, rows), :] = values[:, half:].astype(F32)

        @pl.when(home >= 8)
        def _():
            result_ref[pl.ds(row, rows), :] = values.astype(F32)


def local(
    sentence_layer_entry,
    sentence_word_ids,
    picture_tile_activations,
    picture_detail_flag,
    matched_picture_ids,
    mixer_layernorm_gamma,
    mixer_layernorm_offset,
    mixer_triple_matrix,
    mixer_pair_offsets,
    mixer_result_matrix,
    mixer_result_offset,
    perceptron_layernorm_gamma,
    perceptron_layernorm_offset,
    widening_matrix,
    widening_offset,
    narrowing_matrix,
    narrowing_offset,
    sharpening_log,
    locked_layernorm_gammas,
    locked_mixer_triple_matrix,
    locked_mixer_result_matrix,
    locked_widening_matrix,
    locked_narrowing_matrix,
):
    captions = matched_picture_ids.shape[0]
    tokens, model_width = sentence_layer_entry.shape
    local_width = mixer_result_matrix.shape[0]
    hidden = narrowing_matrix.shape[0]
    devices = lax.axis_size("dp")
    all_pairs = captions * devices
    place, core = lax.axis_index("dp"), lax.axis_index("mp")
    blocks = tokens // BLOCK
    full = (tokens, model_width)
    short = (captions, model_width)
    square = (model_width, model_width)
    half_square = (model_width // 2, model_width)
    dealt = ((half_square, BF16),) * 4

    steps = group_steps(devices)

    image_emb = image_tower(
        picture_detail_flag,
        picture_tile_activations,
        locked_layernorm_gammas,
        locked_mixer_triple_matrix,
        locked_mixer_result_matrix,
        locked_widening_matrix,
        locked_narrowing_matrix,
    )
    normed, qkv, soft, mixed, part, mark = call(
        text_mix_kernel,
        (
            sentence_layer_entry,
            sentence_word_ids,
            mixer_layernorm_gamma,
            mixer_layernorm_offset,
            mixer_triple_matrix,
            mixer_pair_offsets,
            mixer_result_matrix,
        ),
        (
            (full, BF16),
            ((3, tokens, local_width), BF16),
            ((blocks, local_width // PAIR, 2 * BLOCK, BLOCK), F32),
            ((tokens, local_width), BF16),
            (full, F32),
        ),
        after=(image_emb,),
        limit=60,
        mark=True,
    )
    other = mp_other(part)
    near_images = dp_gather(image_emb, steps[:0:-1], [mark] * (len(steps) - 1))
    residual, normed2, slope, hidden_sums, resid_sum, branch = call(
        text_widen_kernel,
        (
            sentence_layer_entry,
            part,
            other,
            mixer_result_offset,
            perceptron_layernorm_gamma,
            perceptron_layernorm_offset,
            widening_offset,
            sentence_word_ids,
        ),
        (
            (full, F32),
            (full, BF16),
            ((tokens, hidden), F32),
            ((captions, hidden), BF16),
            (short, F32),
            (short, F32),
        ),
        outside=(widening_matrix, narrowing_matrix),
        scratch=(pltpu.VMEM((captions, hidden), F32),),
        after=(near_images,),
    )

    near_images = dp_gather(near_images, steps[:1], (branch,))
    sums_parts = dp_parts(hidden_sums, steps[0])
    images, unit, factor, logits, powers, row_sum, col_sum, row_loss = call(
        functools.partial(logits_kernel, gather_masks(steps[::-1])),
        (
            near_images,
            mp_other(near_images),
            resid_sum,
            branch,
            mp_other(branch),
            narrowing_offset,
            sentence_word_ids,
        ),
        (
            ((all_pairs, model_width), BF16),
            (short, F32),
            ((captions, 128), F32),
            ((captions, all_pairs), F32),
            ((captions, all_pairs), F32),
            ((captions, 128), F32),
            ((1, all_pairs), F32),
            ((8, 128), F32),
        ),
        index=(place, core),
        small=(matched_picture_ids, sharpening_log),
    )
    after = (unit,)
    for step in steps[2:] + [None]:
        rows = sums_parts[0].shape[0]
        joined_sums, mark = move(
            sums_parts,
            (4 * rows,),
            [(place, 0, rows, 0, place * rows) for place in range(4)],
            after,
            mark=True,
        )
        after = (mark,)
        if step is not None:
            sums_parts = dp_parts(joined_sums, step)
    sums_high = dp_swap(joined_sums, 2 * Z_STRIDE)
    sums_parts = [joined_sums, dp_swap(joined_sums, Z_STRIDE), sums_high]
    sums_parts.append(dp_swap(sums_high, Z_STRIDE))
    col_parts = dp_parts(col_sum, steps[0])
    for step in steps[1:]:
        (col_sum,) = call(sum_kernel, col_parts, ((col_sum.shape, F32),), after=after)
        col_parts = dp_parts(col_sum, step)
    grad_caption, grad_caption_low, grad_pre, part, loss_stat = call(
        loss_grad_kernel,
        (
            *col_parts,
            logits,
            powers,
            row_sum,
            unit,
            factor,
            images,
            sentence_word_ids,
            row_loss,
        ),
        (
            (short, F32),
            (short, BF16),
            ((tokens, hidden), BF16),
            (full, F32),
            ((8, model_width), F32),
        ),
        outside=(narrowing_matrix, slope, widening_matrix),
        small=(matched_picture_ids, sharpening_log),
    )

    other = mp_other(part)
    *widen_dealt, mark = call(
        widen_grad_kernel,
        (normed2, grad_pre),
        dealt,
        scratch=(pltpu.VMEM(square, BF16),) * 2,
        index=(place,),
        mark=True,
    )
    grad_residual, grad_branch1, flat, part, mixer_stat = call(
        mixer_back_kernel,
        (
            part,
            other,
            residual,
            grad_caption,
            sentence_word_ids,
            perceptron_layernorm_gamma,
            mixer_result_matrix,
        ),
        (
            (full, F32),
            (full, BF16),
            ((3, tokens, local_width), BF16),
            (full, F32),
            ((8, model_width), F32),
        ),
        outside=(qkv, soft, mixer_triple_matrix),
        after=(mark,),
    )
    other = mp_other(part)
    extra = []
    widen_sum = scatter_steps(widen_dealt, place, extra)
    next(widen_sum)
    *mixer_dealt, mark = call(
        mixer_grad_kernel,
        (normed, flat, mixed, grad_branch1),
        dealt,
        scratch=(pltpu.VMEM(square, BF16),) * 2,
        index=(place,),
        after=sums_parts[1:3],
        mark=True,
    )
    mixer_sum = scatter_steps(mixer_dealt, place)
    next(mixer_sum)
    last = widen_sum.send((mark,))
    last = widen_sum.send((last,))
    extra_rows = captions // 2 + 16
    grad_input, mine = call(
        entry_grad_kernel,
        (
            part,
            other,
            sentence_layer_entry,
            mixer_layernorm_gamma,
            grad_residual,
            loss_stat,
            mixer_stat,
            grad_caption_low,
        ),
        ((full, F32), ((extra_rows, model_width), BF16)),
        scratch=(pltpu.VMEM((16, model_width), F32),),
        index=(core,),
        after=(last,),
    )
    extra.append(dp_gather(mine, steps[:1:-1], [mine] * len(steps)))
    last = mixer_sum.send((mine,))
    last = widen_sum.send((last,))
    last = mixer_sum.send((last,))
    last = widen_sum.send((last,))
    last = mixer_sum.send((last,))
    last = widen_sum.send((last,))
    last = mixer_sum.send((last,))
    widen_pieces = widen_sum.send(())
    near_grads, *results = call(
        functools.partial(collect_kernel, 1.0 / (2.0 * all_pairs), extra_rows),
        (*widen_pieces, loss_stat),
        (
            ((all_pairs // 2, model_width), BF16),
            ((1,), F32),
            ((2, local_width), F32),
            ((model_width,), F32),
            ((hidden,), F32),
        )
        + (((model_width,), F32),) * 5
        + (((1,), F32),),
        after=(last,),
    )
    error, grad_pair, grad_b_out, grad_b_up, grad_b_down = results[:5]
    grad_w_up, mark = call(
        unpack_widen_kernel,
        widen_pieces,
        ((widening_matrix.shape, F32),),
        index=(place,),
        after=(results[0],),
        limit=56,
        mark=True,
    )
    last = mixer_sum.send((mark,))
    grad_w_down, mark = call(
        functools.partial(narrow_grad_kernel, captions // 2),
        (*sums_parts, near_grads, mp_other(near_grads)),
        ((narrowing_matrix.shape, F32),),
        scratch=(pltpu.VMEM((all_pairs, model_width), BF16),),
        index=(core,),
        after=(last,),
        mark=True,
    )
    grad_qkv, grad_w_out = call(
        unpack_mixer_kernel,
        mixer_sum.send(()),
        ((mixer_triple_matrix.shape, F32), (mixer_result_matrix.shape, F32)),
        index=(place,),
        after=(mark,),
        limit=56,
    )
    return (
        error,
        grad_input,
        grad_qkv,
        grad_pair,
        grad_w_out,
        grad_b_out,
        grad_w_up,
        grad_b_up,
        grad_w_down,
        grad_b_down,
        *results[5:],
    )


def solution(mesh):
    placed = (
        P("dp", None),
        P("dp"),
        P(("dp", "mp"), None, None),
        P(("dp", "mp")),
        P("dp"),
        P(),
        P(),
        P(None, None, "mp"),
        P(None, "mp"),
        P("mp", None),
        P(),
        P(),
        P(),
        P(None, "mp"),
        P("mp"),
        P("mp", None),
        P(),
        P(),
        P(),
        P(),
        P(),
        P(),
        P(),
    )
    return jax.shard_map(
        local,
        mesh=mesh,
        in_specs=placed,
        out_specs=(
            P(),
            P("dp", None),
            P(None, None, "mp"),
            P(None, "mp"),
            P("mp", None),
            P(),
            P(None, "mp"),
            P("mp"),
            P("mp", None),
            P(),
            P(),
            P(),
            P(),
            P(),
            P(),
        ),
        check_vma=False,
    )
```

```python
import functools

import jax
import jax.numpy as jnp
from jax import lax
from jax.experimental import pallas as pl
from jax.experimental.pallas import tpu as pltpu
from jax.sharding import PartitionSpec as P

HEAD = 64
IMG_TOK = 145
LOW_TOK = 50
CAP_LEN = 16


EPS_TEXT = 1e-05
EPS_UNIT = 1e-06
MASKED_SCORE = -1e30
BF16 = jnp.bfloat16
F32 = jnp.float32


def mp_other(values):
    return lax.ppermute(values, "mp", [(0, 1), (1, 0)])


def dp_swap(values, mask):
    size = lax.axis_size("dp")
    return lax.ppermute(values, "dp", [(index, index ^ mask) for index in range(size)])


def group_steps(size):
    steps, stride = [], 1
    while stride < size:
        steps.append([stride, 2 * stride, 3 * stride])
        stride *= 4
    return steps


def gather_masks(steps):
    masks = [0]
    for step in steps:
        masks = [mask ^ base for mask in [0] + step for base in masks]
    return masks


def dp_parts(values, step):
    return [values] + [dp_swap(values, mask) for mask in step]


def dp_gather(values, steps, waits):
    for step, wait in zip(steps, waits):
        parts = dp_parts(values, step)
        rows = values.shape[0]
        (values,) = move(
            parts,
            (len(parts) * rows,),
            [(place, 0, rows, 0, place * rows) for place in range(len(parts))],
            (wait,),
        )
    return values


HIGH_ROWS = 160
LOW_ROWS = 64
TILE = 256
PAIR = 2 * HEAD
LANES = 128
POOL_ROWS = 32
NT = (((1,), (1,)), ((), ()))
VMEM_LIMIT = 60 * 1024 * 1024
BUSY = 10**12


def dot(left, right):
    return jnp.dot(left, right, preferred_element_type=F32)


def wide_dot(left, right):
    high = left.astype(BF16)
    rest = (left - high.astype(F32)).astype(BF16)
    return dot(high, right) + dot(rest, right)


def standard(values, epsilon):
    centered = values - jnp.mean(values, axis=-1, keepdims=True)
    variance = jnp.mean(centered * centered, axis=-1, keepdims=True)
    return centered * lax.rsqrt(variance + epsilon)


def gelu(values):
    return (0.5 * values) * (1.0 + lax.erf(values * (0.5**0.5)))


def image_kernel(
    flag_ref,
    token_ref,
    gain_ref,
    triple_hbm,
    result_hbm,
    widen_hbm,
    narrow_hbm,
    out_ref,
    wide,
    packed,
    mixed,
    queries,
    keys,
    values,
    triple,
    result,
    widen,
    narrow,
    resid_groups,
    hidden_groups,
    pooled,
    ready,
    starts,
    high_starts,
    low_starts,
    sems,
):
    _, images, width = token_ref.shape
    hidden = widen.shape[1]
    copies = fetch(
        (triple_hbm, result_hbm, widen_hbm, narrow_hbm), (triple, result, widen, narrow), sems
    )
    lane_tiles = [slice(lane, lane + LANES) for lane in range(0, width, LANES)]

    def spread(position, carry):
        rows = pl.ds(pl.multiple_of(position * images, images), images)
        for place, lanes in enumerate(lane_tiles):
            wide[place, rows, :] = token_ref[position, :, lanes].astype(F32)
        return carry

    def begin(image, carry):
        start, highs = carry
        starts[image] = start
        high = flag_ref[image] == 1

        @pl.when(high)
        def _():
            high_starts[highs] = start

        @pl.when(jnp.logical_not(high))
        def _():
            low_starts[image - highs] = start

        return start + jnp.where(high, HIGH_ROWS, LOW_ROWS), highs + jnp.where(high, 1, 0)

    total, highs = lax.fori_loop(0, images, begin, (jnp.int32(0), jnp.int32(0)))
    lax.fori_loop(0, LOW_ROWS, spread, 0, unroll=4)

    @pl.when(total > images * LOW_ROWS)
    def _():
        lax.fori_loop(LOW_ROWS, IMG_TOK, spread, 0, unroll=3)

    tail = IMG_TOK // 16 * 16

    def pack(image, carry):
        start = pl.multiple_of(starts[image], POOL_ROWS)
        high = flag_ref[image] == 1

        @pl.when(high)
        def _():
            row = lax.broadcasted_iota(jnp.int32, (HIGH_ROWS - tail, LANES), 0)
            for place, lanes in enumerate(lane_tiles):
                packed[pl.ds(start, tail), lanes] = wide[
                    place, pl.ds(image, tail, stride=images), :
                ].astype(BF16)
                last = wide[place, pl.ds(image + tail * images, 1), :]
                packed[pl.ds(start + tail, HIGH_ROWS - tail), lanes] = jnp.where(
                    row == 0, last, 0.0
                ).astype(BF16)

        @pl.when(jnp.logical_not(high))
        def _():
            for place, lanes in enumerate(lane_tiles):
                packed[pl.ds(start, LOW_ROWS), lanes] = wide[
                    place, pl.ds(image, LOW_ROWS, stride=images), :
                ].astype(BF16)

        return carry

    lax.fori_loop(0, images, pack, 0)
    packed[pl.ds(pl.multiple_of(total, POOL_ROWS), TILE), :] = jnp.zeros((TILE, width), BF16)
    tiles = lax.div(total + (TILE - 1), jnp.int32(TILE))

    copies[0].wait()

    def prepare(tile):
        rows = pl.ds(pl.multiple_of(tile * TILE, TILE), TILE)
        ready[tile % 2] = (
            standard(packed[rows, :].astype(F32), EPS_UNIT) * gain_ref[0:1, :]
        ).astype(BF16)

    def project(tile, carry):
        rows = pl.ds(pl.multiple_of(tile * TILE, TILE), TILE)
        normed = ready[tile % 2]
        queries[rows, :] = (dot(normed, triple[0]) * HEAD ** (-0.5)).astype(BF16)
        prepare(tile + 1)
        keys[rows, :] = dot(normed, triple[1]).astype(BF16)
        values[rows, :] = dot(normed, triple[2]).astype(BF16)
        return carry

    prepare(jnp.int32(0))
    lax.fori_loop(0, tiles, project, 0)

    def attend(begins, count, live):
        left = lax.broadcasted_iota(jnp.int32, (count, PAIR), 1) < HEAD
        key_live = lax.broadcasted_iota(jnp.int32, (2 * count, count), 1) < live
        places = [
            (pl.ds(pl.multiple_of(start, POOL_ROWS), count), slice(lane, lane + PAIR))
            for start in begins
            for lane in range(0, width, PAIR)
        ]
        all_scores = [dot_t(two_heads(queries[place], left), keys[place]) for place in places]
        all_powers = []
        for scores in all_scores:
            scores = jnp.where(key_live, scores, MASKED_SCORE)
            top = jnp.max(scores, axis=-1, keepdims=True)
            all_powers.append(jnp.exp(scores - top).astype(BF16))
        for place, powers in zip(places, all_powers):
            value = values[place]
            one = jnp.ones_like(value)
            first = dot(powers[:count], jnp.where(left, value, one))
            second = dot(powers[count:], jnp.where(left, one, value))
            sums = pltpu.roll(jnp.where(left, second, first), HEAD, 1)
            mixed[place] = (jnp.where(left, first, second) / sums).astype(BF16)

    def attend_all(begins, number, together, count, live):
        groups = lax.div(number, jnp.int32(together))

        def group(index, carry):
            attend([begins[index * together + step] for step in range(together)], count, live)
            return carry

        def rest(index, carry):
            attend([begins[index]], count, live)
            return carry

        lax.fori_loop(0, groups, group, 0)
        if together > 1:
            lax.fori_loop(groups * together, number, rest, 0)

    attend_all(high_starts, highs, 1, HIGH_ROWS, IMG_TOK)
    attend_all(low_starts, images - highs, 4, LOW_ROWS, LOW_TOK)

    slot = lax.broadcasted_iota(jnp.int32, (1, images), 1)
    first_row = jnp.zeros((1, images), jnp.int32)
    live_rows = jnp.zeros((1, images), jnp.int32)
    for image in range(images):
        first_row = jnp.where(slot == image, starts[image], first_row)
        live_rows = jnp.where(
            slot == image, jnp.where(flag_ref[image] == 1, IMG_TOK, LOW_TOK), live_rows
        )
    copies[1].wait()
    copies[2].wait()
    groups = TILE // POOL_ROWS

    def group_sum(rows):
        return jnp.sum(rows.reshape(groups, POOL_ROWS // 8, 8, rows.shape[1]), axis=1)

    def resume(tile):
        base = pl.multiple_of(tile * TILE, TILE)
        rows = pl.ds(base, TILE)
        place = base + lax.broadcasted_iota(jnp.int32, (TILE, images), 0)
        alive = jnp.sum(
            jnp.where((place >= first_row) & (place < first_row + live_rows), 1.0, 0.0),
            axis=1,
            keepdims=True,
        )
        residual = (packed[rows, :].astype(F32) + dot(mixed[rows, :], result[...])) * alive
        group = pl.ds(pl.multiple_of(tile * groups, groups), groups)
        resid_groups[group] = group_sum(residual)
        ready[tile % 2] = (standard(residual, EPS_UNIT) * gain_ref[1:2, :]).astype(BF16)

    def perceptron(tile, carry):
        group = pl.ds(pl.multiple_of(tile * groups, groups), groups)
        normed = ready[tile % 2]
        for chunk in range(hidden // width):
            if chunk == 1:
                resume(tile + 1)
            lanes = slice(chunk * width, (chunk + 1) * width)
            units = gelu(dot(normed, widen[:, lanes])).astype(BF16)
            hidden_groups[group, :, lanes] = group_sum(units.astype(F32))
        return carry

    resume(jnp.int32(0))
    lax.fori_loop(0, tiles, perceptron, 0)

    def pool(image, carry):
        group = lax.div(starts[image], jnp.int32(POOL_ROWS))
        high = flag_ref[image] == 1

        def add(count):
            residual, units = resid_groups[group], hidden_groups[group]
            for step in range(1, count):
                residual = residual + resid_groups[group + step]
                units = units + hidden_groups[group + step]
            pooled[pl.ds(image, 1), :width] = jnp.sum(residual, axis=0, keepdims=True)
            pooled[pl.ds(image, 1), width:] = jnp.sum(units, axis=0, keepdims=True)

        @pl.when(high)
        def _():
            add(HIGH_ROWS // POOL_ROWS)

        @pl.when(jnp.logical_not(high))
        def _():
            add(LOW_ROWS // POOL_ROWS)

        return carry

    lax.fori_loop(0, images, pool, 0)
    copies[3].wait()
    units = pooled[:, width:]
    upper = units.astype(BF16)
    lower = (units - upper.astype(F32)).astype(BF16)
    branch = dot(jnp.concatenate([upper, lower], axis=0), narrow[...])
    live = jnp.where(number_column(flag_ref) == 1, IMG_TOK, LOW_TOK).astype(F32)
    mean = (pooled[:, :width] + branch[:images] + branch[images:]) / live
    out_ref[...] = (
        mean * lax.rsqrt(jnp.sum(mean * mean, axis=-1, keepdims=True) + EPS_UNIT)
    ).astype(BF16)


def image_tower(flags, tokens, gains, triple, result, widen, narrow):
    images, _, width = tokens.shape
    hidden = widen.shape[1]
    rows = images * HIGH_ROWS + TILE
    groups = rows // POOL_ROWS
    outside = pl.BlockSpec(memory_space=pl.ANY)
    inside = pl.BlockSpec(memory_space=pltpu.VMEM)
    return pl.pallas_call(
        image_kernel,
        out_shape=jax.ShapeDtypeStruct((images, width), BF16),
        in_specs=[pl.BlockSpec(memory_space=pltpu.SMEM), inside, inside]
        + [outside] * 4,
        out_specs=inside,
        scratch_shapes=[pltpu.VMEM((width // LANES, IMG_TOK * images, LANES), F32)]
        + [pltpu.VMEM((rows, width), BF16)] * 5
        + [pltpu.VMEM(weight.shape, BF16) for weight in (triple, result, widen, narrow)]
        + [
            pltpu.VMEM((groups, 8, width), F32),
            pltpu.VMEM((groups, 8, hidden), F32),
            pltpu.VMEM((images, width + hidden), F32),
            pltpu.VMEM((2, TILE, width), BF16),
            pltpu.SMEM((images,), jnp.int32),
            pltpu.SMEM((images,), jnp.int32),
            pltpu.SMEM((images,), jnp.int32),
            pltpu.SemaphoreType.DMA((4,)),
        ],
        compiler_params=pltpu.CompilerParams(vmem_limit_bytes=VMEM_LIMIT),
        cost_estimate=pl.CostEstimate(flops=BUSY, bytes_accessed=BUSY, transcendentals=0),
    )(flags, jnp.transpose(tokens, (1, 0, 2)), gains, triple, result, widen, narrow)


TN = (((0,), (0,)), ((), ()))
BLOCK = 128
ROOT_HALF = 0.5**0.5
DENSITY = 0.3989422804014327


def dot_t(left, right):
    return lax.dot_general(left, right, NT, preferred_element_type=F32)


def t_dot(left, right):
    return lax.dot_general(left, right, TN, preferred_element_type=F32)


def fetch(sources, targets, sems):
    copies = [
        pltpu.make_async_copy(source, target, sems.at[place])
        for place, (source, target) in enumerate(zip(sources, targets))
    ]
    for copy in copies:
        copy.start()
    return copies


def caption_pool(ids_ref, captions):
    ids_row = ids_ref[...].reshape(1, -1)
    tokens = ids_row.shape[1]
    shape = (captions, tokens)
    caption = lax.broadcasted_iota(jnp.int32, shape, 0)
    token = lax.broadcasted_iota(jnp.int32, shape, 1)
    inside = (token // (tokens // captions)) == caption
    return jnp.where(inside & (ids_row != 0), 1.0, 0.0)


def valid_column(pool):
    pool = pool.astype(BF16)
    return t_dot(pool, jnp.ones((pool.shape[0], 128), BF16))[:, 0:1]


def number_column(ref):
    shape = (ref.shape[0], 1)
    place = lax.broadcasted_iota(jnp.int32, shape, 0)
    column = jnp.zeros(shape, jnp.int32)
    for index in range(shape[0]):
        column = jnp.where(place == index, ref[index], column)
    return column


def as_row(ref):
    return ref[...].reshape(1, -1)


def pair_masks(rows, pair_width):
    return lax.broadcasted_iota(jnp.int32, (rows, pair_width), 1) < HEAD


def two_heads(values, left):
    zero = jnp.zeros_like(values)
    return jnp.concatenate(
        [jnp.where(left, values, zero), jnp.where(left, zero, values)], axis=0
    )


def text_mix_kernel(
    entry_ref,
    ids_ref,
    gain_ref,
    shift_ref,
    triple_ref,
    pair_ref,
    result_ref,
    normed_ref,
    qkv_ref,
    soft_ref,
    mixed_ref,
    part_ref,
):
    tokens = entry_ref.shape[0]
    width = result_ref.shape[0]
    normed = (
        standard(entry_ref[...].astype(F32), EPS_TEXT) * as_row(gain_ref) + as_row(shift_ref)
    ).astype(BF16)
    normed_ref[...] = normed
    qkv_ref[0] = (dot(normed, triple_ref[0]) + pair_ref[0:1, :]).astype(BF16)
    qkv_ref[1] = dot(normed, triple_ref[1]).astype(BF16)
    qkv_ref[2] = (dot(normed, triple_ref[2]) + pair_ref[1:2, :]).astype(BF16)
    ids = as_row(ids_ref)
    left = pair_masks(BLOCK, PAIR)
    shape = (2 * BLOCK, BLOCK)
    query_caption = lax.broadcasted_iota(jnp.int32, shape, 0) % BLOCK // CAP_LEN
    same = query_caption == lax.broadcasted_iota(jnp.int32, shape, 1) // CAP_LEN
    for block in range(tokens // BLOCK):
        rows = slice(block * BLOCK, (block + 1) * BLOCK)
        seen = same & (ids[:, rows] != 0)
        for pair in range(width // PAIR):
            lanes = slice(pair * PAIR, (pair + 1) * PAIR)
            scores = dot_t(two_heads(qkv_ref[0, rows, lanes], left), qkv_ref[1, rows, lanes])
            scores = jnp.where(seen, scores * HEAD ** (-0.5), MASKED_SCORE)
            powers = jnp.exp(scores - jnp.max(scores, axis=-1, keepdims=True))
            soft = powers / jnp.sum(powers, axis=-1, keepdims=True)
            soft_ref[block, pair] = soft
            low = soft.astype(BF16)
            value = qkv_ref[2, rows, lanes]
            mixed_ref[rows, lanes] = jnp.where(
                left, dot(low[:BLOCK], value), dot(low[BLOCK:], value)
            ).astype(BF16)
    part_ref[...] = dot(mixed_ref[...], result_ref[...])


def text_widen_kernel(
    entry_ref,
    own_ref,
    other_ref,
    result_offset_ref,
    gain_ref,
    shift_ref,
    widen_offset_ref,
    ids_ref,
    widen_hbm,
    narrow_hbm,
    residual_ref,
    normed_ref,
    slope_ref,
    sums_ref,
    resid_sum_ref,
    branch_ref,
    widen,
    narrow,
    hidden_sum,
    sems,
):
    captions = sums_ref.shape[0]
    width = entry_ref.shape[1]
    copies = fetch((widen_hbm, narrow_hbm), (widen, narrow), sems)
    residual = entry_ref[...].astype(F32) + (
        (own_ref[...] + other_ref[...]) + as_row(result_offset_ref)
    )
    residual_ref[...] = residual
    normed = (standard(residual, EPS_TEXT) * as_row(gain_ref) + as_row(shift_ref)).astype(BF16)
    normed_ref[...] = normed
    pool = caption_pool(ids_ref, captions).astype(BF16)
    widen_offset = as_row(widen_offset_ref)
    upper = residual.astype(BF16)
    resid_sum_ref[...] = dot(pool, upper) + dot(
        pool, (residual - upper.astype(F32)).astype(BF16)
    )
    valid = valid_column(pool)
    copies[0].wait()
    for chunk in range(widen.shape[1] // width):
        lanes = slice(chunk * width, (chunk + 1) * width)
        before = dot(normed, widen[:, lanes]) + widen_offset[:, lanes]
        share = 0.5 * (1.0 + lax.erf(before * ROOT_HALF))
        hidden_sum[:, lanes] = dot(pool, (before * share).astype(BF16))
        slope = share + before * (jnp.exp(-0.5 * before * before) * DENSITY)
        slope_ref[:, lanes] = slope * valid
    sums_ref[...] = hidden_sum[...].astype(BF16)
    copies[1].wait()
    branch_ref[...] = wide_dot(hidden_sum[...], narrow[...])


def logits_kernel(
    masks,
    index_ref,
    matched_ref,
    sharpen_ref,
    near_ref,
    far_ref,
    resid_sum_ref,
    own_ref,
    other_ref,
    narrow_offset_ref,
    ids_ref,
    images_ref,
    unit_ref,
    factor_ref,
    logits_ref,
    powers_ref,
    row_sum_ref,
    col_sum_ref,
    loss_ref,
):
    captions, pairs = logits_ref.shape
    rows = images_ref.shape[0] // (2 * len(masks))
    core = index_ref[1]
    for place, mask in enumerate(masks):
        start = (index_ref[0] ^ mask) * (2 * rows)
        images_ref[pl.ds(pl.multiple_of(start + core * rows, rows), rows), :] = near_ref[
            place * rows : (place + 1) * rows, :
        ]
        images_ref[pl.ds(pl.multiple_of(start + (1 - core) * rows, rows), rows), :] = far_ref[
            place * rows : (place + 1) * rows, :
        ]
    count = jnp.sum(caption_pool(ids_ref, captions), axis=1, keepdims=True)
    pooled = (resid_sum_ref[...] + (own_ref[...] + other_ref[...])) / count + as_row(
        narrow_offset_ref
    )
    inverse = lax.rsqrt(jnp.sum(pooled * pooled, axis=-1, keepdims=True) + EPS_UNIT)
    unit = pooled * inverse
    unit_ref[...] = unit
    factor_ref[...] = jnp.broadcast_to(inverse / count, factor_ref.shape)
    logits = jnp.exp(jnp.full((1, 1), sharpen_ref[0], F32)) * dot_t(unit.astype(BF16), images_ref[...])
    logits_ref[...] = logits
    powers = jnp.exp(logits)
    powers_ref[...] = powers
    row_sum = jnp.sum(powers, axis=1, keepdims=True)
    row_sum_ref[...] = jnp.broadcast_to(row_sum, row_sum_ref.shape)
    col_sum_ref[...] = jnp.sum(powers, axis=0, keepdims=True)
    positive = number_column(matched_ref) == lax.broadcasted_iota(jnp.int32, (captions, pairs), 1)
    wanted = jnp.sum(jnp.where(positive, logits, 0.0), axis=1, keepdims=True)
    loss_ref[...] = jnp.broadcast_to(
        jnp.sum(jnp.log(row_sum) - 2.0 * wanted, axis=0, keepdims=True), loss_ref.shape
    )


def sum_kernel(first_ref, second_ref, third_ref, fourth_ref, out_ref):
    out_ref[...] = (first_ref[...] + second_ref[...]) + (third_ref[...] + fourth_ref[...])


def loss_grad_kernel(
    matched_ref,
    sharpen_ref,
    col_ref,
    col1_ref,
    col2_ref,
    col3_ref,
    logits_ref,
    powers_ref,
    row_sum_ref,
    unit_ref,
    factor_ref,
    images_ref,
    ids_ref,
    loss_ref,
    narrow_hbm,
    slope_hbm,
    widen_hbm,
    grad_ref,
    low_ref,
    before_ref,
    part_ref,
    stat_ref,
    narrow,
    slope,
    widen,
    sems,
):
    captions, pairs = logits_ref.shape
    tokens, hidden = slope.shape
    width = grad_ref.shape[1]
    copies = fetch((narrow_hbm, slope_hbm, widen_hbm), (narrow, slope, widen), sems)
    logits, powers = logits_ref[...], powers_ref[...]
    col_sum = (col_ref[...] + col1_ref[...]) + (col2_ref[...] + col3_ref[...])
    positive = number_column(matched_ref) == lax.broadcasted_iota(jnp.int32, (captions, pairs), 1)
    derivative = (
        powers / row_sum_ref[:, 0:1] + powers / col_sum - jnp.where(positive, 2.0, 0.0)
    ) / (2.0 * pairs)
    temperature = jnp.sum(
        jnp.sum(derivative * logits, axis=1, keepdims=True), axis=0, keepdims=True
    )
    col_loss = jnp.sum(jnp.log(col_sum), axis=1, keepdims=True)
    text = dot((derivative * jnp.exp(jnp.full((1, 1), sharpen_ref[0], F32))).astype(BF16), images_ref[...])
    unit = unit_ref[...]
    grad = (text - unit * jnp.sum(unit * text, axis=-1, keepdims=True)) * factor_ref[:, 0:1]
    grad_ref[...] = grad
    low = grad.astype(BF16)
    low_ref[...] = low
    copies[0].wait()
    copies[1].wait()
    copies[2].wait()
    ones = jnp.ones((8, tokens), BF16)
    part = jnp.zeros(part_ref.shape, F32)
    for chunk in range(hidden // width):
        lanes = slice(chunk * width, (chunk + 1) * width)
        back = dot_t(low, narrow[lanes, :])
        before = (
            (back[:, None, :] * slope[:, lanes].reshape(captions, CAP_LEN, width))
            .reshape(tokens, width)
            .astype(BF16)
        )
        before_ref[:, lanes] = before
        stat_ref[chunk : chunk + 1, :] = dot(ones, before)[0:1]
        part = part + dot_t(before, widen[:, lanes])
    part_ref[...] = part
    count = jnp.sum(caption_pool(ids_ref, captions), axis=1, keepdims=True)
    stat_ref[2:3, :] = jnp.sum(low.astype(F32) * count, axis=0, keepdims=True)
    lane = lax.broadcasted_iota(jnp.int32, (1, width), 1)
    stat_ref[3:4, :] = jnp.where(
        lane == 0,
        temperature,
        jnp.where(lane == 1, loss_ref[0:1, 0:1], jnp.where(lane == 2, col_loss, 0.0)),
    )
    stat_ref[4:8, :] = jnp.zeros((4, width), F32)


def deal(index_ref, first, second, outs):
    half = first.shape[0] // 2
    for place, (values, bit) in enumerate(((first, 1), (second, 2))):
        mine = index_ref[0] // bit % 2
        for ref, which in ((outs[2 * place], 1 - mine), (outs[2 * place + 1], mine)):
            ref[...] = values[pl.ds(pl.multiple_of(which * half, half), half), :]


def widen_grad_kernel(index_ref, normed_ref, before_ref, *refs):
    outs, (first, second) = refs[:4], refs[4:]
    width = first.shape[1]
    normed = normed_ref[...]
    first[...] = t_dot(normed, before_ref[:, :width]).astype(BF16)
    second[...] = t_dot(normed, before_ref[:, width:]).astype(BF16)
    deal(index_ref, first, second, outs)


def mixer_back_kernel(
    own_ref,
    other_ref,
    residual_ref,
    grad_ref,
    ids_ref,
    gain_ref,
    result_ref,
    qkv_hbm,
    soft_hbm,
    triple_hbm,
    grad_residual_ref,
    low_ref,
    flat_ref,
    part_ref,
    stat_ref,
    qkv,
    soft_all,
    triple,
    sems,
):
    tokens, width = residual_ref.shape
    captions = grad_ref.shape[0]
    local_width = result_ref.shape[0]
    copies = fetch((qkv_hbm, soft_hbm, triple_hbm), (qkv, soft_all, triple), sems)
    residual = residual_ref[...]
    centered = residual - jnp.mean(residual, axis=-1, keepdims=True)
    rate = lax.rsqrt(jnp.mean(centered * centered, axis=-1, keepdims=True) + EPS_TEXT)
    unit = centered * rate
    grad = own_ref[...] + other_ref[...]
    stat_ref[1:2, :] = jnp.sum(grad * unit, axis=0, keepdims=True)
    stat_ref[2:3, :] = jnp.sum(grad, axis=0, keepdims=True)
    scaled = grad * as_row(gain_ref)
    inner = rate * (
        scaled
        - jnp.mean(scaled, axis=-1, keepdims=True)
        - unit * jnp.mean(scaled * unit, axis=-1, keepdims=True)
    )
    spread = jnp.broadcast_to(
        grad_ref[...][:, None, :], (captions, tokens // captions, width)
    ).reshape(tokens, width)
    grad_residual = spread * valid_column(caption_pool(ids_ref, captions)) + inner
    grad_residual_ref[...] = grad_residual
    low = grad_residual.astype(BF16)
    low_ref[...] = low
    ones = jnp.ones((8, tokens), BF16)
    stat_ref[0:1, :] = dot(ones, low)[0:1]
    grad_mixed = dot_t(low, result_ref[...]).astype(BF16)
    for copy in copies:
        copy.wait()
    left = pair_masks(BLOCK, PAIR)
    places = [
        (block, pair, slice(block * BLOCK, (block + 1) * BLOCK), slice(pair * PAIR, (pair + 1) * PAIR))
        for block in range(tokens // BLOCK)
        for pair in range(local_width // PAIR)
    ]
    mixed = [two_heads(grad_mixed[rows, lanes], left) for _, _, rows, lanes in places]
    softs = [soft_all[block, pair] for block, pair, _, _ in places]
    grads = [
        dot_t(value, qkv[2, rows, lanes]) for value, (_, _, rows, lanes) in zip(mixed, places)
    ]
    scores = [
        (soft * (grad - jnp.sum(grad * soft, axis=-1, keepdims=True))).astype(BF16)
        for soft, grad in zip(softs, grads)
    ]
    for value, soft, (_, _, rows, lanes) in zip(mixed, softs, places):
        flat_ref[2, rows, lanes] = t_dot(soft.astype(BF16), value).astype(BF16)
    for score, (_, _, rows, lanes) in zip(scores, places):
        key = qkv[1, rows, lanes]
        back = jnp.where(left, dot(score[:BLOCK], key), dot(score[BLOCK:], key))
        flat_ref[0, rows, lanes] = (back * HEAD ** (-0.5)).astype(BF16)
    for score, (_, _, rows, lanes) in zip(scores, places):
        flat_ref[1, rows, lanes] = (
            t_dot(score, two_heads(qkv[0, rows, lanes], left)) * HEAD ** (-0.5)
        ).astype(BF16)
    part_ref[...] = (
        dot_t(flat_ref[0], triple[0])
        + dot_t(flat_ref[1], triple[1])
        + dot_t(flat_ref[2], triple[2])
    )
    stat_ref[3:4, :local_width] = dot(ones, flat_ref[0])[0:1]
    stat_ref[3:4, local_width:] = dot(ones, flat_ref[2])[0:1]
    stat_ref[4:8, :] = jnp.zeros((4, width), F32)


def mixer_grad_kernel(index_ref, normed_ref, flat_ref, mixed_ref, low_ref, *refs):
    outs, (first, second) = refs[:4], refs[4:]
    half = flat_ref.shape[2]
    rows = first.shape[0] // 2
    normed = normed_ref[...]
    for part, (target, place) in enumerate(((first, 0), (first, rows), (second, 0))):
        grad = t_dot(normed, flat_ref[part]).astype(BF16)
        target[place : place + rows, :half] = grad[:rows]
        target[place : place + rows, half:] = grad[rows:]
    second[rows:, :] = t_dot(mixed_ref[...], low_ref[...]).astype(BF16)
    deal(index_ref, first, second, outs)


def narrow_grad_kernel(half, index_ref, *refs):
    parts, (near_ref, far_ref, out_ref, grads) = refs[:-4], refs[-4:]
    rows, width = parts[0].shape[0], grads.shape[1]
    devices = near_ref.shape[0] // half
    for place in range(devices):
        plane, group, high = place % 4, place // 4 % (devices // GROUP), place * 4 // devices
        source = (plane * Z_SIZE + high) * (devices // GROUP) + group
        for ref, which in ((near_ref, index_ref[0]), (far_ref, 1 - index_ref[0])):
            start = pl.multiple_of((2 * place + which) * half, half)
            grads[pl.ds(start, half), :] = ref[source * half : (source + 1) * half, :]
    for chunk in range(out_ref.shape[0] // width):
        lanes = slice(chunk * width, (chunk + 1) * width)
        total = t_dot(parts[0][:, lanes], grads[:rows, :])
        for place in range(1, len(parts)):
            total = total + t_dot(
                parts[place][:, lanes], grads[place * rows : (place + 1) * rows, :]
            )
        out_ref[lanes, :] = total


def entry_grad_kernel(
    index_ref,
    own_ref,
    other_ref,
    entry_ref,
    gain_ref,
    grad_residual_ref,
    loss_stat_ref,
    mixer_stat_ref,
    caption_ref,
    out_ref,
    extra_ref,
    pack,
):
    entry = entry_ref[...].astype(F32)
    centered = entry - jnp.mean(entry, axis=-1, keepdims=True)
    rate = lax.rsqrt(jnp.mean(centered * centered, axis=-1, keepdims=True) + EPS_TEXT)
    unit = centered * rate
    grad = own_ref[...] + other_ref[...]
    pack[0:8, :] = loss_stat_ref[...]
    pack[8:16, :] = mixer_stat_ref[...]
    pack[4:5, :] = jnp.sum(grad * unit, axis=0, keepdims=True)
    pack[5:6, :] = jnp.sum(grad, axis=0, keepdims=True)
    half = caption_ref.shape[0] // 2
    extra_ref[:half, :] = caption_ref[
        pl.ds(pl.multiple_of(index_ref[0] * half, half), half), :
    ]
    upper = pack[...].astype(BF16).astype(F32)
    pack[15:16, :] = (pack[...] - upper)[3:4, :]
    extra_ref[half:, :] = pack[...].astype(BF16)
    scaled = grad * as_row(gain_ref)
    out_ref[...] = grad_residual_ref[...] + rate * (
        scaled
        - jnp.mean(scaled, axis=-1, keepdims=True)
        - unit * jnp.mean(scaled * unit, axis=-1, keepdims=True)
    )


def tree_sum(values):
    while len(values) > 1:
        values = [values[place] + values[place + 1] for place in range(0, len(values), 2)]
    return values[0]


def collect_kernel(scale, rows, *refs):
    gathered, loss_ref, near_ref = refs[:8], refs[8], refs[9]
    (
        error_ref,
        pair_ref,
        result_ref,
        widen_ref,
        narrow_ref,
        gain1_ref,
        shift1_ref,
        gain2_ref,
        shift2_ref,
        temperature_ref,
    ) = refs[10:]
    half = rows - 16
    size = gathered[7].shape[0] // Z_SIZE
    more = gathered[1].shape[0] - 2 * size
    totals = []
    for piece in range(4):
        for step in range(Z_SIZE):
            if piece == 3:
                ref, first = gathered[6], Z_SIZE * size + step * more
            elif step < Z_SIZE - 1:
                ref, first = gathered[2 * piece], 3 * size + step * more
            else:
                ref, first = gathered[2 * piece + 1], 2 * size
            for row in range(first, first + more, rows):
                place = len(totals)
                near_ref[place * half : (place + 1) * half, :] = ref[row : row + half, :]
                totals.append(ref[row + half : row + rows, :].astype(F32))
    total = tree_sum(totals)
    scalars = total[3:4] + total[15:16]
    error_ref[...] = ((scalars[:, 1:2] + loss_ref[3:4, 2:3]) * scale).reshape(1)
    temperature_ref[...] = scalars[:, 0:1].reshape(1)
    lanes = pair_ref.shape[1]
    pair_ref[0:1, :] = total[11:12, :lanes]
    pair_ref[1:2, :] = total[11:12, lanes:]
    width = total.shape[1]
    for chunk in range(widen_ref.shape[0] // width):
        widen_ref[chunk * width : (chunk + 1) * width] = total[chunk]
    for ref, place in (
        (narrow_ref, 2),
        (gain1_ref, 4),
        (shift1_ref, 5),
        (result_ref, 8),
        (gain2_ref, 9),
        (shift2_ref, 10),
    ):
        ref[...] = total[place]


def call(kernel, inside, shapes, outside=(), scratch=(), index=(), small=(), after=(), limit=24, mark=False, busy=BUSY):
    vmem = pl.BlockSpec(memory_space=pltpu.VMEM)
    extra = [pltpu.VMEM(array.shape, array.dtype) for array in outside]
    extra += list(scratch)
    if outside:
        extra += [pltpu.SemaphoreType.DMA((len(outside),))]
    index = [jnp.stack(index).astype(jnp.int32)] if index else []
    small = index + list(small)
    before = len(small) + len(inside) + len(outside)

    if mark:
        shapes = tuple(shapes) + (((8, 128), F32),)

    def body(*refs):
        refs = refs[:before] + refs[before + len(after) :]
        if mark:
            last = before + len(shapes) - 1
            refs[last][...] = jnp.zeros((8, 128), F32)
            refs = refs[:last] + refs[last + 1 :]
        kernel(*refs)

    return pl.pallas_call(
        body,
        out_shape=[jax.ShapeDtypeStruct(shape, kind) for shape, kind in shapes],
        in_specs=[pl.BlockSpec(memory_space=pltpu.SMEM)] * len(small)
        + [vmem] * len(inside)
        + [pl.BlockSpec(memory_space=pl.ANY)] * (len(outside) + len(after)),
        out_specs=[vmem] * len(shapes),
        scratch_shapes=extra,
        compiler_params=pltpu.CompilerParams(vmem_limit_bytes=limit * 1024 * 1024),
        cost_estimate=pl.CostEstimate(flops=busy, bytes_accessed=busy, transcendentals=0),
    )(*small, *inside, *outside, *after)


def move(arrays, sizes, plan, after=(), mark=False, busy=BUSY):
    width, kind = arrays[0].shape[1], arrays[0].dtype

    def body(*refs):
        ins, outs = refs[: len(arrays)], refs[len(arrays) :]
        for source, first, rows, target, start in plan:
            outs[target][start : start + rows, :] = ins[source][first : first + rows, :]

    return call(body, arrays, tuple(((size, width), kind) for size in sizes), after=after, mark=mark, busy=busy)


GROUP = 16
Z_STRIDE, Z_SIZE = 4, 4


def block_rows(block, rows):
    return pl.ds(pl.multiple_of(block * rows, rows), rows)


def fold_kernel(index_ref, *refs):
    ins, outs = refs[:4], refs[4:]
    half = outs[0].shape[0]
    for place, bit in ((0, 2), (1, 1)):
        mine = index_ref[0] // bit % 2
        for out, which in ((outs[2 * place], 1 - mine), (outs[2 * place + 1], mine)):
            rows = block_rows(which, half)
            out[...] = (
                ins[2 * place][rows, :].astype(F32) + ins[2 * place + 1][rows, :].astype(F32)
            ).astype(out.dtype)


def cut_kernel(index_ref, *refs):
    ins, outs = refs[:4], refs[4:]
    rows = ins[0].shape[0] // Z_SIZE
    for place in range(2):
        for step, out in enumerate(outs):
            block = block_rows((index_ref[0] // Z_STRIDE % Z_SIZE) ^ step, rows)
            out[place * rows : (place + 1) * rows, :] = (
                ins[2 * place][block, :] + ins[2 * place + 1][block, :].astype(F32)
            ).astype(out.dtype)


def add_kernel(own_ref, *refs):
    out_ref = refs[-1]
    rows = own_ref.shape[0]
    total = own_ref[...]
    for ref in refs[: Z_SIZE - 1]:
        total = total + ref[...].astype(F32)
    out_ref[:rows, :] = total.astype(out_ref.dtype)
    if out_ref.shape[0] > rows:
        out_ref[rows:, :] = refs[Z_SIZE - 1][...]


def scatter_steps(dealt, place, extra=None):
    first_sent, first_kept, second_sent, second_kept = dealt
    rows, width = first_sent.shape
    after = yield
    arrived = (dp_swap(first_sent, 1), dp_swap(second_sent, 2))
    half = (rows // 2, width)
    first_sent, first_kept, second_sent, second_kept, mark = call(
        fold_kernel,
        (first_kept, arrived[0], second_kept, arrived[1]),
        ((half, BF16), (half, F32), (half, BF16), (half, F32)),
        index=(place,),
        after=after,
        mark=True, busy=1,
    )
    after = yield mark
    arrived = (dp_swap(first_sent, 2), dp_swap(second_sent, 1))
    block = (rows // Z_SIZE, width)
    own, *sent, mark = call(
        cut_kernel,
        (first_kept, arrived[0], second_kept, arrived[1]),
        ((block, F32),) + ((block, BF16),) * (Z_SIZE - 1),
        index=(place,),
        after=after,
        mark=True, busy=1,
    )
    after = yield mark
    arrived = [dp_swap(values, step * Z_STRIDE) for step, values in enumerate(sent, 1)]
    size = lax.axis_size("dp")
    more = 0 if extra is None else extra[0].shape[0]
    if size > GROUP:
        mine, mark = call(
            add_kernel, (own, *arrived), ((own.shape, F32),), after=after, mark=True, busy=1
        )
        groups = [list(range(index, size, GROUP)) for index in range(GROUP)]
        mine = lax.psum(mine, "dp", axis_index_groups=groups).astype(BF16)
        if more:
            mine = jnp.concatenate([mine, *extra], axis=0)
    else:
        mine, mark = call(
            add_kernel,
            (own, *arrived) + (tuple(extra) if more else ()),
            (((block[0] + more, width), BF16),),
            after=after,
            mark=True, busy=1,
        )
    after = yield mark
    high = dp_swap(mine, 2 * Z_STRIDE)
    early = (mine, dp_swap(mine, Z_STRIDE), high)
    late = dp_swap(high, Z_STRIDE)
    half = block[0] // 2
    plan, start = [], 0
    for first, count in ((0, half), (2 * half, more), (half, half)):
        for piece in range(len(early)):
            if count:
                plan.append((piece, first, count, 0, start))
            start += count
    joined, mark = move(early, (start,), plan, after, mark=True, busy=1)
    along_x, along_y = dp_swap(joined, 1), dp_swap(joined, 2)
    late_x, late_y = dp_swap(late, 1), dp_swap(late, 2)
    after = yield mark
    plan = [
        (0, 0, 3 * half, 0, 0),
        (1, 0, half, 0, 3 * half),
        (2, 3 * (half + more), 3 * half, 1, 0),
        (3, half, half, 1, 3 * half),
    ]
    if more:
        plan += [
            (0, 3 * half, 3 * more, 0, 4 * half),
            (1, 2 * half, more, 0, 4 * half + 3 * more),
        ]
    first, second, mark = move(
        (along_y, late_y, along_x, late_x),
        (4 * (half + more), 4 * half),
        plan,
        after,
        mark=True,
        busy=1,
    )
    after = yield mark
    far = (dp_swap(first, 1), dp_swap(second, 2))
    yield (joined, late, along_x, late_x, along_y, late_y, *far)


def block_home(index, block, outer, inner):
    high = (block // 8) ^ (index // outer % 2)
    middle = (block // 4 % 2) ^ (index // inner % 2)
    return high * 8 + middle * 4 + ((block % 4) ^ (index // Z_STRIDE % Z_SIZE))


def relative_blocks(refs, tensor):
    rows = refs[7].shape[0] // Z_SIZE
    more = refs[1].shape[0] - 2 * rows
    for piece, early in enumerate((0, 2, 4) if tensor else (0, 4, 2)):
        for step in range(Z_SIZE):
            if step < Z_SIZE - 1:
                ref, first = refs[early], tensor * 3 * (rows + more) + step * rows
            else:
                ref, first = refs[early + 1], tensor * rows
            yield piece * Z_SIZE + step, rows, ref[first : first + rows, :]
    for step in range(Z_SIZE):
        values = refs[6 + tensor][step * rows : (step + 1) * rows, :]
        yield 3 * Z_SIZE + step, rows, values


def unpack_widen_kernel(index_ref, *refs):
    refs, out_ref = refs[:-1], refs[-1]
    width = out_ref.shape[1] // 2
    for tensor, bits in ((0, (1, 2)), (1, (2, 1))):
        for block, rows, values in relative_blocks(refs, tensor):
            start = pl.multiple_of(block_home(index_ref[0], block, *bits) * rows, rows)
            out_ref[pl.ds(start, rows), tensor * width : (tensor + 1) * width] = values.astype(F32)


def unpack_mixer_kernel(index_ref, *refs):
    refs, (triple_ref, result_ref) = refs[:-2], refs[-2:]
    half, split = triple_ref.shape[2], triple_ref.shape[1] // 2
    for block, rows, values in relative_blocks(refs, 0):
        home = block_home(index_ref[0], block, 1, 2)
        part, row = home // 8, pl.multiple_of(home % 8 * rows, rows)
        triple_ref[part, pl.ds(row, rows), :] = values[:, :half].astype(F32)
        triple_ref[part, pl.ds(split + row, rows), :] = values[:, half:].astype(F32)
    for block, rows, values in relative_blocks(refs, 1):
        home = block_home(index_ref[0], block, 2, 1)
        row = pl.multiple_of(home % 8 * rows, rows)

        @pl.when(home < 8)
        def _():
            triple_ref[2, pl.ds(row, rows), :] = values[:, :half].astype(F32)
            triple_ref[2, pl.ds(split + row, rows), :] = values[:, half:].astype(F32)

        @pl.when(home >= 8)
        def _():
            result_ref[pl.ds(row, rows), :] = values.astype(F32)


def local(
    sentence_layer_entry,
    sentence_word_ids,
    picture_tile_activations,
    picture_detail_flag,
    matched_picture_ids,
    mixer_layernorm_gamma,
    mixer_layernorm_offset,
    mixer_triple_matrix,
    mixer_pair_offsets,
    mixer_result_matrix,
    mixer_result_offset,
    perceptron_layernorm_gamma,
    perceptron_layernorm_offset,
    widening_matrix,
    widening_offset,
    narrowing_matrix,
    narrowing_offset,
    sharpening_log,
    locked_layernorm_gammas,
    locked_mixer_triple_matrix,
    locked_mixer_result_matrix,
    locked_widening_matrix,
    locked_narrowing_matrix,
):
    captions = matched_picture_ids.shape[0]
    tokens, model_width = sentence_layer_entry.shape
    local_width = mixer_result_matrix.shape[0]
    hidden = narrowing_matrix.shape[0]
    devices = lax.axis_size("dp")
    all_pairs = captions * devices
    place, core = lax.axis_index("dp"), lax.axis_index("mp")
    blocks = tokens // BLOCK
    full = (tokens, model_width)
    short = (captions, model_width)
    square = (model_width, model_width)
    half_square = (model_width // 2, model_width)
    dealt = ((half_square, BF16),) * 4

    steps = group_steps(devices)

    image_emb = image_tower(
        picture_detail_flag,
        picture_tile_activations,
        locked_layernorm_gammas,
        locked_mixer_triple_matrix,
        locked_mixer_result_matrix,
        locked_widening_matrix,
        locked_narrowing_matrix,
    )
    normed, qkv, soft, mixed, part, mark = call(
        text_mix_kernel,
        (
            sentence_layer_entry,
            sentence_word_ids,
            mixer_layernorm_gamma,
            mixer_layernorm_offset,
            mixer_triple_matrix,
            mixer_pair_offsets,
            mixer_result_matrix,
        ),
        (
            (full, BF16),
            ((3, tokens, local_width), BF16),
            ((blocks, local_width // PAIR, 2 * BLOCK, BLOCK), F32),
            ((tokens, local_width), BF16),
            (full, F32),
        ),
        after=(image_emb,),
        limit=60,
        mark=True,
    )
    other = mp_other(part)
    near_images = dp_gather(image_emb, steps[:0:-1], [mark] * (len(steps) - 1))
    residual, normed2, slope, hidden_sums, resid_sum, branch = call(
        text_widen_kernel,
        (
            sentence_layer_entry,
            part,
            other,
            mixer_result_offset,
            perceptron_layernorm_gamma,
            perceptron_layernorm_offset,
            widening_offset,
            sentence_word_ids,
        ),
        (
            (full, F32),
            (full, BF16),
            ((tokens, hidden), F32),
            ((captions, hidden), BF16),
            (short, F32),
            (short, F32),
        ),
        outside=(widening_matrix, narrowing_matrix),
        scratch=(pltpu.VMEM((captions, hidden), F32),),
        after=(near_images,),
    )

    near_images = dp_gather(near_images, steps[:1], (branch,))
    sums_parts = dp_parts(hidden_sums, steps[0])
    images, unit, factor, logits, powers, row_sum, col_sum, row_loss = call(
        functools.partial(logits_kernel, gather_masks(steps[::-1])),
        (
            near_images,
            mp_other(near_images),
            resid_sum,
            branch,
            mp_other(branch),
            narrowing_offset,
            sentence_word_ids,
        ),
        (
            ((all_pairs, model_width), BF16),
            (short, F32),
            ((captions, 128), F32),
            ((captions, all_pairs), F32),
            ((captions, all_pairs), F32),
            ((captions, 128), F32),
            ((1, all_pairs), F32),
            ((8, 128), F32),
        ),
        index=(place, core),
        small=(matched_picture_ids, sharpening_log),
    )
    after = (unit,)
    for step in steps[2:] + [None]:
        rows = sums_parts[0].shape[0]
        joined_sums, mark = move(
            sums_parts,
            (4 * rows,),
            [(place, 0, rows, 0, place * rows) for place in range(4)],
            after,
            mark=True,
        )
        after = (mark,)
        if step is not None:
            sums_parts = dp_parts(joined_sums, step)
    sums_high = dp_swap(joined_sums, 2 * Z_STRIDE)
    sums_parts = [joined_sums, dp_swap(joined_sums, Z_STRIDE), sums_high]
    sums_parts.append(dp_swap(sums_high, Z_STRIDE))
    col_parts = dp_parts(col_sum, steps[0])
    for step in steps[1:]:
        (col_sum,) = call(sum_kernel, col_parts, ((col_sum.shape, F32),), after=after)
        col_parts = dp_parts(col_sum, step)
    grad_caption, grad_caption_low, grad_pre, part, loss_stat = call(
        loss_grad_kernel,
        (
            *col_parts,
            logits,
            powers,
            row_sum,
            unit,
            factor,
            images,
            sentence_word_ids,
            row_loss,
        ),
        (
            (short, F32),
            (short, BF16),
            ((tokens, hidden), BF16),
            (full, F32),
            ((8, model_width), F32),
        ),
        outside=(narrowing_matrix, slope, widening_matrix),
        small=(matched_picture_ids, sharpening_log),
    )

    other = mp_other(part)
    *widen_dealt, mark = call(
        widen_grad_kernel,
        (normed2, grad_pre),
        dealt,
        scratch=(pltpu.VMEM(square, BF16),) * 2,
        index=(place,),
        mark=True,
    )
    grad_residual, grad_branch1, flat, part, mixer_stat = call(
        mixer_back_kernel,
        (
            part,
            other,
            residual,
            grad_caption,
            sentence_word_ids,
            perceptron_layernorm_gamma,
            mixer_result_matrix,
        ),
        (
            (full, F32),
            (full, BF16),
            ((3, tokens, local_width), BF16),
            (full, F32),
            ((8, model_width), F32),
        ),
        outside=(qkv, soft, mixer_triple_matrix),
        after=(mark,),
    )
    other = mp_other(part)
    extra = []
    widen_sum = scatter_steps(widen_dealt, place, extra)
    next(widen_sum)
    *mixer_dealt, mark = call(
        mixer_grad_kernel,
        (normed, flat, mixed, grad_branch1),
        dealt,
        scratch=(pltpu.VMEM(square, BF16),) * 2,
        index=(place,),
        after=sums_parts[1:3],
        mark=True,
    )
    mixer_sum = scatter_steps(mixer_dealt, place)
    next(mixer_sum)
    last = widen_sum.send((mark,))
    last = widen_sum.send((last,))
    extra_rows = captions // 2 + 16
    grad_input, mine = call(
        entry_grad_kernel,
        (
            part,
            other,
            sentence_layer_entry,
            mixer_layernorm_gamma,
            grad_residual,
            loss_stat,
            mixer_stat,
            grad_caption_low,
        ),
        ((full, F32), ((extra_rows, model_width), BF16)),
        scratch=(pltpu.VMEM((16, model_width), F32),),
        index=(core,),
        after=(last,),
    )
    extra.append(dp_gather(mine, steps[:1:-1], [mine] * len(steps)))
    last = mixer_sum.send((mine,))
    last = widen_sum.send((last,))
    last = mixer_sum.send((last,))
    last = widen_sum.send((last,))
    last = mixer_sum.send((last,))
    last = widen_sum.send((last,))
    last = mixer_sum.send((last,))
    widen_pieces = widen_sum.send(())
    near_grads, *results = call(
        functools.partial(collect_kernel, 1.0 / (2.0 * all_pairs), extra_rows),
        (*widen_pieces, loss_stat),
        (
            ((all_pairs // 2, model_width), BF16),
            ((1,), F32),
            ((2, local_width), F32),
            ((model_width,), F32),
            ((hidden,), F32),
        )
        + (((model_width,), F32),) * 5
        + (((1,), F32),),
        after=(last,),
    )
    error, grad_pair, grad_b_out, grad_b_up, grad_b_down = results[:5]
    grad_w_up, mark = call(
        unpack_widen_kernel,
        widen_pieces,
        ((widening_matrix.shape, F32),),
        index=(place,),
        after=(results[0],),
        limit=56,
        mark=True,
    )
    last = mixer_sum.send((mark,))
    grad_w_down, mark = call(
        functools.partial(narrow_grad_kernel, captions // 2),
        (*sums_parts, near_grads, mp_other(near_grads)),
        ((narrowing_matrix.shape, F32),),
        scratch=(pltpu.VMEM((all_pairs, model_width), BF16),),
        index=(core,),
        after=(last,),
        mark=True,
    )
    grad_qkv, grad_w_out = call(
        unpack_mixer_kernel,
        mixer_sum.send(()),
        ((mixer_triple_matrix.shape, F32), (mixer_result_matrix.shape, F32)),
        index=(place,),
        after=(mark,),
        limit=56,
    )
    return (
        error,
        grad_input,
        grad_qkv,
        grad_pair,
        grad_w_out,
        grad_b_out,
        grad_w_up,
        grad_b_up,
        grad_w_down,
        grad_b_down,
        *results[5:],
    )


def solution(mesh):
    placed = (
        P("dp", None),
        P("dp"),
        P(("dp", "mp"), None, None),
        P(("dp", "mp")),
        P("dp"),
        P(),
        P(),
        P(None, None, "mp"),
        P(None, "mp"),
        P("mp", None),
        P(),
        P(),
        P(),
        P(None, "mp"),
        P("mp"),
        P("mp", None),
        P(),
        P(),
        P(),
        P(),
        P(),
        P(),
        P(),
    )
    return jax.shard_map(
        local,
        mesh=mesh,
        in_specs=placed,
        out_specs=(
            P(),
            P("dp", None),
            P(None, None, "mp"),
            P(None, "mp"),
            P("mp", None),
            P(),
            P(None, "mp"),
            P("mp"),
            P("mp", None),
            P(),
            P(),
            P(),
            P(),
            P(),
            P(),
        ),
        check_vma=False,
    )
```

```python
import functools

import jax
import jax.numpy as jnp
from jax import lax
from jax.experimental import pallas as pl
from jax.experimental.pallas import tpu as pltpu
from jax.sharding import PartitionSpec as P

HEAD = 64
IMG_TOK = 145
LOW_TOK = 50
CAP_LEN = 16


EPS_TEXT = 1e-05
EPS_UNIT = 1e-06
MASKED_SCORE = -1e30
BF16 = jnp.bfloat16
F32 = jnp.float32


def mp_other(values):
    return lax.ppermute(values, "mp", [(0, 1), (1, 0)])


def dp_swap(values, mask):
    size = lax.axis_size("dp")
    return lax.ppermute(values, "dp", [(index, index ^ mask) for index in range(size)])


def group_steps(size):
    steps, stride = [], 1
    while stride < size:
        steps.append([stride, 2 * stride, 3 * stride])
        stride *= 4
    return steps


def gather_masks(steps):
    masks = [0]
    for step in steps:
        masks = [mask ^ base for mask in [0] + step for base in masks]
    return masks


def dp_parts(values, step):
    return [values] + [dp_swap(values, mask) for mask in step]


def dp_gather(values, steps, waits):
    for step, wait in zip(steps, waits):
        parts = dp_parts(values, step)
        rows = values.shape[0]
        (values,) = move(
            parts,
            (len(parts) * rows,),
            [(place, 0, rows, 0, place * rows) for place in range(len(parts))],
            (wait,),
        )
    return values


HIGH_ROWS = 160
LOW_ROWS = 64
TILE = 256
PAIR = 2 * HEAD
LANES = 128
POOL_ROWS = 32
NT = (((1,), (1,)), ((), ()))
VMEM_LIMIT = 60 * 1024 * 1024
BUSY = 10**12


def dot(left, right):
    return jnp.dot(left, right, preferred_element_type=F32)


def wide_dot(left, right):
    high = left.astype(BF16)
    rest = (left - high.astype(F32)).astype(BF16)
    return dot(high, right) + dot(rest, right)


def standard(values, epsilon):
    centered = values - jnp.mean(values, axis=-1, keepdims=True)
    variance = jnp.mean(centered * centered, axis=-1, keepdims=True)
    return centered * lax.rsqrt(variance + epsilon)


def gelu(values):
    return (0.5 * values) * (1.0 + lax.erf(values * (0.5**0.5)))


def image_kernel(
    flag_ref,
    token_ref,
    gain_ref,
    triple_hbm,
    result_hbm,
    widen_hbm,
    narrow_hbm,
    out_ref,
    wide,
    packed,
    mixed,
    queries,
    keys,
    values,
    triple,
    result,
    widen,
    narrow,
    resid_groups,
    hidden_groups,
    pooled,
    ready,
    starts,
    high_starts,
    low_starts,
    sems,
):
    _, images, width = token_ref.shape
    hidden = widen.shape[1]
    copies = fetch(
        (triple_hbm, result_hbm, widen_hbm, narrow_hbm), (triple, result, widen, narrow), sems
    )
    lane_tiles = [slice(lane, lane + LANES) for lane in range(0, width, LANES)]

    def spread(position, carry):
        rows = pl.ds(pl.multiple_of(position * images, images), images)
        for place, lanes in enumerate(lane_tiles):
            wide[place, rows, :] = token_ref[position, :, lanes].astype(F32)
        return carry

    def begin(image, carry):
        start, highs = carry
        starts[image] = start
        high = flag_ref[image] == 1

        @pl.when(high)
        def _():
            high_starts[highs] = start

        @pl.when(jnp.logical_not(high))
        def _():
            low_starts[image - highs] = start

        return start + jnp.where(high, HIGH_ROWS, LOW_ROWS), highs + jnp.where(high, 1, 0)

    total, highs = lax.fori_loop(0, images, begin, (jnp.int32(0), jnp.int32(0)))
    lax.fori_loop(0, LOW_ROWS, spread, 0, unroll=4)

    @pl.when(total > images * LOW_ROWS)
    def _():
        lax.fori_loop(LOW_ROWS, IMG_TOK, spread, 0, unroll=3)

    tail = IMG_TOK // 16 * 16

    def pack(image, carry):
        start = pl.multiple_of(starts[image], POOL_ROWS)
        high = flag_ref[image] == 1

        @pl.when(high)
        def _():
            row = lax.broadcasted_iota(jnp.int32, (HIGH_ROWS - tail, LANES), 0)
            for place, lanes in enumerate(lane_tiles):
                packed[pl.ds(start, tail), lanes] = wide[
                    place, pl.ds(image, tail, stride=images), :
                ].astype(BF16)
                last = wide[place, pl.ds(image + tail * images, 1), :]
                packed[pl.ds(start + tail, HIGH_ROWS - tail), lanes] = jnp.where(
                    row == 0, last, 0.0
                ).astype(BF16)

        @pl.when(jnp.logical_not(high))
        def _():
            for place, lanes in enumerate(lane_tiles):
                packed[pl.ds(start, LOW_ROWS), lanes] = wide[
                    place, pl.ds(image, LOW_ROWS, stride=images), :
                ].astype(BF16)

        return carry

    lax.fori_loop(0, images, pack, 0)
    packed[pl.ds(pl.multiple_of(total, POOL_ROWS), TILE), :] = jnp.zeros((TILE, width), BF16)
    tiles = lax.div(total + (TILE - 1), jnp.int32(TILE))

    copies[0].wait()

    def prepare(tile):
        rows = pl.ds(pl.multiple_of(tile * TILE, TILE), TILE)
        ready[tile % 2] = (
            standard(packed[rows, :].astype(F32), EPS_UNIT) * gain_ref[0:1, :]
        ).astype(BF16)

    def project(tile, carry):
        rows = pl.ds(pl.multiple_of(tile * TILE, TILE), TILE)
        normed = ready[tile % 2]
        queries[rows, :] = (dot(normed, triple[0]) * HEAD ** (-0.5)).astype(BF16)
        prepare(tile + 1)
        keys[rows, :] = dot(normed, triple[1]).astype(BF16)
        values[rows, :] = dot(normed, triple[2]).astype(BF16)
        return carry

    prepare(jnp.int32(0))
    lax.fori_loop(0, tiles, project, 0)

    def attend(begins, count, live):
        left = lax.broadcasted_iota(jnp.int32, (count, PAIR), 1) < HEAD
        key_live = lax.broadcasted_iota(jnp.int32, (2 * count, count), 1) < live
        places = [
            (pl.ds(pl.multiple_of(start, POOL_ROWS), count), slice(lane, lane + PAIR))
            for start in begins
            for lane in range(0, width, PAIR)
        ]
        all_scores = [dot_t(two_heads(queries[place], left), keys[place]) for place in places]
        all_powers = []
        for scores in all_scores:
            scores = jnp.where(key_live, scores, MASKED_SCORE)
            top = jnp.max(scores, axis=-1, keepdims=True)
            all_powers.append(jnp.exp(scores - top).astype(BF16))
        for place, powers in zip(places, all_powers):
            value = values[place]
            one = jnp.ones_like(value)
            first = dot(powers[:count], jnp.where(left, value, one))
            second = dot(powers[count:], jnp.where(left, one, value))
            sums = pltpu.roll(jnp.where(left, second, first), HEAD, 1)
            mixed[place] = (jnp.where(left, first, second) / sums).astype(BF16)

    def attend_all(begins, number, together, count, live):
        groups = lax.div(number, jnp.int32(together))

        def group(index, carry):
            attend([begins[index * together + step] for step in range(together)], count, live)
            return carry

        def rest(index, carry):
            attend([begins[index]], count, live)
            return carry

        lax.fori_loop(0, groups, group, 0)
        if together > 1:
            lax.fori_loop(groups * together, number, rest, 0)

    attend_all(high_starts, highs, 1, HIGH_ROWS, IMG_TOK)
    attend_all(low_starts, images - highs, 4, LOW_ROWS, LOW_TOK)

    slot = lax.broadcasted_iota(jnp.int32, (1, images), 1)
    first_row = jnp.zeros((1, images), jnp.int32)
    live_rows = jnp.zeros((1, images), jnp.int32)
    for image in range(images):
        first_row = jnp.where(slot == image, starts[image], first_row)
        live_rows = jnp.where(
            slot == image, jnp.where(flag_ref[image] == 1, IMG_TOK, LOW_TOK), live_rows
        )
    copies[1].wait()
    copies[2].wait()
    groups = TILE // POOL_ROWS

    def group_sum(rows):
        return jnp.sum(rows.reshape(groups, POOL_ROWS // 8, 8, rows.shape[1]), axis=1)

    def resume(tile):
        base = pl.multiple_of(tile * TILE, TILE)
        rows = pl.ds(base, TILE)
        place = base + lax.broadcasted_iota(jnp.int32, (TILE, images), 0)
        alive = jnp.sum(
            jnp.where((place >= first_row) & (place < first_row + live_rows), 1.0, 0.0),
            axis=1,
            keepdims=True,
        )
        residual = (packed[rows, :].astype(F32) + dot(mixed[rows, :], result[...])) * alive
        group = pl.ds(pl.multiple_of(tile * groups, groups), groups)
        resid_groups[group] = group_sum(residual)
        ready[tile % 2] = (standard(residual, EPS_UNIT) * gain_ref[1:2, :]).astype(BF16)

    def perceptron(tile, carry):
        group = pl.ds(pl.multiple_of(tile * groups, groups), groups)
        normed = ready[tile % 2]
        for chunk in range(hidden // width):
            if chunk == 1:
                resume(tile + 1)
            lanes = slice(chunk * width, (chunk + 1) * width)
            units = gelu(dot(normed, widen[:, lanes])).astype(BF16)
            hidden_groups[group, :, lanes] = group_sum(units.astype(F32))
        return carry

    resume(jnp.int32(0))
    lax.fori_loop(0, tiles, perceptron, 0)

    def pool(image, carry):
        group = lax.div(starts[image], jnp.int32(POOL_ROWS))
        high = flag_ref[image] == 1

        def add(count):
            residual, units = resid_groups[group], hidden_groups[group]
            for step in range(1, count):
                residual = residual + resid_groups[group + step]
                units = units + hidden_groups[group + step]
            pooled[pl.ds(image, 1), :width] = jnp.sum(residual, axis=0, keepdims=True)
            pooled[pl.ds(image, 1), width:] = jnp.sum(units, axis=0, keepdims=True)

        @pl.when(high)
        def _():
            add(HIGH_ROWS // POOL_ROWS)

        @pl.when(jnp.logical_not(high))
        def _():
            add(LOW_ROWS // POOL_ROWS)

        return carry

    lax.fori_loop(0, images, pool, 0)
    copies[3].wait()
    units = pooled[:, width:]
    upper = units.astype(BF16)
    lower = (units - upper.astype(F32)).astype(BF16)
    branch = dot(jnp.concatenate([upper, lower], axis=0), narrow[...])
    live = jnp.where(number_column(flag_ref) == 1, IMG_TOK, LOW_TOK).astype(F32)
    mean = (pooled[:, :width] + branch[:images] + branch[images:]) / live
    out_ref[...] = (
        mean * lax.rsqrt(jnp.sum(mean * mean, axis=-1, keepdims=True) + EPS_UNIT)
    ).astype(BF16)


def image_tower(flags, tokens, gains, triple, result, widen, narrow):
    images, _, width = tokens.shape
    hidden = widen.shape[1]
    rows = images * HIGH_ROWS + TILE
    groups = rows // POOL_ROWS
    outside = pl.BlockSpec(memory_space=pl.ANY)
    inside = pl.BlockSpec(memory_space=pltpu.VMEM)
    return pl.pallas_call(
        image_kernel,
        out_shape=jax.ShapeDtypeStruct((images, width), BF16),
        in_specs=[pl.BlockSpec(memory_space=pltpu.SMEM), inside, inside]
        + [outside] * 4,
        out_specs=inside,
        scratch_shapes=[pltpu.VMEM((width // LANES, IMG_TOK * images, LANES), F32)]
        + [pltpu.VMEM((rows, width), BF16)] * 5
        + [pltpu.VMEM(weight.shape, BF16) for weight in (triple, result, widen, narrow)]
        + [
            pltpu.VMEM((groups, 8, width), F32),
            pltpu.VMEM((groups, 8, hidden), F32),
            pltpu.VMEM((images, width + hidden), F32),
            pltpu.VMEM((2, TILE, width), BF16),
            pltpu.SMEM((images,), jnp.int32),
            pltpu.SMEM((images,), jnp.int32),
            pltpu.SMEM((images,), jnp.int32),
            pltpu.SemaphoreType.DMA((4,)),
        ],
        compiler_params=pltpu.CompilerParams(vmem_limit_bytes=VMEM_LIMIT),
        cost_estimate=pl.CostEstimate(flops=BUSY, bytes_accessed=BUSY, transcendentals=0),
    )(flags, jnp.transpose(tokens, (1, 0, 2)), gains, triple, result, widen, narrow)


TN = (((0,), (0,)), ((), ()))
BLOCK = 128
ROOT_HALF = 0.5**0.5
DENSITY = 0.3989422804014327


def dot_t(left, right):
    return lax.dot_general(left, right, NT, preferred_element_type=F32)


def t_dot(left, right):
    return lax.dot_general(left, right, TN, preferred_element_type=F32)


def fetch(sources, targets, sems):
    copies = [
        pltpu.make_async_copy(source, target, sems.at[place])
        for place, (source, target) in enumerate(zip(sources, targets))
    ]
    for copy in copies:
        copy.start()
    return copies


def caption_pool(ids_ref, captions):
    ids_row = ids_ref[...].reshape(1, -1)
    tokens = ids_row.shape[1]
    shape = (captions, tokens)
    caption = lax.broadcasted_iota(jnp.int32, shape, 0)
    token = lax.broadcasted_iota(jnp.int32, shape, 1)
    inside = (token // (tokens // captions)) == caption
    return jnp.where(inside & (ids_row != 0), 1.0, 0.0)


def valid_column(pool):
    pool = pool.astype(BF16)
    return t_dot(pool, jnp.ones((pool.shape[0], 128), BF16))[:, 0:1]


def number_column(ref):
    shape = (ref.shape[0], 1)
    place = lax.broadcasted_iota(jnp.int32, shape, 0)
    column = jnp.zeros(shape, jnp.int32)
    for index in range(shape[0]):
        column = jnp.where(place == index, ref[index], column)
    return column


def as_row(ref):
    return ref[...].reshape(1, -1)


def pair_masks(rows, pair_width):
    return lax.broadcasted_iota(jnp.int32, (rows, pair_width), 1) < HEAD


def two_heads(values, left):
    zero = jnp.zeros_like(values)
    return jnp.concatenate(
        [jnp.where(left, values, zero), jnp.where(left, zero, values)], axis=0
    )


def text_mix_kernel(
    entry_ref,
    ids_ref,
    gain_ref,
    shift_ref,
    triple_ref,
    pair_ref,
    result_ref,
    normed_ref,
    qkv_ref,
    soft_ref,
    mixed_ref,
    part_ref,
):
    tokens = entry_ref.shape[0]
    width = result_ref.shape[0]
    normed = (
        standard(entry_ref[...].astype(F32), EPS_TEXT) * as_row(gain_ref) + as_row(shift_ref)
    ).astype(BF16)
    normed_ref[...] = normed
    qkv_ref[0] = (dot(normed, triple_ref[0]) + pair_ref[0:1, :]).astype(BF16)
    qkv_ref[1] = dot(normed, triple_ref[1]).astype(BF16)
    qkv_ref[2] = (dot(normed, triple_ref[2]) + pair_ref[1:2, :]).astype(BF16)
    ids = as_row(ids_ref)
    left = pair_masks(BLOCK, PAIR)
    shape = (2 * BLOCK, BLOCK)
    query_caption = lax.broadcasted_iota(jnp.int32, shape, 0) % BLOCK // CAP_LEN
    same = query_caption == lax.broadcasted_iota(jnp.int32, shape, 1) // CAP_LEN
    for block in range(tokens // BLOCK):
        rows = slice(block * BLOCK, (block + 1) * BLOCK)
        seen = same & (ids[:, rows] != 0)
        for pair in range(width // PAIR):
            lanes = slice(pair * PAIR, (pair + 1) * PAIR)
            scores = dot_t(two_heads(qkv_ref[0, rows, lanes], left), qkv_ref[1, rows, lanes])
            scores = jnp.where(seen, scores * HEAD ** (-0.5), MASKED_SCORE)
            powers = jnp.exp(scores - jnp.max(scores, axis=-1, keepdims=True))
            soft = powers / jnp.sum(powers, axis=-1, keepdims=True)
            soft_ref[block, pair] = soft
            low = soft.astype(BF16)
            value = qkv_ref[2, rows, lanes]
            mixed_ref[rows, lanes] = jnp.where(
                left, dot(low[:BLOCK], value), dot(low[BLOCK:], value)
            ).astype(BF16)
    part_ref[...] = dot(mixed_ref[...], result_ref[...])


def text_widen_kernel(
    entry_ref,
    own_ref,
    other_ref,
    result_offset_ref,
    gain_ref,
    shift_ref,
    widen_offset_ref,
    ids_ref,
    widen_hbm,
    narrow_hbm,
    residual_ref,
    normed_ref,
    slope_ref,
    sums_ref,
    resid_sum_ref,
    branch_ref,
    widen,
    narrow,
    hidden_sum,
    sems,
):
    captions = sums_ref.shape[0]
    width = entry_ref.shape[1]
    copies = fetch((widen_hbm, narrow_hbm), (widen, narrow), sems)
    residual = entry_ref[...].astype(F32) + (
        (own_ref[...] + other_ref[...]) + as_row(result_offset_ref)
    )
    residual_ref[...] = residual
    normed = (standard(residual, EPS_TEXT) * as_row(gain_ref) + as_row(shift_ref)).astype(BF16)
    normed_ref[...] = normed
    pool = caption_pool(ids_ref, captions).astype(BF16)
    widen_offset = as_row(widen_offset_ref)
    upper = residual.astype(BF16)
    resid_sum_ref[...] = dot(pool, upper) + dot(
        pool, (residual - upper.astype(F32)).astype(BF16)
    )
    valid = valid_column(pool)
    copies[0].wait()
    for chunk in range(widen.shape[1] // width):
        lanes = slice(chunk * width, (chunk + 1) * width)
        before = dot(normed, widen[:, lanes]) + widen_offset[:, lanes]
        share = 0.5 * (1.0 + lax.erf(before * ROOT_HALF))
        hidden_sum[:, lanes] = dot(pool, (before * share).astype(BF16))
        slope = share + before * (jnp.exp(-0.5 * before * before) * DENSITY)
        slope_ref[:, lanes] = slope * valid
    sums_ref[...] = hidden_sum[...].astype(BF16)
    copies[1].wait()
    branch_ref[...] = wide_dot(hidden_sum[...], narrow[...])


def logits_kernel(
    masks,
    index_ref,
    matched_ref,
    sharpen_ref,
    near_ref,
    far_ref,
    resid_sum_ref,
    own_ref,
    other_ref,
    narrow_offset_ref,
    ids_ref,
    images_ref,
    unit_ref,
    factor_ref,
    logits_ref,
    powers_ref,
    row_sum_ref,
    col_sum_ref,
    loss_ref,
):
    captions, pairs = logits_ref.shape
    rows = images_ref.shape[0] // (2 * len(masks))
    core = index_ref[1]
    for place, mask in enumerate(masks):
        start = (index_ref[0] ^ mask) * (2 * rows)
        images_ref[pl.ds(pl.multiple_of(start + core * rows, rows), rows), :] = near_ref[
            place * rows : (place + 1) * rows, :
        ]
        images_ref[pl.ds(pl.multiple_of(start + (1 - core) * rows, rows), rows), :] = far_ref[
            place * rows : (place + 1) * rows, :
        ]
    count = jnp.sum(caption_pool(ids_ref, captions), axis=1, keepdims=True)
    pooled = (resid_sum_ref[...] + (own_ref[...] + other_ref[...])) / count + as_row(
        narrow_offset_ref
    )
    inverse = lax.rsqrt(jnp.sum(pooled * pooled, axis=-1, keepdims=True) + EPS_UNIT)
    unit = pooled * inverse
    unit_ref[...] = unit
    factor_ref[...] = jnp.broadcast_to(inverse / count, factor_ref.shape)
    logits = jnp.exp(jnp.full((1, 1), sharpen_ref[0], F32)) * dot_t(unit.astype(BF16), images_ref[...])
    logits_ref[...] = logits
    powers = jnp.exp(logits)
    powers_ref[...] = powers
    row_sum = jnp.sum(powers, axis=1, keepdims=True)
    row_sum_ref[...] = jnp.broadcast_to(row_sum, row_sum_ref.shape)
    col_sum_ref[...] = jnp.sum(powers, axis=0, keepdims=True)
    positive = number_column(matched_ref) == lax.broadcasted_iota(jnp.int32, (captions, pairs), 1)
    wanted = jnp.sum(jnp.where(positive, logits, 0.0), axis=1, keepdims=True)
    loss_ref[...] = jnp.broadcast_to(
        jnp.sum(jnp.log(row_sum) - 2.0 * wanted, axis=0, keepdims=True), loss_ref.shape
    )


def sum_kernel(first_ref, second_ref, third_ref, fourth_ref, out_ref):
    out_ref[...] = (first_ref[...] + second_ref[...]) + (third_ref[...] + fourth_ref[...])


def loss_grad_kernel(
    matched_ref,
    sharpen_ref,
    col_ref,
    col1_ref,
    col2_ref,
    col3_ref,
    logits_ref,
    powers_ref,
    row_sum_ref,
    unit_ref,
    factor_ref,
    images_ref,
    ids_ref,
    loss_ref,
    narrow_hbm,
    slope_hbm,
    widen_hbm,
    grad_ref,
    low_ref,
    before_ref,
    part_ref,
    stat_ref,
    narrow,
    slope,
    widen,
    sems,
):
    captions, pairs = logits_ref.shape
    tokens, hidden = slope.shape
    width = grad_ref.shape[1]
    copies = fetch((narrow_hbm, slope_hbm, widen_hbm), (narrow, slope, widen), sems)
    logits, powers = logits_ref[...], powers_ref[...]
    col_sum = (col_ref[...] + col1_ref[...]) + (col2_ref[...] + col3_ref[...])
    positive = number_column(matched_ref) == lax.broadcasted_iota(jnp.int32, (captions, pairs), 1)
    derivative = (
        powers / row_sum_ref[:, 0:1] + powers / col_sum - jnp.where(positive, 2.0, 0.0)
    ) / (2.0 * pairs)
    temperature = jnp.sum(
        jnp.sum(derivative * logits, axis=1, keepdims=True), axis=0, keepdims=True
    )
    col_loss = jnp.sum(jnp.log(col_sum), axis=1, keepdims=True)
    text = dot((derivative * jnp.exp(jnp.full((1, 1), sharpen_ref[0], F32))).astype(BF16), images_ref[...])
    unit = unit_ref[...]
    grad = (text - unit * jnp.sum(unit * text, axis=-1, keepdims=True)) * factor_ref[:, 0:1]
    grad_ref[...] = grad
    low = grad.astype(BF16)
    low_ref[...] = low
    copies[0].wait()
    copies[1].wait()
    copies[2].wait()
    ones = jnp.ones((8, tokens), BF16)
    part = jnp.zeros(part_ref.shape, F32)
    for chunk in range(hidden // width):
        lanes = slice(chunk * width, (chunk + 1) * width)
        back = dot_t(low, narrow[lanes, :])
        before = (
            (back[:, None, :] * slope[:, lanes].reshape(captions, CAP_LEN, width))
            .reshape(tokens, width)
            .astype(BF16)
        )
        before_ref[:, lanes] = before
        stat_ref[chunk : chunk + 1, :] = dot(ones, before)[0:1]
        part = part + dot_t(before, widen[:, lanes])
    part_ref[...] = part
    count = jnp.sum(caption_pool(ids_ref, captions), axis=1, keepdims=True)
    stat_ref[2:3, :] = jnp.sum(low.astype(F32) * count, axis=0, keepdims=True)
    lane = lax.broadcasted_iota(jnp.int32, (1, width), 1)
    stat_ref[3:4, :] = jnp.where(
        lane == 0,
        temperature,
        jnp.where(lane == 1, loss_ref[0:1, 0:1], jnp.where(lane == 2, col_loss, 0.0)),
    )
    stat_ref[4:8, :] = jnp.zeros((4, width), F32)


def deal(index_ref, first, second, outs):
    half = first.shape[0] // 2
    for place, (values, bit) in enumerate(((first, 1), (second, 2))):
        mine = index_ref[0] // bit % 2
        for ref, which in ((outs[2 * place], 1 - mine), (outs[2 * place + 1], mine)):
            ref[...] = values[pl.ds(pl.multiple_of(which * half, half), half), :]


def widen_grad_kernel(index_ref, normed_ref, before_ref, *refs):
    outs, (first, second) = refs[:4], refs[4:]
    width = first.shape[1]
    normed = normed_ref[...]
    first[...] = t_dot(normed, before_ref[:, :width]).astype(BF16)
    second[...] = t_dot(normed, before_ref[:, width:]).astype(BF16)
    deal(index_ref, first, second, outs)


def mixer_back_kernel(
    own_ref,
    other_ref,
    residual_ref,
    grad_ref,
    ids_ref,
    gain_ref,
    result_ref,
    qkv_hbm,
    soft_hbm,
    triple_hbm,
    grad_residual_ref,
    low_ref,
    flat_ref,
    part_ref,
    stat_ref,
    qkv,
    soft_all,
    triple,
    sems,
):
    tokens, width = residual_ref.shape
    captions = grad_ref.shape[0]
    local_width = result_ref.shape[0]
    copies = fetch((qkv_hbm, soft_hbm, triple_hbm), (qkv, soft_all, triple), sems)
    residual = residual_ref[...]
    centered = residual - jnp.mean(residual, axis=-1, keepdims=True)
    rate = lax.rsqrt(jnp.mean(centered * centered, axis=-1, keepdims=True) + EPS_TEXT)
    unit = centered * rate
    grad = own_ref[...] + other_ref[...]
    stat_ref[1:2, :] = jnp.sum(grad * unit, axis=0, keepdims=True)
    stat_ref[2:3, :] = jnp.sum(grad, axis=0, keepdims=True)
    scaled = grad * as_row(gain_ref)
    inner = rate * (
        scaled
        - jnp.mean(scaled, axis=-1, keepdims=True)
        - unit * jnp.mean(scaled * unit, axis=-1, keepdims=True)
    )
    spread = jnp.broadcast_to(
        grad_ref[...][:, None, :], (captions, tokens // captions, width)
    ).reshape(tokens, width)
    grad_residual = spread * valid_column(caption_pool(ids_ref, captions)) + inner
    grad_residual_ref[...] = grad_residual
    low = grad_residual.astype(BF16)
    low_ref[...] = low
    ones = jnp.ones((8, tokens), BF16)
    stat_ref[0:1, :] = dot(ones, low)[0:1]
    grad_mixed = dot_t(low, result_ref[...]).astype(BF16)
    for copy in copies:
        copy.wait()
    left = pair_masks(BLOCK, PAIR)
    places = [
        (block, pair, slice(block * BLOCK, (block + 1) * BLOCK), slice(pair * PAIR, (pair + 1) * PAIR))
        for block in range(tokens // BLOCK)
        for pair in range(local_width // PAIR)
    ]
    mixed = [two_heads(grad_mixed[rows, lanes], left) for _, _, rows, lanes in places]
    softs = [soft_all[block, pair] for block, pair, _, _ in places]
    grads = [
        dot_t(value, qkv[2, rows, lanes]) for value, (_, _, rows, lanes) in zip(mixed, places)
    ]
    scores = [
        (soft * (grad - jnp.sum(grad * soft, axis=-1, keepdims=True))).astype(BF16)
        for soft, grad in zip(softs, grads)
    ]
    for value, soft, (_, _, rows, lanes) in zip(mixed, softs, places):
        flat_ref[2, rows, lanes] = t_dot(soft.astype(BF16), value).astype(BF16)
    for score, (_, _, rows, lanes) in zip(scores, places):
        key = qkv[1, rows, lanes]
        back = jnp.where(left, dot(score[:BLOCK], key), dot(score[BLOCK:], key))
        flat_ref[0, rows, lanes] = (back * HEAD ** (-0.5)).astype(BF16)
    for score, (_, _, rows, lanes) in zip(scores, places):
        flat_ref[1, rows, lanes] = (
            t_dot(score, two_heads(qkv[0, rows, lanes], left)) * HEAD ** (-0.5)
        ).astype(BF16)
    part_ref[...] = (
        dot_t(flat_ref[0], triple[0])
        + dot_t(flat_ref[1], triple[1])
        + dot_t(flat_ref[2], triple[2])
    )
    stat_ref[3:4, :local_width] = dot(ones, flat_ref[0])[0:1]
    stat_ref[3:4, local_width:] = dot(ones, flat_ref[2])[0:1]
    stat_ref[4:8, :] = jnp.zeros((4, width), F32)


def mixer_grad_kernel(index_ref, normed_ref, flat_ref, mixed_ref, low_ref, *refs):
    outs, (first, second) = refs[:4], refs[4:]
    half = flat_ref.shape[2]
    rows = first.shape[0] // 2
    normed = normed_ref[...]
    for part, (target, place) in enumerate(((first, 0), (first, rows), (second, 0))):
        grad = t_dot(normed, flat_ref[part]).astype(BF16)
        target[place : place + rows, :half] = grad[:rows]
        target[place : place + rows, half:] = grad[rows:]
    second[rows:, :] = t_dot(mixed_ref[...], low_ref[...]).astype(BF16)
    deal(index_ref, first, second, outs)


def narrow_grad_kernel(half, index_ref, *refs):
    parts, (near_ref, far_ref, out_ref, grads) = refs[:-4], refs[-4:]
    rows, width = parts[0].shape[0], grads.shape[1]
    devices = near_ref.shape[0] // half
    for place in range(devices):
        plane, group, high = place % 4, place // 4 % (devices // GROUP), place * 4 // devices
        source = (plane * Z_SIZE + high) * (devices // GROUP) + group
        for ref, which in ((near_ref, index_ref[0]), (far_ref, 1 - index_ref[0])):
            start = pl.multiple_of((2 * place + which) * half, half)
            grads[pl.ds(start, half), :] = ref[source * half : (source + 1) * half, :]
    for chunk in range(out_ref.shape[0] // width):
        lanes = slice(chunk * width, (chunk + 1) * width)
        total = t_dot(parts[0][:, lanes], grads[:rows, :])
        for place in range(1, len(parts)):
            total = total + t_dot(
                parts[place][:, lanes], grads[place * rows : (place + 1) * rows, :]
            )
        out_ref[lanes, :] = total


def entry_grad_kernel(
    index_ref,
    own_ref,
    other_ref,
    entry_ref,
    gain_ref,
    grad_residual_ref,
    loss_stat_ref,
    mixer_stat_ref,
    caption_ref,
    out_ref,
    extra_ref,
    pack,
):
    entry = entry_ref[...].astype(F32)
    centered = entry - jnp.mean(entry, axis=-1, keepdims=True)
    rate = lax.rsqrt(jnp.mean(centered * centered, axis=-1, keepdims=True) + EPS_TEXT)
    unit = centered * rate
    grad = own_ref[...] + other_ref[...]
    pack[0:8, :] = loss_stat_ref[...]
    pack[8:16, :] = mixer_stat_ref[...]
    pack[4:5, :] = jnp.sum(grad * unit, axis=0, keepdims=True)
    pack[5:6, :] = jnp.sum(grad, axis=0, keepdims=True)
    half = caption_ref.shape[0] // 2
    extra_ref[:half, :] = caption_ref[
        pl.ds(pl.multiple_of(index_ref[0] * half, half), half), :
    ]
    upper = pack[...].astype(BF16).astype(F32)
    pack[15:16, :] = (pack[...] - upper)[3:4, :]
    extra_ref[half:, :] = pack[...].astype(BF16)
    scaled = grad * as_row(gain_ref)
    out_ref[...] = grad_residual_ref[...] + rate * (
        scaled
        - jnp.mean(scaled, axis=-1, keepdims=True)
        - unit * jnp.mean(scaled * unit, axis=-1, keepdims=True)
    )


def tree_sum(values):
    while len(values) > 1:
        values = [values[place] + values[place + 1] for place in range(0, len(values), 2)]
    return values[0]


def collect_kernel(scale, rows, *refs):
    gathered, loss_ref, near_ref = refs[:8], refs[8], refs[9]
    (
        error_ref,
        pair_ref,
        result_ref,
        widen_ref,
        narrow_ref,
        gain1_ref,
        shift1_ref,
        gain2_ref,
        shift2_ref,
        temperature_ref,
    ) = refs[10:]
    half = rows - 16
    size = gathered[7].shape[0] // Z_SIZE
    more = gathered[1].shape[0] - 2 * size
    totals = []
    for piece in range(4):
        for step in range(Z_SIZE):
            if piece == 3:
                ref, first = gathered[6], Z_SIZE * size + step * more
            elif step < Z_SIZE - 1:
                ref, first = gathered[2 * piece], 3 * size + step * more
            else:
                ref, first = gathered[2 * piece + 1], 2 * size
            for row in range(first, first + more, rows):
                place = len(totals)
                near_ref[place * half : (place + 1) * half, :] = ref[row : row + half, :]
                totals.append(ref[row + half : row + rows, :].astype(F32))
    total = tree_sum(totals)
    scalars = total[3:4] + total[15:16]
    error_ref[...] = ((scalars[:, 1:2] + loss_ref[3:4, 2:3]) * scale).reshape(1)
    temperature_ref[...] = scalars[:, 0:1].reshape(1)
    lanes = pair_ref.shape[1]
    pair_ref[0:1, :] = total[11:12, :lanes]
    pair_ref[1:2, :] = total[11:12, lanes:]
    width = total.shape[1]
    for chunk in range(widen_ref.shape[0] // width):
        widen_ref[chunk * width : (chunk + 1) * width] = total[chunk]
    for ref, place in (
        (narrow_ref, 2),
        (gain1_ref, 4),
        (shift1_ref, 5),
        (result_ref, 8),
        (gain2_ref, 9),
        (shift2_ref, 10),
    ):
        ref[...] = total[place]


def call(kernel, inside, shapes, outside=(), scratch=(), index=(), small=(), after=(), limit=24, mark=False, busy=BUSY):
    vmem = pl.BlockSpec(memory_space=pltpu.VMEM)
    extra = [pltpu.VMEM(array.shape, array.dtype) for array in outside]
    extra += list(scratch)
    if outside:
        extra += [pltpu.SemaphoreType.DMA((len(outside),))]
    index = [jnp.stack(index).astype(jnp.int32)] if index else []
    small = index + list(small)
    before = len(small) + len(inside) + len(outside)

    if mark:
        shapes = tuple(shapes) + (((8, 128), F32),)

    def body(*refs):
        refs = refs[:before] + refs[before + len(after) :]
        if mark:
            last = before + len(shapes) - 1
            refs[last][...] = jnp.zeros((8, 128), F32)
            refs = refs[:last] + refs[last + 1 :]
        kernel(*refs)

    return pl.pallas_call(
        body,
        out_shape=[jax.ShapeDtypeStruct(shape, kind) for shape, kind in shapes],
        in_specs=[pl.BlockSpec(memory_space=pltpu.SMEM)] * len(small)
        + [vmem] * len(inside)
        + [pl.BlockSpec(memory_space=pl.ANY)] * (len(outside) + len(after)),
        out_specs=[vmem] * len(shapes),
        scratch_shapes=extra,
        compiler_params=pltpu.CompilerParams(vmem_limit_bytes=limit * 1024 * 1024),
        cost_estimate=pl.CostEstimate(flops=busy, bytes_accessed=busy, transcendentals=0),
    )(*small, *inside, *outside, *after)


def move(arrays, sizes, plan, after=(), mark=False, busy=BUSY):
    width, kind = arrays[0].shape[1], arrays[0].dtype

    def body(*refs):
        ins, outs = refs[: len(arrays)], refs[len(arrays) :]
        for source, first, rows, target, start in plan:
            outs[target][start : start + rows, :] = ins[source][first : first + rows, :]

    return call(body, arrays, tuple(((size, width), kind) for size in sizes), after=after, mark=mark, busy=busy)


GROUP = 16
Z_STRIDE, Z_SIZE = 4, 4


def block_rows(block, rows):
    return pl.ds(pl.multiple_of(block * rows, rows), rows)


def fold_kernel(index_ref, *refs):
    ins, outs = refs[:4], refs[4:]
    half = outs[0].shape[0]
    for place, bit in ((0, 2), (1, 1)):
        mine = index_ref[0] // bit % 2
        for out, which in ((outs[2 * place], 1 - mine), (outs[2 * place + 1], mine)):
            rows = block_rows(which, half)
            out[...] = (
                ins[2 * place][rows, :].astype(F32) + ins[2 * place + 1][rows, :].astype(F32)
            ).astype(out.dtype)


def cut_kernel(index_ref, *refs):
    ins, outs = refs[:4], refs[4:]
    rows = ins[0].shape[0] // Z_SIZE
    for place in range(2):
        for step, out in enumerate(outs):
            block = block_rows((index_ref[0] // Z_STRIDE % Z_SIZE) ^ step, rows)
            out[place * rows : (place + 1) * rows, :] = (
                ins[2 * place][block, :] + ins[2 * place + 1][block, :].astype(F32)
            ).astype(out.dtype)


def add_kernel(own_ref, *refs):
    out_ref = refs[-1]
    rows = own_ref.shape[0]
    total = own_ref[...]
    for ref in refs[: Z_SIZE - 1]:
        total = total + ref[...].astype(F32)
    out_ref[:rows, :] = total.astype(out_ref.dtype)
    if out_ref.shape[0] > rows:
        out_ref[rows:, :] = refs[Z_SIZE - 1][...]


def scatter_steps(dealt, place, extra=None):
    first_sent, first_kept, second_sent, second_kept = dealt
    rows, width = first_sent.shape
    after = yield
    arrived = (dp_swap(first_sent, 1), dp_swap(second_sent, 2))
    half = (rows // 2, width)
    first_sent, first_kept, second_sent, second_kept, mark = call(
        fold_kernel,
        (first_kept, arrived[0], second_kept, arrived[1]),
        ((half, BF16), (half, F32), (half, BF16), (half, F32)),
        index=(place,),
        after=after,
        mark=True, busy=1,
    )
    after = yield mark
    arrived = (dp_swap(first_sent, 2), dp_swap(second_sent, 1))
    block = (rows // Z_SIZE, width)
    own, *sent, mark = call(
        cut_kernel,
        (first_kept, arrived[0], second_kept, arrived[1]),
        ((block, F32),) + ((block, BF16),) * (Z_SIZE - 1),
        index=(place,),
        after=after,
        mark=True, busy=1,
    )
    after = yield mark
    arrived = [dp_swap(values, step * Z_STRIDE) for step, values in enumerate(sent, 1)]
    size = lax.axis_size("dp")
    more = 0 if extra is None else extra[0].shape[0]
    if size > GROUP:
        mine, mark = call(
            add_kernel, (own, *arrived), ((own.shape, F32),), after=after, mark=True, busy=1
        )
        groups = [list(range(index, size, GROUP)) for index in range(GROUP)]
        mine = lax.psum(mine, "dp", axis_index_groups=groups).astype(BF16)
        if more:
            mine = jnp.concatenate([mine, *extra], axis=0)
    else:
        mine, mark = call(
            add_kernel,
            (own, *arrived) + (tuple(extra) if more else ()),
            (((block[0] + more, width), BF16),),
            after=after,
            mark=True, busy=1,
        )
    after = yield mark
    high = dp_swap(mine, 2 * Z_STRIDE)
    early = (mine, dp_swap(mine, Z_STRIDE), high)
    late = dp_swap(high, Z_STRIDE)
    half = block[0] // 2
    plan, start = [], 0
    for first, count in ((0, half), (2 * half, more), (half, half)):
        for piece in range(len(early)):
            if count:
                plan.append((piece, first, count, 0, start))
            start += count
    joined, mark = move(early, (start,), plan, after, mark=True, busy=1)
    along_x, along_y = dp_swap(joined, 1), dp_swap(joined, 2)
    late_x, late_y = dp_swap(late, 1), dp_swap(late, 2)
    after = yield mark
    plan = [
        (0, 0, 3 * half, 0, 0),
        (1, 0, half, 0, 3 * half),
        (2, 3 * (half + more), 3 * half, 1, 0),
        (3, half, half, 1, 3 * half),
    ]
    if more:
        plan += [
            (0, 3 * half, 3 * more, 0, 4 * half),
            (1, 2 * half, more, 0, 4 * half + 3 * more),
        ]
    first, second, mark = move(
        (along_y, late_y, along_x, late_x),
        (4 * (half + more), 4 * half),
        plan,
        after,
        mark=True,
        busy=1,
    )
    after = yield mark
    far = (dp_swap(first, 1), dp_swap(second, 2))
    yield (joined, late, along_x, late_x, along_y, late_y, *far)


def block_home(index, block, outer, inner):
    high = (block // 8) ^ (index // outer % 2)
    middle = (block // 4 % 2) ^ (index // inner % 2)
    return high * 8 + middle * 4 + ((block % 4) ^ (index // Z_STRIDE % Z_SIZE))


def relative_blocks(refs, tensor):
    rows = refs[7].shape[0] // Z_SIZE
    more = refs[1].shape[0] - 2 * rows
    for piece, early in enumerate((0, 2, 4) if tensor else (0, 4, 2)):
        for step in range(Z_SIZE):
            if step < Z_SIZE - 1:
                ref, first = refs[early], tensor * 3 * (rows + more) + step * rows
            else:
                ref, first = refs[early + 1], tensor * rows
            yield piece * Z_SIZE + step, rows, ref[first : first + rows, :]
    for step in range(Z_SIZE):
        values = refs[6 + tensor][step * rows : (step + 1) * rows, :]
        yield 3 * Z_SIZE + step, rows, values


def unpack_widen_kernel(index_ref, *refs):
    refs, out_ref = refs[:-1], refs[-1]
    width = out_ref.shape[1] // 2
    for tensor, bits in ((0, (1, 2)), (1, (2, 1))):
        for block, rows, values in relative_blocks(refs, tensor):
            start = pl.multiple_of(block_home(index_ref[0], block, *bits) * rows, rows)
            out_ref[pl.ds(start, rows), tensor * width : (tensor + 1) * width] = values.astype(F32)


def unpack_mixer_kernel(index_ref, *refs):
    refs, (triple_ref, result_ref) = refs[:-2], refs[-2:]
    half, split = triple_ref.shape[2], triple_ref.shape[1] // 2
    for block, rows, values in relative_blocks(refs, 0):
        home = block_home(index_ref[0], block, 1, 2)
        part, row = home // 8, pl.multiple_of(home % 8 * rows, rows)
        triple_ref[part, pl.ds(row, rows), :] = values[:, :half].astype(F32)
        triple_ref[part, pl.ds(split + row, rows), :] = values[:, half:].astype(F32)
    for block, rows, values in relative_blocks(refs, 1):
        home = block_home(index_ref[0], block, 2, 1)
        row = pl.multiple_of(home % 8 * rows, rows)

        @pl.when(home < 8)
        def _():
            triple_ref[2, pl.ds(row, rows), :] = values[:, :half].astype(F32)
            triple_ref[2, pl.ds(split + row, rows), :] = values[:, half:].astype(F32)

        @pl.when(home >= 8)
        def _():
            result_ref[pl.ds(row, rows), :] = values.astype(F32)


def local(
    sentence_layer_entry,
    sentence_word_ids,
    picture_tile_activations,
    picture_detail_flag,
    matched_picture_ids,
    mixer_layernorm_gamma,
    mixer_layernorm_offset,
    mixer_triple_matrix,
    mixer_pair_offsets,
    mixer_result_matrix,
    mixer_result_offset,
    perceptron_layernorm_gamma,
    perceptron_layernorm_offset,
    widening_matrix,
    widening_offset,
    narrowing_matrix,
    narrowing_offset,
    sharpening_log,
    locked_layernorm_gammas,
    locked_mixer_triple_matrix,
    locked_mixer_result_matrix,
    locked_widening_matrix,
    locked_narrowing_matrix,
):
    captions = matched_picture_ids.shape[0]
    tokens, model_width = sentence_layer_entry.shape
    local_width = mixer_result_matrix.shape[0]
    hidden = narrowing_matrix.shape[0]
    devices = lax.axis_size("dp")
    all_pairs = captions * devices
    place, core = lax.axis_index("dp"), lax.axis_index("mp")
    blocks = tokens // BLOCK
    full = (tokens, model_width)
    short = (captions, model_width)
    square = (model_width, model_width)
    half_square = (model_width // 2, model_width)
    dealt = ((half_square, BF16),) * 4

    steps = group_steps(devices)

    image_emb = image_tower(
        picture_detail_flag,
        picture_tile_activations,
        locked_layernorm_gammas,
        locked_mixer_triple_matrix,
        locked_mixer_result_matrix,
        locked_widening_matrix,
        locked_narrowing_matrix,
    )
    normed, qkv, soft, mixed, part, mark = call(
        text_mix_kernel,
        (
            sentence_layer_entry,
            sentence_word_ids,
            mixer_layernorm_gamma,
            mixer_layernorm_offset,
            mixer_triple_matrix,
            mixer_pair_offsets,
            mixer_result_matrix,
        ),
        (
            (full, BF16),
            ((3, tokens, local_width), BF16),
            ((blocks, local_width // PAIR, 2 * BLOCK, BLOCK), F32),
            ((tokens, local_width), BF16),
            (full, F32),
        ),
        after=(image_emb,),
        limit=60,
        mark=True,
    )
    other = mp_other(part)
    near_images = dp_gather(image_emb, steps[:0:-1], [mark] * (len(steps) - 1))
    residual, normed2, slope, hidden_sums, resid_sum, branch = call(
        text_widen_kernel,
        (
            sentence_layer_entry,
            part,
            other,
            mixer_result_offset,
            perceptron_layernorm_gamma,
            perceptron_layernorm_offset,
            widening_offset,
            sentence_word_ids,
        ),
        (
            (full, F32),
            (full, BF16),
            ((tokens, hidden), F32),
            ((captions, hidden), BF16),
            (short, F32),
            (short, F32),
        ),
        outside=(widening_matrix, narrowing_matrix),
        scratch=(pltpu.VMEM((captions, hidden), F32),),
        after=(near_images,),
    )

    near_images = dp_gather(near_images, steps[:1], (branch,))
    sums_parts = dp_parts(hidden_sums, steps[0])
    images, unit, factor, logits, powers, row_sum, col_sum, row_loss = call(
        functools.partial(logits_kernel, gather_masks(steps[::-1])),
        (
            near_images,
            mp_other(near_images),
            resid_sum,
            branch,
            mp_other(branch),
            narrowing_offset,
            sentence_word_ids,
        ),
        (
            ((all_pairs, model_width), BF16),
            (short, F32),
            ((captions, 128), F32),
            ((captions, all_pairs), F32),
            ((captions, all_pairs), F32),
            ((captions, 128), F32),
            ((1, all_pairs), F32),
            ((8, 128), F32),
        ),
        index=(place, core),
        small=(matched_picture_ids, sharpening_log),
    )
    col_parts = dp_parts(col_sum, steps[0])
    for step in steps[1:]:
        (col_sum,) = call(sum_kernel, col_parts, ((col_sum.shape, F32),))
        col_parts = dp_parts(col_sum, step)
    after = (col_sum,)
    for step in steps[2:] + [None]:
        rows = sums_parts[0].shape[0]
        joined_sums, mark = move(
            sums_parts,
            (4 * rows,),
            [(place, 0, rows, 0, place * rows) for place in range(4)],
            after,
            mark=True,
        )
        after = (mark,)
        if step is not None:
            sums_parts = dp_parts(joined_sums, step)
    sums_high = dp_swap(joined_sums, 2 * Z_STRIDE)
    sums_parts = [joined_sums, dp_swap(joined_sums, Z_STRIDE), sums_high]
    sums_parts.append(dp_swap(sums_high, Z_STRIDE))
    grad_caption, grad_caption_low, grad_pre, part, loss_stat = call(
        loss_grad_kernel,
        (
            *col_parts,
            logits,
            powers,
            row_sum,
            unit,
            factor,
            images,
            sentence_word_ids,
            row_loss,
        ),
        (
            (short, F32),
            (short, BF16),
            ((tokens, hidden), BF16),
            (full, F32),
            ((8, model_width), F32),
        ),
        outside=(narrowing_matrix, slope, widening_matrix),
        after=after,
        small=(matched_picture_ids, sharpening_log),
    )

    other = mp_other(part)
    *widen_dealt, mark = call(
        widen_grad_kernel,
        (normed2, grad_pre),
        dealt,
        scratch=(pltpu.VMEM(square, BF16),) * 2,
        index=(place,),
        mark=True,
    )
    grad_residual, grad_branch1, flat, part, mixer_stat = call(
        mixer_back_kernel,
        (
            part,
            other,
            residual,
            grad_caption,
            sentence_word_ids,
            perceptron_layernorm_gamma,
            mixer_result_matrix,
        ),
        (
            (full, F32),
            (full, BF16),
            ((3, tokens, local_width), BF16),
            (full, F32),
            ((8, model_width), F32),
        ),
        outside=(qkv, soft, mixer_triple_matrix),
        after=(mark,),
    )
    other = mp_other(part)
    extra = []
    widen_sum = scatter_steps(widen_dealt, place, extra)
    next(widen_sum)
    *mixer_dealt, mark = call(
        mixer_grad_kernel,
        (normed, flat, mixed, grad_branch1),
        dealt,
        scratch=(pltpu.VMEM(square, BF16),) * 2,
        index=(place,),
        after=sums_parts[1:3],
        mark=True,
    )
    mixer_sum = scatter_steps(mixer_dealt, place)
    next(mixer_sum)
    last = widen_sum.send((mark,))
    last = widen_sum.send((last,))
    extra_rows = captions // 2 + 16
    grad_input, mine = call(
        entry_grad_kernel,
        (
            part,
            other,
            sentence_layer_entry,
            mixer_layernorm_gamma,
            grad_residual,
            loss_stat,
            mixer_stat,
            grad_caption_low,
        ),
        ((full, F32), ((extra_rows, model_width), BF16)),
        scratch=(pltpu.VMEM((16, model_width), F32),),
        index=(core,),
        after=(last,),
    )
    extra.append(dp_gather(mine, steps[:1:-1], [mine] * len(steps)))
    last = mixer_sum.send((mine,))
    last = widen_sum.send((last,))
    last = mixer_sum.send((last,))
    last = widen_sum.send((last,))
    last = mixer_sum.send((last,))
    last = widen_sum.send((last,))
    last = mixer_sum.send((last,))
    widen_pieces = widen_sum.send(())
    near_grads, *results = call(
        functools.partial(collect_kernel, 1.0 / (2.0 * all_pairs), extra_rows),
        (*widen_pieces, loss_stat),
        (
            ((all_pairs // 2, model_width), BF16),
            ((1,), F32),
            ((2, local_width), F32),
            ((model_width,), F32),
            ((hidden,), F32),
        )
        + (((model_width,), F32),) * 5
        + (((1,), F32),),
        after=(last,),
    )
    error, grad_pair, grad_b_out, grad_b_up, grad_b_down = results[:5]
    grad_w_up, mark = call(
        unpack_widen_kernel,
        widen_pieces,
        ((widening_matrix.shape, F32),),
        index=(place,),
        after=(results[0],),
        limit=56,
        mark=True,
    )
    last = mixer_sum.send((mark,))
    grad_w_down, mark = call(
        functools.partial(narrow_grad_kernel, captions // 2),
        (*sums_parts, near_grads, mp_other(near_grads)),
        ((narrowing_matrix.shape, F32),),
        scratch=(pltpu.VMEM((all_pairs, model_width), BF16),),
        index=(core,),
        after=(last,),
        mark=True,
    )
    grad_qkv, grad_w_out = call(
        unpack_mixer_kernel,
        mixer_sum.send(()),
        ((mixer_triple_matrix.shape, F32), (mixer_result_matrix.shape, F32)),
        index=(place,),
        after=(mark,),
        limit=56,
    )
    return (
        error,
        grad_input,
        grad_qkv,
        grad_pair,
        grad_w_out,
        grad_b_out,
        grad_w_up,
        grad_b_up,
        grad_w_down,
        grad_b_down,
        *results[5:],
    )


def solution(mesh):
    placed = (
        P("dp", None),
        P("dp"),
        P(("dp", "mp"), None, None),
        P(("dp", "mp")),
        P("dp"),
        P(),
        P(),
        P(None, None, "mp"),
        P(None, "mp"),
        P("mp", None),
        P(),
        P(),
        P(),
        P(None, "mp"),
        P("mp"),
        P("mp", None),
        P(),
        P(),
        P(),
        P(),
        P(),
        P(),
        P(),
    )
    return jax.shard_map(
        local,
        mesh=mesh,
        in_specs=placed,
        out_specs=(
            P(),
            P("dp", None),
            P(None, None, "mp"),
            P(None, "mp"),
            P("mp", None),
            P(),
            P(None, "mp"),
            P("mp"),
            P("mp", None),
            P(),
            P(),
            P(),
            P(),
            P(),
            P(),
        ),
        check_vma=False,
    )
```

```python
import functools

import jax
import jax.numpy as jnp
from jax import lax
from jax.experimental import pallas as pl
from jax.experimental.pallas import tpu as pltpu
from jax.sharding import PartitionSpec as P

HEAD = 64
IMG_TOK = 145
LOW_TOK = 50
CAP_LEN = 16


EPS_TEXT = 1e-05
EPS_UNIT = 1e-06
MASKED_SCORE = -1e30
BF16 = jnp.bfloat16
F32 = jnp.float32


def mp_other(values):
    return lax.ppermute(values, "mp", [(0, 1), (1, 0)])


def dp_swap(values, mask):
    size = lax.axis_size("dp")
    return lax.ppermute(values, "dp", [(index, index ^ mask) for index in range(size)])


def group_steps(size):
    steps, stride = [], 1
    while stride < size:
        steps.append([stride, 2 * stride, 3 * stride])
        stride *= 4
    return steps


def gather_masks(steps):
    masks = [0]
    for step in steps:
        masks = [mask ^ base for mask in [0] + step for base in masks]
    return masks


def dp_parts(values, step):
    return [values] + [dp_swap(values, mask) for mask in step]


def dp_gather(values, steps, waits):
    for step, wait in zip(steps, waits):
        parts = dp_parts(values, step)
        rows = values.shape[0]
        (values,) = move(
            parts,
            (len(parts) * rows,),
            [(place, 0, rows, 0, place * rows) for place in range(len(parts))],
            (wait,),
        )
    return values


HIGH_ROWS = 160
LOW_ROWS = 64
TILE = 256
PAIR = 2 * HEAD
LANES = 128
POOL_ROWS = 32
NT = (((1,), (1,)), ((), ()))
VMEM_LIMIT = 60 * 1024 * 1024
BUSY = 10**12


def dot(left, right):
    return jnp.dot(left, right, preferred_element_type=F32)


def wide_dot(left, right):
    high = left.astype(BF16)
    rest = (left - high.astype(F32)).astype(BF16)
    return dot(high, right) + dot(rest, right)


def standard(values, epsilon):
    centered = values - jnp.mean(values, axis=-1, keepdims=True)
    variance = jnp.mean(centered * centered, axis=-1, keepdims=True)
    return centered * lax.rsqrt(variance + epsilon)


def gelu(values):
    return (0.5 * values) * (1.0 + lax.erf(values * (0.5**0.5)))


def image_kernel(
    flag_ref,
    token_ref,
    gain_ref,
    triple_hbm,
    result_hbm,
    widen_hbm,
    narrow_hbm,
    out_ref,
    wide,
    packed,
    mixed,
    queries,
    keys,
    values,
    triple,
    result,
    widen,
    narrow,
    resid_groups,
    hidden_groups,
    pooled,
    ready,
    starts,
    high_starts,
    low_starts,
    sems,
):
    _, images, width = token_ref.shape
    hidden = widen.shape[1]
    copies = fetch(
        (triple_hbm, result_hbm, widen_hbm, narrow_hbm), (triple, result, widen, narrow), sems
    )
    lane_tiles = [slice(lane, lane + LANES) for lane in range(0, width, LANES)]

    def spread(position, carry):
        rows = pl.ds(pl.multiple_of(position * images, images), images)
        for place, lanes in enumerate(lane_tiles):
            wide[place, rows, :] = token_ref[position, :, lanes].astype(F32)
        return carry

    def begin(image, carry):
        start, highs = carry
        starts[image] = start
        high = flag_ref[image] == 1

        @pl.when(high)
        def _():
            high_starts[highs] = start

        @pl.when(jnp.logical_not(high))
        def _():
            low_starts[image - highs] = start

        return start + jnp.where(high, HIGH_ROWS, LOW_ROWS), highs + jnp.where(high, 1, 0)

    total, highs = lax.fori_loop(0, images, begin, (jnp.int32(0), jnp.int32(0)))
    lax.fori_loop(0, LOW_ROWS, spread, 0, unroll=4)

    @pl.when(total > images * LOW_ROWS)
    def _():
        lax.fori_loop(LOW_ROWS, IMG_TOK, spread, 0, unroll=3)

    tail = IMG_TOK // 16 * 16

    def pack(image, carry):
        start = pl.multiple_of(starts[image], POOL_ROWS)
        high = flag_ref[image] == 1

        @pl.when(high)
        def _():
            row = lax.broadcasted_iota(jnp.int32, (HIGH_ROWS - tail, LANES), 0)
            for place, lanes in enumerate(lane_tiles):
                packed[pl.ds(start, tail), lanes] = wide[
                    place, pl.ds(image, tail, stride=images), :
                ].astype(BF16)
                last = wide[place, pl.ds(image + tail * images, 1), :]
                packed[pl.ds(start + tail, HIGH_ROWS - tail), lanes] = jnp.where(
                    row == 0, last, 0.0
                ).astype(BF16)

        @pl.when(jnp.logical_not(high))
        def _():
            for place, lanes in enumerate(lane_tiles):
                packed[pl.ds(start, LOW_ROWS), lanes] = wide[
                    place, pl.ds(image, LOW_ROWS, stride=images), :
                ].astype(BF16)

        return carry

    lax.fori_loop(0, images, pack, 0)
    packed[pl.ds(pl.multiple_of(total, POOL_ROWS), TILE), :] = jnp.zeros((TILE, width), BF16)
    tiles = lax.div(total + (TILE - 1), jnp.int32(TILE))

    copies[0].wait()

    def prepare(tile):
        rows = pl.ds(pl.multiple_of(tile * TILE, TILE), TILE)
        ready[tile % 2] = (
            standard(packed[rows, :].astype(F32), EPS_UNIT) * gain_ref[0:1, :]
        ).astype(BF16)

    def project(tile, carry):
        rows = pl.ds(pl.multiple_of(tile * TILE, TILE), TILE)
        normed = ready[tile % 2]
        queries[rows, :] = (dot(normed, triple[0]) * HEAD ** (-0.5)).astype(BF16)
        prepare(tile + 1)
        keys[rows, :] = dot(normed, triple[1]).astype(BF16)
        values[rows, :] = dot(normed, triple[2]).astype(BF16)
        return carry

    prepare(jnp.int32(0))
    lax.fori_loop(0, tiles, project, 0)

    def attend(begins, count, live):
        left = lax.broadcasted_iota(jnp.int32, (count, PAIR), 1) < HEAD
        key_live = lax.broadcasted_iota(jnp.int32, (2 * count, count), 1) < live
        places = [
            (pl.ds(pl.multiple_of(start, POOL_ROWS), count), slice(lane, lane + PAIR))
            for start in begins
            for lane in range(0, width, PAIR)
        ]
        all_scores = [dot_t(two_heads(queries[place], left), keys[place]) for place in places]
        all_powers = []
        for scores in all_scores:
            scores = jnp.where(key_live, scores, MASKED_SCORE)
            top = jnp.max(scores, axis=-1, keepdims=True)
            all_powers.append(jnp.exp(scores - top).astype(BF16))
        for place, powers in zip(places, all_powers):
            value = values[place]
            one = jnp.ones_like(value)
            first = dot(powers[:count], jnp.where(left, value, one))
            second = dot(powers[count:], jnp.where(left, one, value))
            sums = pltpu.roll(jnp.where(left, second, first), HEAD, 1)
            mixed[place] = (jnp.where(left, first, second) / sums).astype(BF16)

    def attend_all(begins, number, together, count, live):
        groups = lax.div(number, jnp.int32(together))

        def group(index, carry):
            attend([begins[index * together + step] for step in range(together)], count, live)
            return carry

        def rest(index, carry):
            attend([begins[index]], count, live)
            return carry

        lax.fori_loop(0, groups, group, 0)
        if together > 1:
            lax.fori_loop(groups * together, number, rest, 0)

    attend_all(high_starts, highs, 1, HIGH_ROWS, IMG_TOK)
    attend_all(low_starts, images - highs, 4, LOW_ROWS, LOW_TOK)

    slot = lax.broadcasted_iota(jnp.int32, (1, images), 1)
    first_row = jnp.zeros((1, images), jnp.int32)
    live_rows = jnp.zeros((1, images), jnp.int32)
    for image in range(images):
        first_row = jnp.where(slot == image, starts[image], first_row)
        live_rows = jnp.where(
            slot == image, jnp.where(flag_ref[image] == 1, IMG_TOK, LOW_TOK), live_rows
        )
    copies[1].wait()
    copies[2].wait()
    groups = TILE // POOL_ROWS

    def group_sum(rows):
        return jnp.sum(rows.reshape(groups, POOL_ROWS // 8, 8, rows.shape[1]), axis=1)

    def resume(tile):
        base = pl.multiple_of(tile * TILE, TILE)
        rows = pl.ds(base, TILE)
        place = base + lax.broadcasted_iota(jnp.int32, (TILE, images), 0)
        alive = jnp.sum(
            jnp.where((place >= first_row) & (place < first_row + live_rows), 1.0, 0.0),
            axis=1,
            keepdims=True,
        )
        residual = (packed[rows, :].astype(F32) + dot(mixed[rows, :], result[...])) * alive
        group = pl.ds(pl.multiple_of(tile * groups, groups), groups)
        resid_groups[group] = group_sum(residual)
        ready[tile % 2] = (standard(residual, EPS_UNIT) * gain_ref[1:2, :]).astype(BF16)

    def perceptron(tile, carry):
        group = pl.ds(pl.multiple_of(tile * groups, groups), groups)
        normed = ready[tile % 2]
        for chunk in range(hidden // width):
            if chunk == 1:
                resume(tile + 1)
            lanes = slice(chunk * width, (chunk + 1) * width)
            units = gelu(dot(normed, widen[:, lanes])).astype(BF16)
            hidden_groups[group, :, lanes] = group_sum(units.astype(F32))
        return carry

    resume(jnp.int32(0))
    lax.fori_loop(0, tiles, perceptron, 0)

    def pool(image, carry):
        group = lax.div(starts[image], jnp.int32(POOL_ROWS))
        high = flag_ref[image] == 1

        def add(count):
            residual, units = resid_groups[group], hidden_groups[group]
            for step in range(1, count):
                residual = residual + resid_groups[group + step]
                units = units + hidden_groups[group + step]
            pooled[pl.ds(image, 1), :width] = jnp.sum(residual, axis=0, keepdims=True)
            pooled[pl.ds(image, 1), width:] = jnp.sum(units, axis=0, keepdims=True)

        @pl.when(high)
        def _():
            add(HIGH_ROWS // POOL_ROWS)

        @pl.when(jnp.logical_not(high))
        def _():
            add(LOW_ROWS // POOL_ROWS)

        return carry

    lax.fori_loop(0, images, pool, 0)
    copies[3].wait()
    units = pooled[:, width:]
    upper = units.astype(BF16)
    lower = (units - upper.astype(F32)).astype(BF16)
    branch = dot(jnp.concatenate([upper, lower], axis=0), narrow[...])
    live = jnp.where(number_column(flag_ref) == 1, IMG_TOK, LOW_TOK).astype(F32)
    mean = (pooled[:, :width] + branch[:images] + branch[images:]) / live
    out_ref[...] = (
        mean * lax.rsqrt(jnp.sum(mean * mean, axis=-1, keepdims=True) + EPS_UNIT)
    ).astype(BF16)


def image_tower(flags, tokens, gains, triple, result, widen, narrow):
    images, _, width = tokens.shape
    hidden = widen.shape[1]
    rows = images * HIGH_ROWS + TILE
    groups = rows // POOL_ROWS
    outside = pl.BlockSpec(memory_space=pl.ANY)
    inside = pl.BlockSpec(memory_space=pltpu.VMEM)
    return pl.pallas_call(
        image_kernel,
        out_shape=jax.ShapeDtypeStruct((images, width), BF16),
        in_specs=[pl.BlockSpec(memory_space=pltpu.SMEM), inside, inside]
        + [outside] * 4,
        out_specs=inside,
        scratch_shapes=[pltpu.VMEM((width // LANES, IMG_TOK * images, LANES), F32)]
        + [pltpu.VMEM((rows, width), BF16)] * 5
        + [pltpu.VMEM(weight.shape, BF16) for weight in (triple, result, widen, narrow)]
        + [
            pltpu.VMEM((groups, 8, width), F32),
            pltpu.VMEM((groups, 8, hidden), F32),
            pltpu.VMEM((images, width + hidden), F32),
            pltpu.VMEM((2, TILE, width), BF16),
            pltpu.SMEM((images,), jnp.int32),
            pltpu.SMEM((images,), jnp.int32),
            pltpu.SMEM((images,), jnp.int32),
            pltpu.SemaphoreType.DMA((4,)),
        ],
        compiler_params=pltpu.CompilerParams(vmem_limit_bytes=VMEM_LIMIT),
        cost_estimate=pl.CostEstimate(flops=BUSY, bytes_accessed=BUSY, transcendentals=0),
    )(flags, jnp.transpose(tokens, (1, 0, 2)), gains, triple, result, widen, narrow)


TN = (((0,), (0,)), ((), ()))
BLOCK = 128
ROOT_HALF = 0.5**0.5
DENSITY = 0.3989422804014327


def dot_t(left, right):
    return lax.dot_general(left, right, NT, preferred_element_type=F32)


def t_dot(left, right):
    return lax.dot_general(left, right, TN, preferred_element_type=F32)


def fetch(sources, targets, sems):
    copies = [
        pltpu.make_async_copy(source, target, sems.at[place])
        for place, (source, target) in enumerate(zip(sources, targets))
    ]
    for copy in copies:
        copy.start()
    return copies


def caption_pool(ids_ref, captions):
    ids_row = ids_ref[...].reshape(1, -1)
    tokens = ids_row.shape[1]
    shape = (captions, tokens)
    caption = lax.broadcasted_iota(jnp.int32, shape, 0)
    token = lax.broadcasted_iota(jnp.int32, shape, 1)
    inside = (token // (tokens // captions)) == caption
    return jnp.where(inside & (ids_row != 0), 1.0, 0.0)


def valid_column(pool):
    pool = pool.astype(BF16)
    return t_dot(pool, jnp.ones((pool.shape[0], 128), BF16))[:, 0:1]


def number_column(ref):
    shape = (ref.shape[0], 1)
    place = lax.broadcasted_iota(jnp.int32, shape, 0)
    column = jnp.zeros(shape, jnp.int32)
    for index in range(shape[0]):
        column = jnp.where(place == index, ref[index], column)
    return column


def as_row(ref):
    return ref[...].reshape(1, -1)


def pair_masks(rows, pair_width):
    return lax.broadcasted_iota(jnp.int32, (rows, pair_width), 1) < HEAD


def two_heads(values, left):
    zero = jnp.zeros_like(values)
    return jnp.concatenate(
        [jnp.where(left, values, zero), jnp.where(left, zero, values)], axis=0
    )


def text_mix_kernel(
    entry_ref,
    ids_ref,
    gain_ref,
    shift_ref,
    triple_ref,
    pair_ref,
    result_ref,
    normed_ref,
    qkv_ref,
    soft_ref,
    mixed_ref,
    part_ref,
):
    tokens = entry_ref.shape[0]
    width = result_ref.shape[0]
    normed = (
        standard(entry_ref[...].astype(F32), EPS_TEXT) * as_row(gain_ref) + as_row(shift_ref)
    ).astype(BF16)
    normed_ref[...] = normed
    qkv_ref[0] = (dot(normed, triple_ref[0]) + pair_ref[0:1, :]).astype(BF16)
    qkv_ref[1] = dot(normed, triple_ref[1]).astype(BF16)
    qkv_ref[2] = (dot(normed, triple_ref[2]) + pair_ref[1:2, :]).astype(BF16)
    ids = as_row(ids_ref)
    left = pair_masks(BLOCK, PAIR)
    shape = (2 * BLOCK, BLOCK)
    query_caption = lax.broadcasted_iota(jnp.int32, shape, 0) % BLOCK // CAP_LEN
    same = query_caption == lax.broadcasted_iota(jnp.int32, shape, 1) // CAP_LEN
    for block in range(tokens // BLOCK):
        rows = slice(block * BLOCK, (block + 1) * BLOCK)
        seen = same & (ids[:, rows] != 0)
        for pair in range(width // PAIR):
            lanes = slice(pair * PAIR, (pair + 1) * PAIR)
            scores = dot_t(two_heads(qkv_ref[0, rows, lanes], left), qkv_ref[1, rows, lanes])
            scores = jnp.where(seen, scores * HEAD ** (-0.5), MASKED_SCORE)
            powers = jnp.exp(scores - jnp.max(scores, axis=-1, keepdims=True))
            soft = powers / jnp.sum(powers, axis=-1, keepdims=True)
            soft_ref[block, pair] = soft
            low = soft.astype(BF16)
            value = qkv_ref[2, rows, lanes]
            mixed_ref[rows, lanes] = jnp.where(
                left, dot(low[:BLOCK], value), dot(low[BLOCK:], value)
            ).astype(BF16)
    part_ref[...] = dot(mixed_ref[...], result_ref[...])


def text_widen_kernel(
    entry_ref,
    own_ref,
    other_ref,
    result_offset_ref,
    gain_ref,
    shift_ref,
    widen_offset_ref,
    ids_ref,
    widen_hbm,
    narrow_hbm,
    residual_ref,
    normed_ref,
    slope_ref,
    sums_ref,
    resid_sum_ref,
    branch_ref,
    widen,
    narrow,
    hidden_sum,
    sems,
):
    captions = sums_ref.shape[0]
    width = entry_ref.shape[1]
    copies = fetch((widen_hbm, narrow_hbm), (widen, narrow), sems)
    residual = entry_ref[...].astype(F32) + (
        (own_ref[...] + other_ref[...]) + as_row(result_offset_ref)
    )
    residual_ref[...] = residual
    normed = (standard(residual, EPS_TEXT) * as_row(gain_ref) + as_row(shift_ref)).astype(BF16)
    normed_ref[...] = normed
    pool = caption_pool(ids_ref, captions).astype(BF16)
    widen_offset = as_row(widen_offset_ref)
    upper = residual.astype(BF16)
    resid_sum_ref[...] = dot(pool, upper) + dot(
        pool, (residual - upper.astype(F32)).astype(BF16)
    )
    valid = valid_column(pool)
    copies[0].wait()
    for chunk in range(widen.shape[1] // width):
        lanes = slice(chunk * width, (chunk + 1) * width)
        before = dot(normed, widen[:, lanes]) + widen_offset[:, lanes]
        share = 0.5 * (1.0 + lax.erf(before * ROOT_HALF))
        hidden_sum[:, lanes] = dot(pool, (before * share).astype(BF16))
        slope = share + before * (jnp.exp(-0.5 * before * before) * DENSITY)
        slope_ref[:, lanes] = slope * valid
    sums_ref[...] = hidden_sum[...].astype(BF16)
    copies[1].wait()
    branch_ref[...] = wide_dot(hidden_sum[...], narrow[...])


def logits_kernel(
    masks,
    index_ref,
    matched_ref,
    sharpen_ref,
    near_ref,
    far_ref,
    resid_sum_ref,
    own_ref,
    other_ref,
    narrow_offset_ref,
    ids_ref,
    images_ref,
    unit_ref,
    factor_ref,
    logits_ref,
    powers_ref,
    row_sum_ref,
    col_sum_ref,
    loss_ref,
):
    captions, pairs = logits_ref.shape
    rows = images_ref.shape[0] // (2 * len(masks))
    core = index_ref[1]
    for place, mask in enumerate(masks):
        start = (index_ref[0] ^ mask) * (2 * rows)
        images_ref[pl.ds(pl.multiple_of(start + core * rows, rows), rows), :] = near_ref[
            place * rows : (place + 1) * rows, :
        ]
        images_ref[pl.ds(pl.multiple_of(start + (1 - core) * rows, rows), rows), :] = far_ref[
            place * rows : (place + 1) * rows, :
        ]
    count = jnp.sum(caption_pool(ids_ref, captions), axis=1, keepdims=True)
    pooled = (resid_sum_ref[...] + (own_ref[...] + other_ref[...])) / count + as_row(
        narrow_offset_ref
    )
    inverse = lax.rsqrt(jnp.sum(pooled * pooled, axis=-1, keepdims=True) + EPS_UNIT)
    unit = pooled * inverse
    unit_ref[...] = unit
    factor_ref[...] = jnp.broadcast_to(inverse / count, factor_ref.shape)
    logits = jnp.exp(jnp.full((1, 1), sharpen_ref[0], F32)) * dot_t(unit.astype(BF16), images_ref[...])
    logits_ref[...] = logits
    powers = jnp.exp(logits)
    powers_ref[...] = powers
    row_sum = jnp.sum(powers, axis=1, keepdims=True)
    row_sum_ref[...] = jnp.broadcast_to(row_sum, row_sum_ref.shape)
    col_sum_ref[...] = jnp.sum(powers, axis=0, keepdims=True)
    positive = number_column(matched_ref) == lax.broadcasted_iota(jnp.int32, (captions, pairs), 1)
    wanted = jnp.sum(jnp.where(positive, logits, 0.0), axis=1, keepdims=True)
    loss_ref[...] = jnp.broadcast_to(
        jnp.sum(jnp.log(row_sum) - 2.0 * wanted, axis=0, keepdims=True), loss_ref.shape
    )


def sum_kernel(first_ref, second_ref, third_ref, fourth_ref, out_ref):
    out_ref[...] = (first_ref[...] + second_ref[...]) + (third_ref[...] + fourth_ref[...])


def loss_grad_kernel(
    matched_ref,
    sharpen_ref,
    col_ref,
    col1_ref,
    col2_ref,
    col3_ref,
    logits_ref,
    powers_ref,
    row_sum_ref,
    unit_ref,
    factor_ref,
    images_ref,
    ids_ref,
    loss_ref,
    narrow_hbm,
    slope_hbm,
    widen_hbm,
    grad_ref,
    low_ref,
    before_ref,
    part_ref,
    stat_ref,
    narrow,
    slope,
    widen,
    sems,
):
    captions, pairs = logits_ref.shape
    tokens, hidden = slope.shape
    width = grad_ref.shape[1]
    copies = fetch((narrow_hbm, slope_hbm, widen_hbm), (narrow, slope, widen), sems)
    logits, powers = logits_ref[...], powers_ref[...]
    col_sum = (col_ref[...] + col1_ref[...]) + (col2_ref[...] + col3_ref[...])
    positive = number_column(matched_ref) == lax.broadcasted_iota(jnp.int32, (captions, pairs), 1)
    derivative = (
        powers / row_sum_ref[:, 0:1] + powers / col_sum - jnp.where(positive, 2.0, 0.0)
    ) / (2.0 * pairs)
    temperature = jnp.sum(
        jnp.sum(derivative * logits, axis=1, keepdims=True), axis=0, keepdims=True
    )
    col_loss = jnp.sum(jnp.log(col_sum), axis=1, keepdims=True)
    text = dot((derivative * jnp.exp(jnp.full((1, 1), sharpen_ref[0], F32))).astype(BF16), images_ref[...])
    unit = unit_ref[...]
    grad = (text - unit * jnp.sum(unit * text, axis=-1, keepdims=True)) * factor_ref[:, 0:1]
    grad_ref[...] = grad
    low = grad.astype(BF16)
    low_ref[...] = low
    copies[0].wait()
    copies[1].wait()
    copies[2].wait()
    ones = jnp.ones((8, tokens), BF16)
    part = jnp.zeros(part_ref.shape, F32)
    for chunk in range(hidden // width):
        lanes = slice(chunk * width, (chunk + 1) * width)
        back = dot_t(low, narrow[lanes, :])
        before = (
            (back[:, None, :] * slope[:, lanes].reshape(captions, CAP_LEN, width))
            .reshape(tokens, width)
            .astype(BF16)
        )
        before_ref[:, lanes] = before
        stat_ref[chunk : chunk + 1, :] = dot(ones, before)[0:1]
        part = part + dot_t(before, widen[:, lanes])
    part_ref[...] = part
    count = jnp.sum(caption_pool(ids_ref, captions), axis=1, keepdims=True)
    stat_ref[2:3, :] = jnp.sum(low.astype(F32) * count, axis=0, keepdims=True)
    lane = lax.broadcasted_iota(jnp.int32, (1, width), 1)
    stat_ref[3:4, :] = jnp.where(
        lane == 0,
        temperature,
        jnp.where(lane == 1, loss_ref[0:1, 0:1], jnp.where(lane == 2, col_loss, 0.0)),
    )
    stat_ref[4:8, :] = jnp.zeros((4, width), F32)


def deal(index_ref, first, second, outs):
    half = first.shape[0] // 2
    for place, (values, bit) in enumerate(((first, 1), (second, 2))):
        mine = index_ref[0] // bit % 2
        for ref, which in ((outs[2 * place], 1 - mine), (outs[2 * place + 1], mine)):
            ref[...] = values[pl.ds(pl.multiple_of(which * half, half), half), :]


def widen_grad_kernel(index_ref, normed_ref, before_ref, *refs):
    outs, (first, second) = refs[:4], refs[4:]
    width = first.shape[1]
    normed = normed_ref[...]
    first[...] = t_dot(normed, before_ref[:, :width]).astype(BF16)
    second[...] = t_dot(normed, before_ref[:, width:]).astype(BF16)
    deal(index_ref, first, second, outs)


def mixer_back_kernel(
    own_ref,
    other_ref,
    residual_ref,
    grad_ref,
    ids_ref,
    gain_ref,
    result_ref,
    qkv_hbm,
    soft_hbm,
    triple_hbm,
    grad_residual_ref,
    low_ref,
    flat_ref,
    part_ref,
    stat_ref,
    qkv,
    soft_all,
    triple,
    sems,
):
    tokens, width = residual_ref.shape
    captions = grad_ref.shape[0]
    local_width = result_ref.shape[0]
    copies = fetch((qkv_hbm, soft_hbm, triple_hbm), (qkv, soft_all, triple), sems)
    residual = residual_ref[...]
    centered = residual - jnp.mean(residual, axis=-1, keepdims=True)
    rate = lax.rsqrt(jnp.mean(centered * centered, axis=-1, keepdims=True) + EPS_TEXT)
    unit = centered * rate
    grad = own_ref[...] + other_ref[...]
    stat_ref[1:2, :] = jnp.sum(grad * unit, axis=0, keepdims=True)
    stat_ref[2:3, :] = jnp.sum(grad, axis=0, keepdims=True)
    scaled = grad * as_row(gain_ref)
    inner = rate * (
        scaled
        - jnp.mean(scaled, axis=-1, keepdims=True)
        - unit * jnp.mean(scaled * unit, axis=-1, keepdims=True)
    )
    spread = jnp.broadcast_to(
        grad_ref[...][:, None, :], (captions, tokens // captions, width)
    ).reshape(tokens, width)
    grad_residual = spread * valid_column(caption_pool(ids_ref, captions)) + inner
    grad_residual_ref[...] = grad_residual
    low = grad_residual.astype(BF16)
    low_ref[...] = low
    ones = jnp.ones((8, tokens), BF16)
    stat_ref[0:1, :] = dot(ones, low)[0:1]
    grad_mixed = dot_t(low, result_ref[...]).astype(BF16)
    for copy in copies:
        copy.wait()
    left = pair_masks(BLOCK, PAIR)
    places = [
        (block, pair, slice(block * BLOCK, (block + 1) * BLOCK), slice(pair * PAIR, (pair + 1) * PAIR))
        for block in range(tokens // BLOCK)
        for pair in range(local_width // PAIR)
    ]
    mixed = [two_heads(grad_mixed[rows, lanes], left) for _, _, rows, lanes in places]
    softs = [soft_all[block, pair] for block, pair, _, _ in places]
    grads = [
        dot_t(value, qkv[2, rows, lanes]) for value, (_, _, rows, lanes) in zip(mixed, places)
    ]
    scores = [
        (soft * (grad - jnp.sum(grad * soft, axis=-1, keepdims=True))).astype(BF16)
        for soft, grad in zip(softs, grads)
    ]
    for value, soft, (_, _, rows, lanes) in zip(mixed, softs, places):
        flat_ref[2, rows, lanes] = t_dot(soft.astype(BF16), value).astype(BF16)
    for score, (_, _, rows, lanes) in zip(scores, places):
        key = qkv[1, rows, lanes]
        back = jnp.where(left, dot(score[:BLOCK], key), dot(score[BLOCK:], key))
        flat_ref[0, rows, lanes] = (back * HEAD ** (-0.5)).astype(BF16)
    for score, (_, _, rows, lanes) in zip(scores, places):
        flat_ref[1, rows, lanes] = (
            t_dot(score, two_heads(qkv[0, rows, lanes], left)) * HEAD ** (-0.5)
        ).astype(BF16)
    part_ref[...] = (
        dot_t(flat_ref[0], triple[0])
        + dot_t(flat_ref[1], triple[1])
        + dot_t(flat_ref[2], triple[2])
    )
    stat_ref[3:4, :local_width] = dot(ones, flat_ref[0])[0:1]
    stat_ref[3:4, local_width:] = dot(ones, flat_ref[2])[0:1]
    stat_ref[4:8, :] = jnp.zeros((4, width), F32)


def mixer_grad_kernel(index_ref, normed_ref, flat_ref, mixed_ref, low_ref, *refs):
    outs, (first, second) = refs[:4], refs[4:]
    half = flat_ref.shape[2]
    rows = first.shape[0] // 2
    normed = normed_ref[...]
    for part, (target, place) in enumerate(((first, 0), (first, rows), (second, 0))):
        grad = t_dot(normed, flat_ref[part]).astype(BF16)
        target[place : place + rows, :half] = grad[:rows]
        target[place : place + rows, half:] = grad[rows:]
    second[rows:, :] = t_dot(mixed_ref[...], low_ref[...]).astype(BF16)
    deal(index_ref, first, second, outs)


def narrow_grad_kernel(half, index_ref, *refs):
    parts, (near_ref, far_ref, out_ref, grads, sums) = refs[:-5], refs[-5:]
    rows, width = parts[0].shape[0], grads.shape[1]
    devices = near_ref.shape[0] // half
    for place in range(devices):
        plane, group, high = place % 4, place // 4 % (devices // GROUP), place * 4 // devices
        source = (plane * Z_SIZE + high) * (devices // GROUP) + group
        for ref, which in ((near_ref, index_ref[0]), (far_ref, 1 - index_ref[0])):
            start = pl.multiple_of((2 * place + which) * half, half)
            grads[pl.ds(start, half), :] = ref[source * half : (source + 1) * half, :]
    for place, part in enumerate(parts):
        sums[place * rows : (place + 1) * rows, :] = part[...]
    for chunk in range(out_ref.shape[0] // width):
        lanes = slice(chunk * width, (chunk + 1) * width)
        out_ref[lanes, :] = t_dot(sums[:, lanes], grads[...])


def entry_grad_kernel(
    index_ref,
    own_ref,
    other_ref,
    entry_ref,
    gain_ref,
    grad_residual_ref,
    loss_stat_ref,
    mixer_stat_ref,
    caption_ref,
    out_ref,
    extra_ref,
    pack,
):
    entry = entry_ref[...].astype(F32)
    centered = entry - jnp.mean(entry, axis=-1, keepdims=True)
    rate = lax.rsqrt(jnp.mean(centered * centered, axis=-1, keepdims=True) + EPS_TEXT)
    unit = centered * rate
    grad = own_ref[...] + other_ref[...]
    pack[0:8, :] = loss_stat_ref[...]
    pack[8:16, :] = mixer_stat_ref[...]
    pack[4:5, :] = jnp.sum(grad * unit, axis=0, keepdims=True)
    pack[5:6, :] = jnp.sum(grad, axis=0, keepdims=True)
    half = caption_ref.shape[0] // 2
    extra_ref[:half, :] = caption_ref[
        pl.ds(pl.multiple_of(index_ref[0] * half, half), half), :
    ]
    upper = pack[...].astype(BF16).astype(F32)
    pack[15:16, :] = (pack[...] - upper)[3:4, :]
    extra_ref[half:, :] = pack[...].astype(BF16)
    scaled = grad * as_row(gain_ref)
    out_ref[...] = grad_residual_ref[...] + rate * (
        scaled
        - jnp.mean(scaled, axis=-1, keepdims=True)
        - unit * jnp.mean(scaled * unit, axis=-1, keepdims=True)
    )


def tree_sum(values):
    while len(values) > 1:
        values = [values[place] + values[place + 1] for place in range(0, len(values), 2)]
    return values[0]


def collect_kernel(scale, rows, *refs):
    gathered, loss_ref, near_ref = refs[:8], refs[8], refs[9]
    (
        error_ref,
        pair_ref,
        result_ref,
        widen_ref,
        narrow_ref,
        gain1_ref,
        shift1_ref,
        gain2_ref,
        shift2_ref,
        temperature_ref,
    ) = refs[10:]
    half = rows - 16
    size = gathered[7].shape[0] // Z_SIZE
    more = gathered[1].shape[0] - 2 * size
    totals = []
    for piece in range(4):
        for step in range(Z_SIZE):
            if piece == 3:
                ref, first = gathered[6], Z_SIZE * size + step * more
            elif step < Z_SIZE - 1:
                ref, first = gathered[2 * piece], 3 * size + step * more
            else:
                ref, first = gathered[2 * piece + 1], 2 * size
            for row in range(first, first + more, rows):
                place = len(totals)
                near_ref[place * half : (place + 1) * half, :] = ref[row : row + half, :]
                totals.append(ref[row + half : row + rows, :].astype(F32))
    total = tree_sum(totals)
    scalars = total[3:4] + total[15:16]
    error_ref[...] = ((scalars[:, 1:2] + loss_ref[3:4, 2:3]) * scale).reshape(1)
    temperature_ref[...] = scalars[:, 0:1].reshape(1)
    lanes = pair_ref.shape[1]
    pair_ref[0:1, :] = total[11:12, :lanes]
    pair_ref[1:2, :] = total[11:12, lanes:]
    width = total.shape[1]
    for chunk in range(widen_ref.shape[0] // width):
        widen_ref[chunk * width : (chunk + 1) * width] = total[chunk]
    for ref, place in (
        (narrow_ref, 2),
        (gain1_ref, 4),
        (shift1_ref, 5),
        (result_ref, 8),
        (gain2_ref, 9),
        (shift2_ref, 10),
    ):
        ref[...] = total[place]


def call(kernel, inside, shapes, outside=(), scratch=(), index=(), small=(), after=(), limit=24, mark=False, busy=BUSY):
    vmem = pl.BlockSpec(memory_space=pltpu.VMEM)
    extra = [pltpu.VMEM(array.shape, array.dtype) for array in outside]
    extra += list(scratch)
    if outside:
        extra += [pltpu.SemaphoreType.DMA((len(outside),))]
    index = [jnp.stack(index).astype(jnp.int32)] if index else []
    small = index + list(small)
    before = len(small) + len(inside) + len(outside)

    if mark:
        shapes = tuple(shapes) + (((8, 128), F32),)

    def body(*refs):
        refs = refs[:before] + refs[before + len(after) :]
        if mark:
            last = before + len(shapes) - 1
            refs[last][...] = jnp.zeros((8, 128), F32)
            refs = refs[:last] + refs[last + 1 :]
        kernel(*refs)

    return pl.pallas_call(
        body,
        out_shape=[jax.ShapeDtypeStruct(shape, kind) for shape, kind in shapes],
        in_specs=[pl.BlockSpec(memory_space=pltpu.SMEM)] * len(small)
        + [vmem] * len(inside)
        + [pl.BlockSpec(memory_space=pl.ANY)] * (len(outside) + len(after)),
        out_specs=[vmem] * len(shapes),
        scratch_shapes=extra,
        compiler_params=pltpu.CompilerParams(vmem_limit_bytes=limit * 1024 * 1024),
        cost_estimate=pl.CostEstimate(flops=busy, bytes_accessed=busy, transcendentals=0),
    )(*small, *inside, *outside, *after)


def move(arrays, sizes, plan, after=(), mark=False, busy=BUSY):
    width, kind = arrays[0].shape[1], arrays[0].dtype

    def body(*refs):
        ins, outs = refs[: len(arrays)], refs[len(arrays) :]
        for source, first, rows, target, start in plan:
            outs[target][start : start + rows, :] = ins[source][first : first + rows, :]

    return call(body, arrays, tuple(((size, width), kind) for size in sizes), after=after, mark=mark, busy=busy)


GROUP = 16
Z_STRIDE, Z_SIZE = 4, 4


def block_rows(block, rows):
    return pl.ds(pl.multiple_of(block * rows, rows), rows)


def fold_kernel(index_ref, *refs):
    ins, outs = refs[:4], refs[4:]
    half = outs[0].shape[0]
    for place, bit in ((0, 2), (1, 1)):
        mine = index_ref[0] // bit % 2
        for out, which in ((outs[2 * place], 1 - mine), (outs[2 * place + 1], mine)):
            rows = block_rows(which, half)
            out[...] = (
                ins[2 * place][rows, :].astype(F32) + ins[2 * place + 1][rows, :].astype(F32)
            ).astype(out.dtype)


def cut_kernel(index_ref, *refs):
    ins, outs = refs[:4], refs[4:]
    rows = ins[0].shape[0] // Z_SIZE
    for place in range(2):
        for step, out in enumerate(outs):
            block = block_rows((index_ref[0] // Z_STRIDE % Z_SIZE) ^ step, rows)
            out[place * rows : (place + 1) * rows, :] = (
                ins[2 * place][block, :] + ins[2 * place + 1][block, :].astype(F32)
            ).astype(out.dtype)


def add_kernel(own_ref, *refs):
    out_ref = refs[-1]
    rows = own_ref.shape[0]
    total = own_ref[...]
    for ref in refs[: Z_SIZE - 1]:
        total = total + ref[...].astype(F32)
    out_ref[:rows, :] = total.astype(out_ref.dtype)
    if out_ref.shape[0] > rows:
        out_ref[rows:, :] = refs[Z_SIZE - 1][...]


def scatter_steps(dealt, place, extra=None):
    first_sent, first_kept, second_sent, second_kept = dealt
    rows, width = first_sent.shape
    after = yield
    arrived = (dp_swap(first_sent, 1), dp_swap(second_sent, 2))
    half = (rows // 2, width)
    first_sent, first_kept, second_sent, second_kept, mark = call(
        fold_kernel,
        (first_kept, arrived[0], second_kept, arrived[1]),
        ((half, BF16), (half, F32), (half, BF16), (half, F32)),
        index=(place,),
        after=after,
        mark=True, busy=1,
    )
    after = yield mark
    arrived = (dp_swap(first_sent, 2), dp_swap(second_sent, 1))
    block = (rows // Z_SIZE, width)
    own, *sent, mark = call(
        cut_kernel,
        (first_kept, arrived[0], second_kept, arrived[1]),
        ((block, F32),) + ((block, BF16),) * (Z_SIZE - 1),
        index=(place,),
        after=after,
        mark=True, busy=1,
    )
    after = yield mark
    arrived = [dp_swap(values, step * Z_STRIDE) for step, values in enumerate(sent, 1)]
    size = lax.axis_size("dp")
    more = 0 if extra is None else extra[0].shape[0]
    if size > GROUP:
        mine, mark = call(
            add_kernel, (own, *arrived), ((own.shape, F32),), after=after, mark=True, busy=1
        )
        groups = [list(range(index, size, GROUP)) for index in range(GROUP)]
        mine = lax.psum(mine, "dp", axis_index_groups=groups).astype(BF16)
        if more:
            mine = jnp.concatenate([mine, *extra], axis=0)
    else:
        mine, mark = call(
            add_kernel,
            (own, *arrived) + (tuple(extra) if more else ()),
            (((block[0] + more, width), BF16),),
            after=after,
            mark=True, busy=1,
        )
    after = yield mark
    high = dp_swap(mine, 2 * Z_STRIDE)
    early = (mine, dp_swap(mine, Z_STRIDE), high)
    late = dp_swap(high, Z_STRIDE)
    half = block[0] // 2
    plan, start = [], 0
    for first, count in ((0, half), (2 * half, more), (half, half)):
        for piece in range(len(early)):
            if count:
                plan.append((piece, first, count, 0, start))
            start += count
    joined, mark = move(early, (start,), plan, after, mark=True, busy=1)
    along_x, along_y = dp_swap(joined, 1), dp_swap(joined, 2)
    late_x, late_y = dp_swap(late, 1), dp_swap(late, 2)
    after = yield mark
    plan = [
        (0, 0, 3 * half, 0, 0),
        (1, 0, half, 0, 3 * half),
        (2, 3 * (half + more), 3 * half, 1, 0),
        (3, half, half, 1, 3 * half),
    ]
    if more:
        plan += [
            (0, 3 * half, 3 * more, 0, 4 * half),
            (1, 2 * half, more, 0, 4 * half + 3 * more),
        ]
    first, second, mark = move(
        (along_y, late_y, along_x, late_x),
        (4 * (half + more), 4 * half),
        plan,
        after,
        mark=True,
        busy=1,
    )
    after = yield mark
    far = (dp_swap(first, 1), dp_swap(second, 2))
    yield (joined, late, along_x, late_x, along_y, late_y, *far)


def block_home(index, block, outer, inner):
    high = (block // 8) ^ (index // outer % 2)
    middle = (block // 4 % 2) ^ (index // inner % 2)
    return high * 8 + middle * 4 + ((block % 4) ^ (index // Z_STRIDE % Z_SIZE))


def relative_blocks(refs, tensor):
    rows = refs[7].shape[0] // Z_SIZE
    more = refs[1].shape[0] - 2 * rows
    for piece, early in enumerate((0, 2, 4) if tensor else (0, 4, 2)):
        for step in range(Z_SIZE):
            if step < Z_SIZE - 1:
                ref, first = refs[early], tensor * 3 * (rows + more) + step * rows
            else:
                ref, first = refs[early + 1], tensor * rows
            yield piece * Z_SIZE + step, rows, ref[first : first + rows, :]
    for step in range(Z_SIZE):
        values = refs[6 + tensor][step * rows : (step + 1) * rows, :]
        yield 3 * Z_SIZE + step, rows, values


def unpack_widen_kernel(index_ref, *refs):
    refs, out_ref = refs[:-1], refs[-1]
    width = out_ref.shape[1] // 2
    for tensor, bits in ((0, (1, 2)), (1, (2, 1))):
        for block, rows, values in relative_blocks(refs, tensor):
            start = pl.multiple_of(block_home(index_ref[0], block, *bits) * rows, rows)
            out_ref[pl.ds(start, rows), tensor * width : (tensor + 1) * width] = values.astype(F32)


def unpack_mixer_kernel(index_ref, *refs):
    refs, (triple_ref, result_ref) = refs[:-2], refs[-2:]
    half, split = triple_ref.shape[2], triple_ref.shape[1] // 2
    for block, rows, values in relative_blocks(refs, 0):
        home = block_home(index_ref[0], block, 1, 2)
        part, row = home // 8, pl.multiple_of(home % 8 * rows, rows)
        triple_ref[part, pl.ds(row, rows), :] = values[:, :half].astype(F32)
        triple_ref[part, pl.ds(split + row, rows), :] = values[:, half:].astype(F32)
    for block, rows, values in relative_blocks(refs, 1):
        home = block_home(index_ref[0], block, 2, 1)
        row = pl.multiple_of(home % 8 * rows, rows)

        @pl.when(home < 8)
        def _():
            triple_ref[2, pl.ds(row, rows), :] = values[:, :half].astype(F32)
            triple_ref[2, pl.ds(split + row, rows), :] = values[:, half:].astype(F32)

        @pl.when(home >= 8)
        def _():
            result_ref[pl.ds(row, rows), :] = values.astype(F32)


def local(
    sentence_layer_entry,
    sentence_word_ids,
    picture_tile_activations,
    picture_detail_flag,
    matched_picture_ids,
    mixer_layernorm_gamma,
    mixer_layernorm_offset,
    mixer_triple_matrix,
    mixer_pair_offsets,
    mixer_result_matrix,
    mixer_result_offset,
    perceptron_layernorm_gamma,
    perceptron_layernorm_offset,
    widening_matrix,
    widening_offset,
    narrowing_matrix,
    narrowing_offset,
    sharpening_log,
    locked_layernorm_gammas,
    locked_mixer_triple_matrix,
    locked_mixer_result_matrix,
    locked_widening_matrix,
    locked_narrowing_matrix,
):
    captions = matched_picture_ids.shape[0]
    tokens, model_width = sentence_layer_entry.shape
    local_width = mixer_result_matrix.shape[0]
    hidden = narrowing_matrix.shape[0]
    devices = lax.axis_size("dp")
    all_pairs = captions * devices
    place, core = lax.axis_index("dp"), lax.axis_index("mp")
    blocks = tokens // BLOCK
    full = (tokens, model_width)
    short = (captions, model_width)
    square = (model_width, model_width)
    half_square = (model_width // 2, model_width)
    dealt = ((half_square, BF16),) * 4

    steps = group_steps(devices)

    image_emb = image_tower(
        picture_detail_flag,
        picture_tile_activations,
        locked_layernorm_gammas,
        locked_mixer_triple_matrix,
        locked_mixer_result_matrix,
        locked_widening_matrix,
        locked_narrowing_matrix,
    )
    normed, qkv, soft, mixed, part, mark = call(
        text_mix_kernel,
        (
            sentence_layer_entry,
            sentence_word_ids,
            mixer_layernorm_gamma,
            mixer_layernorm_offset,
            mixer_triple_matrix,
            mixer_pair_offsets,
            mixer_result_matrix,
        ),
        (
            (full, BF16),
            ((3, tokens, local_width), BF16),
            ((blocks, local_width // PAIR, 2 * BLOCK, BLOCK), F32),
            ((tokens, local_width), BF16),
            (full, F32),
        ),
        after=(image_emb,),
        limit=60,
        mark=True,
    )
    other = mp_other(part)
    near_images = dp_gather(image_emb, steps[:0:-1], [mark] * (len(steps) - 1))
    residual, normed2, slope, hidden_sums, resid_sum, branch = call(
        text_widen_kernel,
        (
            sentence_layer_entry,
            part,
            other,
            mixer_result_offset,
            perceptron_layernorm_gamma,
            perceptron_layernorm_offset,
            widening_offset,
            sentence_word_ids,
        ),
        (
            (full, F32),
            (full, BF16),
            ((tokens, hidden), F32),
            ((captions, hidden), BF16),
            (short, F32),
            (short, F32),
        ),
        outside=(widening_matrix, narrowing_matrix),
        scratch=(pltpu.VMEM((captions, hidden), F32),),
        after=(near_images,),
    )

    near_images = dp_gather(near_images, steps[:1], (branch,))
    sums_parts = dp_parts(hidden_sums, steps[0])
    images, unit, factor, logits, powers, row_sum, col_sum, row_loss = call(
        functools.partial(logits_kernel, gather_masks(steps[::-1])),
        (
            near_images,
            mp_other(near_images),
            resid_sum,
            branch,
            mp_other(branch),
            narrowing_offset,
            sentence_word_ids,
        ),
        (
            ((all_pairs, model_width), BF16),
            (short, F32),
            ((captions, 128), F32),
            ((captions, all_pairs), F32),
            ((captions, all_pairs), F32),
            ((captions, 128), F32),
            ((1, all_pairs), F32),
            ((8, 128), F32),
        ),
        index=(place, core),
        small=(matched_picture_ids, sharpening_log),
    )
    col_parts = dp_parts(col_sum, steps[0])
    for step in steps[1:]:
        (col_sum,) = call(sum_kernel, col_parts, ((col_sum.shape, F32),))
        col_parts = dp_parts(col_sum, step)
    after = (col_sum,)
    for step in steps[2:] + [None]:
        rows = sums_parts[0].shape[0]
        joined_sums, mark = move(
            sums_parts,
            (4 * rows,),
            [(place, 0, rows, 0, place * rows) for place in range(4)],
            after,
            mark=True,
        )
        after = (mark,)
        if step is not None:
            sums_parts = dp_parts(joined_sums, step)
    sums_high = dp_swap(joined_sums, 2 * Z_STRIDE)
    sums_parts = [joined_sums, dp_swap(joined_sums, Z_STRIDE), sums_high]
    sums_parts.append(dp_swap(sums_high, Z_STRIDE))
    grad_caption, grad_caption_low, grad_pre, part, loss_stat = call(
        loss_grad_kernel,
        (
            *col_parts,
            logits,
            powers,
            row_sum,
            unit,
            factor,
            images,
            sentence_word_ids,
            row_loss,
        ),
        (
            (short, F32),
            (short, BF16),
            ((tokens, hidden), BF16),
            (full, F32),
            ((8, model_width), F32),
        ),
        outside=(narrowing_matrix, slope, widening_matrix),
        after=after,
        small=(matched_picture_ids, sharpening_log),
    )

    other = mp_other(part)
    *widen_dealt, mark = call(
        widen_grad_kernel,
        (normed2, grad_pre),
        dealt,
        scratch=(pltpu.VMEM(square, BF16),) * 2,
        index=(place,),
        mark=True,
    )
    grad_residual, grad_branch1, flat, part, mixer_stat = call(
        mixer_back_kernel,
        (
            part,
            other,
            residual,
            grad_caption,
            sentence_word_ids,
            perceptron_layernorm_gamma,
            mixer_result_matrix,
        ),
        (
            (full, F32),
            (full, BF16),
            ((3, tokens, local_width), BF16),
            (full, F32),
            ((8, model_width), F32),
        ),
        outside=(qkv, soft, mixer_triple_matrix),
        after=(mark,),
    )
    other = mp_other(part)
    extra = []
    widen_sum = scatter_steps(widen_dealt, place, extra)
    next(widen_sum)
    *mixer_dealt, mark = call(
        mixer_grad_kernel,
        (normed, flat, mixed, grad_branch1),
        dealt,
        scratch=(pltpu.VMEM(square, BF16),) * 2,
        index=(place,),
        after=sums_parts[1:3],
        mark=True,
    )
    mixer_sum = scatter_steps(mixer_dealt, place)
    next(mixer_sum)
    last = widen_sum.send((mark,))
    last = widen_sum.send((last,))
    extra_rows = captions // 2 + 16
    grad_input, mine = call(
        entry_grad_kernel,
        (
            part,
            other,
            sentence_layer_entry,
            mixer_layernorm_gamma,
            grad_residual,
            loss_stat,
            mixer_stat,
            grad_caption_low,
        ),
        ((full, F32), ((extra_rows, model_width), BF16)),
        scratch=(pltpu.VMEM((16, model_width), F32),),
        index=(core,),
        after=(last,),
    )
    extra.append(dp_gather(mine, steps[:1:-1], [mine] * len(steps)))
    last = mixer_sum.send((mine,))
    last = widen_sum.send((last,))
    last = mixer_sum.send((last,))
    last = widen_sum.send((last,))
    last = mixer_sum.send((last,))
    last = widen_sum.send((last,))
    last = mixer_sum.send((last,))
    widen_pieces = widen_sum.send(())
    near_grads, *results = call(
        functools.partial(collect_kernel, 1.0 / (2.0 * all_pairs), extra_rows),
        (*widen_pieces, loss_stat),
        (
            ((all_pairs // 2, model_width), BF16),
            ((1,), F32),
            ((2, local_width), F32),
            ((model_width,), F32),
            ((hidden,), F32),
        )
        + (((model_width,), F32),) * 5
        + (((1,), F32),),
        after=(last,),
    )
    error, grad_pair, grad_b_out, grad_b_up, grad_b_down = results[:5]
    grad_w_up, mark = call(
        unpack_widen_kernel,
        widen_pieces,
        ((widening_matrix.shape, F32),),
        index=(place,),
        after=(results[0],),
        limit=56,
        mark=True,
    )
    last = mixer_sum.send((mark,))
    grad_w_down, mark = call(
        functools.partial(narrow_grad_kernel, captions // 2),
        (*sums_parts, near_grads, mp_other(near_grads)),
        ((narrowing_matrix.shape, F32),),
        scratch=(
            pltpu.VMEM((all_pairs, model_width), BF16),
            pltpu.VMEM((all_pairs, hidden), BF16),
        ),
        index=(core,),
        after=(last,),
        mark=True,
    )
    grad_qkv, grad_w_out = call(
        unpack_mixer_kernel,
        mixer_sum.send(()),
        ((mixer_triple_matrix.shape, F32), (mixer_result_matrix.shape, F32)),
        index=(place,),
        after=(mark,),
        limit=56,
    )
    return (
        error,
        grad_input,
        grad_qkv,
        grad_pair,
        grad_w_out,
        grad_b_out,
        grad_w_up,
        grad_b_up,
        grad_w_down,
        grad_b_down,
        *results[5:],
    )


def solution(mesh):
    placed = (
        P("dp", None),
        P("dp"),
        P(("dp", "mp"), None, None),
        P(("dp", "mp")),
        P("dp"),
        P(),
        P(),
        P(None, None, "mp"),
        P(None, "mp"),
        P("mp", None),
        P(),
        P(),
        P(),
        P(None, "mp"),
        P("mp"),
        P("mp", None),
        P(),
        P(),
        P(),
        P(),
        P(),
        P(),
        P(),
    )
    return jax.shard_map(
        local,
        mesh=mesh,
        in_specs=placed,
        out_specs=(
            P(),
            P("dp", None),
            P(None, None, "mp"),
            P(None, "mp"),
            P("mp", None),
            P(),
            P(None, "mp"),
            P("mp"),
            P("mp", None),
            P(),
            P(),
            P(),
            P(),
            P(),
            P(),
        ),
        check_vma=False,
    )
```
